32 devices in a mesh: groups: 2 (over x), cache: 16 (over z, y, core).
Axes of the slice: x: 2, y: 2, z: 4, core: 2. Of those that a mesh axis runs over, the one named last changes fastest.
Arguments:
- prefix_len: int32 [32], P('groups'), parts along dimension 0, may hold values from 128 to 1024, as said below
- hits: int32 [32, 1], P('groups'), parts along dimension 0, may hold values from 0 to 15, as said below
- span_block: int32 [32, 16], P('groups'), parts along dimension 0, may hold values from 0 to 15, each once within a row
- queries: bfloat16 [2048, 2048], P(('groups', 'cache')), parts along dimension 0, may hold values from -100 to 100
- fresh_keys: bfloat16 [2048, 128], P(('groups', 'cache')), parts along dimension 0, may hold values from -4 to 4
- fresh_values: bfloat16 [2048, 128], P(('groups', 'cache')), parts along dimension 0, may hold values from -4 to 4
- cache_keys: bfloat16 [65536, 128], P(('groups', 'cache')), parts along dimension 0, may hold values from -4 to 4
- cache_values: bfloat16 [65536, 128], P(('groups', 'cache')), parts along dimension 0, may hold values from -4 to 4
Outputs:
- attended: bfloat16 [2048, 2048], P(('groups', 'cache')), parts along dimension 0
The draws below stay inside these ranges and needn't reach their ends.
There are 2 independent parts, one for each index of `groups`. The reference program is written for one: setup_inputs(seed, part) draws one part's arguments, and reference() takes and returns one part's arrays. A program takes and returns all parts, laid end to end along the dimension named above; each array names one. Nothing has to cross between parts.
Inputs may be any that keep to these rules, and one draw needn't show every extreme that they name: `prefix_len`: every request's prefix holds at least 128 tokens, and one request in every draw holds exactly 1024. `hits`: each row names 1 different devices. Each device is named by at most 2 requests; 4 devices are named by exactly 2, half of them by one, a quarter by none. `span_block`: each row is a permutation.
All inputs are finite; a program needn't handle non-finite values.
Results may differ from the reference program's by a relative error of at most 0.0065.
Values may be sent and summed in bfloat16 or wider, within the bound.
No kernel may reach another device: no remote copies, remote signals or barrier semaphores. Data moves between devices by JAX's collectives and lax.ppermute only.
A program may use at most 64 MiB of HBM per device.

```python
import jax
import jax.numpy as jnp
from jax import lax

HEADS = 16
HD = 128
PAGE = 128
CAP = 2
REQUESTS = 16
TOK_REQ = 4
PAGES_DEV = 16
HITS = 1
TOKENS = 1024
CACHE_ROWS = 32768
PREFIX = 1024
N_CACHE = 16


def hit_table(key):
    seeded = jax.random.fold_in(key, 101)
    shuffled = jax.random.permutation(jax.random.fold_in(seeded, 1), N_CACHE)
    doubled = N_CACHE // 4
    listing = jnp.concatenate([shuffled[:N_CACHE - doubled], shuffled[:doubled]]).reshape(REQUESTS, HITS)
    row_order = jax.random.permutation(jax.random.fold_in(seeded, 2), REQUESTS)
    listing = jnp.take(listing, row_order, axis=0)
    row_keys = jax.random.split(jax.random.fold_in(seeded, 3), REQUESTS)

    def one_order(row_key):
        return jax.random.permutation(row_key, HITS)
    col_order = jax.vmap(one_order)(row_keys)
    return jnp.take_along_axis(listing, col_order, axis=1).astype(jnp.int32)


def paired_table(key, count, salt):
    drawn_values = jax.random.normal(jax.random.fold_in(key, salt + 2), (count, HD), jnp.float32)
    return jnp.clip(drawn_values, -4.0, 4.0)


def draw_prefix_len(key, part):
    lengths = jax.random.randint(jax.random.fold_in(key, 202), (REQUESTS,), PREFIX // 8, PREFIX + 1)
    longest = jax.random.randint(jax.random.fold_in(key, 203), (), 0, REQUESTS)
    return lengths.at[longest].set(PREFIX).astype(jnp.int32)


def draw_hits(key, part):
    return hit_table(key)


def draw_fresh_keys(key, part):
    return paired_table(key, TOKENS, 301).astype(jnp.bfloat16)


def draw_cache_keys(key, part):
    return paired_table(key, CACHE_ROWS, 311).astype(jnp.bfloat16)


def draw_queries(key, part):
    drawn_values = jnp.clip(jax.random.normal(jax.random.fold_in(key, 402), (TOKENS, HEADS, HD), jnp.float32), -4.0, 4.0)
    return drawn_values.reshape(TOKENS, HEADS * HD).astype(jnp.bfloat16)


def level_of(stream_key, shape, cuts, low, top_value):
    loudness, own = 1.0, jax.random.fold_in(stream_key, 6)
    for axis_at, blocks in cuts:
        steps = jnp.exp(jax.random.uniform(jax.random.fold_in(own, axis_at), (blocks,), jnp.float32, low / len(cuts), top_value / len(cuts)))
        loudness = loudness * jnp.repeat(steps, shape[axis_at] // blocks).reshape([-1 if axis == axis_at else 1 for axis in range(len(shape))])
    return loudness


def normal_values(key, shape, scale, most, pieces=(), held_as=jnp.bfloat16):
    values = scale * jax.random.normal(key, shape, jnp.float32)
    if pieces:
        values = values * level_of(key, shape, pieces, -0.22, 0.18)
    return jnp.clip(values, -most, most).astype(held_as)


def setup_inputs(seed: int = 0, part: int = 0) -> dict:
    keys = jax.random.split(jax.random.key(seed), 9)
    part_keys = jax.random.split(jax.random.fold_in(keys[8], part), 9)
    prefix_len = draw_prefix_len(jax.random.fold_in(jax.random.fold_in(keys[8], part), 71), part)
    hits = draw_hits(jax.random.fold_in(jax.random.fold_in(keys[8], part), 71), part)
    span_block = jax.vmap(lambda own: jax.random.permutation(own, N_CACHE))(jax.random.split(part_keys[2], REQUESTS)).reshape((REQUESTS, N_CACHE)).astype(jnp.int32)
    queries = draw_queries(jax.random.fold_in(jax.random.fold_in(keys[8], part), 71), part)
    fresh_keys = draw_fresh_keys(jax.random.fold_in(jax.random.fold_in(keys[8], part), 71), part)
    fresh_values = normal_values(part_keys[5], (TOKENS, HD), 1.0, 4.0, ((0, 16),))
    cache_keys = draw_cache_keys(jax.random.fold_in(jax.random.fold_in(keys[8], part), 71), part)
    cache_values = normal_values(part_keys[7], (CACHE_ROWS, HD), 1.0, 4.0, ((0, 16),))
    return {"prefix_len": prefix_len, "hits": hits, "span_block": span_block, "queries": queries, "fresh_keys": fresh_keys, "fresh_values": fresh_values, "cache_keys": cache_keys, "cache_values": cache_values}


floor_score = -1e30


def attend(query_rows, key_rows, value_rows, visible, rounding):
    scale = HD ** -0.5
    scores = jnp.einsum("qhd,kd->qhk", query_rows, key_rows, precision=lax.Precision.HIGHEST) * scale
    scores = jnp.where(visible[:, None, :], scores, floor_score)
    maxima = jnp.max(scores, axis=2)
    weights = jnp.exp(scores - maxima[:, :, None]) * visible[:, None, :]
    totals = jnp.sum(weights, axis=2)
    if rounding:
        weights = lax.optimization_barrier(weights.astype(jnp.bfloat16)).astype(jnp.float32)
    summed = jnp.einsum("qhk,kd->qhd", weights, value_rows, precision=lax.Precision.HIGHEST)
    return maxima, totals, summed


def reference(prefix_len, hits, span_block, queries, fresh_keys, fresh_values, cache_keys, cache_values):
    region = (PAGES_DEV // CAP) * PAGE
    per_device = REQUESTS * TOK_REQ
    matches = jnp.any(hits[:, :, None, None] == hits[None, None, :, :], axis=3)
    earlier = jnp.arange(REQUESTS)[None, None, :] < jnp.arange(REQUESTS)[:, None, None]
    slot_rank = jnp.sum(matches & earlier, axis=2).astype(jnp.int32)
    offsets = jnp.arange(TOK_REQ, dtype=jnp.int32)
    devices = jnp.arange(N_CACHE, dtype=jnp.int32)
    spots = jnp.arange(region, dtype=jnp.int32)

    def one_request(request):
        row_index = (devices[:, None] * per_device + request * TOK_REQ + offsets[None, :]).reshape(-1).astype(jnp.int32)
        query_rows = jnp.take(queries, row_index, axis=0).astype(jnp.float32).reshape(-1, HEADS, HD)
        key_rows = jnp.take(fresh_keys, row_index, axis=0).astype(jnp.float32)
        value_rows = jnp.take(fresh_values, row_index, axis=0).astype(jnp.float32)
        positions = (span_block[request][:, None] * TOK_REQ + offsets[None, :]).reshape(-1)
        causal = positions[None, :] <= positions[:, None]
        maxima, totals, summed = attend(query_rows, key_rows, value_rows, causal, False)
        prompt_out = summed / totals[:, :, None]
        prompt_lse = maxima + jnp.log(totals)

        def one_owner(which):
            owner = hits[request, which]
            start = (owner * PAGES_DEV * PAGE + slot_rank[request, which] * region).astype(jnp.int32)
            page_keys = lax.dynamic_slice_in_dim(cache_keys, start, region, 0).astype(jnp.float32)
            page_values = lax.dynamic_slice_in_dim(cache_values, start, region, 0).astype(jnp.float32)
            visible = ((which * region + spots) < prefix_len[request])[None, :]
            owner_max, owner_total, owner_sum = attend(query_rows, page_keys, page_values, visible, True)
            owner_total = jnp.maximum(owner_total, 1.0)
            owner_out = (owner_sum / owner_total[:, :, None]).astype(jnp.bfloat16)
            return owner_out, owner_max + jnp.log(owner_total)

        owner_out, owner_lse = lax.map(one_owner, jnp.arange(HITS, dtype=jnp.int32))
        owner_wide = lax.optimization_barrier(owner_out).astype(jnp.float32)
        every_lse = jnp.concatenate([prompt_lse[None], owner_lse], axis=0)
        highest = jnp.max(every_lse, axis=0)
        shares = jnp.exp(every_lse - highest[None])
        combined = shares[0][:, :, None] * prompt_out + jnp.sum(shares[1:][:, :, :, None] * owner_wide, axis=0)
        result = combined / jnp.sum(shares, axis=0)[:, :, None]
        return result.astype(jnp.bfloat16).reshape(N_CACHE, TOK_REQ, HEADS * HD)

    blocks = lax.map(one_request, jnp.arange(REQUESTS, dtype=jnp.int32))
    return jnp.transpose(blocks, (1, 0, 2, 3)).reshape(N_CACHE * per_device, HEADS * HD)
```

```python
import functools
import math

import jax
import jax.numpy as jnp
from jax import lax
from jax.experimental import pallas as pl
from jax.experimental.pallas import tpu as pltpu
from jax.sharding import PartitionSpec as P

HEADS = 16
HD = 128
PAGE = 128
CAP = 2
REQUESTS = 16
TOK_REQ = 4
PAGES_DEV = 16

REGION = PAGES_DEV // CAP * PAGE
HALF = HEADS // 2
MSG = 2 * TOK_REQ
WIDE = HALF * HD
ROWS = REQUESTS * TOK_REQ
SCALE = HD**-0.5
FLOOR = -1e30
NT = (((1,), (1,)), ((), ()))
NN = (((1,), (0,)), ((), ()))
TN = (((0,), (0,)), ((), ()))


def iota(shape, axis):
    return lax.broadcasted_iota(jnp.int32, shape, axis)


def dot(a, b, dims, **kw):
    return lax.dot_general(a, b, dims, preferred_element_type=jnp.float32, **kw)


def pack_kernel(devices, hit_count, hits, q, k, v, *refs):
    sends, places, held, count = refs[:CAP], refs[CAP], refs[CAP + 1], refs[CAP + 2]
    held[:ROWS, :WIDE] = q[:, :WIDE]
    held[ROWS:, :WIDE] = q[:, WIDE:]
    held[:ROWS, WIDE:] = k[...]
    held[ROWS:, WIDE:] = v[...]
    lane = iota((1, 2 * ROWS), 1)
    lane_request = (lane % ROWS) // TOK_REQ
    for r in range(REQUESTS):
        for i in range(hit_count):
            count[hits[r, i]] = 0
    rows = [[jnp.full((1, 2 * ROWS), -4 * MSG, jnp.int32)] * hit_count for _ in range(CAP)]
    for r in range(REQUESTS):
        for i in range(hit_count):
            owner = hits[r, i]
            rank = count[owner]
            count[owner] = rank + 1
            for s in range(CAP):
                place = jnp.where(rank == s, owner * MSG, -4 * MSG)
                rows[s][i] = jnp.where(lane_request == r, place, rows[s][i])
    inner = lane // ROWS * TOK_REQ + lane % TOK_REQ
    target = iota((devices * MSG, 2 * ROWS), 0)
    for s in range(CAP):
        chosen = None
        for i in range(hit_count):
            row = rows[s][i] + inner
            places[s * hit_count + i : s * hit_count + i + 1, :] = row
            hit = target == row
            chosen = hit if chosen is None else chosen | hit
        chosen = jnp.where(chosen, 1.0, 0.0).astype(jnp.bfloat16)
        sends[s][...] = dot(chosen, held[...], NN).astype(jnp.bfloat16)


def attend_kernel(
    slot, devices, hit_count, hits, prefix_len, span, got, keys, values, *refs
):
    if hit_count > 1:
        out, lse = refs[:2]
        refs = refs[2:]
    else:
        out, lse = refs[0], None
        refs = refs[1:]
    key_rows, value_rows, sems = refs
    copies = [
        pltpu.make_async_copy(keys.at[pl.ds(slot * REGION, REGION)], key_rows, sems.at[0]),
        pltpu.make_async_copy(
            values.at[pl.ds(slot * REGION, REGION)], value_rows.at[:, pl.ds(0, HD)], sems.at[1]
        ),
    ]
    for copy in copies:
        copy.start()
    value_rows[:, HD:] = jnp.ones((REGION, HD), jnp.bfloat16)
    me = lax.axis_index("cache")
    seen = jnp.int32(0)
    request = jnp.int32(0)
    which = jnp.int32(0)
    for r in range(REQUESTS):
        for i in range(hit_count):
            mine = hits[r, i] == me
            here = mine & (seen == slot)
            request = jnp.where(here, r, request)
            which = jnp.where(here, i, which)
            seen = seen + mine.astype(jnp.int32)
    occupied = seen > slot
    limit = prefix_len[request] - which * REGION
    for copy in copies:
        copy.wait()

    @pl.when(jnp.logical_not(occupied))
    def _():
        out[...] = jnp.zeros(out.shape, out.dtype)
        if lse is not None:
            lse[...] = jnp.zeros(lse.shape, lse.dtype)

    @pl.when(occupied)
    def _():
        total_rows = devices * MSG
        span_row = span[pl.ds(request, 1), :].astype(jnp.float32)
        source = iota((devices, total_rows), 0)
        spread = (iota((devices, total_rows), 1) // MSG == source).astype(jnp.float32)
        spans = jnp.broadcast_to(span_row, (16, devices)).astype(jnp.bfloat16)
        key_span = dot(spans, spread.astype(jnp.bfloat16), NN)[:1]
        lane = iota((1, total_rows), 1)
        key_spot = key_span.astype(jnp.int32) * TOK_REQ + lane % TOK_REQ
        is_key = lane % MSG < TOK_REQ
        if hit_count > 1:
            is_key = is_key & (which == 0)
        key_spot = jnp.where(is_key, key_spot, devices * TOK_REQ)
        prompt_keys = got[:, WIDE:]
        moved = pltpu.roll(prompt_keys.astype(jnp.float32), total_rows - TOK_REQ, 0)
        prompt_values = jnp.concatenate(
            [moved.astype(jnp.bfloat16), jnp.ones((total_rows, HD), jnp.bfloat16)], axis=1
        )
        cached_bias = jnp.where(iota((1, REGION), 1) < limit, 0.0, FLOOR)
        block = 16 * MSG

        def one_block(at):
            row = iota((block, devices), 0)
            row_source = at * 16 + row // MSG
            mine = iota((block, devices), 1) == row_source
            row_span = jnp.sum(jnp.where(mine, span_row, 0.0), axis=1, keepdims=True)
            row_spot = row_span.astype(jnp.int32) * TOK_REQ + iota((block, 1), 0) % TOK_REQ
            prompt_bias = jnp.where(key_spot <= row_spot, 0.0, FLOOR)
            prompt_bias = jnp.concatenate([prompt_bias, prompt_bias], axis=0)
            here = pl.ds(pl.multiple_of(at * block, block), block)
            lane_id = iota((block, HD), 1)
            logs = jnp.zeros((block, HD), jnp.float32)
            for c in range(0, HALF, 2):
                pair = jnp.concatenate(
                    [got[here, c * HD : (c + 1) * HD], got[here, (c + 1) * HD : (c + 2) * HD]],
                    axis=0,
                )
                cached = dot(pair, key_rows[...], NT) + cached_bias
                prompt = dot(pair, prompt_keys, NT) + prompt_bias
                top = jnp.maximum(
                    jnp.max(cached, axis=1, keepdims=True), jnp.max(prompt, axis=1, keepdims=True)
                )
                if hit_count > 1:
                    top = jnp.maximum(top, 0.1 * FLOOR)
                factor = SCALE * math.log2(math.e)
                cached = jnp.exp2((cached - top) * factor).astype(jnp.bfloat16)
                prompt = jnp.exp2((prompt - top) * factor).astype(jnp.bfloat16)
                summed = dot(cached, value_rows[...], NN) + dot(prompt, prompt_values, NN)
                totals = summed[:, HD:]
                if hit_count > 1:
                    totals = jnp.maximum(totals, 1.0)
                    level = top * SCALE + jnp.log(totals)
                    logs = jnp.where(lane_id == c, level[:block], logs)
                    logs = jnp.where(lane_id == c + 1, level[block:], logs)
                result = (summed[:, :HD] / totals).astype(jnp.bfloat16)
                out[here, c * HD : (c + 1) * HD] = result[:block]
                out[here, (c + 1) * HD : (c + 2) * HD] = result[block:]
            if lse is not None:
                lse[here, :] = logs

        blocks = devices // 16
        if blocks == 1:
            one_block(0)
        else:

            @pl.loop(0, blocks)
            def _(at):
                one_block(at)


def unpack_kernel(devices, hit_count, places, *refs):
    outs, logs, result = refs[:CAP], refs[CAP:-1], refs[-1]
    target = iota((devices * MSG, 2 * ROWS), 0)

    def chosen(s, i, dtype):
        place = s * hit_count + i
        return jnp.where(target == places[place : place + 1, :], 1.0, 0.0).astype(dtype)

    def rows_of(i):
        parts = [dot(chosen(s, i, jnp.bfloat16), outs[s][...], TN) for s in range(CAP)]
        return sum(parts[1:], parts[0])

    def logs_of(i):
        parts = [
            dot(chosen(s, i, jnp.float32), logs[s][...], TN, precision=lax.Precision.HIGHEST)
            for s in range(CAP)
        ]
        return sum(parts[1:], parts[0])

    if hit_count == 1:
        joined = rows_of(0)
    else:
        levels = [logs_of(i) for i in range(hit_count)]
        top = functools.reduce(jnp.maximum, levels)
        shares = [jnp.exp(level - top) for level in levels]
        total = sum(shares[1:], shares[0])
        pieces = [rows_of(i) for i in range(hit_count)]
        columns = []
        for c in range(HALF):
            part = sum(
                shares[i][:, c : c + 1] * pieces[i][:, c * HD : (c + 1) * HD]
                for i in range(hit_count)
            )
            columns.append(part / total[:, c : c + 1])
        joined = jnp.concatenate(columns, axis=1)
    joined = joined.astype(jnp.bfloat16)
    result[:, :WIDE] = joined[:ROWS]
    result[:, WIDE:] = joined[ROWS:]


def vmem(count):
    return [pl.BlockSpec(memory_space=pltpu.VMEM)] * count


def smem(count):
    return [pl.BlockSpec(memory_space=pltpu.SMEM)] * count


def body(prefix_len, hits, span_block, queries, fresh_keys, fresh_values, cache_keys, cache_values):
    devices = lax.axis_size("cache")
    hit_count = hits.shape[1]
    rows = devices * MSG
    params = pltpu.CompilerParams(vmem_limit_bytes=40 * 2**20)
    message = jax.ShapeDtypeStruct((rows, WIDE + HD), jnp.bfloat16)
    answer = jax.ShapeDtypeStruct((rows, WIDE), jnp.bfloat16)
    level = jax.ShapeDtypeStruct((rows, HD), jnp.float32)

    def exchange(x):
        return lax.all_to_all(x, "cache", split_axis=0, concat_axis=0, tiled=True)

    *sends, places = pl.pallas_call(
        functools.partial(pack_kernel, devices, hit_count),
        out_shape=[message] * CAP
        + [jax.ShapeDtypeStruct((CAP * hit_count, 2 * ROWS), jnp.int32)],
        in_specs=smem(1) + vmem(3),
        out_specs=vmem(CAP + 1),
        scratch_shapes=[
            pltpu.VMEM((2 * ROWS, WIDE + HD), jnp.bfloat16),
            pltpu.SMEM((devices,), jnp.int32),
        ],
        compiler_params=params,
        name="pack",
    )(hits, queries, fresh_keys, fresh_values)
    got = [exchange(x) for x in sends]
    pairs = rows * HALF * (REGION + rows)
    answers = []
    for slot in range(CAP):
        answers.append(
            pl.pallas_call(
                functools.partial(attend_kernel, slot, devices, hit_count),
                out_shape=[answer] + [level] * (hit_count > 1),
                in_specs=smem(2) + vmem(2) + [pl.BlockSpec(memory_space=pl.ANY)] * 2,
                out_specs=vmem(1 + (hit_count > 1)),
                scratch_shapes=[
                    pltpu.VMEM((REGION, HD), jnp.bfloat16),
                    pltpu.VMEM((REGION, 2 * HD), jnp.bfloat16),
                    pltpu.SemaphoreType.DMA((2,)),
                ],
                compiler_params=params,
                cost_estimate=pl.CostEstimate(
                    flops=4 * pairs * HD, bytes_accessed=4 * rows * WIDE, transcendentals=pairs
                ),
                name="attend",
            )(hits, prefix_len, span_block, got[slot], cache_keys, cache_values)
        )
    returned = [exchange(a[0]) for a in answers] + [exchange(a[1]) for a in answers if len(a) > 1]
    return pl.pallas_call(
        functools.partial(unpack_kernel, devices, hit_count),
        out_shape=jax.ShapeDtypeStruct((ROWS, HEADS * HD), jnp.bfloat16),
        in_specs=vmem(1 + len(returned)),
        out_specs=vmem(1)[0],
        compiler_params=params,
        name="unpack",
    )(places, *returned)


def solution(mesh):
    in_specs = (
        P("groups"),
        P("groups", None),
        P("groups", None),
        P(("groups", "cache"), None),
        P(("groups", "cache"), None),
        P(("groups", "cache"), None),
        P(("groups", "cache"), None),
        P(("groups", "cache"), None),
    )
    out_specs = P(("groups", "cache"), None)
    return jax.shard_map(body, mesh=mesh, in_specs=in_specs, out_specs=out_specs, check_vma=False)
```

```python
import functools
import math

import jax
import jax.numpy as jnp
from jax import lax
from jax.experimental import pallas as pl
from jax.experimental.pallas import tpu as pltpu
from jax.sharding import PartitionSpec as P

HEADS = 16
HD = 128
PAGE = 128
CAP = 2
REQUESTS = 16
TOK_REQ = 4
PAGES_DEV = 16

REGION = PAGES_DEV // CAP * PAGE
HALF = HEADS // 2
MSG = 2 * TOK_REQ
WIDE = HALF * HD
ROWS = REQUESTS * TOK_REQ
SCALE = HD**-0.5
FLOOR = -1e30
NT = (((1,), (1,)), ((), ()))
NN = (((1,), (0,)), ((), ()))
TN = (((0,), (0,)), ((), ()))


def iota(shape, axis):
    return lax.broadcasted_iota(jnp.int32, shape, axis)


def dot(a, b, dims, **kw):
    return lax.dot_general(a, b, dims, preferred_element_type=jnp.float32, **kw)


def pack_kernel(devices, hit_count, hits, q, k, v, send, places, held, count, sems):
    copies = [
        pltpu.make_async_copy(source, held.at[pl.ds(row, ROWS), pl.ds(column, width)], sems.at[n])
        for n, (source, row, column, width) in enumerate(
            [
                (q.at[:, pl.ds(0, WIDE)], 0, 0, WIDE),
                (q.at[:, pl.ds(WIDE, WIDE)], ROWS, 0, WIDE),
                (k, 0, WIDE, HD),
                (v, ROWS, WIDE, HD),
            ]
        )
    ]
    for copy in copies:
        copy.start()
    lane = iota((1, 2 * ROWS), 1)
    lane_request = (lane % ROWS) // TOK_REQ
    for r in range(REQUESTS):
        for i in range(hit_count):
            count[hits[r * hit_count + i]] = 0
    rows = [[jnp.full((1, 2 * ROWS), -4 * MSG, jnp.int32)] * hit_count for _ in range(CAP)]
    for r in range(REQUESTS):
        for i in range(hit_count):
            owner = hits[r * hit_count + i]
            rank = count[owner]
            count[owner] = rank + 1
            for s in range(CAP):
                place = jnp.where(rank == s, owner * MSG, -4 * MSG)
                rows[s][i] = jnp.where(lane_request == r, place, rows[s][i])
    inner = lane // ROWS * TOK_REQ + lane % TOK_REQ
    target = iota((devices * MSG, 2 * ROWS), 0)
    picks = []
    for s in range(CAP):
        chosen = None
        for i in range(hit_count):
            row = rows[s][i] + inner
            places[s * hit_count + i : s * hit_count + i + 1, :] = row
            hit = target == row
            chosen = hit if chosen is None else chosen | hit
        picks.append(jnp.where(chosen, 1.0, 0.0).astype(jnp.bfloat16))
    for copy in copies:
        copy.wait()
    for s in range(CAP):
        here = slice(s * (WIDE + HD), (s + 1) * (WIDE + HD))
        send[:, here] = dot(picks[s], held[...], NN).astype(jnp.bfloat16)


def prep_kernel(devices, hit_count, hits, prefix_len, span, values, busy, prompt, cached, wide):
    me = lax.axis_index("cache")
    total_rows = devices * MSG
    wide[:, :HD] = values[...]
    wide[:, HD:] = jnp.ones((CAP * REGION, HD), jnp.bfloat16)
    for slot in range(CAP):
        seen = jnp.int32(0)
        request = jnp.int32(0)
        which = jnp.int32(0)
        for r in range(REQUESTS):
            for i in range(hit_count):
                mine = hits[r * hit_count + i] == me
                here = mine & (seen == slot)
                request = jnp.where(here, r, request)
                which = jnp.where(here, i, which)
                seen = seen + mine.astype(jnp.int32)
        busy[slot] = (seen > slot).astype(jnp.int32)
        limit = prefix_len[request] - which * REGION
        cached[slot : slot + 1, :] = jnp.where(iota((1, REGION), 1) < limit, 0.0, FLOOR)
        span_row = span[pl.ds(request, 1), :].astype(jnp.float32)
        source = iota((devices, total_rows), 0)
        spread = (iota((devices, total_rows), 1) // MSG == source).astype(jnp.bfloat16)
        spans = jnp.broadcast_to(span_row, (16, devices)).astype(jnp.bfloat16)
        key_span = dot(spans, spread, NN)[:1]
        lane = iota((1, total_rows), 1)
        key_spot = key_span.astype(jnp.int32) * TOK_REQ + lane % TOK_REQ
        is_key = lane % MSG < TOK_REQ
        if hit_count > 1:
            is_key = is_key & (which == 0)
        key_spot = jnp.where(is_key, key_spot, devices * TOK_REQ)
        block = 16 * MSG

        def one_block(at):
            row_source = at * 16 + iota((block, devices), 0) // MSG
            mine = iota((block, devices), 1) == row_source
            row_span = jnp.sum(jnp.where(mine, span_row, 0.0), axis=1, keepdims=True)
            row_spot = row_span.astype(jnp.int32) * TOK_REQ + iota((block, 1), 0) % TOK_REQ
            here = pl.ds(slot * total_rows + at * block, block)
            prompt[here, :] = jnp.where(key_spot <= row_spot, 0.0, FLOOR)

        each_block(devices, one_block)


def each_block(devices, one_block):
    blocks = devices // 16
    if blocks == 1:
        one_block(0)
    else:
        pl.loop(0, blocks)(one_block)


def attend_kernel(devices, hit_count, busy, prompt_mask, cached_mask, got, keys, wide, out, *levels):
    total_rows = devices * MSG
    block = 16 * MSG
    factor = SCALE * math.log2(math.e)
    for slot in range(CAP):
        base = slot * (WIDE + HD)
        region = slice(slot * REGION, (slot + 1) * REGION)
        first = slot * WIDE

        @pl.when(busy[slot] == 0)
        def _():
            out[:, first : first + WIDE] = jnp.zeros((total_rows, WIDE), jnp.bfloat16)
            for lse in levels:
                lse[:, slot * HD : (slot + 1) * HD] = jnp.zeros((total_rows, HD), jnp.float32)

        @pl.when(busy[slot] != 0)
        def _():
            prompt_keys = got[:, base + WIDE : base + WIDE + HD]
            moved = pltpu.roll(prompt_keys.astype(jnp.float32), total_rows - TOK_REQ, 0)
            prompt_values = jnp.concatenate(
                [moved.astype(jnp.bfloat16), jnp.ones((total_rows, HD), jnp.bfloat16)], axis=1
            )

            def one_block(at):
                here = pl.ds(at * block, block)
                prompt_bias = prompt_mask[pl.ds(slot * total_rows + at * block, block), :]
                prompt_bias = jnp.concatenate([prompt_bias, prompt_bias], axis=0)
                lane = iota((block, HD), 1)
                logs = jnp.zeros((block, HD), jnp.float32)
                for c in range(0, HALF, 2):
                    at_c = [base + (c + n) * HD for n in range(2)]
                    pair = jnp.concatenate([got[here, n : n + HD] for n in at_c], axis=0)
                    cached = dot(pair, keys[region, :], NT) + cached_mask[slot : slot + 1, :]
                    prompt = dot(pair, prompt_keys, NT) + prompt_bias
                    top = jnp.maximum(
                        jnp.max(cached, axis=1, keepdims=True),
                        jnp.max(prompt, axis=1, keepdims=True),
                    )
                    if hit_count > 1:
                        top = jnp.maximum(top, 0.1 * FLOOR)
                    cached = jnp.exp2((cached - top) * factor).astype(jnp.bfloat16)
                    prompt = jnp.exp2((prompt - top) * factor).astype(jnp.bfloat16)
                    summed = dot(cached, wide[region, :], NN) + dot(prompt, prompt_values, NN)
                    totals = summed[:, HD:]
                    if hit_count > 1:
                        totals = jnp.maximum(totals, 1.0)
                        level = top * SCALE + jnp.log(totals)
                        logs = jnp.where(lane == c, level[:block], logs)
                        logs = jnp.where(lane == c + 1, level[block:], logs)
                    result = (summed[:, :HD] / totals).astype(jnp.bfloat16)
                    for n in range(2):
                        column = first + (c + n) * HD
                        out[here, column : column + HD] = result[n * block : (n + 1) * block]
                for lse in levels:
                    lse[here, slot * HD : (slot + 1) * HD] = logs

            each_block(devices, one_block)


def unpack_kernel(devices, hit_count, places, *refs):
    outs, logs, result = refs[0], refs[1:-1], refs[-1]
    target = iota((devices * MSG, 2 * ROWS), 0)

    def chosen(s, i, dtype):
        place = s * hit_count + i
        return jnp.where(target == places[place : place + 1, :], 1.0, 0.0).astype(dtype)

    def rows_of(i):
        parts = [
            dot(chosen(s, i, jnp.bfloat16), outs[:, s * WIDE : (s + 1) * WIDE], TN)
            for s in range(CAP)
        ]
        return sum(parts[1:], parts[0])

    def logs_of(i):
        parts = [
            dot(
                chosen(s, i, jnp.float32),
                logs[0][:, s * HD : (s + 1) * HD],
                TN,
                precision=lax.Precision.HIGHEST,
            )
            for s in range(CAP)
        ]
        return sum(parts[1:], parts[0])

    if hit_count == 1:
        joined = rows_of(0)
    else:
        levels = [logs_of(i) for i in range(hit_count)]
        top = functools.reduce(jnp.maximum, levels)
        shares = [jnp.exp(level - top) for level in levels]
        total = sum(shares[1:], shares[0])
        pieces = [rows_of(i) for i in range(hit_count)]
        columns = []
        for c in range(HALF):
            part = sum(
                shares[i][:, c : c + 1] * pieces[i][:, c * HD : (c + 1) * HD]
                for i in range(hit_count)
            )
            columns.append(part / total[:, c : c + 1])
        joined = jnp.concatenate(columns, axis=1)
    joined = joined.astype(jnp.bfloat16)
    result[:, :WIDE] = joined[:ROWS]
    result[:, WIDE:] = joined[ROWS:]


def vmem(count):
    return [pl.BlockSpec(memory_space=pltpu.VMEM)] * count


def smem(count):
    return [pl.BlockSpec(memory_space=pltpu.SMEM)] * count


def hbm(count):
    return [pl.BlockSpec(memory_space=pltpu.HBM)] * count


def body(prefix_len, hits, span_block, queries, fresh_keys, fresh_values, cache_keys, cache_values):
    devices = lax.axis_size("cache")
    hit_count = hits.shape[1]
    rows = devices * MSG
    owners = hits.reshape(REQUESTS * hit_count)

    def exchange(x):
        return lax.all_to_all(x, "cache", split_axis=0, concat_axis=0, tiled=True)

    def call(kernel, out_shape, name, grant=40, **kw):
        return pl.pallas_call(
            functools.partial(kernel, devices, hit_count),
            out_shape=[jax.ShapeDtypeStruct(*leaf) for leaf in out_shape],
            compiler_params=pltpu.CompilerParams(vmem_limit_bytes=grant * 2**20),
            name=name,
            **kw,
        )

    send, places = call(
        pack_kernel,
        [((rows, CAP * (WIDE + HD)), jnp.bfloat16), ((CAP * hit_count, 2 * ROWS), jnp.int32)],
        "pack",
        grant=60,
        in_specs=smem(1) + hbm(3),
        out_specs=vmem(2),
        scratch_shapes=[
            pltpu.VMEM((2 * ROWS, WIDE + HD), jnp.bfloat16),
            pltpu.SMEM((devices,), jnp.int32),
            pltpu.SemaphoreType.DMA((4,)),
        ],
    )(owners, queries, fresh_keys, fresh_values)
    got = exchange(send)
    busy, prompt_mask, cached_mask, wide = call(
        prep_kernel,
        [
            ((CAP,), jnp.int32),
            ((CAP * rows, rows), jnp.float32),
            ((CAP, REGION), jnp.float32),
            ((CAP * REGION, 2 * HD), jnp.bfloat16),
        ],
        "prep",
        in_specs=smem(2) + vmem(2),
        out_specs=smem(1) + vmem(3),
        cost_estimate=pl.CostEstimate(flops=10**6, bytes_accessed=2**22, transcendentals=0),
    )(owners, prefix_len, span_block, cache_values)
    pairs = CAP * rows * HALF * (REGION + rows)
    answers = call(
        attend_kernel,
        [((rows, CAP * WIDE), jnp.bfloat16)]
        + [((rows, CAP * HD), jnp.float32)] * (hit_count > 1),
        "attend",
        in_specs=smem(1) + vmem(5),
        out_specs=vmem(1 + (hit_count > 1)),
        cost_estimate=pl.CostEstimate(
            flops=4 * pairs * HD, bytes_accessed=8 * rows * WIDE, transcendentals=pairs
        ),
    )(busy, prompt_mask, cached_mask, got, cache_keys, wide)
    returned = [exchange(answer) for answer in answers]
    return call(
        unpack_kernel,
        [((ROWS, HEADS * HD), jnp.bfloat16)],
        "unpack",
        in_specs=vmem(1 + len(returned)),
        out_specs=vmem(1),
    )(places, *returned)[0]


def solution(mesh):
    in_specs = (
        P("groups"),
        P("groups", None),
        P("groups", None),
        P(("groups", "cache"), None),
        P(("groups", "cache"), None),
        P(("groups", "cache"), None),
        P(("groups", "cache"), None),
        P(("groups", "cache"), None),
    )
    out_specs = P(("groups", "cache"), None)
    return jax.shard_map(body, mesh=mesh, in_specs=in_specs, out_specs=out_specs, check_vma=False)
```

```python
import functools
import math

import jax
import jax.numpy as jnp
from jax import lax
from jax.experimental import pallas as pl
from jax.experimental.pallas import tpu as pltpu
from jax.sharding import PartitionSpec as P

HEADS = 16
HD = 128
PAGE = 128
CAP = 2
REQUESTS = 16
TOK_REQ = 4
PAGES_DEV = 16

REGION = PAGES_DEV // CAP * PAGE
HALF = HEADS // 2
MSG = 2 * TOK_REQ
WIDE = HALF * HD
ROWS = REQUESTS * TOK_REQ
SCALE = HD**-0.5
FLOOR = -1e30
NT = (((1,), (1,)), ((), ()))
NN = (((1,), (0,)), ((), ()))
TN = (((0,), (0,)), ((), ()))


def iota(shape, axis):
    return lax.broadcasted_iota(jnp.int32, shape, axis)


def dot(a, b, dims, **kw):
    return lax.dot_general(a, b, dims, preferred_element_type=jnp.float32, **kw)


def pairwise(devices):
    return devices <= 16


def partner(devices, me, order):
    return order ^ me if pairwise(devices) else order


def pack_kernel(devices, hit_count, hits, q, k, v, *refs):
    *sends, places, held, count, sems = refs
    me = lax.axis_index("cache")
    copies = [
        pltpu.make_async_copy(source, held.at[pl.ds(row, ROWS), pl.ds(column, width)], sems.at[n])
        for n, (source, row, column, width) in enumerate(
            [
                (q.at[:, pl.ds(0, WIDE)], 0, 0, WIDE),
                (q.at[:, pl.ds(WIDE, WIDE)], ROWS, 0, WIDE),
                (k, 0, WIDE, HD),
                (v, ROWS, WIDE, HD),
            ]
        )
    ]
    for copy in copies:
        copy.start()
    lane = iota((1, 2 * ROWS), 1)
    lane_request = (lane % ROWS) // TOK_REQ
    for r in range(REQUESTS):
        for i in range(hit_count):
            count[hits[r * hit_count + i]] = 0
    rows = [[jnp.full((1, 2 * ROWS), -4 * MSG, jnp.int32)] * hit_count for _ in range(CAP)]
    for r in range(REQUESTS):
        for i in range(hit_count):
            owner = hits[r * hit_count + i]
            rank = count[owner]
            count[owner] = rank + 1
            message = partner(devices, me, owner) * MSG
            for s in range(CAP):
                place = jnp.where(rank == s, message, -4 * MSG)
                rows[s][i] = jnp.where(lane_request == r, place, rows[s][i])
    inner = lane // ROWS * TOK_REQ + lane % TOK_REQ
    target = iota((devices * MSG, 2 * ROWS), 0)
    picks = []
    for s in range(CAP):
        chosen = None
        for i in range(hit_count):
            row = rows[s][i] + inner
            places[s * hit_count + i : s * hit_count + i + 1, :] = row
            hit = target == row
            chosen = hit if chosen is None else chosen | hit
        picks.append(jnp.where(chosen, 1.0, 0.0).astype(jnp.bfloat16))
    for copy in copies:
        copy.wait()
    for s in range(CAP):
        here = slice(s * (WIDE + HD), (s + 1) * (WIDE + HD))
        packed = dot(picks[s], held[...], NN).astype(jnp.bfloat16)
        height = packed.shape[0] // len(sends)
        for m, send in enumerate(sends):
            send[:, here] = packed[m * height : (m + 1) * height]


def prep_kernel(devices, hit_count, hits, prefix_len, span, values, busy, prompt, cached, wide):
    me = lax.axis_index("cache")
    total_rows = devices * MSG
    wide[:, :HD] = values[...]
    wide[:, HD:] = jnp.ones((CAP * REGION, HD), jnp.bfloat16)
    for slot in range(CAP):
        seen = jnp.int32(0)
        request = jnp.int32(0)
        which = jnp.int32(0)
        for r in range(REQUESTS):
            for i in range(hit_count):
                mine = hits[r * hit_count + i] == me
                here = mine & (seen == slot)
                request = jnp.where(here, r, request)
                which = jnp.where(here, i, which)
                seen = seen + mine.astype(jnp.int32)
        busy[slot] = (seen > slot).astype(jnp.int32)
        limit = prefix_len[request] - which * REGION
        cached[slot : slot + 1, :] = jnp.where(iota((1, REGION), 1) < limit, 0.0, FLOOR)
        span_row = span[pl.ds(request, 1), :].astype(jnp.float32)
        source = partner(devices, me, iota((devices, total_rows), 0))
        spread = (iota((devices, total_rows), 1) // MSG == source).astype(jnp.bfloat16)
        spans = jnp.broadcast_to(span_row, (16, devices)).astype(jnp.bfloat16)
        key_span = dot(spans, spread, NN)[:1]
        lane = iota((1, total_rows), 1)
        key_spot = key_span.astype(jnp.int32) * TOK_REQ + lane % TOK_REQ
        is_key = lane % MSG < TOK_REQ
        if hit_count > 1:
            is_key = is_key & (which == 0)
        key_spot = jnp.where(is_key, key_spot, devices * TOK_REQ)
        block = 16 * MSG

        def one_block(at):
            row_source = partner(devices, me, at * 16 + iota((block, devices), 0) // MSG)
            mine = iota((block, devices), 1) == row_source
            row_span = jnp.sum(jnp.where(mine, span_row, 0.0), axis=1, keepdims=True)
            row_spot = row_span.astype(jnp.int32) * TOK_REQ + iota((block, 1), 0) % TOK_REQ
            here = pl.ds(slot * total_rows + at * block, block)
            prompt[here, :] = jnp.where(key_spot <= row_spot, 0.0, FLOOR)

        each_block(devices, one_block)


def each_block(devices, one_block):
    blocks = devices // 16
    if blocks == 1:
        one_block(0)
    else:
        pl.loop(0, blocks)(one_block)


def attend_kernel(devices, hit_count, busy, prompt_mask, cached_mask, keys, wide, *refs):
    parts = devices if pairwise(devices) else 1
    gots, outs, levels, got = refs[:parts], refs[parts : 2 * parts], refs[2 * parts : -1], refs[-1]
    if parts == 1:
        got, levels = gots[0], refs[2:]
    else:
        for m in range(parts):
            got[m * MSG : (m + 1) * MSG, :] = gots[m][...]
    height = devices * MSG // parts
    total_rows = devices * MSG
    block = 16 * MSG
    factor = SCALE * math.log2(math.e)
    for slot in range(CAP):
        base = slot * (WIDE + HD)
        region = slice(slot * REGION, (slot + 1) * REGION)
        first = slot * WIDE

        @pl.when(busy[slot] == 0)
        def _():
            for out in outs:
                out[:, first : first + WIDE] = jnp.zeros((height, WIDE), jnp.bfloat16)
            for lse in levels:
                lse[:, slot * HD : (slot + 1) * HD] = jnp.zeros((total_rows, HD), jnp.float32)

        @pl.when(busy[slot] != 0)
        def _():
            prompt_keys = got[:, base + WIDE : base + WIDE + HD]
            moved = pltpu.roll(prompt_keys.astype(jnp.float32), total_rows - TOK_REQ, 0)
            prompt_values = jnp.concatenate(
                [moved.astype(jnp.bfloat16), jnp.ones((total_rows, HD), jnp.bfloat16)], axis=1
            )

            def one_block(at):
                here = pl.ds(at * block, block)
                prompt_bias = prompt_mask[pl.ds(slot * total_rows + at * block, block), :]
                prompt_bias = jnp.concatenate([prompt_bias, prompt_bias], axis=0)
                lane = iota((block, HD), 1)
                logs = jnp.zeros((block, HD), jnp.float32)
                for c in range(0, HALF, 2):
                    at_c = [base + (c + n) * HD for n in range(2)]
                    pair = jnp.concatenate([got[here, n : n + HD] for n in at_c], axis=0)
                    cached = dot(pair, keys[region, :], NT) + cached_mask[slot : slot + 1, :]
                    prompt = dot(pair, prompt_keys, NT) + prompt_bias
                    top = jnp.maximum(
                        jnp.max(cached, axis=1, keepdims=True),
                        jnp.max(prompt, axis=1, keepdims=True),
                    )
                    if hit_count > 1:
                        top = jnp.maximum(top, 0.1 * FLOOR)
                    cached = jnp.exp2((cached - top) * factor).astype(jnp.bfloat16)
                    prompt = jnp.exp2((prompt - top) * factor).astype(jnp.bfloat16)
                    summed = dot(cached, wide[region, :], NN) + dot(prompt, prompt_values, NN)
                    totals = summed[:, HD:]
                    if hit_count > 1:
                        totals = jnp.maximum(totals, 1.0)
                        level = top * SCALE + jnp.log(totals)
                        logs = jnp.where(lane == c, level[:block], logs)
                        logs = jnp.where(lane == c + 1, level[block:], logs)
                    result = (summed[:, :HD] / totals).astype(jnp.bfloat16)
                    for n in range(2):
                        column = first + (c + n) * HD
                        if parts == 1:
                            rows = result[n * block : (n + 1) * block]
                            outs[0][here, column : column + HD] = rows
                        for m in range(parts if parts > 1 else 0):
                            rows = result[n * block + m * MSG : n * block + (m + 1) * MSG]
                            outs[m][:, column : column + HD] = rows
                for lse in levels:
                    lse[here, slot * HD : (slot + 1) * HD] = logs

            each_block(devices, one_block)


def unpack_kernel(devices, hit_count, places, *refs):
    parts = devices if pairwise(devices) else 1
    logs, result = refs[parts:-1], refs[-1]
    outs = jnp.concatenate([part[...] for part in refs[:parts]], axis=0) if parts > 1 else refs[0]
    target = iota((devices * MSG, 2 * ROWS), 0)

    def chosen(s, i, dtype):
        place = s * hit_count + i
        return jnp.where(target == places[place : place + 1, :], 1.0, 0.0).astype(dtype)

    def rows_of(i):
        parts = [
            dot(chosen(s, i, jnp.bfloat16), outs[:, s * WIDE : (s + 1) * WIDE], TN)
            for s in range(CAP)
        ]
        return sum(parts[1:], parts[0])

    def logs_of(i):
        parts = [
            dot(
                chosen(s, i, jnp.float32),
                logs[0][:, s * HD : (s + 1) * HD],
                TN,
                precision=lax.Precision.HIGHEST,
            )
            for s in range(CAP)
        ]
        return sum(parts[1:], parts[0])

    if hit_count == 1:
        joined = rows_of(0)
    else:
        levels = [logs_of(i) for i in range(hit_count)]
        top = functools.reduce(jnp.maximum, levels)
        shares = [jnp.exp(level - top) for level in levels]
        total = sum(shares[1:], shares[0])
        pieces = [rows_of(i) for i in range(hit_count)]
        columns = []
        for c in range(HALF):
            part = sum(
                shares[i][:, c : c + 1] * pieces[i][:, c * HD : (c + 1) * HD]
                for i in range(hit_count)
            )
            columns.append(part / total[:, c : c + 1])
        joined = jnp.concatenate(columns, axis=1)
    joined = joined.astype(jnp.bfloat16)
    result[:, :WIDE] = joined[:ROWS]
    result[:, WIDE:] = joined[ROWS:]


def vmem(count):
    return [pl.BlockSpec(memory_space=pltpu.VMEM)] * count


def smem(count):
    return [pl.BlockSpec(memory_space=pltpu.SMEM)] * count


def hbm(count):
    return [pl.BlockSpec(memory_space=pltpu.HBM)] * count


def body(prefix_len, hits, span_block, queries, fresh_keys, fresh_values, cache_keys, cache_values):
    devices = lax.axis_size("cache")
    hit_count = hits.shape[1]
    rows = devices * MSG
    owners = hits.reshape(REQUESTS * hit_count)

    def together(x):
        return lax.all_to_all(x, "cache", split_axis=0, concat_axis=0, tiled=True)

    def exchange(messages):
        if not pairwise(devices):
            return [together(x) for x in messages]
        moved = list(messages)
        for m in reversed(range(1, devices)):
            moved[m] = lax.ppermute(messages[m], "cache", [(d, d ^ m) for d in range(devices)])
        return moved

    def call(kernel, out_shape, name, grant=40, **kw):
        return pl.pallas_call(
            functools.partial(kernel, devices, hit_count),
            out_shape=[jax.ShapeDtypeStruct(*leaf) for leaf in out_shape],
            compiler_params=pltpu.CompilerParams(vmem_limit_bytes=grant * 2**20),
            name=name,
            **kw,
        )

    parts = devices if pairwise(devices) else 1
    *sends, places = call(
        pack_kernel,
        [((rows // parts, CAP * (WIDE + HD)), jnp.bfloat16)] * parts
        + [((CAP * hit_count, 2 * ROWS), jnp.int32)],
        "pack",
        grant=60,
        in_specs=smem(1) + hbm(3),
        out_specs=vmem(parts + 1),
        scratch_shapes=[
            pltpu.VMEM((2 * ROWS, WIDE + HD), jnp.bfloat16),
            pltpu.SMEM((devices,), jnp.int32),
            pltpu.SemaphoreType.DMA((4,)),
        ],
    )(owners, queries, fresh_keys, fresh_values)
    got = exchange(sends)
    busy, prompt_mask, cached_mask, wide = call(
        prep_kernel,
        [
            ((CAP,), jnp.int32),
            ((CAP * rows, rows), jnp.float32),
            ((CAP, REGION), jnp.float32),
            ((CAP * REGION, 2 * HD), jnp.bfloat16),
        ],
        "prep",
        in_specs=smem(2) + vmem(2),
        out_specs=smem(1) + vmem(3),
        cost_estimate=pl.CostEstimate(flops=10**6, bytes_accessed=2**22, transcendentals=0),
    )(owners, prefix_len, span_block, cache_values)
    pairs = CAP * rows * HALF * (REGION + rows)
    answers = call(
        attend_kernel,
        [((rows // parts, CAP * WIDE), jnp.bfloat16)] * parts
        + [((rows, CAP * HD), jnp.float32)] * (hit_count > 1),
        "attend",
        in_specs=smem(1) + vmem(4 + parts),
        out_specs=vmem(parts + (hit_count > 1)),
        scratch_shapes=[pltpu.VMEM((rows, CAP * (WIDE + HD)), jnp.bfloat16)] * (parts > 1),
        cost_estimate=pl.CostEstimate(
            flops=4 * pairs * HD, bytes_accessed=8 * rows * WIDE, transcendentals=pairs
        ),
    )(busy, prompt_mask, cached_mask, cache_keys, wide, *got)
    returned = exchange(answers[:parts])
    for level in answers[parts:]:
        if pairwise(devices):
            blocks = level.reshape(devices, MSG, CAP * HD)
            level = jnp.concatenate(exchange([blocks[m] for m in range(devices)]), axis=0)
        else:
            level = together(level)
        returned.append(level)
    return call(
        unpack_kernel,
        [((ROWS, HEADS * HD), jnp.bfloat16)],
        "unpack",
        in_specs=vmem(1 + len(returned)),
        out_specs=vmem(1),
    )(places, *returned)[0]


def solution(mesh):
    in_specs = (
        P("groups"),
        P("groups", None),
        P("groups", None),
        P(("groups", "cache"), None),
        P(("groups", "cache"), None),
        P(("groups", "cache"), None),
        P(("groups", "cache"), None),
        P(("groups", "cache"), None),
    )
    out_specs = P(("groups", "cache"), None)
    return jax.shard_map(body, mesh=mesh, in_specs=in_specs, out_specs=out_specs, check_vma=False)
```

```python
import functools
import math

import jax
import jax.numpy as jnp
from jax import lax
from jax.experimental import pallas as pl
from jax.experimental.pallas import tpu as pltpu
from jax.sharding import PartitionSpec as P

HEADS = 16
HD = 128
PAGE = 128
CAP = 2
REQUESTS = 16
TOK_REQ = 4
PAGES_DEV = 16

REGION = PAGES_DEV // CAP * PAGE
HALF = HEADS // 2
MSG = 2 * TOK_REQ
WIDE = HALF * HD
ROWS = REQUESTS * TOK_REQ
SCALE = HD**-0.5
FLOOR = -1e30
NT = (((1,), (1,)), ((), ()))
NN = (((1,), (0,)), ((), ()))
TN = (((0,), (0,)), ((), ()))


def iota(shape, axis):
    return lax.broadcasted_iota(jnp.int32, shape, axis)


def dot(a, b, dims, **kw):
    return lax.dot_general(a, b, dims, preferred_element_type=jnp.float32, **kw)


def pairwise(devices):
    return devices <= 16


def partner(devices, me, order):
    return order ^ me if pairwise(devices) else order


def pack_kernel(devices, hit_count, hits, q, k, v, *refs):
    *sends, places, held, count, sems = refs
    me = lax.axis_index("cache")
    copies = [
        pltpu.make_async_copy(source, held.at[pl.ds(row, ROWS), pl.ds(column, width)], sems.at[n])
        for n, (source, row, column, width) in enumerate(
            [
                (q.at[:, pl.ds(0, WIDE)], 0, 0, WIDE),
                (q.at[:, pl.ds(WIDE, WIDE)], ROWS, 0, WIDE),
                (k, 0, WIDE, HD),
                (v, ROWS, WIDE, HD),
            ]
        )
    ]
    for copy in copies:
        copy.start()
    lane = iota((1, 2 * ROWS), 1)
    lane_request = (lane % ROWS) // TOK_REQ
    for r in range(REQUESTS):
        for i in range(hit_count):
            count[hits[r * hit_count + i]] = 0
    rows = [[jnp.full((1, 2 * ROWS), -4 * MSG, jnp.int32)] * hit_count for _ in range(CAP)]
    for r in range(REQUESTS):
        for i in range(hit_count):
            owner = hits[r * hit_count + i]
            rank = count[owner]
            count[owner] = rank + 1
            message = partner(devices, me, owner) * MSG
            for s in range(CAP):
                place = jnp.where(rank == s, message, -4 * MSG)
                rows[s][i] = jnp.where(lane_request == r, place, rows[s][i])
    inner = lane // ROWS * TOK_REQ + lane % TOK_REQ
    target = iota((devices * MSG, 2 * ROWS), 0)
    picks = []
    for s in range(CAP):
        chosen = None
        for i in range(hit_count):
            row = rows[s][i] + inner
            places[s * hit_count + i : s * hit_count + i + 1, :] = row
            hit = target == row
            chosen = hit if chosen is None else chosen | hit
        picks.append(jnp.where(chosen, 1.0, 0.0).astype(jnp.bfloat16))
    for copy in copies:
        copy.wait()
    for s in range(CAP):
        here = slice(s * (WIDE + HD), (s + 1) * (WIDE + HD))
        packed = dot(picks[s], held[...], NN).astype(jnp.bfloat16)
        height = packed.shape[0] // len(sends)
        for m, send in enumerate(sends):
            send[:, here] = packed[m * height : (m + 1) * height]


def prep_kernel(devices, hit_count, hits, prefix_len, span, values, busy, prompt, cached, wide):
    me = lax.axis_index("cache")
    total_rows = devices * MSG
    wide[:, :HD] = values[...]
    wide[:, HD:] = jnp.ones((CAP * REGION, HD), jnp.bfloat16)
    for slot in range(CAP):
        seen = jnp.int32(0)
        request = jnp.int32(0)
        which = jnp.int32(0)
        for r in range(REQUESTS):
            for i in range(hit_count):
                mine = hits[r * hit_count + i] == me
                here = mine & (seen == slot)
                request = jnp.where(here, r, request)
                which = jnp.where(here, i, which)
                seen = seen + mine.astype(jnp.int32)
        busy[slot] = (seen > slot).astype(jnp.int32)
        limit = prefix_len[request] - which * REGION
        cached[slot : slot + 1, :] = jnp.where(iota((1, REGION), 1) < limit, 0.0, FLOOR)
        span_row = span[pl.ds(request, 1), :].astype(jnp.float32)
        source = partner(devices, me, iota((devices, total_rows), 0))
        spread = (iota((devices, total_rows), 1) // MSG == source).astype(jnp.bfloat16)
        spans = jnp.broadcast_to(span_row, (16, devices)).astype(jnp.bfloat16)
        key_span = dot(spans, spread, NN)[:1]
        lane = iota((1, total_rows), 1)
        key_spot = key_span.astype(jnp.int32) * TOK_REQ + lane % TOK_REQ
        is_key = lane % MSG < TOK_REQ
        if hit_count > 1:
            is_key = is_key & (which == 0)
        key_spot = jnp.where(is_key, key_spot, devices * TOK_REQ)
        block = 16 * MSG

        def one_block(at):
            row_source = partner(devices, me, at * 16 + iota((block, devices), 0) // MSG)
            mine = iota((block, devices), 1) == row_source
            row_span = jnp.sum(jnp.where(mine, span_row, 0.0), axis=1, keepdims=True)
            row_spot = row_span.astype(jnp.int32) * TOK_REQ + iota((block, 1), 0) % TOK_REQ
            here = pl.ds(slot * total_rows + at * block, block)
            prompt[here, :] = jnp.where(key_spot <= row_spot, 0.0, FLOOR)

        each_block(devices, one_block)


def each_block(devices, one_block):
    blocks = devices // 16
    if blocks == 1:
        one_block(0)
    else:
        pl.loop(0, blocks)(one_block)


def attend_kernel(devices, hit_count, busy, prompt_mask, cached_mask, keys, wide, *refs):
    parts = devices if pairwise(devices) else 1
    gots, outs, levels, got = refs[:parts], refs[parts : 2 * parts], refs[2 * parts : -1], refs[-1]
    if parts == 1:
        got, levels = gots[0], refs[2:]
    else:
        for m in range(parts):
            got[m * MSG : (m + 1) * MSG, :] = gots[m][...]
    height = devices * MSG // parts
    total_rows = devices * MSG
    block = 16 * MSG
    factor = SCALE * math.log2(math.e)
    for slot in range(CAP):
        base = slot * (WIDE + HD)
        region = slice(slot * REGION, (slot + 1) * REGION)
        first = slot * WIDE

        @pl.when(busy[slot] == 0)
        def _():
            for out in outs:
                out[:, first : first + WIDE] = jnp.zeros((height, WIDE), jnp.bfloat16)
            for lse in levels:
                lse[:, slot * HD : (slot + 1) * HD] = jnp.zeros((total_rows, HD), jnp.float32)

        @pl.when(busy[slot] != 0)
        def _():
            prompt_keys = got[:, base + WIDE : base + WIDE + HD]
            moved = pltpu.roll(prompt_keys.astype(jnp.float32), total_rows - TOK_REQ, 0)
            prompt_values = jnp.concatenate(
                [moved.astype(jnp.bfloat16), jnp.ones((total_rows, HD), jnp.bfloat16)], axis=1
            )

            def one_block(at):
                here = pl.ds(at * block, block)
                prompt_bias = prompt_mask[pl.ds(slot * total_rows + at * block, block), :]
                prompt_bias = jnp.concatenate([prompt_bias, prompt_bias], axis=0)
                lane = iota((block, HD), 1)
                logs = jnp.zeros((block, HD), jnp.float32)
                for c in range(0, HALF, 2):
                    at_c = [base + (c + n) * HD for n in range(2)]
                    pair = jnp.concatenate([got[here, n : n + HD] for n in at_c], axis=0)
                    cached = dot(pair, keys[region, :], NT) + cached_mask[slot : slot + 1, :]
                    prompt = dot(pair, prompt_keys, NT) + prompt_bias
                    top = jnp.maximum(
                        jnp.max(cached, axis=1, keepdims=True),
                        jnp.max(prompt, axis=1, keepdims=True),
                    )
                    if hit_count > 1:
                        top = jnp.maximum(top, 0.1 * FLOOR)
                    cached = jnp.exp2((cached - top) * factor).astype(jnp.bfloat16)
                    prompt = jnp.exp2((prompt - top) * factor).astype(jnp.bfloat16)
                    summed = dot(cached, wide[region, :], NN) + dot(prompt, prompt_values, NN)
                    totals = summed[:, HD:]
                    if hit_count > 1:
                        totals = jnp.maximum(totals, 1.0)
                        level = top * SCALE + jnp.log(totals)
                        logs = jnp.where(lane == c, level[:block], logs)
                        logs = jnp.where(lane == c + 1, level[block:], logs)
                    result = (summed[:, :HD] / totals).astype(jnp.bfloat16)
                    for n in range(2):
                        column = first + (c + n) * HD
                        if parts == 1:
                            rows = result[n * block : (n + 1) * block]
                            outs[0][here, column : column + HD] = rows
                        for m in range(parts if parts > 1 else 0):
                            rows = result[n * block + m * MSG : n * block + (m + 1) * MSG]
                            outs[m][:, column : column + HD] = rows
                for lse in levels:
                    lse[here, slot * HD : (slot + 1) * HD] = logs

            each_block(devices, one_block)


def unpack_kernel(devices, hit_count, places, *refs):
    parts = devices if pairwise(devices) else 1
    logs, result = refs[parts:-1], refs[-1]
    outs = jnp.concatenate([part[...] for part in refs[:parts]], axis=0) if parts > 1 else refs[0]
    target = iota((devices * MSG, 2 * ROWS), 0)

    def chosen(s, i, dtype):
        place = s * hit_count + i
        return jnp.where(target == places[place : place + 1, :], 1.0, 0.0).astype(dtype)

    def rows_of(i):
        parts = [
            dot(chosen(s, i, jnp.bfloat16), outs[:, s * WIDE : (s + 1) * WIDE], TN)
            for s in range(CAP)
        ]
        return sum(parts[1:], parts[0])

    def logs_of(i):
        parts = [
            dot(
                chosen(s, i, jnp.float32),
                logs[0][:, s * HD : (s + 1) * HD],
                TN,
                precision=lax.Precision.HIGHEST,
            )
            for s in range(CAP)
        ]
        return sum(parts[1:], parts[0])

    if hit_count == 1:
        joined = rows_of(0)
    else:
        levels = [logs_of(i) for i in range(hit_count)]
        top = functools.reduce(jnp.maximum, levels)
        shares = [jnp.exp(level - top) for level in levels]
        total = sum(shares[1:], shares[0])
        pieces = [rows_of(i) for i in range(hit_count)]
        columns = []
        for c in range(HALF):
            part = sum(
                shares[i][:, c : c + 1] * pieces[i][:, c * HD : (c + 1) * HD]
                for i in range(hit_count)
            )
            columns.append(part / total[:, c : c + 1])
        joined = jnp.concatenate(columns, axis=1)
    joined = joined.astype(jnp.bfloat16)
    result[:, :WIDE] = joined[:ROWS]
    result[:, WIDE:] = joined[ROWS:]


def vmem(count):
    return [pl.BlockSpec(memory_space=pltpu.VMEM)] * count


def smem(count):
    return [pl.BlockSpec(memory_space=pltpu.SMEM)] * count


def hbm(count):
    return [pl.BlockSpec(memory_space=pltpu.HBM)] * count


def body(prefix_len, hits, span_block, queries, fresh_keys, fresh_values, cache_keys, cache_values):
    devices = lax.axis_size("cache")
    hit_count = hits.shape[1]
    rows = devices * MSG
    owners = hits.reshape(REQUESTS * hit_count)
    fresh = (owners, queries, fresh_keys, fresh_values)

    def together(x):
        return lax.all_to_all(x, "cache", split_axis=0, concat_axis=0, tiled=True)

    def exchange(messages):
        if not pairwise(devices):
            return [together(x) for x in messages]
        moved = list(messages)
        for m in sorted(range(1, devices), key=lambda m: (-m % (devices // 2), -m)):
            moved[m] = lax.ppermute(messages[m], "cache", [(d, d ^ m) for d in range(devices)])
        return moved

    def call(kernel, out_shape, name, grant=40, **kw):
        return pl.pallas_call(
            functools.partial(kernel, devices, hit_count),
            out_shape=[jax.ShapeDtypeStruct(*leaf) for leaf in out_shape],
            compiler_params=pltpu.CompilerParams(vmem_limit_bytes=grant * 2**20),
            name=name,
            **kw,
        )

    parts = devices if pairwise(devices) else 1
    *sends, places = call(
        pack_kernel,
        [((rows // parts, CAP * (WIDE + HD)), jnp.bfloat16)] * parts
        + [((CAP * hit_count, 2 * ROWS), jnp.int32)],
        "pack",
        in_specs=smem(1) + hbm(3),
        out_specs=vmem(parts + 1),
        scratch_shapes=[
            pltpu.VMEM((2 * ROWS, WIDE + HD), jnp.bfloat16),
            pltpu.SMEM((devices,), jnp.int32),
            pltpu.SemaphoreType.DMA((4,)),
        ],
    )(*(pltpu.with_memory_space_constraint(x, pltpu.HBM) for x in fresh))
    got = exchange(sends)
    busy, prompt_mask, cached_mask, wide = call(
        prep_kernel,
        [
            ((CAP,), jnp.int32),
            ((CAP * rows, rows), jnp.float32),
            ((CAP, REGION), jnp.float32),
            ((CAP * REGION, 2 * HD), jnp.bfloat16),
        ],
        "prep",
        in_specs=smem(2) + vmem(2),
        out_specs=smem(1) + vmem(3),
        cost_estimate=pl.CostEstimate(flops=10**6, bytes_accessed=2**22, transcendentals=0),
    )(owners, prefix_len, span_block, cache_values)
    pairs = CAP * rows * HALF * (REGION + rows)
    answers = call(
        attend_kernel,
        [((rows // parts, CAP * WIDE), jnp.bfloat16)] * parts
        + [((rows, CAP * HD), jnp.float32)] * (hit_count > 1),
        "attend",
        in_specs=smem(1) + vmem(4 + parts),
        out_specs=vmem(parts + (hit_count > 1)),
        scratch_shapes=[pltpu.VMEM((rows, CAP * (WIDE + HD)), jnp.bfloat16)] * (parts > 1),
        cost_estimate=pl.CostEstimate(
            flops=4 * pairs * HD, bytes_accessed=8 * rows * WIDE, transcendentals=pairs
        ),
    )(busy, prompt_mask, cached_mask, cache_keys, wide, *got)
    returned = exchange(answers[:parts])
    for level in answers[parts:]:
        if pairwise(devices):
            blocks = level.reshape(devices, MSG, CAP * HD)
            level = jnp.concatenate(exchange([blocks[m] for m in range(devices)]), axis=0)
        else:
            level = together(level)
        returned.append(level)
    return call(
        unpack_kernel,
        [((ROWS, HEADS * HD), jnp.bfloat16)],
        "unpack",
        in_specs=vmem(1 + len(returned)),
        out_specs=vmem(1),
    )(places, *returned)[0]


def solution(mesh):
    in_specs = (
        P("groups"),
        P("groups", None),
        P("groups", None),
        P(("groups", "cache"), None),
        P(("groups", "cache"), None),
        P(("groups", "cache"), None),
        P(("groups", "cache"), None),
        P(("groups", "cache"), None),
    )
    out_specs = P(("groups", "cache"), None)
    return jax.shard_map(body, mesh=mesh, in_specs=in_specs, out_specs=out_specs, check_vma=False)
```

```python
import functools
import math

import jax
import jax.numpy as jnp
from jax import lax
from jax.experimental import pallas as pl
from jax.experimental.pallas import tpu as pltpu
from jax.sharding import PartitionSpec as P

HEADS = 16
HD = 128
PAGE = 128
CAP = 2
REQUESTS = 16
TOK_REQ = 4
PAGES_DEV = 16

REGION = PAGES_DEV // CAP * PAGE
HALF = HEADS // 2
MSG = 2 * TOK_REQ
WIDE = HALF * HD
ROWS = REQUESTS * TOK_REQ
SCALE = HD**-0.5
FLOOR = -1e30
NT = (((1,), (1,)), ((), ()))
NN = (((1,), (0,)), ((), ()))
TN = (((0,), (0,)), ((), ()))


def iota(shape, axis):
    return lax.broadcasted_iota(jnp.int32, shape, axis)


def dot(a, b, dims, **kw):
    return lax.dot_general(a, b, dims, preferred_element_type=jnp.float32, **kw)


def pairwise(devices):
    return devices <= 16


def step(devices):
    return devices // 2 - 1


def message_for(devices, me, device):
    if not pairwise(devices):
        return device
    return (step(devices) * (device - me + devices)) % devices


def source_of(devices, me, message):
    if not pairwise(devices):
        return message
    return (me + step(devices) * (devices - message)) % devices


def pack_kernel(devices, hit_count, hits, q, k, v, *refs):
    *sends, places, held, count, sems = refs
    me = lax.axis_index("cache")
    copies = [
        pltpu.make_async_copy(source, held.at[pl.ds(row, ROWS), pl.ds(column, width)], sems.at[n])
        for n, (source, row, column, width) in enumerate(
            [
                (q.at[:, pl.ds(0, WIDE)], 0, 0, WIDE),
                (q.at[:, pl.ds(WIDE, WIDE)], ROWS, 0, WIDE),
                (k, 0, WIDE, HD),
                (v, ROWS, WIDE, HD),
            ]
        )
    ]
    for copy in copies:
        copy.start()
    lane = iota((1, 2 * ROWS), 1)
    lane_request = (lane % ROWS) // TOK_REQ
    for r in range(REQUESTS):
        for i in range(hit_count):
            count[hits[r * hit_count + i]] = 0
    rows = [[jnp.full((1, 2 * ROWS), -4 * MSG, jnp.int32)] * hit_count for _ in range(CAP)]
    for r in range(REQUESTS):
        for i in range(hit_count):
            owner = hits[r * hit_count + i]
            rank = count[owner]
            count[owner] = rank + 1
            message = message_for(devices, me, owner) * MSG
            for s in range(CAP):
                place = jnp.where(rank == s, message, -4 * MSG)
                rows[s][i] = jnp.where(lane_request == r, place, rows[s][i])
    inner = lane // ROWS * TOK_REQ + lane % TOK_REQ
    target = iota((devices * MSG, 2 * ROWS), 0)
    picks = []
    for s in range(CAP):
        chosen = None
        for i in range(hit_count):
            row = rows[s][i] + inner
            places[s * hit_count + i : s * hit_count + i + 1, :] = row
            hit = target == row
            chosen = hit if chosen is None else chosen | hit
        picks.append(jnp.where(chosen, 1.0, 0.0).astype(jnp.bfloat16))
    for copy in copies:
        copy.wait()
    for s in range(CAP):
        here = slice(s * (WIDE + HD), (s + 1) * (WIDE + HD))
        packed = dot(picks[s], held[...], NN).astype(jnp.bfloat16)
        height = packed.shape[0] // len(sends)
        for m, send in enumerate(sends):
            send[:, here] = packed[m * height : (m + 1) * height]


def prep_kernel(devices, hit_count, hits, prefix_len, span, values, busy, prompt, cached, wide):
    me = lax.axis_index("cache")
    total_rows = devices * MSG
    wide[:, :HD] = values[...]
    wide[:, HD:] = jnp.ones((CAP * REGION, HD), jnp.bfloat16)
    for slot in range(CAP):
        seen = jnp.int32(0)
        request = jnp.int32(0)
        which = jnp.int32(0)
        for r in range(REQUESTS):
            for i in range(hit_count):
                mine = hits[r * hit_count + i] == me
                here = mine & (seen == slot)
                request = jnp.where(here, r, request)
                which = jnp.where(here, i, which)
                seen = seen + mine.astype(jnp.int32)
        busy[slot] = (seen > slot).astype(jnp.int32)
        limit = prefix_len[request] - which * REGION
        cached[slot : slot + 1, :] = jnp.where(iota((1, REGION), 1) < limit, 0.0, FLOOR)
        span_row = span[pl.ds(request, 1), :].astype(jnp.float32)
        source = source_of(devices, me, iota((devices, total_rows), 1) // MSG)
        spread = (iota((devices, total_rows), 0) == source).astype(jnp.bfloat16)
        spans = jnp.broadcast_to(span_row, (16, devices)).astype(jnp.bfloat16)
        key_span = dot(spans, spread, NN)[:1]
        lane = iota((1, total_rows), 1)
        key_spot = key_span.astype(jnp.int32) * TOK_REQ + lane % TOK_REQ
        is_key = lane % MSG < TOK_REQ
        if hit_count > 1:
            is_key = is_key & (which == 0)
        key_spot = jnp.where(is_key, key_spot, devices * TOK_REQ)
        block = 16 * MSG

        def one_block(at):
            row_source = source_of(devices, me, at * 16 + iota((block, devices), 0) // MSG)
            mine = iota((block, devices), 1) == row_source
            row_span = jnp.sum(jnp.where(mine, span_row, 0.0), axis=1, keepdims=True)
            row_spot = row_span.astype(jnp.int32) * TOK_REQ + iota((block, 1), 0) % TOK_REQ
            here = pl.ds(slot * total_rows + at * block, block)
            prompt[here, :] = jnp.where(key_spot <= row_spot, 0.0, FLOOR)

        each_block(devices, one_block)


def each_block(devices, one_block):
    blocks = devices // 16
    if blocks == 1:
        one_block(0)
    else:
        pl.loop(0, blocks)(one_block)


def attend_kernel(devices, hit_count, busy, prompt_mask, cached_mask, keys, wide, *refs):
    parts = devices if pairwise(devices) else 1
    gots, outs, levels, got = refs[:parts], refs[parts : 2 * parts], refs[2 * parts : -1], refs[-1]
    if parts == 1:
        got, levels = gots[0], refs[2:]
    else:
        for m in range(parts):
            got[m * MSG : (m + 1) * MSG, :] = gots[m][...]
    height = devices * MSG // parts
    total_rows = devices * MSG
    block = 16 * MSG
    factor = SCALE * math.log2(math.e)
    for slot in range(CAP):
        base = slot * (WIDE + HD)
        region = slice(slot * REGION, (slot + 1) * REGION)
        first = slot * WIDE

        @pl.when(busy[slot] == 0)
        def _():
            for out in outs:
                out[:, first : first + WIDE] = jnp.zeros((height, WIDE), jnp.bfloat16)
            for lse in levels:
                lse[:, slot * HD : (slot + 1) * HD] = jnp.zeros((total_rows, HD), jnp.float32)

        @pl.when(busy[slot] != 0)
        def _():
            prompt_keys = got[:, base + WIDE : base + WIDE + HD]
            moved = pltpu.roll(prompt_keys.astype(jnp.float32), total_rows - TOK_REQ, 0)
            prompt_values = jnp.concatenate(
                [moved.astype(jnp.bfloat16), jnp.ones((total_rows, HD), jnp.bfloat16)], axis=1
            )

            def one_block(at):
                here = pl.ds(at * block, block)
                prompt_bias = prompt_mask[pl.ds(slot * total_rows + at * block, block), :]
                prompt_bias = jnp.concatenate([prompt_bias, prompt_bias], axis=0)
                lane = iota((block, HD), 1)
                logs = jnp.zeros((block, HD), jnp.float32)
                for c in range(0, HALF, 2):
                    at_c = [base + (c + n) * HD for n in range(2)]
                    pair = jnp.concatenate([got[here, n : n + HD] for n in at_c], axis=0)
                    cached = dot(pair, keys[region, :], NT) + cached_mask[slot : slot + 1, :]
                    prompt = dot(pair, prompt_keys, NT) + prompt_bias
                    top = jnp.maximum(
                        jnp.max(cached, axis=1, keepdims=True),
                        jnp.max(prompt, axis=1, keepdims=True),
                    )
                    if hit_count > 1:
                        top = jnp.maximum(top, 0.1 * FLOOR)
                    cached = jnp.exp2((cached - top) * factor).astype(jnp.bfloat16)
                    prompt = jnp.exp2((prompt - top) * factor).astype(jnp.bfloat16)
                    summed = dot(cached, wide[region, :], NN) + dot(prompt, prompt_values, NN)
                    totals = summed[:, HD:]
                    if hit_count > 1:
                        totals = jnp.maximum(totals, 1.0)
                        level = top * SCALE + jnp.log(totals)
                        logs = jnp.where(lane == c, level[:block], logs)
                        logs = jnp.where(lane == c + 1, level[block:], logs)
                    result = (summed[:, :HD] / totals).astype(jnp.bfloat16)
                    for n in range(2):
                        column = first + (c + n) * HD
                        if parts == 1:
                            rows = result[n * block : (n + 1) * block]
                            outs[0][here, column : column + HD] = rows
                        for m in range(parts if parts > 1 else 0):
                            rows = result[n * block + m * MSG : n * block + (m + 1) * MSG]
                            outs[m][:, column : column + HD] = rows
                for lse in levels:
                    lse[here, slot * HD : (slot + 1) * HD] = logs

            each_block(devices, one_block)


def unpack_kernel(devices, hit_count, places, *refs):
    parts = devices if pairwise(devices) else 1
    logs, result = refs[parts:-1], refs[-1]
    outs = jnp.concatenate([part[...] for part in refs[:parts]], axis=0) if parts > 1 else refs[0]
    target = iota((devices * MSG, 2 * ROWS), 0)

    def chosen(s, i, dtype):
        place = s * hit_count + i
        return jnp.where(target == places[place : place + 1, :], 1.0, 0.0).astype(dtype)

    def rows_of(i):
        parts = [
            dot(chosen(s, i, jnp.bfloat16), outs[:, s * WIDE : (s + 1) * WIDE], TN)
            for s in range(CAP)
        ]
        return sum(parts[1:], parts[0])

    def logs_of(i):
        parts = [
            dot(
                chosen(s, i, jnp.float32),
                logs[0][:, s * HD : (s + 1) * HD],
                TN,
                precision=lax.Precision.HIGHEST,
            )
            for s in range(CAP)
        ]
        return sum(parts[1:], parts[0])

    if hit_count == 1:
        joined = rows_of(0)
    else:
        levels = [logs_of(i) for i in range(hit_count)]
        top = functools.reduce(jnp.maximum, levels)
        shares = [jnp.exp(level - top) for level in levels]
        total = sum(shares[1:], shares[0])
        pieces = [rows_of(i) for i in range(hit_count)]
        columns = []
        for c in range(HALF):
            part = sum(
                shares[i][:, c : c + 1] * pieces[i][:, c * HD : (c + 1) * HD]
                for i in range(hit_count)
            )
            columns.append(part / total[:, c : c + 1])
        joined = jnp.concatenate(columns, axis=1)
    joined = joined.astype(jnp.bfloat16)
    result[:, :WIDE] = joined[:ROWS]
    result[:, WIDE:] = joined[ROWS:]


def vmem(count):
    return [pl.BlockSpec(memory_space=pltpu.VMEM)] * count


def smem(count):
    return [pl.BlockSpec(memory_space=pltpu.SMEM)] * count


def hbm(count):
    return [pl.BlockSpec(memory_space=pltpu.HBM)] * count


def body(prefix_len, hits, span_block, queries, fresh_keys, fresh_values, cache_keys, cache_values):
    devices = lax.axis_size("cache")
    hit_count = hits.shape[1]
    rows = devices * MSG
    owners = hits.reshape(REQUESTS * hit_count)
    fresh = (owners, queries, fresh_keys, fresh_values)

    def together(x):
        return lax.all_to_all(x, "cache", split_axis=0, concat_axis=0, tiled=True)

    def exchange(messages, sign):
        if not pairwise(devices):
            return [together(x) for x in messages]
        moved = list(messages)
        for m in range(1, devices):
            far = sign * m * step(devices)
            pairs = [(d, (d + far) % devices) for d in range(devices)]
            moved[m] = lax.ppermute(messages[m], "cache", pairs)
        return moved

    def call(kernel, out_shape, name, grant=40, **kw):
        return pl.pallas_call(
            functools.partial(kernel, devices, hit_count),
            out_shape=[jax.ShapeDtypeStruct(*leaf) for leaf in out_shape],
            compiler_params=pltpu.CompilerParams(vmem_limit_bytes=grant * 2**20),
            name=name,
            **kw,
        )

    parts = devices if pairwise(devices) else 1
    *sends, places = call(
        pack_kernel,
        [((rows // parts, CAP * (WIDE + HD)), jnp.bfloat16)] * parts
        + [((CAP * hit_count, 2 * ROWS), jnp.int32)],
        "pack",
        in_specs=smem(1) + hbm(3),
        out_specs=vmem(parts + 1),
        scratch_shapes=[
            pltpu.VMEM((2 * ROWS, WIDE + HD), jnp.bfloat16),
            pltpu.SMEM((devices,), jnp.int32),
            pltpu.SemaphoreType.DMA((4,)),
        ],
    )(*(pltpu.with_memory_space_constraint(x, pltpu.HBM) for x in fresh))
    got = exchange(sends, 1)
    busy, prompt_mask, cached_mask, wide = call(
        prep_kernel,
        [
            ((CAP,), jnp.int32),
            ((CAP * rows, rows), jnp.float32),
            ((CAP, REGION), jnp.float32),
            ((CAP * REGION, 2 * HD), jnp.bfloat16),
        ],
        "prep",
        in_specs=smem(2) + vmem(2),
        out_specs=smem(1) + vmem(3),
        cost_estimate=pl.CostEstimate(flops=10**6, bytes_accessed=2**22, transcendentals=0),
    )(owners, prefix_len, span_block, cache_values)
    pairs = CAP * rows * HALF * (REGION + rows)
    answers = call(
        attend_kernel,
        [((rows // parts, CAP * WIDE), jnp.bfloat16)] * parts
        + [((rows, CAP * HD), jnp.float32)] * (hit_count > 1),
        "attend",
        in_specs=smem(1) + vmem(4 + parts),
        out_specs=vmem(parts + (hit_count > 1)),
        scratch_shapes=[pltpu.VMEM((rows, CAP * (WIDE + HD)), jnp.bfloat16)] * (parts > 1),
        cost_estimate=pl.CostEstimate(
            flops=4 * pairs * HD, bytes_accessed=8 * rows * WIDE, transcendentals=pairs
        ),
    )(busy, prompt_mask, cached_mask, cache_keys, wide, *got)
    returned = exchange(answers[:parts], -1)
    for level in answers[parts:]:
        if pairwise(devices):
            blocks = level.reshape(devices, MSG, CAP * HD)
            level = jnp.concatenate(exchange([blocks[m] for m in range(devices)], -1), axis=0)
        else:
            level = together(level)
        returned.append(level)
    return call(
        unpack_kernel,
        [((ROWS, HEADS * HD), jnp.bfloat16)],
        "unpack",
        in_specs=vmem(1 + len(returned)),
        out_specs=vmem(1),
    )(places, *returned)[0]


def solution(mesh):
    in_specs = (
        P("groups"),
        P("groups", None),
        P("groups", None),
        P(("groups", "cache"), None),
        P(("groups", "cache"), None),
        P(("groups", "cache"), None),
        P(("groups", "cache"), None),
        P(("groups", "cache"), None),
    )
    out_specs = P(("groups", "cache"), None)
    return jax.shard_map(body, mesh=mesh, in_specs=in_specs, out_specs=out_specs, check_vma=False)
```

```python
import functools
import math

import jax
import jax.numpy as jnp
from jax import lax
from jax.experimental import pallas as pl
from jax.experimental.pallas import tpu as pltpu
from jax.sharding import PartitionSpec as P

HEADS = 16
HD = 128
PAGE = 128
CAP = 2
REQUESTS = 16
TOK_REQ = 4
PAGES_DEV = 16

REGION = PAGES_DEV // CAP * PAGE
HALF = HEADS // 2
MSG = 2 * TOK_REQ
WIDE = HALF * HD
ROWS = REQUESTS * TOK_REQ
STRIP = 256
SCALE = HD**-0.5
FLOOR = -1e30
NT = (((1,), (1,)), ((), ()))
NN = (((1,), (0,)), ((), ()))
TN = (((0,), (0,)), ((), ()))


def iota(shape, axis):
    return lax.broadcasted_iota(jnp.int32, shape, axis)


def dot(a, b, dims, **kw):
    return lax.dot_general(a, b, dims, preferred_element_type=jnp.float32, **kw)


def pack_kernel(devices, hit_count, owners, q, k, v, send, places, held, hits, count, sems):
    copies = [
        pltpu.make_async_copy(source, held.at[pl.ds(row, ROWS), pl.ds(column, width)], sems.at[n])
        for n, (source, row, column, width) in enumerate(
            [
                (q.at[:, pl.ds(0, WIDE)], 0, 0, WIDE),
                (q.at[:, pl.ds(WIDE, WIDE)], ROWS, 0, WIDE),
                (k, 0, WIDE, HD),
                (v, ROWS, WIDE, HD),
            ]
        )
    ]
    first = pltpu.make_async_copy(owners, hits, sems.at[4])
    first.start()
    for copy in copies:
        copy.start()
    lane = iota((1, 2 * ROWS), 1)
    lane_request = (lane % ROWS) // TOK_REQ
    first.wait()
    for r in range(REQUESTS):
        for i in range(hit_count):
            count[hits[r * hit_count + i]] = 0
    rows = [[jnp.full((1, 2 * ROWS), -4 * MSG, jnp.int32)] * hit_count for _ in range(CAP)]
    for r in range(REQUESTS):
        for i in range(hit_count):
            owner = hits[r * hit_count + i]
            rank = count[owner]
            count[owner] = rank + 1
            for s in range(CAP):
                place = jnp.where(rank == s, owner * MSG, -4 * MSG)
                rows[s][i] = jnp.where(lane_request == r, place, rows[s][i])
    inner = lane // ROWS * TOK_REQ + lane % TOK_REQ
    target = iota((devices * MSG, 2 * ROWS), 0)
    picks = []
    for s in range(CAP):
        chosen = None
        for i in range(hit_count):
            row = rows[s][i] + inner
            places[s * hit_count + i : s * hit_count + i + 1, :] = row
            hit = target == row
            chosen = hit if chosen is None else chosen | hit
        picks.append(jnp.where(chosen, 1.0, 0.0).astype(jnp.bfloat16))
    for copy in copies:
        copy.wait()
    for s in range(CAP):
        here = slice(s * (WIDE + HD), (s + 1) * (WIDE + HD))
        send[:, here] = dot(picks[s], held[...], NN).astype(jnp.bfloat16)


def prep_kernel(devices, hit_count, hits, prefix_len, span, values, busy, prompt, cached, wide):
    me = lax.axis_index("cache")
    total_rows = devices * MSG
    wide[:, :HD] = values[...]
    wide[:, HD:] = jnp.ones((CAP * REGION, HD), jnp.bfloat16)
    for slot in range(CAP):
        seen = jnp.int32(0)
        request = jnp.int32(0)
        which = jnp.int32(0)
        for r in range(REQUESTS):
            for i in range(hit_count):
                mine = hits[r * hit_count + i] == me
                here = mine & (seen == slot)
                request = jnp.where(here, r, request)
                which = jnp.where(here, i, which)
                seen = seen + mine.astype(jnp.int32)
        limit = prefix_len[request] - which * REGION
        blocks = jnp.clip((limit + STRIP - 1) // STRIP, 1, REGION // STRIP)
        busy[slot] = jnp.where(seen > slot, blocks, 0)
        cached[slot : slot + 1, :] = jnp.where(iota((1, REGION), 1) < limit, 0.0, FLOOR)
        span_row = span[pl.ds(request, 1), :].astype(jnp.float32)
        source = iota((devices, total_rows), 0)
        spread = (iota((devices, total_rows), 1) // MSG == source).astype(jnp.bfloat16)
        spans = jnp.broadcast_to(span_row, (16, devices)).astype(jnp.bfloat16)
        key_span = dot(spans, spread, NN)[:1]
        lane = iota((1, total_rows), 1)
        key_spot = key_span.astype(jnp.int32) * TOK_REQ + lane % TOK_REQ
        is_key = lane % MSG < TOK_REQ
        if hit_count > 1:
            is_key = is_key & (which == 0)
        key_spot = jnp.where(is_key, key_spot, devices * TOK_REQ)
        block = 16 * MSG

        def one_block(at):
            row_source = at * 16 + iota((block, devices), 0) // MSG
            mine = iota((block, devices), 1) == row_source
            row_span = jnp.sum(jnp.where(mine, span_row, 0.0), axis=1, keepdims=True)
            row_spot = row_span.astype(jnp.int32) * TOK_REQ + iota((block, 1), 0) % TOK_REQ
            here = pl.ds(slot * total_rows + at * block, block)
            prompt[here, :] = jnp.where(key_spot <= row_spot, 0.0, FLOOR)

        each_block(devices, one_block)


def each_block(devices, one_block):
    blocks = devices // 16
    if blocks == 1:
        one_block(0)
    else:
        pl.loop(0, blocks)(one_block)


def lanes_max(parts):
    pieces = [part[:, n : n + HD] for part in parts for n in range(0, part.shape[1], HD)]
    return jnp.max(functools.reduce(jnp.maximum, pieces), axis=1, keepdims=True)


def attend_kernel(devices, hit_count, busy, prompt_mask, cached_mask, got, keys, wide, out, *levels):
    total_rows = devices * MSG
    block = 16 * MSG
    factor = SCALE * math.log2(math.e)

    def nothing(slot):
        out[:, pl.ds(slot * WIDE, WIDE)] = jnp.zeros((total_rows, WIDE), jnp.bfloat16)
        for lse in levels:
            lse[:, pl.ds(slot * HD, HD)] = jnp.zeros((total_rows, HD), jnp.float32)

    def attend(slot, strips):
        whole = (strips - 1) * STRIP
        base = pl.multiple_of(slot * (WIDE + HD), HD)
        region = pl.multiple_of(slot * REGION, REGION)
        head = pl.ds(region, whole) if whole else None
        tail = pl.ds(pl.multiple_of(region + whole, STRIP), STRIP)
        tail_mask = cached_mask[pl.ds(slot, 1), whole : whole + STRIP]
        prompt_keys = got[:, pl.ds(base + WIDE, HD)]
        moved = pltpu.roll(prompt_keys.astype(jnp.float32), total_rows - TOK_REQ, 0)
        prompt_values = jnp.concatenate(
            [moved.astype(jnp.bfloat16), jnp.ones((total_rows, HD), jnp.bfloat16)], axis=1
        )

        def one_block(at):
            here = pl.ds(at * block, block)
            prompt_bias = prompt_mask[pl.ds(slot * total_rows + at * block, block), :]
            prompt_bias = jnp.concatenate([prompt_bias, prompt_bias], axis=0)
            lane = iota((block, HD), 1)

            def scores(c):
                pair = jnp.concatenate(
                    [got[here, pl.ds(base + (c + n) * HD, HD)] for n in range(2)], axis=0
                )
                parts = [dot(pair, keys[head, :], NT)] if whole else []
                parts.append(dot(pair, keys[tail, :], NT) + tail_mask)
                parts.append(dot(pair, prompt_keys, NT) + prompt_bias)
                return parts

            logs = jnp.zeros((block, HD), jnp.float32)
            parts = scores(0)
            for c in range(0, HALF, 2):
                later = scores(c + 2) if c + 2 < HALF else None
                top = lanes_max(parts)
                if hit_count > 1:
                    top = jnp.maximum(top, 0.1 * FLOOR)
                parts = [jnp.exp2((x - top) * factor).astype(jnp.bfloat16) for x in parts]
                summed = dot(parts[-1], prompt_values, NN) + dot(parts[-2], wide[tail, :], NN)
                if whole:
                    summed = summed + dot(parts[0], wide[head, :], NN)
                totals = summed[:, HD:]
                if hit_count > 1:
                    totals = jnp.maximum(totals, 1.0)
                    level = top * SCALE + jnp.log(totals)
                    logs = jnp.where(lane == c, level[:block], logs)
                    logs = jnp.where(lane == c + 1, level[block:], logs)
                result = (summed[:, :HD] / totals).astype(jnp.bfloat16)
                for n in range(2):
                    column = pl.multiple_of(slot * WIDE + (c + n) * HD, HD)
                    out[here, pl.ds(column, HD)] = result[n * block : (n + 1) * block]
                parts = later
            for lse in levels:
                lse[here, pl.ds(pl.multiple_of(slot * HD, HD), HD)] = logs

        each_block(devices, one_block)

    @pl.loop(0, CAP)
    def _(slot):
        strips = busy[slot]
        pl.when(strips == 0)(lambda: nothing(slot))
        for count in range(1, REGION // STRIP + 1):
            pl.when(strips == count)(functools.partial(attend, slot, count))


def unpack_kernel(devices, hit_count, places, *refs):
    outs, logs, result = refs[0], refs[1:-1], refs[-1]
    target = iota((devices * MSG, 2 * ROWS), 0)

    def chosen(s, i, dtype):
        place = s * hit_count + i
        return jnp.where(target == places[place : place + 1, :], 1.0, 0.0).astype(dtype)

    def rows_of(i):
        parts = [
            dot(chosen(s, i, jnp.bfloat16), outs[:, s * WIDE : (s + 1) * WIDE], TN)
            for s in range(CAP)
        ]
        return sum(parts[1:], parts[0])

    def logs_of(i):
        parts = [
            dot(
                chosen(s, i, jnp.float32),
                logs[0][:, s * HD : (s + 1) * HD],
                TN,
                precision=lax.Precision.HIGHEST,
            )
            for s in range(CAP)
        ]
        return sum(parts[1:], parts[0])

    if hit_count == 1:
        joined = rows_of(0)
    else:
        levels = [logs_of(i) for i in range(hit_count)]
        top = functools.reduce(jnp.maximum, levels)
        shares = [jnp.exp(level - top) for level in levels]
        total = sum(shares[1:], shares[0])
        pieces = [rows_of(i) for i in range(hit_count)]
        columns = []
        for c in range(HALF):
            part = sum(
                shares[i][:, c : c + 1] * pieces[i][:, c * HD : (c + 1) * HD]
                for i in range(hit_count)
            )
            columns.append(part / total[:, c : c + 1])
        joined = jnp.concatenate(columns, axis=1)
    joined = joined.astype(jnp.bfloat16)
    result[:, :WIDE] = joined[:ROWS]
    result[:, WIDE:] = joined[ROWS:]


def vmem(count):
    return [pl.BlockSpec(memory_space=pltpu.VMEM)] * count


def smem(count):
    return [pl.BlockSpec(memory_space=pltpu.SMEM)] * count


def hbm(count):
    return [pl.BlockSpec(memory_space=pltpu.HBM)] * count


def body(prefix_len, hits, span_block, queries, fresh_keys, fresh_values, cache_keys, cache_values):
    devices = lax.axis_size("cache")
    hit_count = hits.shape[1]
    rows = devices * MSG
    owners = hits.reshape(REQUESTS * hit_count)
    fresh = (owners, queries, fresh_keys, fresh_values)

    def exchange(x):
        return lax.all_to_all(x, "cache", split_axis=0, concat_axis=0, tiled=True)

    def call(kernel, out_shape, name, grant=40, **kw):
        return pl.pallas_call(
            functools.partial(kernel, devices, hit_count),
            out_shape=[jax.ShapeDtypeStruct(*leaf) for leaf in out_shape],
            compiler_params=pltpu.CompilerParams(vmem_limit_bytes=grant * 2**20),
            name=name,
            **kw,
        )

    send, places = call(
        pack_kernel,
        [((rows, CAP * (WIDE + HD)), jnp.bfloat16), ((CAP * hit_count, 2 * ROWS), jnp.int32)],
        "pack",
        in_specs=hbm(4),
        out_specs=vmem(2),
        scratch_shapes=[
            pltpu.VMEM((2 * ROWS, WIDE + HD), jnp.bfloat16),
            pltpu.SMEM((REQUESTS * hit_count,), jnp.int32),
            pltpu.SMEM((devices,), jnp.int32),
            pltpu.SemaphoreType.DMA((5,)),
        ],
    )(*(pltpu.with_memory_space_constraint(x, pltpu.HBM) for x in fresh))
    got = exchange(send)
    busy, prompt_mask, cached_mask, wide = call(
        prep_kernel,
        [
            ((CAP,), jnp.int32),
            ((CAP * rows, rows), jnp.float32),
            ((CAP, REGION), jnp.float32),
            ((CAP * REGION, 2 * HD), jnp.bfloat16),
        ],
        "prep",
        in_specs=smem(2) + vmem(2),
        out_specs=smem(1) + vmem(3),
        cost_estimate=pl.CostEstimate(flops=10**6, bytes_accessed=2**22, transcendentals=0),
    )(owners, prefix_len, span_block, cache_values)
    pairs = CAP * rows * HALF * (REGION + rows)
    answers = call(
        attend_kernel,
        [((rows, CAP * WIDE), jnp.bfloat16)]
        + [((rows, CAP * HD), jnp.float32)] * (hit_count > 1),
        "attend",
        in_specs=smem(1) + vmem(5),
        out_specs=vmem(1 + (hit_count > 1)),
        cost_estimate=pl.CostEstimate(
            flops=4 * pairs * HD, bytes_accessed=8 * rows * WIDE, transcendentals=pairs
        ),
    )(busy, prompt_mask, cached_mask, got, cache_keys, wide)
    returned = [exchange(answer) for answer in answers]
    return call(
        unpack_kernel,
        [((ROWS, HEADS * HD), jnp.bfloat16)],
        "unpack",
        in_specs=vmem(1 + len(returned)),
        out_specs=vmem(1),
    )(places, *returned)[0]


def solution(mesh):
    in_specs = (
        P("groups"),
        P("groups", None),
        P("groups", None),
        P(("groups", "cache"), None),
        P(("groups", "cache"), None),
        P(("groups", "cache"), None),
        P(("groups", "cache"), None),
        P(("groups", "cache"), None),
    )
    out_specs = P(("groups", "cache"), None)
    return jax.shard_map(body, mesh=mesh, in_specs=in_specs, out_specs=out_specs, check_vma=False)
```

```python
import functools
import math

import jax
import jax.numpy as jnp
from jax import lax
from jax.experimental import pallas as pl
from jax.experimental.pallas import tpu as pltpu
from jax.sharding import PartitionSpec as P

HEADS = 16
HD = 128
PAGE = 128
CAP = 2
REQUESTS = 16
TOK_REQ = 4
PAGES_DEV = 16

REGION = PAGES_DEV // CAP * PAGE
HALF = HEADS // 2
MSG = 2 * TOK_REQ
WIDE = HALF * HD
ROWS = REQUESTS * TOK_REQ
STRIP = 256
SCALE = HD**-0.5
FLOOR = -1e30
NT = (((1,), (1,)), ((), ()))
NN = (((1,), (0,)), ((), ()))
TN = (((0,), (0,)), ((), ()))


def iota(shape, axis):
    return lax.broadcasted_iota(jnp.int32, shape, axis)


def dot(a, b, dims, **kw):
    return lax.dot_general(a, b, dims, preferred_element_type=jnp.float32, **kw)


def place_of(devices, device):
    return device % (devices // 2) * 2 + device // (devices // 2)


def device_at(devices, place):
    return place % 2 * (devices // 2) + place // 2


def pack_kernel(devices, hit_count, owners, q, k, v, send, places, held, hits, count, sems):
    copies = [
        pltpu.make_async_copy(source, held.at[pl.ds(row, ROWS), pl.ds(column, width)], sems.at[n])
        for n, (source, row, column, width) in enumerate(
            [
                (q.at[:, pl.ds(0, WIDE)], 0, 0, WIDE),
                (q.at[:, pl.ds(WIDE, WIDE)], ROWS, 0, WIDE),
                (k, 0, WIDE, HD),
                (v, ROWS, WIDE, HD),
            ]
        )
    ]
    first = pltpu.make_async_copy(owners, hits, sems.at[4])
    first.start()
    for copy in copies:
        copy.start()
    lane = iota((1, 2 * ROWS), 1)
    lane_request = (lane % ROWS) // TOK_REQ
    first.wait()
    for r in range(REQUESTS):
        for i in range(hit_count):
            count[hits[r * hit_count + i]] = 0
    rows = [[jnp.full((1, 2 * ROWS), -4 * MSG, jnp.int32)] * hit_count for _ in range(CAP)]
    for r in range(REQUESTS):
        for i in range(hit_count):
            owner = hits[r * hit_count + i]
            rank = count[owner]
            count[owner] = rank + 1
            message = place_of(devices, owner) * MSG
            for s in range(CAP):
                place = jnp.where(rank == s, message, -4 * MSG)
                rows[s][i] = jnp.where(lane_request == r, place, rows[s][i])
    inner = lane // ROWS * TOK_REQ + lane % TOK_REQ
    target = iota((devices * MSG, 2 * ROWS), 0)
    picks = []
    for s in range(CAP):
        chosen = None
        for i in range(hit_count):
            row = rows[s][i] + inner
            places[s * hit_count + i : s * hit_count + i + 1, :] = row
            hit = target == row
            chosen = hit if chosen is None else chosen | hit
        picks.append(jnp.where(chosen, 1.0, 0.0).astype(jnp.bfloat16))
    for copy in copies:
        copy.wait()
    for s in range(CAP):
        here = slice(s * (WIDE + HD), (s + 1) * (WIDE + HD))
        send[:, here] = dot(picks[s], held[...], NN).astype(jnp.bfloat16)


def prep_kernel(devices, hit_count, hits, prefix_len, span, values, busy, prompt, cached, wide):
    me = lax.axis_index("cache")
    total_rows = devices * MSG
    wide[:, :HD] = values[...]
    wide[:, HD:] = jnp.ones((CAP * REGION, HD), jnp.bfloat16)
    for slot in range(CAP):
        seen = jnp.int32(0)
        request = jnp.int32(0)
        which = jnp.int32(0)
        for r in range(REQUESTS):
            for i in range(hit_count):
                mine = hits[r * hit_count + i] == me
                here = mine & (seen == slot)
                request = jnp.where(here, r, request)
                which = jnp.where(here, i, which)
                seen = seen + mine.astype(jnp.int32)
        limit = prefix_len[request] - which * REGION
        blocks = jnp.clip((limit + STRIP - 1) // STRIP, 1, REGION // STRIP)
        busy[slot] = jnp.where(seen > slot, blocks, 0)
        cached[slot : slot + 1, :] = jnp.where(iota((1, REGION), 1) < limit, 0.0, FLOOR)
        span_row = span[pl.ds(request, 1), :].astype(jnp.float32)
        source = device_at(devices, iota((devices, total_rows), 1) // MSG)
        spread = (iota((devices, total_rows), 0) == source).astype(jnp.bfloat16)
        spans = jnp.broadcast_to(span_row, (16, devices)).astype(jnp.bfloat16)
        key_span = dot(spans, spread, NN)[:1]
        lane = iota((1, total_rows), 1)
        key_spot = key_span.astype(jnp.int32) * TOK_REQ + lane % TOK_REQ
        is_key = lane % MSG < TOK_REQ
        if hit_count > 1:
            is_key = is_key & (which == 0)
        key_spot = jnp.where(is_key, key_spot, devices * TOK_REQ)
        block = 16 * MSG

        def one_block(at):
            row_source = device_at(devices, at * 16 + iota((block, devices), 0) // MSG)
            mine = iota((block, devices), 1) == row_source
            row_span = jnp.sum(jnp.where(mine, span_row, 0.0), axis=1, keepdims=True)
            row_spot = row_span.astype(jnp.int32) * TOK_REQ + iota((block, 1), 0) % TOK_REQ
            here = pl.ds(slot * total_rows + at * block, block)
            prompt[here, :] = jnp.where(key_spot <= row_spot, 0.0, FLOOR)

        each_block(devices, one_block)


def each_block(devices, one_block):
    blocks = devices // 16
    if blocks == 1:
        one_block(0)
    else:
        pl.loop(0, blocks)(one_block)


def lanes_max(parts):
    pieces = [part[:, n : n + HD] for part in parts for n in range(0, part.shape[1], HD)]
    return jnp.max(functools.reduce(jnp.maximum, pieces), axis=1, keepdims=True)


def attend_kernel(devices, hit_count, busy, prompt_mask, cached_mask, got, keys, wide, out, *levels):
    total_rows = devices * MSG
    block = 16 * MSG
    factor = SCALE * math.log2(math.e)

    def nothing(slot):
        out[:, pl.ds(slot * WIDE, WIDE)] = jnp.zeros((total_rows, WIDE), jnp.bfloat16)
        for lse in levels:
            lse[:, pl.ds(slot * HD, HD)] = jnp.zeros((total_rows, HD), jnp.float32)

    def attend(slot, strips):
        whole = (strips - 1) * STRIP
        base = pl.multiple_of(slot * (WIDE + HD), HD)
        region = pl.multiple_of(slot * REGION, REGION)
        head = pl.ds(region, whole) if whole else None
        tail = pl.ds(pl.multiple_of(region + whole, STRIP), STRIP)
        tail_mask = cached_mask[pl.ds(slot, 1), whole : whole + STRIP]
        prompt_keys = got[:, pl.ds(base + WIDE, HD)]
        moved = pltpu.roll(prompt_keys.astype(jnp.float32), total_rows - TOK_REQ, 0)
        prompt_values = jnp.concatenate(
            [moved.astype(jnp.bfloat16), jnp.ones((total_rows, HD), jnp.bfloat16)], axis=1
        )

        def one_block(at):
            here = pl.ds(at * block, block)
            prompt_bias = prompt_mask[pl.ds(slot * total_rows + at * block, block), :]
            prompt_bias = jnp.concatenate([prompt_bias, prompt_bias], axis=0)
            lane = iota((block, HD), 1)

            def scores(c):
                pair = jnp.concatenate(
                    [got[here, pl.ds(base + (c + n) * HD, HD)] for n in range(2)], axis=0
                )
                parts = [dot(pair, keys[head, :], NT)] if whole else []
                parts.append(dot(pair, keys[tail, :], NT) + tail_mask)
                parts.append(dot(pair, prompt_keys, NT) + prompt_bias)
                return parts

            logs = jnp.zeros((block, HD), jnp.float32)
            parts = scores(0)
            for c in range(0, HALF, 2):
                later = scores(c + 2) if c + 2 < HALF else None
                top = lanes_max(parts)
                if hit_count > 1:
                    top = jnp.maximum(top, 0.1 * FLOOR)
                parts = [jnp.exp2((x - top) * factor).astype(jnp.bfloat16) for x in parts]
                summed = dot(parts[-1], prompt_values, NN) + dot(parts[-2], wide[tail, :], NN)
                if whole:
                    summed = summed + dot(parts[0], wide[head, :], NN)
                totals = summed[:, HD:]
                if hit_count > 1:
                    totals = jnp.maximum(totals, 1.0)
                    level = top * SCALE + jnp.log(totals)
                    logs = jnp.where(lane == c, level[:block], logs)
                    logs = jnp.where(lane == c + 1, level[block:], logs)
                result = (summed[:, :HD] / totals).astype(jnp.bfloat16)
                for n in range(2):
                    column = pl.multiple_of(slot * WIDE + (c + n) * HD, HD)
                    out[here, pl.ds(column, HD)] = result[n * block : (n + 1) * block]
                parts = later
            for lse in levels:
                lse[here, pl.ds(pl.multiple_of(slot * HD, HD), HD)] = logs

        each_block(devices, one_block)

    @pl.loop(0, CAP)
    def _(slot):
        strips = busy[slot]
        pl.when(strips == 0)(lambda: nothing(slot))
        for count in range(1, REGION // STRIP + 1):
            pl.when(strips == count)(functools.partial(attend, slot, count))


def unpack_kernel(devices, hit_count, places, *refs):
    outs, logs, result = refs[0], refs[1:-1], refs[-1]
    target = iota((devices * MSG, 2 * ROWS), 0)

    def chosen(s, i, dtype):
        place = s * hit_count + i
        return jnp.where(target == places[place : place + 1, :], 1.0, 0.0).astype(dtype)

    def rows_of(i):
        parts = [
            dot(chosen(s, i, jnp.bfloat16), outs[:, s * WIDE : (s + 1) * WIDE], TN)
            for s in range(CAP)
        ]
        return sum(parts[1:], parts[0])

    def logs_of(i):
        parts = [
            dot(
                chosen(s, i, jnp.float32),
                logs[0][:, s * HD : (s + 1) * HD],
                TN,
                precision=lax.Precision.HIGHEST,
            )
            for s in range(CAP)
        ]
        return sum(parts[1:], parts[0])

    if hit_count == 1:
        joined = rows_of(0)
    else:
        levels = [logs_of(i) for i in range(hit_count)]
        top = functools.reduce(jnp.maximum, levels)
        shares = [jnp.exp(level - top) for level in levels]
        total = sum(shares[1:], shares[0])
        pieces = [rows_of(i) for i in range(hit_count)]
        columns = []
        for c in range(HALF):
            part = sum(
                shares[i][:, c : c + 1] * pieces[i][:, c * HD : (c + 1) * HD]
                for i in range(hit_count)
            )
            columns.append(part / total[:, c : c + 1])
        joined = jnp.concatenate(columns, axis=1)
    joined = joined.astype(jnp.bfloat16)
    result[:, :WIDE] = joined[:ROWS]
    result[:, WIDE:] = joined[ROWS:]


def vmem(count):
    return [pl.BlockSpec(memory_space=pltpu.VMEM)] * count


def smem(count):
    return [pl.BlockSpec(memory_space=pltpu.SMEM)] * count


def hbm(count):
    return [pl.BlockSpec(memory_space=pltpu.HBM)] * count


def body(prefix_len, hits, span_block, queries, fresh_keys, fresh_values, cache_keys, cache_values):
    devices = lax.axis_size("cache")
    hit_count = hits.shape[1]
    rows = devices * MSG
    owners = hits.reshape(REQUESTS * hit_count)
    fresh = (owners, queries, fresh_keys, fresh_values)

    order = [[device_at(devices, place) for place in range(devices)]]

    def exchange(x):
        return lax.all_to_all(
            x, "cache", split_axis=0, concat_axis=0, axis_index_groups=order, tiled=True
        )

    def call(kernel, out_shape, name, grant=40, **kw):
        return pl.pallas_call(
            functools.partial(kernel, devices, hit_count),
            out_shape=[jax.ShapeDtypeStruct(*leaf) for leaf in out_shape],
            compiler_params=pltpu.CompilerParams(vmem_limit_bytes=grant * 2**20),
            name=name,
            **kw,
        )

    send, places = call(
        pack_kernel,
        [((rows, CAP * (WIDE + HD)), jnp.bfloat16), ((CAP * hit_count, 2 * ROWS), jnp.int32)],
        "pack",
        in_specs=hbm(4),
        out_specs=vmem(2),
        scratch_shapes=[
            pltpu.VMEM((2 * ROWS, WIDE + HD), jnp.bfloat16),
            pltpu.SMEM((REQUESTS * hit_count,), jnp.int32),
            pltpu.SMEM((devices,), jnp.int32),
            pltpu.SemaphoreType.DMA((5,)),
        ],
    )(*(pltpu.with_memory_space_constraint(x, pltpu.HBM) for x in fresh))
    got = exchange(send)
    busy, prompt_mask, cached_mask, wide = call(
        prep_kernel,
        [
            ((CAP,), jnp.int32),
            ((CAP * rows, rows), jnp.float32),
            ((CAP, REGION), jnp.float32),
            ((CAP * REGION, 2 * HD), jnp.bfloat16),
        ],
        "prep",
        in_specs=smem(2) + vmem(2),
        out_specs=smem(1) + vmem(3),
        cost_estimate=pl.CostEstimate(flops=10**6, bytes_accessed=2**22, transcendentals=0),
    )(owners, prefix_len, span_block, cache_values)
    pairs = CAP * rows * HALF * (REGION + rows)
    answers = call(
        attend_kernel,
        [((rows, CAP * WIDE), jnp.bfloat16)]
        + [((rows, CAP * HD), jnp.float32)] * (hit_count > 1),
        "attend",
        in_specs=smem(1) + vmem(5),
        out_specs=vmem(1 + (hit_count > 1)),
        cost_estimate=pl.CostEstimate(
            flops=4 * pairs * HD, bytes_accessed=8 * rows * WIDE, transcendentals=pairs
        ),
    )(busy, prompt_mask, cached_mask, got, cache_keys, wide)
    returned = [exchange(answer) for answer in answers]
    return call(
        unpack_kernel,
        [((ROWS, HEADS * HD), jnp.bfloat16)],
        "unpack",
        in_specs=vmem(1 + len(returned)),
        out_specs=vmem(1),
    )(places, *returned)[0]


def solution(mesh):
    in_specs = (
        P("groups"),
        P("groups", None),
        P("groups", None),
        P(("groups", "cache"), None),
        P(("groups", "cache"), None),
        P(("groups", "cache"), None),
        P(("groups", "cache"), None),
        P(("groups", "cache"), None),
    )
    out_specs = P(("groups", "cache"), None)
    return jax.shard_map(body, mesh=mesh, in_specs=in_specs, out_specs=out_specs, check_vma=False)
```

```python
import functools
import math

import jax
import jax.numpy as jnp
from jax import lax
from jax.experimental import pallas as pl
from jax.experimental.pallas import tpu as pltpu
from jax.sharding import PartitionSpec as P

HEADS = 16
HD = 128
PAGE = 128
CAP = 2
REQUESTS = 16
TOK_REQ = 4
PAGES_DEV = 16

REGION = PAGES_DEV // CAP * PAGE
HALF = HEADS // 2
MSG = 2 * TOK_REQ
WIDE = HALF * HD
ROWS = REQUESTS * TOK_REQ
STRIP = 256
SCALE = HD**-0.5
FLOOR = -1e30
NT = (((1,), (1,)), ((), ()))
NN = (((1,), (0,)), ((), ()))
TN = (((0,), (0,)), ((), ()))


def iota(shape, axis):
    return lax.broadcasted_iota(jnp.int32, shape, axis)


def dot(a, b, dims, **kw):
    return lax.dot_general(a, b, dims, preferred_element_type=jnp.float32, **kw)


def place_of(devices, device):
    return device * (devices // 2 - 1) % devices


device_at = place_of


def pack_kernel(devices, hit_count, owners, q, k, v, send, places, held, hits, count, sems):
    copies = [
        pltpu.make_async_copy(source, held.at[pl.ds(row, ROWS), pl.ds(column, width)], sems.at[n])
        for n, (source, row, column, width) in enumerate(
            [
                (q.at[:, pl.ds(0, WIDE)], 0, 0, WIDE),
                (q.at[:, pl.ds(WIDE, WIDE)], ROWS, 0, WIDE),
                (k, 0, WIDE, HD),
                (v, ROWS, WIDE, HD),
            ]
        )
    ]
    first = pltpu.make_async_copy(owners, hits, sems.at[4])
    first.start()
    for copy in copies:
        copy.start()
    lane = iota((1, 2 * ROWS), 1)
    lane_request = (lane % ROWS) // TOK_REQ
    first.wait()
    for r in range(REQUESTS):
        for i in range(hit_count):
            count[hits[r * hit_count + i]] = 0
    rows = [[jnp.full((1, 2 * ROWS), -4 * MSG, jnp.int32)] * hit_count for _ in range(CAP)]
    for r in range(REQUESTS):
        for i in range(hit_count):
            owner = hits[r * hit_count + i]
            rank = count[owner]
            count[owner] = rank + 1
            message = place_of(devices, owner) * MSG
            for s in range(CAP):
                place = jnp.where(rank == s, message, -4 * MSG)
                rows[s][i] = jnp.where(lane_request == r, place, rows[s][i])
    inner = lane // ROWS * TOK_REQ + lane % TOK_REQ
    target = iota((devices * MSG, 2 * ROWS), 0)
    picks = []
    for s in range(CAP):
        chosen = None
        for i in range(hit_count):
            row = rows[s][i] + inner
            places[s * hit_count + i : s * hit_count + i + 1, :] = row
            hit = target == row
            chosen = hit if chosen is None else chosen | hit
        picks.append(jnp.where(chosen, 1.0, 0.0).astype(jnp.bfloat16))
    for copy in copies:
        copy.wait()
    for s in range(CAP):
        here = slice(s * (WIDE + HD), (s + 1) * (WIDE + HD))
        send[:, here] = dot(picks[s], held[...], NN).astype(jnp.bfloat16)


def prep_kernel(devices, hit_count, hits, prefix_len, span, values, busy, prompt, cached, wide):
    me = lax.axis_index("cache")
    total_rows = devices * MSG
    wide[:, :HD] = values[...]
    wide[:, HD:] = jnp.ones((CAP * REGION, HD), jnp.bfloat16)
    for slot in range(CAP):
        seen = jnp.int32(0)
        request = jnp.int32(0)
        which = jnp.int32(0)
        for r in range(REQUESTS):
            for i in range(hit_count):
                mine = hits[r * hit_count + i] == me
                here = mine & (seen == slot)
                request = jnp.where(here, r, request)
                which = jnp.where(here, i, which)
                seen = seen + mine.astype(jnp.int32)
        limit = prefix_len[request] - which * REGION
        blocks = jnp.clip((limit + STRIP - 1) // STRIP, 1, REGION // STRIP)
        busy[slot] = jnp.where(seen > slot, blocks, 0)
        cached[slot : slot + 1, :] = jnp.where(iota((1, REGION), 1) < limit, 0.0, FLOOR)
        span_row = span[pl.ds(request, 1), :].astype(jnp.float32)
        source = device_at(devices, iota((devices, total_rows), 1) // MSG)
        spread = (iota((devices, total_rows), 0) == source).astype(jnp.bfloat16)
        spans = jnp.broadcast_to(span_row, (16, devices)).astype(jnp.bfloat16)
        key_span = dot(spans, spread, NN)[:1]
        lane = iota((1, total_rows), 1)
        key_spot = key_span.astype(jnp.int32) * TOK_REQ + lane % TOK_REQ
        is_key = lane % MSG < TOK_REQ
        if hit_count > 1:
            is_key = is_key & (which == 0)
        key_spot = jnp.where(is_key, key_spot, devices * TOK_REQ)
        block = 16 * MSG

        def one_block(at):
            row_source = device_at(devices, at * 16 + iota((block, devices), 0) // MSG)
            mine = iota((block, devices), 1) == row_source
            row_span = jnp.sum(jnp.where(mine, span_row, 0.0), axis=1, keepdims=True)
            row_spot = row_span.astype(jnp.int32) * TOK_REQ + iota((block, 1), 0) % TOK_REQ
            here = pl.ds(slot * total_rows + at * block, block)
            prompt[here, :] = jnp.where(key_spot <= row_spot, 0.0, FLOOR)

        each_block(devices, one_block)


def each_block(devices, one_block):
    blocks = devices // 16
    if blocks == 1:
        one_block(0)
    else:
        pl.loop(0, blocks)(one_block)


def lanes_max(parts):
    pieces = [part[:, n : n + HD] for part in parts for n in range(0, part.shape[1], HD)]
    return jnp.max(functools.reduce(jnp.maximum, pieces), axis=1, keepdims=True)


def attend_kernel(devices, hit_count, busy, prompt_mask, cached_mask, got, keys, wide, out, *levels):
    total_rows = devices * MSG
    block = 16 * MSG
    factor = SCALE * math.log2(math.e)

    def nothing(slot):
        out[:, pl.ds(slot * WIDE, WIDE)] = jnp.zeros((total_rows, WIDE), jnp.bfloat16)
        for lse in levels:
            lse[:, pl.ds(slot * HD, HD)] = jnp.zeros((total_rows, HD), jnp.float32)

    def attend(slot, strips):
        whole = (strips - 1) * STRIP
        base = pl.multiple_of(slot * (WIDE + HD), HD)
        region = pl.multiple_of(slot * REGION, REGION)
        head = pl.ds(region, whole) if whole else None
        tail = pl.ds(pl.multiple_of(region + whole, STRIP), STRIP)
        tail_mask = cached_mask[pl.ds(slot, 1), whole : whole + STRIP]
        prompt_keys = got[:, pl.ds(base + WIDE, HD)]
        moved = pltpu.roll(prompt_keys.astype(jnp.float32), total_rows - TOK_REQ, 0)
        prompt_values = jnp.concatenate(
            [moved.astype(jnp.bfloat16), jnp.ones((total_rows, HD), jnp.bfloat16)], axis=1
        )

        def one_block(at):
            here = pl.ds(at * block, block)
            prompt_bias = prompt_mask[pl.ds(slot * total_rows + at * block, block), :]
            prompt_bias = jnp.concatenate([prompt_bias, prompt_bias], axis=0)
            lane = iota((block, HD), 1)

            def scores(c):
                pair = jnp.concatenate(
                    [got[here, pl.ds(base + (c + n) * HD, HD)] for n in range(2)], axis=0
                )
                parts = [dot(pair, keys[head, :], NT)] if whole else []
                parts.append(dot(pair, keys[tail, :], NT) + tail_mask)
                parts.append(dot(pair, prompt_keys, NT) + prompt_bias)
                return parts

            logs = jnp.zeros((block, HD), jnp.float32)
            parts = scores(0)
            for c in range(0, HALF, 2):
                later = scores(c + 2) if c + 2 < HALF else None
                top = lanes_max(parts)
                if hit_count > 1:
                    top = jnp.maximum(top, 0.1 * FLOOR)
                parts = [jnp.exp2((x - top) * factor).astype(jnp.bfloat16) for x in parts]
                summed = dot(parts[-1], prompt_values, NN) + dot(parts[-2], wide[tail, :], NN)
                if whole:
                    summed = summed + dot(parts[0], wide[head, :], NN)
                totals = summed[:, HD:]
                if hit_count > 1:
                    totals = jnp.maximum(totals, 1.0)
                    level = top * SCALE + jnp.log(totals)
                    logs = jnp.where(lane == c, level[:block], logs)
                    logs = jnp.where(lane == c + 1, level[block:], logs)
                result = (summed[:, :HD] / totals).astype(jnp.bfloat16)
                for n in range(2):
                    column = pl.multiple_of(slot * WIDE + (c + n) * HD, HD)
                    out[here, pl.ds(column, HD)] = result[n * block : (n + 1) * block]
                parts = later
            for lse in levels:
                lse[here, pl.ds(pl.multiple_of(slot * HD, HD), HD)] = logs

        each_block(devices, one_block)

    @pl.loop(0, CAP)
    def _(slot):
        strips = busy[slot]
        pl.when(strips == 0)(lambda: nothing(slot))
        for count in range(1, REGION // STRIP + 1):
            pl.when(strips == count)(functools.partial(attend, slot, count))


def unpack_kernel(devices, hit_count, places, *refs):
    outs, logs, result = refs[0], refs[1:-1], refs[-1]
    target = iota((devices * MSG, 2 * ROWS), 0)

    def chosen(s, i, dtype):
        place = s * hit_count + i
        return jnp.where(target == places[place : place + 1, :], 1.0, 0.0).astype(dtype)

    def rows_of(i):
        parts = [
            dot(chosen(s, i, jnp.bfloat16), outs[:, s * WIDE : (s + 1) * WIDE], TN)
            for s in range(CAP)
        ]
        return sum(parts[1:], parts[0])

    def logs_of(i):
        parts = [
            dot(
                chosen(s, i, jnp.float32),
                logs[0][:, s * HD : (s + 1) * HD],
                TN,
                precision=lax.Precision.HIGHEST,
            )
            for s in range(CAP)
        ]
        return sum(parts[1:], parts[0])

    if hit_count == 1:
        joined = rows_of(0)
    else:
        levels = [logs_of(i) for i in range(hit_count)]
        top = functools.reduce(jnp.maximum, levels)
        shares = [jnp.exp(level - top) for level in levels]
        total = sum(shares[1:], shares[0])
        pieces = [rows_of(i) for i in range(hit_count)]
        columns = []
        for c in range(HALF):
            part = sum(
                shares[i][:, c : c + 1] * pieces[i][:, c * HD : (c + 1) * HD]
                for i in range(hit_count)
            )
            columns.append(part / total[:, c : c + 1])
        joined = jnp.concatenate(columns, axis=1)
    joined = joined.astype(jnp.bfloat16)
    result[:, :WIDE] = joined[:ROWS]
    result[:, WIDE:] = joined[ROWS:]


def vmem(count):
    return [pl.BlockSpec(memory_space=pltpu.VMEM)] * count


def smem(count):
    return [pl.BlockSpec(memory_space=pltpu.SMEM)] * count


def hbm(count):
    return [pl.BlockSpec(memory_space=pltpu.HBM)] * count


def body(prefix_len, hits, span_block, queries, fresh_keys, fresh_values, cache_keys, cache_values):
    devices = lax.axis_size("cache")
    hit_count = hits.shape[1]
    rows = devices * MSG
    owners = hits.reshape(REQUESTS * hit_count)
    fresh = (owners, queries, fresh_keys, fresh_values)

    order = [[device_at(devices, place) for place in range(devices)]]

    def exchange(x):
        return lax.all_to_all(
            x, "cache", split_axis=0, concat_axis=0, axis_index_groups=order, tiled=True
        )

    def call(kernel, out_shape, name, grant=40, **kw):
        return pl.pallas_call(
            functools.partial(kernel, devices, hit_count),
            out_shape=[jax.ShapeDtypeStruct(*leaf) for leaf in out_shape],
            compiler_params=pltpu.CompilerParams(vmem_limit_bytes=grant * 2**20),
            name=name,
            **kw,
        )

    send, places = call(
        pack_kernel,
        [((rows, CAP * (WIDE + HD)), jnp.bfloat16), ((CAP * hit_count, 2 * ROWS), jnp.int32)],
        "pack",
        in_specs=hbm(4),
        out_specs=vmem(2),
        scratch_shapes=[
            pltpu.VMEM((2 * ROWS, WIDE + HD), jnp.bfloat16),
            pltpu.SMEM((REQUESTS * hit_count,), jnp.int32),
            pltpu.SMEM((devices,), jnp.int32),
            pltpu.SemaphoreType.DMA((5,)),
        ],
    )(*(pltpu.with_memory_space_constraint(x, pltpu.HBM) for x in fresh))
    got = exchange(send)
    busy, prompt_mask, cached_mask, wide = call(
        prep_kernel,
        [
            ((CAP,), jnp.int32),
            ((CAP * rows, rows), jnp.float32),
            ((CAP, REGION), jnp.float32),
            ((CAP * REGION, 2 * HD), jnp.bfloat16),
        ],
        "prep",
        in_specs=smem(2) + vmem(2),
        out_specs=smem(1) + vmem(3),
        cost_estimate=pl.CostEstimate(flops=10**6, bytes_accessed=2**22, transcendentals=0),
    )(owners, prefix_len, span_block, cache_values)
    pairs = CAP * rows * HALF * (REGION + rows)
    answers = call(
        attend_kernel,
        [((rows, CAP * WIDE), jnp.bfloat16)]
        + [((rows, CAP * HD), jnp.float32)] * (hit_count > 1),
        "attend",
        in_specs=smem(1) + vmem(5),
        out_specs=vmem(1 + (hit_count > 1)),
        cost_estimate=pl.CostEstimate(
            flops=4 * pairs * HD, bytes_accessed=8 * rows * WIDE, transcendentals=pairs
        ),
    )(busy, prompt_mask, cached_mask, got, cache_keys, wide)
    returned = [exchange(answer) for answer in answers]
    return call(
        unpack_kernel,
        [((ROWS, HEADS * HD), jnp.bfloat16)],
        "unpack",
        in_specs=vmem(1 + len(returned)),
        out_specs=vmem(1),
    )(places, *returned)[0]


def solution(mesh):
    in_specs = (
        P("groups"),
        P("groups", None),
        P("groups", None),
        P(("groups", "cache"), None),
        P(("groups", "cache"), None),
        P(("groups", "cache"), None),
        P(("groups", "cache"), None),
        P(("groups", "cache"), None),
    )
    out_specs = P(("groups", "cache"), None)
    return jax.shard_map(body, mesh=mesh, in_specs=in_specs, out_specs=out_specs, check_vma=False)
```

```python
import functools
import math

import jax
import jax.numpy as jnp
from jax import lax
from jax.experimental import pallas as pl
from jax.experimental.pallas import tpu as pltpu
from jax.sharding import PartitionSpec as P

HEADS = 16
HD = 128
PAGE = 128
CAP = 2
REQUESTS = 16
TOK_REQ = 4
PAGES_DEV = 16

REGION = PAGES_DEV // CAP * PAGE
HALF = HEADS // 2
MSG = 2 * TOK_REQ
WIDE = HALF * HD
ROWS = REQUESTS * TOK_REQ
STRIP = 256
SCALE = HD**-0.5
FLOOR = -1e30
NN = (((1,), (0,)), ((), ()))


def iota(shape, axis):
    return lax.broadcasted_iota(jnp.int32, shape, axis)


def dot(a, b, dims, **kw):
    return lax.dot_general(a, b, dims, preferred_element_type=jnp.float32, **kw)


def pack_kernel(devices, hit_count, owners, q, k, v, send, places, held, hits, count, sems):
    copies = [
        pltpu.make_async_copy(source, held.at[pl.ds(row, ROWS), pl.ds(column, width)], sems.at[n])
        for n, (source, row, column, width) in enumerate(
            [
                (q.at[:, pl.ds(0, WIDE)], 0, 0, WIDE),
                (q.at[:, pl.ds(WIDE, WIDE)], ROWS, 0, WIDE),
                (k, 0, WIDE, HD),
                (v, ROWS, WIDE, HD),
            ]
        )
    ]
    first = pltpu.make_async_copy(owners, hits, sems.at[4])
    first.start()
    for copy in copies:
        copy.start()
    lane = iota((1, 2 * ROWS), 1)
    lane_request = (lane % ROWS) // TOK_REQ
    first.wait()
    for r in range(REQUESTS):
        for i in range(hit_count):
            count[hits[r * hit_count + i]] = 0
    rows = [[jnp.full((1, 2 * ROWS), -4 * MSG, jnp.int32)] * hit_count for _ in range(CAP)]
    for r in range(REQUESTS):
        for i in range(hit_count):
            owner = hits[r * hit_count + i]
            rank = count[owner]
            count[owner] = rank + 1
            for s in range(CAP):
                place = jnp.where(rank == s, owner * MSG, -4 * MSG)
                rows[s][i] = jnp.where(lane_request == r, place, rows[s][i])
    inner = lane // ROWS * TOK_REQ + lane % TOK_REQ
    target = iota((devices * MSG, 2 * ROWS), 0)
    picks = []
    for s in range(CAP):
        chosen = None
        for i in range(hit_count):
            row = rows[s][i] + inner
            places[s * hit_count + i : s * hit_count + i + 1, :] = row
            hit = target == row
            chosen = hit if chosen is None else chosen | hit
        picks.append(jnp.where(chosen, 1.0, 0.0).astype(jnp.bfloat16))
    for copy in copies:
        copy.wait()
    packed = dot(jnp.concatenate(picks, axis=0), held[...], NN).astype(jnp.bfloat16)
    for s in range(CAP):
        rows = slice(s * devices * MSG, (s + 1) * devices * MSG)
        send[:, s * (WIDE + HD) : (s + 1) * (WIDE + HD)] = packed[rows]


def prep_kernel(
    devices, hit_count, hits, prefix_len, span, places, keys, values, *outs
):
    busy, prompt, cached, turned, wide, picks = outs
    rows = iota((devices * MSG, 2 * ROWS), 0)
    for n in range(CAP * hit_count):
        chosen = jnp.where(rows == places[n : n + 1, :], 1.0, 0.0)
        picks[n * 2 * ROWS : (n + 1) * 2 * ROWS, :] = chosen.T.astype(jnp.bfloat16)
    for n in range(0, CAP * REGION, STRIP):
        turned[:, n : n + STRIP] = keys[n : n + STRIP, :].T
    me = lax.axis_index("cache")
    total_rows = devices * MSG
    wide[:, :HD] = values[...]
    wide[:, HD:] = jnp.ones((CAP * REGION, HD), jnp.bfloat16)
    for slot in range(CAP):
        seen = jnp.int32(0)
        request = jnp.int32(0)
        which = jnp.int32(0)
        for r in range(REQUESTS):
            for i in range(hit_count):
                mine = hits[r * hit_count + i] == me
                here = mine & (seen == slot)
                request = jnp.where(here, r, request)
                which = jnp.where(here, i, which)
                seen = seen + mine.astype(jnp.int32)
        limit = prefix_len[request] - which * REGION
        blocks = jnp.clip((limit + STRIP - 1) // STRIP, 1, REGION // STRIP)
        busy[slot] = jnp.where(seen > slot, blocks, 0)
        cached[slot : slot + 1, :] = jnp.where(iota((1, REGION), 1) < limit, 0.0, FLOOR)
        span_row = span[pl.ds(request, 1), :].astype(jnp.float32)
        source = iota((devices, total_rows), 0)
        spread = (iota((devices, total_rows), 1) // MSG == source).astype(jnp.bfloat16)
        spans = jnp.broadcast_to(span_row, (16, devices)).astype(jnp.bfloat16)
        key_span = dot(spans, spread, NN)[:1]
        lane = iota((1, total_rows), 1)
        key_spot = key_span.astype(jnp.int32) * TOK_REQ + lane % TOK_REQ
        is_key = lane % MSG < TOK_REQ
        if hit_count > 1:
            is_key = is_key & (which == 0)
        key_spot = jnp.where(is_key, key_spot, devices * TOK_REQ)
        block = 16 * MSG

        def one_block(at):
            row_source = at * 16 + iota((block, devices), 0) // MSG
            mine = iota((block, devices), 1) == row_source
            row_span = jnp.sum(jnp.where(mine, span_row, 0.0), axis=1, keepdims=True)
            row_spot = row_span.astype(jnp.int32) * TOK_REQ + iota((block, 1), 0) % TOK_REQ
            here = pl.ds(slot * total_rows + at * block, block)
            prompt[here, :] = jnp.where(key_spot <= row_spot, 0.0, FLOOR)

        each_block(devices, one_block)


def each_block(devices, one_block):
    blocks = devices // 16
    if blocks == 1:
        one_block(0)
    else:
        pl.loop(0, blocks)(one_block)


def lanes_max(parts):
    pieces = [part[:, n : n + HD] for part in parts for n in range(0, part.shape[1], HD)]
    return jnp.max(functools.reduce(jnp.maximum, pieces), axis=1, keepdims=True)


def attend_kernel(
    devices, hit_count, busy, prompt_mask, cached_mask, got, turned, wide, out, *levels
):
    total_rows = devices * MSG
    block = 16 * MSG
    factor = SCALE * math.log2(math.e)

    def nothing(slot):
        out[:, pl.ds(slot * WIDE, WIDE)] = jnp.zeros((total_rows, WIDE), jnp.bfloat16)
        for lse in levels:
            lse[:, pl.ds(slot * HD, HD)] = jnp.zeros((total_rows, HD), jnp.float32)

    def attend(slot, strips):
        whole = (strips - 1) * STRIP
        base = pl.multiple_of(slot * (WIDE + HD), HD)
        region = pl.multiple_of(slot * REGION, REGION)
        head = pl.ds(region, whole) if whole else None
        tail = pl.ds(pl.multiple_of(region + whole, STRIP), STRIP)
        tail_mask = cached_mask[pl.ds(slot, 1), whole : whole + STRIP]
        prompt_keys = got[:, pl.ds(base + WIDE, HD)].astype(jnp.float32)
        moved = pltpu.roll(prompt_keys, total_rows - TOK_REQ, 0)
        prompt_keys = prompt_keys.T.astype(jnp.bfloat16)
        prompt_values = jnp.concatenate(
            [moved.astype(jnp.bfloat16), jnp.ones((total_rows, HD), jnp.bfloat16)], axis=1
        )

        def one_block(at):
            here = pl.ds(at * block, block)
            prompt_bias = prompt_mask[pl.ds(slot * total_rows + at * block, block), :]
            prompt_bias = jnp.concatenate([prompt_bias, prompt_bias], axis=0)
            lane = iota((block, HD), 1)

            def scores(c):
                pair = jnp.concatenate(
                    [got[here, pl.ds(base + (c + n) * HD, HD)] for n in range(2)], axis=0
                )
                parts = [dot(pair, turned[:, head], NN)] if whole else []
                parts.append(dot(pair, turned[:, tail], NN) + tail_mask)
                parts.append(dot(pair, prompt_keys, NN) + prompt_bias)
                return parts

            logs = jnp.zeros((block, HD), jnp.float32)
            parts = scores(0)
            for c in range(0, HALF, 2):
                later = scores(c + 2) if c + 2 < HALF else None
                top = lanes_max(parts)
                if hit_count > 1:
                    top = jnp.maximum(top, 0.1 * FLOOR)
                parts = [jnp.exp2((x - top) * factor).astype(jnp.bfloat16) for x in parts]
                summed = dot(parts[-1], prompt_values, NN) + dot(parts[-2], wide[tail, :], NN)
                if whole:
                    summed = summed + dot(parts[0], wide[head, :], NN)
                totals = summed[:, HD:]
                if hit_count > 1:
                    totals = jnp.maximum(totals, 1.0)
                    level = top * SCALE + jnp.log(totals)
                    logs = jnp.where(lane == c, level[:block], logs)
                    logs = jnp.where(lane == c + 1, level[block:], logs)
                result = (summed[:, :HD] / totals).astype(jnp.bfloat16)
                for n in range(2):
                    column = pl.multiple_of(slot * WIDE + (c + n) * HD, HD)
                    out[here, pl.ds(column, HD)] = result[n * block : (n + 1) * block]
                parts = later
            for lse in levels:
                lse[here, pl.ds(pl.multiple_of(slot * HD, HD), HD)] = logs

        each_block(devices, one_block)

    @pl.loop(0, CAP)
    def _(slot):
        strips = busy[slot]
        pl.when(strips == 0)(lambda: nothing(slot))
        for count in range(1, REGION // STRIP + 1):
            pl.when(strips == count)(functools.partial(attend, slot, count))


def unpack_kernel(devices, hit_count, picks, *refs):
    outs, logs, result = refs[0], refs[1:-1], refs[-1]

    def chosen(s, i):
        place = s * hit_count + i
        return picks[place * 2 * ROWS : (place + 1) * 2 * ROWS, :]

    def rows_of(i):
        parts = [
            dot(chosen(s, i), outs[:, s * WIDE : (s + 1) * WIDE], NN)
            for s in range(CAP)
        ]
        return sum(parts[1:], parts[0])

    def logs_of(i):
        parts = [
            dot(
                chosen(s, i).astype(jnp.float32),
                logs[0][:, s * HD : (s + 1) * HD],
                NN,
                precision=lax.Precision.HIGHEST,
            )
            for s in range(CAP)
        ]
        return sum(parts[1:], parts[0])

    if hit_count == 1:
        joined = rows_of(0)
    else:
        levels = [logs_of(i) for i in range(hit_count)]
        top = functools.reduce(jnp.maximum, levels)
        shares = [jnp.exp(level - top) for level in levels]
        total = sum(shares[1:], shares[0])
        pieces = [rows_of(i) for i in range(hit_count)]
        columns = []
        for c in range(HALF):
            part = sum(
                shares[i][:, c : c + 1] * pieces[i][:, c * HD : (c + 1) * HD]
                for i in range(hit_count)
            )
            columns.append(part / total[:, c : c + 1])
        joined = jnp.concatenate(columns, axis=1)
    joined = joined.astype(jnp.bfloat16)
    result[:, :WIDE] = joined[:ROWS]
    result[:, WIDE:] = joined[ROWS:]


def vmem(count):
    return [pl.BlockSpec(memory_space=pltpu.VMEM)] * count


def smem(count):
    return [pl.BlockSpec(memory_space=pltpu.SMEM)] * count


def hbm(count):
    return [pl.BlockSpec(memory_space=pltpu.HBM)] * count


def body(prefix_len, hits, span_block, queries, fresh_keys, fresh_values, cache_keys, cache_values):
    devices = lax.axis_size("cache")
    hit_count = hits.shape[1]
    rows = devices * MSG
    owners = hits.reshape(REQUESTS * hit_count)
    fresh = (owners, queries, fresh_keys, fresh_values)

    def exchange(x):
        return lax.all_to_all(x, "cache", split_axis=0, concat_axis=0, tiled=True)

    def call(kernel, out_shape, name, grant=40, **kw):
        return pl.pallas_call(
            functools.partial(kernel, devices, hit_count),
            out_shape=[jax.ShapeDtypeStruct(*leaf) for leaf in out_shape],
            compiler_params=pltpu.CompilerParams(vmem_limit_bytes=grant * 2**20),
            name=name,
            **kw,
        )

    send, places = call(
        pack_kernel,
        [((rows, CAP * (WIDE + HD)), jnp.bfloat16), ((CAP * hit_count, 2 * ROWS), jnp.int32)],
        "pack",
        in_specs=hbm(4),
        out_specs=vmem(2),
        scratch_shapes=[
            pltpu.VMEM((2 * ROWS, WIDE + HD), jnp.bfloat16),
            pltpu.SMEM((REQUESTS * hit_count,), jnp.int32),
            pltpu.SMEM((devices,), jnp.int32),
            pltpu.SemaphoreType.DMA((5,)),
        ],
    )(*(pltpu.with_memory_space_constraint(x, pltpu.HBM) for x in fresh))
    got = exchange(send)
    busy, prompt_mask, cached_mask, turned, wide, picks = call(
        prep_kernel,
        [
            ((CAP,), jnp.int32),
            ((CAP * rows, rows), jnp.float32),
            ((CAP, REGION), jnp.float32),
            ((HD, CAP * REGION), jnp.bfloat16),
            ((CAP * REGION, 2 * HD), jnp.bfloat16),
            ((CAP * hit_count * 2 * ROWS, rows), jnp.bfloat16),
        ],
        "prep",
        in_specs=smem(2) + vmem(4),
        out_specs=smem(1) + vmem(5),
        cost_estimate=pl.CostEstimate(flops=10**6, bytes_accessed=2**22, transcendentals=0),
    )(owners, prefix_len, span_block, places, cache_keys, cache_values)
    pairs = CAP * rows * HALF * (REGION + rows)
    answers = call(
        attend_kernel,
        [((rows, CAP * WIDE), jnp.bfloat16)]
        + [((rows, CAP * HD), jnp.float32)] * (hit_count > 1),
        "attend",
        in_specs=smem(1) + vmem(5),
        out_specs=vmem(1 + (hit_count > 1)),
        cost_estimate=pl.CostEstimate(
            flops=4 * pairs * HD, bytes_accessed=8 * rows * WIDE, transcendentals=pairs
        ),
    )(busy, prompt_mask, cached_mask, got, turned, wide)
    returned = [exchange(answer) for answer in answers]
    return call(
        unpack_kernel,
        [((ROWS, HEADS * HD), jnp.bfloat16)],
        "unpack",
        in_specs=vmem(1 + len(returned)),
        out_specs=vmem(1),
    )(picks, *returned)[0]


def solution(mesh):
    in_specs = (
        P("groups"),
        P("groups", None),
        P("groups", None),
        P(("groups", "cache"), None),
        P(("groups", "cache"), None),
        P(("groups", "cache"), None),
        P(("groups", "cache"), None),
        P(("groups", "cache"), None),
    )
    out_specs = P(("groups", "cache"), None)
    return jax.shard_map(body, mesh=mesh, in_specs=in_specs, out_specs=out_specs, check_vma=False)
```

```python
import functools
import math

import jax
import jax.numpy as jnp
from jax import lax
from jax.experimental import pallas as pl
from jax.experimental.pallas import tpu as pltpu
from jax.sharding import PartitionSpec as P

HEADS = 16
HD = 128
PAGE = 128
CAP = 2
REQUESTS = 16
TOK_REQ = 4
PAGES_DEV = 16

REGION = PAGES_DEV // CAP * PAGE
HALF = HEADS // 2
MSG = 2 * TOK_REQ
WIDE = HALF * HD
ROWS = REQUESTS * TOK_REQ
STRIP = 256
GUEST_MSG = WIDE + HD + WIDE // 2 + HD
SCALE = HD**-0.5
FLOOR = -1e30
NN = (((1,), (0,)), ((), ()))


def iota(shape, axis):
    return lax.broadcasted_iota(jnp.int32, shape, axis)


def dot(a, b, dims, **kw):
    return lax.dot_general(a, b, dims, preferred_element_type=jnp.float32, **kw)


def pack_kernel(devices, hit_count, owners, q, k, v, send, places, held, hits, count, sems):
    copies = [
        pltpu.make_async_copy(source, held.at[pl.ds(row, ROWS), pl.ds(column, width)], sems.at[n])
        for n, (source, row, column, width) in enumerate(
            [
                (q.at[:, pl.ds(0, WIDE)], 0, 0, WIDE),
                (q.at[:, pl.ds(WIDE, WIDE)], ROWS, 0, WIDE),
                (k, 0, WIDE, HD),
                (v, ROWS, WIDE, HD),
            ]
        )
    ]
    first = pltpu.make_async_copy(owners, hits, sems.at[4])
    first.start()
    for copy in copies:
        copy.start()
    lane = iota((1, 2 * ROWS), 1)
    lane_request = (lane % ROWS) // TOK_REQ
    first.wait()
    for r in range(REQUESTS):
        for i in range(hit_count):
            count[hits[r * hit_count + i]] = 0
    rows = [[jnp.full((1, 2 * ROWS), -4 * MSG, jnp.int32)] * hit_count for _ in range(CAP)]
    for r in range(REQUESTS):
        for i in range(hit_count):
            owner = hits[r * hit_count + i]
            rank = count[owner]
            count[owner] = rank + 1
            for s in range(CAP):
                place = jnp.where(rank == s, owner * MSG, -4 * MSG)
                rows[s][i] = jnp.where(lane_request == r, place, rows[s][i])
    inner = lane // ROWS * TOK_REQ + lane % TOK_REQ
    target = iota((devices * MSG, 2 * ROWS), 0)
    picks = []
    for s in range(CAP):
        chosen = None
        for i in range(hit_count):
            row = rows[s][i] + inner
            places[s * hit_count + i : s * hit_count + i + 1, :] = row
            hit = target == row
            chosen = hit if chosen is None else chosen | hit
        picks.append(jnp.where(chosen, 1.0, 0.0).astype(jnp.bfloat16))
    for copy in copies:
        copy.wait()
    packed = dot(jnp.concatenate(picks, axis=0), held[...], NN).astype(jnp.bfloat16)
    for s in range(CAP):
        rows = slice(s * devices * MSG, (s + 1) * devices * MSG)
        send[:, s * (WIDE + HD) : (s + 1) * (WIDE + HD)] = packed[rows]


def prep_kernel(
    devices, hit_count, hits, prefix_len, span, places, keys, values, *outs
):
    busy, prompt, cached, turned, wide, picks = outs
    rows = iota((devices * MSG, 2 * ROWS), 0)
    for n in range(CAP * hit_count):
        chosen = jnp.where(rows == places[n : n + 1, :], 1.0, 0.0)
        picks[n * 2 * ROWS : (n + 1) * 2 * ROWS, :] = chosen.T.astype(jnp.bfloat16)
    for n in range(0, CAP * REGION, STRIP):
        turned[:, n : n + STRIP] = keys[n : n + STRIP, :].T
    me = lax.axis_index("cache")
    wide[:, :HD] = values[...]
    wide[:, HD:] = jnp.ones((CAP * REGION, HD), jnp.bfloat16)
    for slot in range(CAP):
        seen = jnp.int32(0)
        request = jnp.int32(0)
        which = jnp.int32(0)
        for r in range(REQUESTS):
            for i in range(hit_count):
                mine = hits[r * hit_count + i] == me
                here = mine & (seen == slot)
                request = jnp.where(here, r, request)
                which = jnp.where(here, i, which)
                seen = seen + mine.astype(jnp.int32)
        limit = prefix_len[request] - which * REGION
        blocks = jnp.clip((limit + STRIP - 1) // STRIP, 1, REGION // STRIP)
        busy[slot] = jnp.where(seen > slot, blocks, 0)
        cached[slot : slot + 1, :] = jnp.where(iota((1, REGION), 1) < limit, 0.0, FLOOR)
        prompt_rows(devices, prompt, span, request, slot, hit_count == 1 or which == 0)


def prompt_rows(devices, prompt, span, request, slot, counted):
    total_rows = devices * MSG
    span_row = span[pl.ds(request, 1), :].astype(jnp.float32)
    source = iota((devices, total_rows), 0)
    spread = (iota((devices, total_rows), 1) // MSG == source).astype(jnp.bfloat16)
    spans = jnp.broadcast_to(span_row, (16, devices)).astype(jnp.bfloat16)
    key_span = dot(spans, spread, NN)[:1]
    lane = iota((1, total_rows), 1)
    key_spot = key_span.astype(jnp.int32) * TOK_REQ + lane % TOK_REQ
    is_key = (lane % MSG < TOK_REQ) & counted
    key_spot = jnp.where(is_key, key_spot, devices * TOK_REQ)
    block = 16 * MSG

    def one_block(at):
        row_source = at * 16 + iota((block, devices), 0) // MSG
        mine = iota((block, devices), 1) == row_source
        row_span = jnp.sum(jnp.where(mine, span_row, 0.0), axis=1, keepdims=True)
        row_spot = row_span.astype(jnp.int32) * TOK_REQ + iota((block, 1), 0) % TOK_REQ
        here = pl.ds(slot * total_rows + at * block, block)
        prompt[here, :] = jnp.where(key_spot <= row_spot, 0.0, FLOOR)

    each_block(devices, one_block)


def each_block(devices, one_block):
    blocks = devices // 16
    if blocks == 1:
        one_block(0)
    else:
        pl.loop(0, blocks)(one_block)


def lanes_max(parts):
    pieces = [part[:, n : n + HD] for part in parts for n in range(0, part.shape[1], HD)]
    return jnp.max(functools.reduce(jnp.maximum, pieces), axis=1, keepdims=True)


def attend_kernel(
    devices, hit_count, busy, prompt_mask, cached_mask, got, turned, wide, out, *levels
):
    total_rows = devices * MSG
    block = 16 * MSG
    factor = SCALE * math.log2(math.e)

    def nothing(slot):
        out[:, pl.ds(slot * WIDE, WIDE)] = jnp.zeros((total_rows, WIDE), jnp.bfloat16)
        for lse in levels:
            lse[:, pl.ds(slot * HD, HD)] = jnp.zeros((total_rows, HD), jnp.float32)

    def attend(slot, strips):
        whole = (strips - 1) * STRIP
        base = pl.multiple_of(slot * (WIDE + HD), HD)
        region = pl.multiple_of(slot * REGION, REGION)
        head = pl.ds(region, whole) if whole else None
        tail = pl.ds(pl.multiple_of(region + whole, STRIP), STRIP)
        tail_mask = cached_mask[pl.ds(slot, 1), whole : whole + STRIP]
        prompt_keys = got[:, pl.ds(base + WIDE, HD)].astype(jnp.float32)
        moved = pltpu.roll(prompt_keys, total_rows - TOK_REQ, 0)
        prompt_keys = prompt_keys.T.astype(jnp.bfloat16)
        prompt_values = jnp.concatenate(
            [moved.astype(jnp.bfloat16), jnp.ones((total_rows, HD), jnp.bfloat16)], axis=1
        )

        def one_block(at):
            here = pl.ds(at * block, block)
            prompt_bias = prompt_mask[pl.ds(slot * total_rows + at * block, block), :]
            prompt_bias = jnp.concatenate([prompt_bias, prompt_bias], axis=0)
            lane = iota((block, HD), 1)

            def scores(c):
                pair = jnp.concatenate(
                    [got[here, pl.ds(base + (c + n) * HD, HD)] for n in range(2)], axis=0
                )
                parts = [dot(pair, turned[:, head], NN)] if whole else []
                parts.append(dot(pair, turned[:, tail], NN) + tail_mask)
                parts.append(dot(pair, prompt_keys, NN) + prompt_bias)
                return parts

            logs = jnp.zeros((block, HD), jnp.float32)
            parts = scores(0)
            for c in range(0, HALF, 2):
                later = scores(c + 2) if c + 2 < HALF else None
                top = lanes_max(parts)
                if hit_count > 1:
                    top = jnp.maximum(top, 0.1 * FLOOR)
                parts = [jnp.exp2((x - top) * factor).astype(jnp.bfloat16) for x in parts]
                summed = dot(parts[-1], prompt_values, NN) + dot(parts[-2], wide[tail, :], NN)
                if whole:
                    summed = summed + dot(parts[0], wide[head, :], NN)
                totals = summed[:, HD:]
                if hit_count > 1:
                    totals = jnp.maximum(totals, 1.0)
                    level = top * SCALE + jnp.log(totals)
                    logs = jnp.where(lane == c, level[:block], logs)
                    logs = jnp.where(lane == c + 1, level[block:], logs)
                result = (summed[:, :HD] / totals).astype(jnp.bfloat16)
                for n in range(2):
                    column = pl.multiple_of(slot * WIDE + (c + n) * HD, HD)
                    out[here, pl.ds(column, HD)] = result[n * block : (n + 1) * block]
                parts = later
            for lse in levels:
                lse[here, pl.ds(pl.multiple_of(slot * HD, HD), HD)] = logs

        each_block(devices, one_block)

    @pl.loop(0, CAP)
    def _(slot):
        strips = busy[slot]
        pl.when(strips == 0)(lambda: nothing(slot))
        for count in range(1, REGION // STRIP + 1):
            pl.when(strips == count)(functools.partial(attend, slot, count))


def guest_plan(devices, owners, count, zero, host):
    chips = devices // 2
    for d in range(devices):
        count[d] = 0
    ranks = []
    for r in range(REQUESTS):
        owner = owners[r]
        ranks.append(count[owner])
        count[owner] = ranks[r] + 1
    seconds = [jnp.where(count[d] > 1, 1, 0) for d in range(devices)]
    for first in (0, chips // 2):
        free, spare = jnp.int32(first), jnp.int32(first)
        for x in range(first, first + chips // 2):
            zero[free] = jnp.int32(x)
            free = free + jnp.where(seconds[2 * x] + seconds[2 * x + 1] == 0, 1, 0)
        for x in range(first, first + chips // 2):
            both = seconds[2 * x] * seconds[2 * x + 1]
            host[2 * x] = jnp.int32(x)
            host[2 * x + 1] = jnp.where(both == 1, zero[spare], x)
            spare = jnp.minimum(spare + both, first + chips // 2 - 1)
    return ranks, seconds


def guest_pack_kernel(
    devices, hit_count, owners, q, k, v, send, places, held, held_guest, hits, *scalars
):
    count, zero, host, sems = scalars
    half = WIDE // 2
    moves = [
        (q.at[:, pl.ds(0, WIDE)], held.at[pl.ds(0, ROWS), pl.ds(0, WIDE)]),
        (q.at[:, pl.ds(WIDE, WIDE)], held.at[pl.ds(ROWS, ROWS), pl.ds(0, WIDE)]),
        (k, held.at[pl.ds(0, ROWS), pl.ds(WIDE, HD)]),
        (v, held.at[pl.ds(ROWS, ROWS), pl.ds(WIDE, HD)]),
    ]
    for g in range(4):
        here = pl.ds(g * ROWS, ROWS)
        moves.append((q.at[:, pl.ds(g * half, half)], held_guest.at[here, pl.ds(0, half)]))
        moves.append((v if g % 2 else k, held_guest.at[here, pl.ds(half, HD)]))
    first = pltpu.make_async_copy(owners, hits, sems.at[len(moves)])
    first.start()
    copies = [pltpu.make_async_copy(a, b, sems.at[n]) for n, (a, b) in enumerate(moves)]
    for copy in copies:
        copy.start()
    first.wait()
    ranks, _ = guest_plan(devices, hits, count, zero, host)
    lane = iota((1, 4 * ROWS), 1)
    lane_request = lane % ROWS // TOK_REQ
    part = lane // ROWS
    nowhere = -4 * MSG
    own = jnp.full((1, 4 * ROWS), nowhere, jnp.int32)
    guest = own
    for r in range(REQUESTS):
        owner = hits[r]
        mine = lane_request == r
        own = jnp.where(mine, jnp.where(ranks[r] == 0, owner * MSG, nowhere), own)
        guest = jnp.where(mine, jnp.where(ranks[r] == 1, host[owner] * 2 * MSG, nowhere), guest)
    own = own + part * TOK_REQ + lane % TOK_REQ
    guest = guest + part * TOK_REQ + lane % TOK_REQ
    places[0:1, :] = own
    places[1:2, :] = guest
    target = iota((devices * MSG, 4 * ROWS), 0)
    pick = jnp.where(target[:, : 2 * ROWS] == own[:, : 2 * ROWS], 1.0, 0.0).astype(jnp.bfloat16)
    pick_guest = jnp.where(target == guest, 1.0, 0.0).astype(jnp.bfloat16)
    for copy in copies:
        copy.wait()
    send[:, : WIDE + HD] = dot(pick, held[...], NN).astype(jnp.bfloat16)
    send[:, WIDE + HD :] = dot(pick_guest, held_guest[...], NN).astype(jnp.bfloat16)


def guest_prep_kernel(
    devices, hit_count, hits, prefix_len, span, places, keys, values, *refs
):
    plan, prompt, cached, turned, wide, picks, picks_guest, count, zero, host = refs
    me = lax.axis_index("cache")
    chip = me // 2
    ranks, seconds = guest_plan(devices, hits, count, zero, host)
    rows = iota((devices * MSG, 4 * ROWS), 0)
    chosen = jnp.where(rows[:, : 2 * ROWS] == places[0:1, : 2 * ROWS], 1.0, 0.0)
    picks[...] = chosen.T.astype(jnp.bfloat16)
    chosen = jnp.where(rows == places[1:2, :], 1.0, 0.0)
    picks_guest[...] = chosen.T.astype(jnp.bfloat16)
    widen(keys[:REGION, :], values[:REGION, :], turned, wide)
    first, guest, source = jnp.int32(-1), jnp.int32(-1), jnp.int32(0)
    for r in range(REQUESTS):
        owner = hits[r]
        here = (ranks[r] == 1) & (host[owner] == chip)
        first = jnp.where((ranks[r] == 0) & (owner == me), r, first)
        guest = jnp.where(here, r, guest)
        source = jnp.where(here, owner, source)
    core = me % 2
    from_first_core = jnp.where(source == 2 * chip, 1, 0)
    plan[2] = jnp.where(core == 1, (source // 2) ^ chip, 0)
    plan[3] = jnp.where(core == from_first_core, 1, 0)
    for job, found in enumerate((first, guest)):
        request = jnp.maximum(found, 0)
        limit = prefix_len[request]
        strips = jnp.clip((limit + STRIP - 1) // STRIP, 1, REGION // STRIP)
        plan[job] = jnp.where(found >= 0, strips, 0)
        cached[job : job + 1, :] = jnp.where(iota((1, REGION), 1) < limit, 0.0, FLOOR)
        prompt_rows(devices, prompt, span, request, job, True)


def widen(keys, values, turned, wide):
    for n in range(0, REGION, STRIP):
        turned[:, n : n + STRIP] = keys[n : n + STRIP].T
    wide[:, :HD] = values
    wide[:, HD:] = jnp.ones((REGION, HD), jnp.bfloat16)


def lend_kernel(devices, hit_count, plan, keys, values, *refs):
    lent, out, sems = refs[:-2], refs[-2], refs[-1]
    own = [keys.at[pl.ds(REGION, REGION)], values.at[pl.ds(REGION, REGION)]]
    sources = [own] + [[x.at[pl.ds(n * REGION, REGION)] for n in range(2)] for x in lent]
    for choice, pair in enumerate(sources):

        @pl.when(plan[2] == choice)
        def _():
            copies = [
                pltpu.make_async_copy(pair[n], out.at[pl.ds(n * REGION, REGION)], sems.at[n])
                for n in range(2)
            ]
            for copy in copies:
                copy.start()
            for copy in copies:
                copy.wait()


def host_kernel(devices, hit_count, plan, mine, other, turned, wide):
    for choice, rows in enumerate((mine, other)):

        @pl.when(plan[3] == choice)
        def _():
            widen(rows[:REGION, :], rows[REGION:, :], turned, wide)


def guest_attend_kernel(
    devices, hit_count, plan, prompt_mask, cached_mask, got, turned, wide, *refs
):
    turned_guest, wide_guest, out = refs
    jobs = [
        (0, 0, HALF, turned, wide),
        (WIDE + HD, WIDE, HALF // 2, turned_guest, wide_guest),
    ]
    for job, (base, first, blocks, keys, values) in enumerate(jobs):
        strips = plan[job]

        @pl.when(strips == 0)
        def _():
            empty = jnp.zeros((devices * MSG, blocks * HD), jnp.bfloat16)
            out[:, first : first + blocks * HD] = empty

        for count in range(1, REGION // STRIP + 1):

            @pl.when(strips == count)
            def _():
                whole = (count - 1) * STRIP
                mask = prompt_mask[job * devices * MSG : (job + 1) * devices * MSG, :]
                attend_rows(
                    got,
                    base,
                    blocks,
                    slice(0, devices * MSG),
                    prompt_parts(got[:, base + blocks * HD : base + (blocks + 1) * HD]),
                    mask,
                    cached_mask[job : job + 1, whole : whole + STRIP],
                    keys[:, :whole] if whole else None,
                    keys[:, whole : whole + STRIP],
                    values[:whole, :] if whole else None,
                    values[whole : whole + STRIP, :],
                    out,
                    first,
                )


def prompt_parts(rows):
    height = rows.shape[0]
    wide = rows.astype(jnp.float32)
    moved = pltpu.roll(wide, height - TOK_REQ, 0).astype(jnp.bfloat16)
    values = jnp.concatenate([moved, jnp.ones((height, HD), jnp.bfloat16)], axis=1)
    return wide.T.astype(jnp.bfloat16), values


def attend_rows(
    got, base, blocks, here, prompt, mask, tail_mask, head, tail, head_values, tail_values, out, first
):
    prompt_keys, prompt_values = prompt
    factor = SCALE * math.log2(math.e)
    mask = jnp.concatenate([mask, mask], axis=0)
    height = mask.shape[0] // 2

    def scores(c):
        pair = jnp.concatenate(
            [got[here, base + (c + n) * HD : base + (c + n + 1) * HD] for n in range(2)], axis=0
        )
        parts = [] if head is None else [dot(pair, head, NN)]
        parts.append(dot(pair, tail, NN) + tail_mask)
        parts.append(dot(pair, prompt_keys, NN) + mask)
        return parts

    parts = scores(0)
    for c in range(0, blocks, 2):
        later = scores(c + 2) if c + 2 < blocks else None
        top = lanes_max(parts)
        parts = [jnp.exp2((x - top) * factor).astype(jnp.bfloat16) for x in parts]
        summed = dot(parts[-1], prompt_values, NN) + dot(parts[-2], tail_values, NN)
        if head is not None:
            summed = summed + dot(parts[0], head_values, NN)
        result = (summed[:, :HD] / summed[:, HD:]).astype(jnp.bfloat16)
        for n in range(2):
            column = first + (c + n) * HD
            out[here, column : column + HD] = result[n * height : (n + 1) * height]
        parts = later


def guest_unpack_kernel(devices, hit_count, picks, picks_guest, outs, result):
    half = WIDE // 2
    own = dot(picks[...], outs[:, :WIDE], NN)
    guest = dot(picks_guest[...], outs[:, WIDE:], NN)
    for g in range(4):
        rows = own[g // 2 * ROWS : (g // 2 + 1) * ROWS, g % 2 * half : (g % 2 + 1) * half]
        rows = rows + guest[g * ROWS : (g + 1) * ROWS]
        result[:, g * half : (g + 1) * half] = rows.astype(jnp.bfloat16)


def unpack_kernel(devices, hit_count, picks, *refs):
    outs, logs, result = refs[0], refs[1:-1], refs[-1]

    def chosen(s, i):
        place = s * hit_count + i
        return picks[place * 2 * ROWS : (place + 1) * 2 * ROWS, :]

    def rows_of(i):
        parts = [
            dot(chosen(s, i), outs[:, s * WIDE : (s + 1) * WIDE], NN)
            for s in range(CAP)
        ]
        return sum(parts[1:], parts[0])

    def logs_of(i):
        parts = [
            dot(
                chosen(s, i).astype(jnp.float32),
                logs[0][:, s * HD : (s + 1) * HD],
                NN,
                precision=lax.Precision.HIGHEST,
            )
            for s in range(CAP)
        ]
        return sum(parts[1:], parts[0])

    if hit_count == 1:
        joined = rows_of(0)
    else:
        levels = [logs_of(i) for i in range(hit_count)]
        top = functools.reduce(jnp.maximum, levels)
        shares = [jnp.exp(level - top) for level in levels]
        total = sum(shares[1:], shares[0])
        pieces = [rows_of(i) for i in range(hit_count)]
        columns = []
        for c in range(HALF):
            part = sum(
                shares[i][:, c : c + 1] * pieces[i][:, c * HD : (c + 1) * HD]
                for i in range(hit_count)
            )
            columns.append(part / total[:, c : c + 1])
        joined = jnp.concatenate(columns, axis=1)
    joined = joined.astype(jnp.bfloat16)
    result[:, :WIDE] = joined[:ROWS]
    result[:, WIDE:] = joined[ROWS:]


def vmem(count):
    return [pl.BlockSpec(memory_space=pltpu.VMEM)] * count


def smem(count):
    return [pl.BlockSpec(memory_space=pltpu.SMEM)] * count


def hbm(count):
    return [pl.BlockSpec(memory_space=pltpu.HBM)] * count


def body(prefix_len, hits, span_block, queries, fresh_keys, fresh_values, cache_keys, cache_values):
    devices = lax.axis_size("cache")
    hit_count = hits.shape[1]
    rows = devices * MSG
    owners = hits.reshape(REQUESTS * hit_count)
    fresh = (owners, queries, fresh_keys, fresh_values)

    def exchange(x):
        return lax.all_to_all(x, "cache", split_axis=0, concat_axis=0, tiled=True)

    def call(kernel, out_shape, name, grant=40, **kw):
        return pl.pallas_call(
            functools.partial(kernel, devices, hit_count),
            out_shape=[jax.ShapeDtypeStruct(*leaf) for leaf in out_shape],
            compiler_params=pltpu.CompilerParams(vmem_limit_bytes=grant * 2**20),
            name=name,
            **kw,
        )

    if hit_count == 1 and devices == 16:
        pairs = rows * (HALF + HALF // 2) * (REGION + rows)
        lent = jnp.concatenate([cache_keys[REGION:], cache_values[REGION:]], axis=0)
        borrowed = [
            lax.ppermute(lent, "cache", [(d, d ^ (2 * n)) for d in range(1, devices, 2)])
            for n in range(1, 4)
        ]
        scalars = [pltpu.SMEM((devices,), jnp.int32)] * 3
        send, places = call(
            guest_pack_kernel,
            [((rows, GUEST_MSG), jnp.bfloat16), ((2, 4 * ROWS), jnp.int32)],
            "pack",
            in_specs=hbm(4),
            out_specs=vmem(2),
            scratch_shapes=[
                pltpu.VMEM((2 * ROWS, WIDE + HD), jnp.bfloat16),
                pltpu.VMEM((4 * ROWS, WIDE // 2 + HD), jnp.bfloat16),
                pltpu.SMEM((REQUESTS,), jnp.int32),
                *scalars,
                pltpu.SemaphoreType.DMA((13,)),
            ],
        )(*(pltpu.with_memory_space_constraint(x, pltpu.HBM) for x in fresh))
        got = exchange(send)
        shapes = [((HD, REGION), jnp.bfloat16), ((REGION, 2 * HD), jnp.bfloat16)]
        plan, prompt_mask, cached_mask, turned, wide, picks, picks_guest = call(
            guest_prep_kernel,
            [((4,), jnp.int32), ((2 * rows, rows), jnp.float32), ((2, REGION), jnp.float32)]
            + shapes
            + [((2 * ROWS, rows), jnp.bfloat16), ((4 * ROWS, rows), jnp.bfloat16)],
            "prep",
            in_specs=smem(2) + vmem(4),
            out_specs=smem(1) + vmem(6),
            scratch_shapes=scalars,
            cost_estimate=pl.CostEstimate(flops=10**6, bytes_accessed=2**22, transcendentals=0),
        )(owners, prefix_len, span_block, places, cache_keys, cache_values)
        (mine,) = call(
            lend_kernel,
            [((2 * REGION, HD), jnp.bfloat16)],
            "lend",
            in_specs=smem(1) + hbm(5),
            out_specs=vmem(1),
            scratch_shapes=[pltpu.SemaphoreType.DMA((2,))],
        )(plan, cache_keys, cache_values, *borrowed)
        other = lax.ppermute(mine, "cache", [(d, d ^ 1) for d in range(devices)])
        turned_guest, wide_guest = call(
            host_kernel, shapes, "host", in_specs=smem(1) + vmem(2), out_specs=vmem(2)
        )(plan, mine, other)
        (answer,) = call(
            guest_attend_kernel,
            [((rows, WIDE + WIDE // 2), jnp.bfloat16)],
            "attend",
            in_specs=smem(1) + vmem(7),
            out_specs=vmem(1),
            cost_estimate=pl.CostEstimate(
                flops=4 * pairs * HD, bytes_accessed=8 * rows * WIDE, transcendentals=pairs
            ),
        )(plan, prompt_mask, cached_mask, got, turned, wide, turned_guest, wide_guest)
        return call(
            guest_unpack_kernel,
            [((ROWS, HEADS * HD), jnp.bfloat16)],
            "unpack",
            in_specs=vmem(3),
            out_specs=vmem(1),
        )(picks, picks_guest, exchange(answer))[0]
    send, places = call(
        pack_kernel,
        [((rows, CAP * (WIDE + HD)), jnp.bfloat16), ((CAP * hit_count, 2 * ROWS), jnp.int32)],
        "pack",
        in_specs=hbm(4),
        out_specs=vmem(2),
        scratch_shapes=[
            pltpu.VMEM((2 * ROWS, WIDE + HD), jnp.bfloat16),
            pltpu.SMEM((REQUESTS * hit_count,), jnp.int32),
            pltpu.SMEM((devices,), jnp.int32),
            pltpu.SemaphoreType.DMA((5,)),
        ],
    )(*(pltpu.with_memory_space_constraint(x, pltpu.HBM) for x in fresh))
    got = exchange(send)
    busy, prompt_mask, cached_mask, turned, wide, picks = call(
        prep_kernel,
        [
            ((CAP,), jnp.int32),
            ((CAP * rows, rows), jnp.float32),
            ((CAP, REGION), jnp.float32),
            ((HD, CAP * REGION), jnp.bfloat16),
            ((CAP * REGION, 2 * HD), jnp.bfloat16),
            ((CAP * hit_count * 2 * ROWS, rows), jnp.bfloat16),
        ],
        "prep",
        in_specs=smem(2) + vmem(4),
        out_specs=smem(1) + vmem(5),
        cost_estimate=pl.CostEstimate(flops=10**6, bytes_accessed=2**22, transcendentals=0),
    )(owners, prefix_len, span_block, places, cache_keys, cache_values)
    pairs = CAP * rows * HALF * (REGION + rows)
    answers = call(
        attend_kernel,
        [((rows, CAP * WIDE), jnp.bfloat16)]
        + [((rows, CAP * HD), jnp.float32)] * (hit_count > 1),
        "attend",
        in_specs=smem(1) + vmem(5),
        out_specs=vmem(1 + (hit_count > 1)),
        cost_estimate=pl.CostEstimate(
            flops=4 * pairs * HD, bytes_accessed=8 * rows * WIDE, transcendentals=pairs
        ),
    )(busy, prompt_mask, cached_mask, got, turned, wide)
    returned = [exchange(answer) for answer in answers]
    return call(
        unpack_kernel,
        [((ROWS, HEADS * HD), jnp.bfloat16)],
        "unpack",
        in_specs=vmem(1 + len(returned)),
        out_specs=vmem(1),
    )(picks, *returned)[0]


def solution(mesh):
    in_specs = (
        P("groups"),
        P("groups", None),
        P("groups", None),
        P(("groups", "cache"), None),
        P(("groups", "cache"), None),
        P(("groups", "cache"), None),
        P(("groups", "cache"), None),
        P(("groups", "cache"), None),
    )
    out_specs = P(("groups", "cache"), None)
    return jax.shard_map(body, mesh=mesh, in_specs=in_specs, out_specs=out_specs, check_vma=False)
```

```python
import functools
import math

import jax
import jax.numpy as jnp
from jax import lax
from jax.experimental import pallas as pl
from jax.experimental.pallas import tpu as pltpu
from jax.sharding import PartitionSpec as P

HEADS = 16
HD = 128
PAGE = 128
CAP = 2
REQUESTS = 16
TOK_REQ = 4
PAGES_DEV = 16

REGION = PAGES_DEV // CAP * PAGE
HALF = HEADS // 2
MSG = 2 * TOK_REQ
WIDE = HALF * HD
ROWS = REQUESTS * TOK_REQ
STRIP = 256
GUEST_MSG = WIDE + HD + WIDE // 2 + HD
SCALE = HD**-0.5
FLOOR = -1e30
NN = (((1,), (0,)), ((), ()))


def iota(shape, axis):
    return lax.broadcasted_iota(jnp.int32, shape, axis)


def dot(a, b, dims, **kw):
    return lax.dot_general(a, b, dims, preferred_element_type=jnp.float32, **kw)


def pack_kernel(devices, hit_count, owners, q, k, v, send, places, held, hits, count, sems):
    copies = [
        pltpu.make_async_copy(source, held.at[pl.ds(row, ROWS), pl.ds(column, width)], sems.at[n])
        for n, (source, row, column, width) in enumerate(
            [
                (q.at[:, pl.ds(0, WIDE)], 0, 0, WIDE),
                (q.at[:, pl.ds(WIDE, WIDE)], ROWS, 0, WIDE),
                (k, 0, WIDE, HD),
                (v, ROWS, WIDE, HD),
            ]
        )
    ]
    first = pltpu.make_async_copy(owners, hits, sems.at[4])
    first.start()
    for copy in copies:
        copy.start()
    lane = iota((1, 2 * ROWS), 1)
    lane_request = (lane % ROWS) // TOK_REQ
    first.wait()
    for r in range(REQUESTS):
        for i in range(hit_count):
            count[hits[r * hit_count + i]] = 0
    rows = [[jnp.full((1, 2 * ROWS), -4 * MSG, jnp.int32)] * hit_count for _ in range(CAP)]
    for r in range(REQUESTS):
        for i in range(hit_count):
            owner = hits[r * hit_count + i]
            rank = count[owner]
            count[owner] = rank + 1
            for s in range(CAP):
                place = jnp.where(rank == s, owner * MSG, -4 * MSG)
                rows[s][i] = jnp.where(lane_request == r, place, rows[s][i])
    inner = lane // ROWS * TOK_REQ + lane % TOK_REQ
    target = iota((devices * MSG, 2 * ROWS), 0)
    picks = []
    for s in range(CAP):
        chosen = None
        for i in range(hit_count):
            row = rows[s][i] + inner
            places[s * hit_count + i : s * hit_count + i + 1, :] = row
            hit = target == row
            chosen = hit if chosen is None else chosen | hit
        picks.append(jnp.where(chosen, 1.0, 0.0).astype(jnp.bfloat16))
    for copy in copies:
        copy.wait()
    packed = dot(jnp.concatenate(picks, axis=0), held[...], NN).astype(jnp.bfloat16)
    for s in range(CAP):
        rows = slice(s * devices * MSG, (s + 1) * devices * MSG)
        send[:, s * (WIDE + HD) : (s + 1) * (WIDE + HD)] = packed[rows]


def prep_kernel(
    devices, hit_count, hits, prefix_len, span, places, keys, values, *outs
):
    busy, prompt, cached, turned, wide, picks = outs
    rows = iota((devices * MSG, 2 * ROWS), 0)
    for n in range(CAP * hit_count):
        chosen = jnp.where(rows == places[n : n + 1, :], 1.0, 0.0)
        picks[n * 2 * ROWS : (n + 1) * 2 * ROWS, :] = chosen.T.astype(jnp.bfloat16)
    for n in range(0, CAP * REGION, STRIP):
        turned[:, n : n + STRIP] = keys[n : n + STRIP, :].T
    me = lax.axis_index("cache")
    wide[:, :HD] = values[...]
    wide[:, HD:] = jnp.ones((CAP * REGION, HD), jnp.bfloat16)
    for slot in range(CAP):
        seen = jnp.int32(0)
        request = jnp.int32(0)
        which = jnp.int32(0)
        for r in range(REQUESTS):
            for i in range(hit_count):
                mine = hits[r * hit_count + i] == me
                here = mine & (seen == slot)
                request = jnp.where(here, r, request)
                which = jnp.where(here, i, which)
                seen = seen + mine.astype(jnp.int32)
        limit = prefix_len[request] - which * REGION
        blocks = jnp.clip((limit + STRIP - 1) // STRIP, 1, REGION // STRIP)
        busy[slot] = jnp.where(seen > slot, blocks, 0)
        cached[slot : slot + 1, :] = jnp.where(iota((1, REGION), 1) < limit, 0.0, FLOOR)
        prompt_rows(devices, prompt, span, request, slot, hit_count == 1 or which == 0)


def prompt_rows(devices, prompt, span, request, slot, counted):
    total_rows = devices * MSG
    span_row = span[pl.ds(request, 1), :].astype(jnp.float32)
    source = iota((devices, total_rows), 0)
    spread = (iota((devices, total_rows), 1) // MSG == source).astype(jnp.bfloat16)
    spans = jnp.broadcast_to(span_row, (16, devices)).astype(jnp.bfloat16)
    key_span = dot(spans, spread, NN)[:1]
    lane = iota((1, total_rows), 1)
    key_spot = key_span.astype(jnp.int32) * TOK_REQ + lane % TOK_REQ
    is_key = (lane % MSG < TOK_REQ) & counted
    key_spot = jnp.where(is_key, key_spot, devices * TOK_REQ)
    block = 16 * MSG

    def one_block(at):
        row_source = at * 16 + iota((block, devices), 0) // MSG
        mine = iota((block, devices), 1) == row_source
        row_span = jnp.sum(jnp.where(mine, span_row, 0.0), axis=1, keepdims=True)
        row_spot = row_span.astype(jnp.int32) * TOK_REQ + iota((block, 1), 0) % TOK_REQ
        here = pl.ds(slot * total_rows + at * block, block)
        prompt[here, :] = jnp.where(key_spot <= row_spot, 0.0, FLOOR)

    each_block(devices, one_block)


def each_block(devices, one_block):
    blocks = devices // 16
    if blocks == 1:
        one_block(0)
    else:
        pl.loop(0, blocks)(one_block)


def lanes_max(parts):
    pieces = [part[:, n : n + HD] for part in parts for n in range(0, part.shape[1], HD)]
    return jnp.max(functools.reduce(jnp.maximum, pieces), axis=1, keepdims=True)


def attend_kernel(
    devices, hit_count, busy, prompt_mask, cached_mask, got, turned, wide, out, *levels
):
    total_rows = devices * MSG
    block = 16 * MSG
    factor = SCALE * math.log2(math.e)

    def nothing(slot):
        out[:, pl.ds(slot * WIDE, WIDE)] = jnp.zeros((total_rows, WIDE), jnp.bfloat16)
        for lse in levels:
            lse[:, pl.ds(slot * HD, HD)] = jnp.zeros((total_rows, HD), jnp.float32)

    def attend(slot, strips):
        whole = (strips - 1) * STRIP
        base = pl.multiple_of(slot * (WIDE + HD), HD)
        region = pl.multiple_of(slot * REGION, REGION)
        head = pl.ds(region, whole) if whole else None
        tail = pl.ds(pl.multiple_of(region + whole, STRIP), STRIP)
        tail_mask = cached_mask[pl.ds(slot, 1), whole : whole + STRIP]
        prompt_keys = got[:, pl.ds(base + WIDE, HD)].astype(jnp.float32)
        moved = pltpu.roll(prompt_keys, total_rows - TOK_REQ, 0)
        prompt_keys = prompt_keys.T.astype(jnp.bfloat16)
        prompt_values = jnp.concatenate(
            [moved.astype(jnp.bfloat16), jnp.ones((total_rows, HD), jnp.bfloat16)], axis=1
        )

        def one_block(at):
            here = pl.ds(at * block, block)
            prompt_bias = prompt_mask[pl.ds(slot * total_rows + at * block, block), :]
            prompt_bias = jnp.concatenate([prompt_bias, prompt_bias], axis=0)
            lane = iota((block, HD), 1)

            def scores(c):
                pair = jnp.concatenate(
                    [got[here, pl.ds(base + (c + n) * HD, HD)] for n in range(2)], axis=0
                )
                parts = [dot(pair, turned[:, head], NN)] if whole else []
                parts.append(dot(pair, turned[:, tail], NN) + tail_mask)
                parts.append(dot(pair, prompt_keys, NN) + prompt_bias)
                return parts

            logs = jnp.zeros((block, HD), jnp.float32)
            parts = scores(0)
            for c in range(0, HALF, 2):
                later = scores(c + 2) if c + 2 < HALF else None
                top = lanes_max(parts)
                if hit_count > 1:
                    top = jnp.maximum(top, 0.1 * FLOOR)
                parts = [jnp.exp2((x - top) * factor).astype(jnp.bfloat16) for x in parts]
                summed = dot(parts[-1], prompt_values, NN) + dot(parts[-2], wide[tail, :], NN)
                if whole:
                    summed = summed + dot(parts[0], wide[head, :], NN)
                totals = summed[:, HD:]
                if hit_count > 1:
                    totals = jnp.maximum(totals, 1.0)
                    level = top * SCALE + jnp.log(totals)
                    logs = jnp.where(lane == c, level[:block], logs)
                    logs = jnp.where(lane == c + 1, level[block:], logs)
                result = (summed[:, :HD] / totals).astype(jnp.bfloat16)
                for n in range(2):
                    column = pl.multiple_of(slot * WIDE + (c + n) * HD, HD)
                    out[here, pl.ds(column, HD)] = result[n * block : (n + 1) * block]
                parts = later
            for lse in levels:
                lse[here, pl.ds(pl.multiple_of(slot * HD, HD), HD)] = logs

        each_block(devices, one_block)

    @pl.loop(0, CAP)
    def _(slot):
        strips = busy[slot]
        pl.when(strips == 0)(lambda: nothing(slot))
        for count in range(1, REGION // STRIP + 1):
            pl.when(strips == count)(functools.partial(attend, slot, count))


def guest_plan(devices, owners, count, host):
    chips = devices // 2
    for d in range(devices):
        count[d] = 0
    ranks = []
    for r in range(REQUESTS):
        owner = owners[r]
        ranks.append(count[owner])
        count[owner] = ranks[r] + 1
    seconds = [count[d] > 1 for d in range(devices)]
    none = [jnp.logical_not(seconds[2 * x] | seconds[2 * x + 1]) for x in range(chips)]
    lends = []
    for x in range(chips):
        other = jnp.where(none[x ^ 1], 1, jnp.where(none[x ^ 2], 2, 3))
        lends.append(jnp.where(seconds[2 * x] & seconds[2 * x + 1], other, 0))
        host[2 * x] = jnp.int32(x)
        host[2 * x + 1] = lends[x] ^ x
    return ranks, lends


def guest_pack_kernel(
    devices, hit_count, owners, q, k, v, send, places, held, held_guest, hits, *scalars
):
    count, host, sems = scalars
    half = WIDE // 2
    moves = [
        (q.at[:, pl.ds(0, WIDE)], held.at[pl.ds(0, ROWS), pl.ds(0, WIDE)]),
        (q.at[:, pl.ds(WIDE, WIDE)], held.at[pl.ds(ROWS, ROWS), pl.ds(0, WIDE)]),
        (k, held.at[pl.ds(0, ROWS), pl.ds(WIDE, HD)]),
        (v, held.at[pl.ds(ROWS, ROWS), pl.ds(WIDE, HD)]),
    ]
    for g in range(4):
        here = pl.ds(g * ROWS, ROWS)
        moves.append((q.at[:, pl.ds(g * half, half)], held_guest.at[here, pl.ds(0, half)]))
        moves.append((v if g % 2 else k, held_guest.at[here, pl.ds(half, HD)]))
    first = pltpu.make_async_copy(owners, hits, sems.at[len(moves)])
    first.start()
    copies = [pltpu.make_async_copy(a, b, sems.at[n]) for n, (a, b) in enumerate(moves)]
    for copy in copies:
        copy.start()
    first.wait()
    ranks, _ = guest_plan(devices, hits, count, host)
    lane = iota((1, 4 * ROWS), 1)
    lane_request = lane % ROWS // TOK_REQ
    part = lane // ROWS
    nowhere = -4 * MSG
    own = jnp.full((1, 4 * ROWS), nowhere, jnp.int32)
    guest = own
    for r in range(REQUESTS):
        owner = hits[r]
        mine = lane_request == r
        own = jnp.where(mine, jnp.where(ranks[r] == 0, owner * MSG, nowhere), own)
        guest = jnp.where(mine, jnp.where(ranks[r] == 1, host[owner] * 2 * MSG, nowhere), guest)
    own = own + part * TOK_REQ + lane % TOK_REQ
    guest = guest + part * TOK_REQ + lane % TOK_REQ
    places[0:1, :] = own
    places[1:2, :] = guest
    target = iota((devices * MSG, 4 * ROWS), 0)
    pick = jnp.where(target[:, : 2 * ROWS] == own[:, : 2 * ROWS], 1.0, 0.0).astype(jnp.bfloat16)
    pick_guest = jnp.where(target == guest, 1.0, 0.0).astype(jnp.bfloat16)
    for copy in copies:
        copy.wait()
    send[:, : WIDE + HD] = dot(pick, held[...], NN).astype(jnp.bfloat16)
    send[:, WIDE + HD :] = dot(pick_guest, held_guest[...], NN).astype(jnp.bfloat16)


def guest_prep_kernel(
    devices, hit_count, hits, prefix_len, span, places, keys, values, *refs
):
    plan, prompt, cached, turned, wide, picks, picks_guest, count, host = refs
    me = lax.axis_index("cache")
    chip = me // 2
    ranks, lends = guest_plan(devices, hits, count, host)
    for way in range(1, 4):
        used = [jnp.where(lent == way, 1, 0) for lent in lends]
        plan[3 + way] = functools.reduce(jnp.maximum, used)
    rows = iota((devices * MSG, 4 * ROWS), 0)
    chosen = jnp.where(rows[:, : 2 * ROWS] == places[0:1, : 2 * ROWS], 1.0, 0.0)
    picks[...] = chosen.T.astype(jnp.bfloat16)
    chosen = jnp.where(rows == places[1:2, :], 1.0, 0.0)
    picks_guest[...] = chosen.T.astype(jnp.bfloat16)
    widen(keys[:REGION, :], values[:REGION, :], turned, wide)
    first, guest, source = jnp.int32(-1), jnp.int32(-1), jnp.int32(0)
    for r in range(REQUESTS):
        owner = hits[r]
        here = (ranks[r] == 1) & (host[owner] == chip)
        first = jnp.where((ranks[r] == 0) & (owner == me), r, first)
        guest = jnp.where(here, r, guest)
        source = jnp.where(here, owner, source)
    core = me % 2
    from_first_core = jnp.where(source == 2 * chip, 1, 0)
    plan[2] = jnp.where(core == 1, (source // 2) ^ chip, 0)
    plan[3] = jnp.where(core == from_first_core, 1, 0)
    for job, found in enumerate((first, guest)):
        request = jnp.maximum(found, 0)
        limit = prefix_len[request]
        strips = jnp.clip((limit + STRIP - 1) // STRIP, 1, REGION // STRIP)
        plan[job] = jnp.where(found >= 0, strips, 0)
        cached[job : job + 1, :] = jnp.where(iota((1, REGION), 1) < limit, 0.0, FLOOR)
        prompt_rows(devices, prompt, span, request, job, True)


def widen(keys, values, turned, wide):
    for n in range(0, REGION, STRIP):
        turned[:, n : n + STRIP] = keys[n : n + STRIP].T
    wide[:, :HD] = values
    wide[:, HD:] = jnp.ones((REGION, HD), jnp.bfloat16)


def lend_kernel(devices, hit_count, plan, keys, values, *refs):
    lent, out, sems = refs[:-2], refs[-2], refs[-1]
    own = [keys.at[pl.ds(REGION, REGION)], values.at[pl.ds(REGION, REGION)]]
    sources = [own] + [[x.at[pl.ds(n * REGION, REGION)] for n in range(2)] for x in lent]
    for choice, pair in enumerate(sources):

        @pl.when(plan[2] == choice)
        def _():
            copies = [
                pltpu.make_async_copy(pair[n], out.at[pl.ds(n * REGION, REGION)], sems.at[n])
                for n in range(2)
            ]
            for copy in copies:
                copy.start()
            for copy in copies:
                copy.wait()


def host_kernel(devices, hit_count, plan, mine, other, turned, wide):
    for choice, rows in enumerate((mine, other)):

        @pl.when(plan[3] == choice)
        def _():
            widen(rows[:REGION, :], rows[REGION:, :], turned, wide)


def guest_attend_kernel(
    devices, hit_count, plan, prompt_mask, cached_mask, got, turned, wide, *refs
):
    turned_guest, wide_guest, out = refs
    jobs = [
        (0, 0, HALF, turned, wide),
        (WIDE + HD, WIDE, HALF // 2, turned_guest, wide_guest),
    ]
    for job, (base, first, blocks, keys, values) in enumerate(jobs):
        strips = plan[job]

        @pl.when(strips == 0)
        def _():
            empty = jnp.zeros((devices * MSG, blocks * HD), jnp.bfloat16)
            out[:, first : first + blocks * HD] = empty

        for count in range(1, REGION // STRIP + 1):

            @pl.when(strips == count)
            def _():
                whole = (count - 1) * STRIP
                mask = prompt_mask[job * devices * MSG : (job + 1) * devices * MSG, :]
                attend_rows(
                    got,
                    base,
                    blocks,
                    slice(0, devices * MSG),
                    prompt_parts(got[:, base + blocks * HD : base + (blocks + 1) * HD]),
                    mask,
                    cached_mask[job : job + 1, whole : whole + STRIP],
                    keys[:, :whole] if whole else None,
                    keys[:, whole : whole + STRIP],
                    values[:whole, :] if whole else None,
                    values[whole : whole + STRIP, :],
                    out,
                    first,
                )


def prompt_parts(rows):
    height = rows.shape[0]
    wide = rows.astype(jnp.float32)
    moved = pltpu.roll(wide, height - TOK_REQ, 0).astype(jnp.bfloat16)
    values = jnp.concatenate([moved, jnp.ones((height, HD), jnp.bfloat16)], axis=1)
    return wide.T.astype(jnp.bfloat16), values


def attend_rows(
    got, base, blocks, here, prompt, mask, tail_mask, head, tail, head_values, tail_values, out, first
):
    prompt_keys, prompt_values = prompt
    factor = SCALE * math.log2(math.e)
    mask = jnp.concatenate([mask, mask], axis=0)
    height = mask.shape[0] // 2

    def scores(c):
        pair = jnp.concatenate(
            [got[here, base + (c + n) * HD : base + (c + n + 1) * HD] for n in range(2)], axis=0
        )
        parts = [] if head is None else [dot(pair, head, NN)]
        parts.append(dot(pair, tail, NN) + tail_mask)
        parts.append(dot(pair, prompt_keys, NN) + mask)
        return parts

    parts = scores(0)
    for c in range(0, blocks, 2):
        later = scores(c + 2) if c + 2 < blocks else None
        top = lanes_max(parts)
        parts = [jnp.exp2((x - top) * factor).astype(jnp.bfloat16) for x in parts]
        summed = dot(parts[-1], prompt_values, NN) + dot(parts[-2], tail_values, NN)
        if head is not None:
            summed = summed + dot(parts[0], head_values, NN)
        result = (summed[:, :HD] / summed[:, HD:]).astype(jnp.bfloat16)
        for n in range(2):
            column = first + (c + n) * HD
            out[here, column : column + HD] = result[n * height : (n + 1) * height]
        parts = later


def guest_unpack_kernel(devices, hit_count, picks, picks_guest, outs, result):
    half = WIDE // 2
    own = dot(picks[...], outs[:, :WIDE], NN)
    guest = dot(picks_guest[...], outs[:, WIDE:], NN)
    for g in range(4):
        rows = own[g // 2 * ROWS : (g // 2 + 1) * ROWS, g % 2 * half : (g % 2 + 1) * half]
        rows = rows + guest[g * ROWS : (g + 1) * ROWS]
        result[:, g * half : (g + 1) * half] = rows.astype(jnp.bfloat16)


def unpack_kernel(devices, hit_count, picks, *refs):
    outs, logs, result = refs[0], refs[1:-1], refs[-1]

    def chosen(s, i):
        place = s * hit_count + i
        return picks[place * 2 * ROWS : (place + 1) * 2 * ROWS, :]

    def rows_of(i):
        parts = [
            dot(chosen(s, i), outs[:, s * WIDE : (s + 1) * WIDE], NN)
            for s in range(CAP)
        ]
        return sum(parts[1:], parts[0])

    def logs_of(i):
        parts = [
            dot(
                chosen(s, i).astype(jnp.float32),
                logs[0][:, s * HD : (s + 1) * HD],
                NN,
                precision=lax.Precision.HIGHEST,
            )
            for s in range(CAP)
        ]
        return sum(parts[1:], parts[0])

    if hit_count == 1:
        joined = rows_of(0)
    else:
        levels = [logs_of(i) for i in range(hit_count)]
        top = functools.reduce(jnp.maximum, levels)
        shares = [jnp.exp(level - top) for level in levels]
        total = sum(shares[1:], shares[0])
        pieces = [rows_of(i) for i in range(hit_count)]
        columns = []
        for c in range(HALF):
            part = sum(
                shares[i][:, c : c + 1] * pieces[i][:, c * HD : (c + 1) * HD]
                for i in range(hit_count)
            )
            columns.append(part / total[:, c : c + 1])
        joined = jnp.concatenate(columns, axis=1)
    joined = joined.astype(jnp.bfloat16)
    result[:, :WIDE] = joined[:ROWS]
    result[:, WIDE:] = joined[ROWS:]


def vmem(count):
    return [pl.BlockSpec(memory_space=pltpu.VMEM)] * count


def smem(count):
    return [pl.BlockSpec(memory_space=pltpu.SMEM)] * count


def hbm(count):
    return [pl.BlockSpec(memory_space=pltpu.HBM)] * count


def body(prefix_len, hits, span_block, queries, fresh_keys, fresh_values, cache_keys, cache_values):
    devices = lax.axis_size("cache")
    hit_count = hits.shape[1]
    rows = devices * MSG
    owners = hits.reshape(REQUESTS * hit_count)
    fresh = (owners, queries, fresh_keys, fresh_values)

    def exchange(x):
        return lax.all_to_all(x, "cache", split_axis=0, concat_axis=0, tiled=True)

    def call(kernel, out_shape, name, grant=40, **kw):
        return pl.pallas_call(
            functools.partial(kernel, devices, hit_count),
            out_shape=[jax.ShapeDtypeStruct(*leaf) for leaf in out_shape],
            compiler_params=pltpu.CompilerParams(vmem_limit_bytes=grant * 2**20),
            name=name,
            **kw,
        )

    if hit_count == 1 and devices == 16:
        pairs = rows * (HALF + HALF // 2) * (REGION + rows)
        scalars = [pltpu.SMEM((devices,), jnp.int32)] * 2
        send, places = call(
            guest_pack_kernel,
            [((rows, GUEST_MSG), jnp.bfloat16), ((2, 4 * ROWS), jnp.int32)],
            "pack",
            in_specs=hbm(4),
            out_specs=vmem(2),
            scratch_shapes=[
                pltpu.VMEM((2 * ROWS, WIDE + HD), jnp.bfloat16),
                pltpu.VMEM((4 * ROWS, WIDE // 2 + HD), jnp.bfloat16),
                pltpu.SMEM((REQUESTS,), jnp.int32),
                *scalars,
                pltpu.SemaphoreType.DMA((13,)),
            ],
        )(*(pltpu.with_memory_space_constraint(x, pltpu.HBM) for x in fresh))
        got = exchange(send)
        shapes = [((HD, REGION), jnp.bfloat16), ((REGION, 2 * HD), jnp.bfloat16)]
        plan, prompt_mask, cached_mask, turned, wide, picks, picks_guest = call(
            guest_prep_kernel,
            [((8,), jnp.int32), ((2 * rows, rows), jnp.float32), ((2, REGION), jnp.float32)]
            + shapes
            + [((2 * ROWS, rows), jnp.bfloat16), ((4 * ROWS, rows), jnp.bfloat16)],
            "prep",
            in_specs=smem(2) + vmem(4),
            out_specs=smem(1) + vmem(6),
            scratch_shapes=scalars,
            cost_estimate=pl.CostEstimate(flops=10**6, bytes_accessed=2**22, transcendentals=0),
        )(owners, prefix_len, span_block, places, cache_keys, cache_values)

        def lent(way, keys, values):
            rows_lent = jnp.concatenate([keys[REGION:], values[REGION:]], axis=0)
            pairs = [(d, d ^ (2 * way)) for d in range(1, devices, 2)]
            return lax.ppermute(rows_lent, "cache", pairs)

        def unused(keys, values):
            return jnp.zeros((2 * REGION, HD), jnp.bfloat16)

        borrowed = [
            lax.cond(
                plan[3 + way] == 1,
                functools.partial(lent, way),
                unused,
                cache_keys,
                cache_values,
            )
            for way in range(1, 4)
        ]
        (mine,) = call(
            lend_kernel,
            [((2 * REGION, HD), jnp.bfloat16)],
            "lend",
            in_specs=smem(1) + hbm(5),
            out_specs=vmem(1),
            scratch_shapes=[pltpu.SemaphoreType.DMA((2,))],
        )(plan, cache_keys, cache_values, *borrowed)
        other = lax.ppermute(mine, "cache", [(d, d ^ 1) for d in range(devices)])
        turned_guest, wide_guest = call(
            host_kernel, shapes, "host", in_specs=smem(1) + vmem(2), out_specs=vmem(2)
        )(plan, mine, other)
        (answer,) = call(
            guest_attend_kernel,
            [((rows, WIDE + WIDE // 2), jnp.bfloat16)],
            "attend",
            in_specs=smem(1) + vmem(7),
            out_specs=vmem(1),
            cost_estimate=pl.CostEstimate(
                flops=4 * pairs * HD, bytes_accessed=8 * rows * WIDE, transcendentals=pairs
            ),
        )(plan, prompt_mask, cached_mask, got, turned, wide, turned_guest, wide_guest)
        return call(
            guest_unpack_kernel,
            [((ROWS, HEADS * HD), jnp.bfloat16)],
            "unpack",
            in_specs=vmem(3),
            out_specs=vmem(1),
        )(picks, picks_guest, exchange(answer))[0]
    send, places = call(
        pack_kernel,
        [((rows, CAP * (WIDE + HD)), jnp.bfloat16), ((CAP * hit_count, 2 * ROWS), jnp.int32)],
        "pack",
        in_specs=hbm(4),
        out_specs=vmem(2),
        scratch_shapes=[
            pltpu.VMEM((2 * ROWS, WIDE + HD), jnp.bfloat16),
            pltpu.SMEM((REQUESTS * hit_count,), jnp.int32),
            pltpu.SMEM((devices,), jnp.int32),
            pltpu.SemaphoreType.DMA((5,)),
        ],
    )(*(pltpu.with_memory_space_constraint(x, pltpu.HBM) for x in fresh))
    got = exchange(send)
    busy, prompt_mask, cached_mask, turned, wide, picks = call(
        prep_kernel,
        [
            ((CAP,), jnp.int32),
            ((CAP * rows, rows), jnp.float32),
            ((CAP, REGION), jnp.float32),
            ((HD, CAP * REGION), jnp.bfloat16),
            ((CAP * REGION, 2 * HD), jnp.bfloat16),
            ((CAP * hit_count * 2 * ROWS, rows), jnp.bfloat16),
        ],
        "prep",
        in_specs=smem(2) + vmem(4),
        out_specs=smem(1) + vmem(5),
        cost_estimate=pl.CostEstimate(flops=10**6, bytes_accessed=2**22, transcendentals=0),
    )(owners, prefix_len, span_block, places, cache_keys, cache_values)
    pairs = CAP * rows * HALF * (REGION + rows)
    answers = call(
        attend_kernel,
        [((rows, CAP * WIDE), jnp.bfloat16)]
        + [((rows, CAP * HD), jnp.float32)] * (hit_count > 1),
        "attend",
        in_specs=smem(1) + vmem(5),
        out_specs=vmem(1 + (hit_count > 1)),
        cost_estimate=pl.CostEstimate(
            flops=4 * pairs * HD, bytes_accessed=8 * rows * WIDE, transcendentals=pairs
        ),
    )(busy, prompt_mask, cached_mask, got, turned, wide)
    returned = [exchange(answer) for answer in answers]
    return call(
        unpack_kernel,
        [((ROWS, HEADS * HD), jnp.bfloat16)],
        "unpack",
        in_specs=vmem(1 + len(returned)),
        out_specs=vmem(1),
    )(picks, *returned)[0]


def solution(mesh):
    in_specs = (
        P("groups"),
        P("groups", None),
        P("groups", None),
        P(("groups", "cache"), None),
        P(("groups", "cache"), None),
        P(("groups", "cache"), None),
        P(("groups", "cache"), None),
        P(("groups", "cache"), None),
    )
    out_specs = P(("groups", "cache"), None)
    return jax.shard_map(body, mesh=mesh, in_specs=in_specs, out_specs=out_specs, check_vma=False)
```

```python
import functools
import math

import jax
import jax.numpy as jnp
from jax import lax
from jax.experimental import pallas as pl
from jax.experimental.pallas import tpu as pltpu
from jax.sharding import PartitionSpec as P

HEADS = 16
HD = 128
PAGE = 128
CAP = 2
REQUESTS = 16
TOK_REQ = 4
PAGES_DEV = 16

REGION = PAGES_DEV // CAP * PAGE
HALF = HEADS // 2
MSG = 2 * TOK_REQ
WIDE = HALF * HD
ROWS = REQUESTS * TOK_REQ
STRIP = 256
GUEST_MSG = WIDE + HD + WIDE // 2 + HD
SCALE = HD**-0.5
FLOOR = -1e30
NN = (((1,), (0,)), ((), ()))


def iota(shape, axis):
    return lax.broadcasted_iota(jnp.int32, shape, axis)


def dot(a, b, dims, **kw):
    return lax.dot_general(a, b, dims, preferred_element_type=jnp.float32, **kw)


def pack_kernel(devices, hit_count, owners, q, k, v, send, places, held, hits, count, sems):
    copies = [
        pltpu.make_async_copy(source, held.at[pl.ds(row, ROWS), pl.ds(column, width)], sems.at[n])
        for n, (source, row, column, width) in enumerate(
            [
                (q.at[:, pl.ds(0, WIDE)], 0, 0, WIDE),
                (q.at[:, pl.ds(WIDE, WIDE)], ROWS, 0, WIDE),
                (k, 0, WIDE, HD),
                (v, ROWS, WIDE, HD),
            ]
        )
    ]
    first = pltpu.make_async_copy(owners, hits, sems.at[4])
    first.start()
    for copy in copies:
        copy.start()
    lane = iota((1, 2 * ROWS), 1)
    lane_request = (lane % ROWS) // TOK_REQ
    first.wait()
    for r in range(REQUESTS):
        for i in range(hit_count):
            count[hits[r * hit_count + i]] = 0
    rows = [[jnp.full((1, 2 * ROWS), -4 * MSG, jnp.int32)] * hit_count for _ in range(CAP)]
    for r in range(REQUESTS):
        for i in range(hit_count):
            owner = hits[r * hit_count + i]
            rank = count[owner]
            count[owner] = rank + 1
            for s in range(CAP):
                place = jnp.where(rank == s, owner * MSG, -4 * MSG)
                rows[s][i] = jnp.where(lane_request == r, place, rows[s][i])
    inner = lane // ROWS * TOK_REQ + lane % TOK_REQ
    target = iota((devices * MSG, 2 * ROWS), 0)
    picks = []
    for s in range(CAP):
        chosen = None
        for i in range(hit_count):
            row = rows[s][i] + inner
            places[s * hit_count + i : s * hit_count + i + 1, :] = row
            hit = target == row
            chosen = hit if chosen is None else chosen | hit
        picks.append(jnp.where(chosen, 1.0, 0.0).astype(jnp.bfloat16))
    for copy in copies:
        copy.wait()
    packed = dot(jnp.concatenate(picks, axis=0), held[...], NN).astype(jnp.bfloat16)
    for s in range(CAP):
        rows = slice(s * devices * MSG, (s + 1) * devices * MSG)
        send[:, s * (WIDE + HD) : (s + 1) * (WIDE + HD)] = packed[rows]


def prep_kernel(
    devices, hit_count, hits, prefix_len, span, places, keys, values, *outs
):
    busy, prompt, cached, turned, wide, picks = outs
    rows = iota((devices * MSG, 2 * ROWS), 0)
    for n in range(CAP * hit_count):
        chosen = jnp.where(rows == places[n : n + 1, :], 1.0, 0.0)
        picks[n * 2 * ROWS : (n + 1) * 2 * ROWS, :] = chosen.T.astype(jnp.bfloat16)
    for n in range(0, CAP * REGION, STRIP):
        turned[:, n : n + STRIP] = keys[n : n + STRIP, :].T
    me = lax.axis_index("cache")
    wide[:, :HD] = values[...]
    wide[:, HD:] = jnp.ones((CAP * REGION, HD), jnp.bfloat16)
    for slot in range(CAP):
        seen = jnp.int32(0)
        request = jnp.int32(0)
        which = jnp.int32(0)
        for r in range(REQUESTS):
            for i in range(hit_count):
                mine = hits[r * hit_count + i] == me
                here = mine & (seen == slot)
                request = jnp.where(here, r, request)
                which = jnp.where(here, i, which)
                seen = seen + mine.astype(jnp.int32)
        limit = prefix_len[request] - which * REGION
        blocks = jnp.clip((limit + STRIP - 1) // STRIP, 1, REGION // STRIP)
        busy[slot] = jnp.where(seen > slot, blocks, 0)
        cached[slot : slot + 1, :] = jnp.where(iota((1, REGION), 1) < limit, 0.0, FLOOR)
        prompt_rows(devices, prompt, span, request, slot, hit_count == 1 or which == 0)


def prompt_rows(devices, prompt, span, request, slot, counted):
    total_rows = devices * MSG
    span_row = span[pl.ds(request, 1), :].astype(jnp.float32)
    source = iota((devices, total_rows), 0)
    spread = (iota((devices, total_rows), 1) // MSG == source).astype(jnp.bfloat16)
    spans = jnp.broadcast_to(span_row, (16, devices)).astype(jnp.bfloat16)
    key_span = dot(spans, spread, NN)[:1]
    lane = iota((1, total_rows), 1)
    key_spot = key_span.astype(jnp.int32) * TOK_REQ + lane % TOK_REQ
    is_key = (lane % MSG < TOK_REQ) & counted
    key_spot = jnp.where(is_key, key_spot, devices * TOK_REQ)
    block = 16 * MSG

    def one_block(at):
        row_source = at * 16 + iota((block, devices), 0) // MSG
        mine = iota((block, devices), 1) == row_source
        row_span = jnp.sum(jnp.where(mine, span_row, 0.0), axis=1, keepdims=True)
        row_spot = row_span.astype(jnp.int32) * TOK_REQ + iota((block, 1), 0) % TOK_REQ
        here = pl.ds(slot * total_rows + at * block, block)
        prompt[here, :] = jnp.where(key_spot <= row_spot, 0.0, FLOOR)

    each_block(devices, one_block)


def each_block(devices, one_block):
    blocks = devices // 16
    if blocks == 1:
        one_block(0)
    else:
        pl.loop(0, blocks)(one_block)


def lanes_max(parts):
    pieces = [part[:, n : n + HD] for part in parts for n in range(0, part.shape[1], HD)]
    return jnp.max(functools.reduce(jnp.maximum, pieces), axis=1, keepdims=True)


def attend_kernel(
    devices, hit_count, busy, prompt_mask, cached_mask, got, turned, wide, out, *levels
):
    total_rows = devices * MSG
    block = 16 * MSG
    factor = SCALE * math.log2(math.e)

    def nothing(slot):
        out[:, pl.ds(slot * WIDE, WIDE)] = jnp.zeros((total_rows, WIDE), jnp.bfloat16)
        for lse in levels:
            lse[:, pl.ds(slot * HD, HD)] = jnp.zeros((total_rows, HD), jnp.float32)

    def attend(slot, strips):
        whole = (strips - 1) * STRIP
        base = pl.multiple_of(slot * (WIDE + HD), HD)
        region = pl.multiple_of(slot * REGION, REGION)
        head = pl.ds(region, whole) if whole else None
        tail = pl.ds(pl.multiple_of(region + whole, STRIP), STRIP)
        tail_mask = cached_mask[pl.ds(slot, 1), whole : whole + STRIP]
        prompt_keys = got[:, pl.ds(base + WIDE, HD)].astype(jnp.float32)
        moved = pltpu.roll(prompt_keys, total_rows - TOK_REQ, 0)
        prompt_keys = prompt_keys.T.astype(jnp.bfloat16)
        prompt_values = jnp.concatenate(
            [moved.astype(jnp.bfloat16), jnp.ones((total_rows, HD), jnp.bfloat16)], axis=1
        )

        def one_block(at):
            here = pl.ds(at * block, block)
            prompt_bias = prompt_mask[pl.ds(slot * total_rows + at * block, block), :]
            prompt_bias = jnp.concatenate([prompt_bias, prompt_bias], axis=0)
            lane = iota((block, HD), 1)

            def scores(c):
                pair = jnp.concatenate(
                    [got[here, pl.ds(base + (c + n) * HD, HD)] for n in range(2)], axis=0
                )
                parts = [dot(pair, turned[:, head], NN)] if whole else []
                parts.append(dot(pair, turned[:, tail], NN) + tail_mask)
                parts.append(dot(pair, prompt_keys, NN) + prompt_bias)
                return parts

            logs = jnp.zeros((block, HD), jnp.float32)
            parts = scores(0)
            for c in range(0, HALF, 2):
                later = scores(c + 2) if c + 2 < HALF else None
                top = lanes_max(parts)
                if hit_count > 1:
                    top = jnp.maximum(top, 0.1 * FLOOR)
                parts = [jnp.exp2((x - top) * factor).astype(jnp.bfloat16) for x in parts]
                summed = dot(parts[-1], prompt_values, NN) + dot(parts[-2], wide[tail, :], NN)
                if whole:
                    summed = summed + dot(parts[0], wide[head, :], NN)
                totals = summed[:, HD:]
                if hit_count > 1:
                    totals = jnp.maximum(totals, 1.0)
                    level = top * SCALE + jnp.log(totals)
                    logs = jnp.where(lane == c, level[:block], logs)
                    logs = jnp.where(lane == c + 1, level[block:], logs)
                result = (summed[:, :HD] / totals).astype(jnp.bfloat16)
                for n in range(2):
                    column = pl.multiple_of(slot * WIDE + (c + n) * HD, HD)
                    out[here, pl.ds(column, HD)] = result[n * block : (n + 1) * block]
                parts = later
            for lse in levels:
                lse[here, pl.ds(pl.multiple_of(slot * HD, HD), HD)] = logs

        each_block(devices, one_block)

    @pl.loop(0, CAP)
    def _(slot):
        strips = busy[slot]
        pl.when(strips == 0)(lambda: nothing(slot))
        for count in range(1, REGION // STRIP + 1):
            pl.when(strips == count)(functools.partial(attend, slot, count))


def guest_plan(devices, owners, count, host):
    chips = devices // 2
    for d in range(devices):
        count[d] = 0
    ranks = []
    for r in range(REQUESTS):
        owner = owners[r]
        ranks.append(count[owner])
        count[owner] = ranks[r] + 1
    seconds = [count[d] > 1 for d in range(devices)]
    none = [jnp.logical_not(seconds[2 * x] | seconds[2 * x + 1]) for x in range(chips)]
    lends = []
    for x in range(chips):
        other = jnp.where(none[x ^ 1], 1, jnp.where(none[x ^ 2], 2, 3))
        lends.append(jnp.where(seconds[2 * x] & seconds[2 * x + 1], other, 0))
        host[2 * x] = jnp.int32(x)
        host[2 * x + 1] = lends[x] ^ x
    return ranks, lends


def guest_pack_kernel(
    devices, hit_count, owners, q, k, v, keys, send, places, lent, held, held_guest, hits, *scalars
):
    count, host, sems = scalars
    half = WIDE // 2
    moves = [
        (keys.at[pl.ds(REGION, REGION)], lent),
        (q.at[:, pl.ds(0, WIDE)], held.at[pl.ds(0, ROWS), pl.ds(0, WIDE)]),
        (q.at[:, pl.ds(WIDE, WIDE)], held.at[pl.ds(ROWS, ROWS), pl.ds(0, WIDE)]),
        (k, held.at[pl.ds(0, ROWS), pl.ds(WIDE, HD)]),
        (v, held.at[pl.ds(ROWS, ROWS), pl.ds(WIDE, HD)]),
    ]
    for g in range(4):
        here = pl.ds(g * ROWS, ROWS)
        moves.append((q.at[:, pl.ds(g * half, half)], held_guest.at[here, pl.ds(0, half)]))
        moves.append((v if g % 2 else k, held_guest.at[here, pl.ds(half, HD)]))
    first = pltpu.make_async_copy(owners, hits, sems.at[len(moves)])
    first.start()
    copies = [pltpu.make_async_copy(a, b, sems.at[n]) for n, (a, b) in enumerate(moves)]
    for copy in copies:
        copy.start()
    first.wait()
    ranks, _ = guest_plan(devices, hits, count, host)
    lane = iota((1, 4 * ROWS), 1)
    lane_request = lane % ROWS // TOK_REQ
    part = lane // ROWS
    nowhere = -4 * MSG
    own = jnp.full((1, 4 * ROWS), nowhere, jnp.int32)
    guest = own
    for r in range(REQUESTS):
        owner = hits[r]
        mine = lane_request == r
        own = jnp.where(mine, jnp.where(ranks[r] == 0, owner * MSG, nowhere), own)
        guest = jnp.where(mine, jnp.where(ranks[r] == 1, host[owner] * 2 * MSG, nowhere), guest)
    own = own + part * TOK_REQ + lane % TOK_REQ
    guest = guest + part * TOK_REQ + lane % TOK_REQ
    places[0:1, :] = own
    places[1:2, :] = guest
    target = iota((devices * MSG, 4 * ROWS), 0)
    pick = jnp.where(target[:, : 2 * ROWS] == own[:, : 2 * ROWS], 1.0, 0.0).astype(jnp.bfloat16)
    pick_guest = jnp.where(target == guest, 1.0, 0.0).astype(jnp.bfloat16)
    for copy in copies:
        copy.wait()
    send[:, : WIDE + HD] = dot(pick, held[...], NN).astype(jnp.bfloat16)
    send[:, WIDE + HD :] = dot(pick_guest, held_guest[...], NN).astype(jnp.bfloat16)


def guest_prep_kernel(
    devices, hit_count, hits, prefix_len, span, places, keys, values, lent, *refs
):
    plan, prompt, cached, turned, wide, picks, picks_guest, count, host = refs
    me = lax.axis_index("cache")
    lent[...] = values[REGION:, :]
    chip = me // 2
    ranks, lends = guest_plan(devices, hits, count, host)
    for way in (2, 3):
        used = [jnp.where(lend == way, 1, 0) for lend in lends]
        plan[2 + way] = functools.reduce(jnp.maximum, used)
    plan[6] = jnp.maximum(plan[4], plan[5])
    rows = iota((devices * MSG, 4 * ROWS), 0)
    chosen = jnp.where(rows[:, : 2 * ROWS] == places[0:1, : 2 * ROWS], 1.0, 0.0)
    picks[...] = chosen.T.astype(jnp.bfloat16)
    chosen = jnp.where(rows == places[1:2, :], 1.0, 0.0)
    picks_guest[...] = chosen.T.astype(jnp.bfloat16)
    widen(keys[:REGION, :], values[:REGION, :], turned, wide)
    first, guest, source = jnp.int32(-1), jnp.int32(-1), jnp.int32(0)
    for r in range(REQUESTS):
        owner = hits[r]
        here = (ranks[r] == 1) & (host[owner] == chip)
        first = jnp.where((ranks[r] == 0) & (owner == me), r, first)
        guest = jnp.where(here, r, guest)
        source = jnp.where(here, owner, source)
    core = me % 2
    from_first_core = jnp.where(source == 2 * chip, 1, 0)
    plan[2] = jnp.where(core == 1, (source // 2) ^ chip, 0)
    plan[3] = jnp.where(core == from_first_core, 1, 0)
    for job, found in enumerate((first, guest)):
        request = jnp.maximum(found, 0)
        limit = prefix_len[request]
        strips = jnp.clip((limit + STRIP - 1) // STRIP, 1, REGION // STRIP)
        plan[job] = jnp.where(found >= 0, strips, 0)
        cached[job : job + 1, :] = jnp.where(iota((1, REGION), 1) < limit, 0.0, FLOOR)
        prompt_rows(devices, prompt, span, request, job, True)


def widen(keys, values, turned, wide):
    for n in range(0, REGION, STRIP):
        turned[:, n : n + STRIP] = keys[n : n + STRIP].T
    wide[:, :HD] = values
    wide[:, HD:] = jnp.ones((REGION, HD), jnp.bfloat16)


def lend_kernel(devices, hit_count, plan, keys, values, near_keys, near_values, far, out, sems):
    sources = [
        [x.at[pl.ds(REGION, REGION)] for x in (keys, values)],
        [near_keys, near_values],
        [far.at[pl.ds(n * REGION, REGION)] for n in range(2)],
    ]
    for choice, pair in enumerate(sources):

        @pl.when(jnp.minimum(plan[2], 2) == choice)
        def _():
            copies = [
                pltpu.make_async_copy(pair[n], out.at[pl.ds(n * REGION, REGION)], sems.at[n])
                for n in range(2)
            ]
            for copy in copies:
                copy.start()
            for copy in copies:
                copy.wait()


def host_kernel(devices, hit_count, plan, mine, other, turned, wide):
    for choice, rows in enumerate((mine, other)):

        @pl.when(plan[3] == choice)
        def _():
            widen(rows[:REGION, :], rows[REGION:, :], turned, wide)


def guest_attend_kernel(
    devices, hit_count, plan, prompt_mask, cached_mask, got, turned, wide, *refs
):
    turned_guest, wide_guest, out = refs
    jobs = [
        (0, 0, HALF, turned, wide),
        (WIDE + HD, WIDE, HALF // 2, turned_guest, wide_guest),
    ]
    for job, (base, first, blocks, keys, values) in enumerate(jobs):
        strips = plan[job]

        @pl.when(strips == 0)
        def _():
            empty = jnp.zeros((devices * MSG, blocks * HD), jnp.bfloat16)
            out[:, first : first + blocks * HD] = empty

        for count in range(1, REGION // STRIP + 1):

            @pl.when(strips == count)
            def _():
                whole = (count - 1) * STRIP
                mask = prompt_mask[job * devices * MSG : (job + 1) * devices * MSG, :]
                attend_rows(
                    got,
                    base,
                    blocks,
                    slice(0, devices * MSG),
                    prompt_parts(got[:, base + blocks * HD : base + (blocks + 1) * HD]),
                    mask,
                    cached_mask[job : job + 1, whole : whole + STRIP],
                    keys[:, :whole] if whole else None,
                    keys[:, whole : whole + STRIP],
                    values[:whole, :] if whole else None,
                    values[whole : whole + STRIP, :],
                    out,
                    first,
                )


def prompt_parts(rows):
    height = rows.shape[0]
    wide = rows.astype(jnp.float32)
    moved = pltpu.roll(wide, height - TOK_REQ, 0).astype(jnp.bfloat16)
    values = jnp.concatenate([moved, jnp.ones((height, HD), jnp.bfloat16)], axis=1)
    return wide.T.astype(jnp.bfloat16), values


def attend_rows(
    got, base, blocks, here, prompt, mask, tail_mask, head, tail, head_values, tail_values, out, first
):
    prompt_keys, prompt_values = prompt
    factor = SCALE * math.log2(math.e)
    mask = jnp.concatenate([mask, mask], axis=0)
    height = mask.shape[0] // 2

    def scores(c):
        pair = jnp.concatenate(
            [got[here, base + (c + n) * HD : base + (c + n + 1) * HD] for n in range(2)], axis=0
        )
        parts = [] if head is None else [dot(pair, head, NN)]
        parts.append(dot(pair, tail, NN) + tail_mask)
        parts.append(dot(pair, prompt_keys, NN) + mask)
        return parts

    parts = scores(0)
    for c in range(0, blocks, 2):
        later = scores(c + 2) if c + 2 < blocks else None
        top = lanes_max(parts)
        parts = [jnp.exp2((x - top) * factor).astype(jnp.bfloat16) for x in parts]
        summed = dot(parts[-1], prompt_values, NN) + dot(parts[-2], tail_values, NN)
        if head is not None:
            summed = summed + dot(parts[0], head_values, NN)
        result = (summed[:, :HD] / summed[:, HD:]).astype(jnp.bfloat16)
        for n in range(2):
            column = first + (c + n) * HD
            out[here, column : column + HD] = result[n * height : (n + 1) * height]
        parts = later


def guest_unpack_kernel(devices, hit_count, picks, picks_guest, outs, result):
    half = WIDE // 2
    own = dot(picks[...], outs[:, :WIDE], NN)
    guest = dot(picks_guest[...], outs[:, WIDE:], NN)
    for g in range(4):
        rows = own[g // 2 * ROWS : (g // 2 + 1) * ROWS, g % 2 * half : (g % 2 + 1) * half]
        rows = rows + guest[g * ROWS : (g + 1) * ROWS]
        result[:, g * half : (g + 1) * half] = rows.astype(jnp.bfloat16)


def unpack_kernel(devices, hit_count, picks, *refs):
    outs, logs, result = refs[0], refs[1:-1], refs[-1]

    def chosen(s, i):
        place = s * hit_count + i
        return picks[place * 2 * ROWS : (place + 1) * 2 * ROWS, :]

    def rows_of(i):
        parts = [
            dot(chosen(s, i), outs[:, s * WIDE : (s + 1) * WIDE], NN)
            for s in range(CAP)
        ]
        return sum(parts[1:], parts[0])

    def logs_of(i):
        parts = [
            dot(
                chosen(s, i).astype(jnp.float32),
                logs[0][:, s * HD : (s + 1) * HD],
                NN,
                precision=lax.Precision.HIGHEST,
            )
            for s in range(CAP)
        ]
        return sum(parts[1:], parts[0])

    if hit_count == 1:
        joined = rows_of(0)
    else:
        levels = [logs_of(i) for i in range(hit_count)]
        top = functools.reduce(jnp.maximum, levels)
        shares = [jnp.exp(level - top) for level in levels]
        total = sum(shares[1:], shares[0])
        pieces = [rows_of(i) for i in range(hit_count)]
        columns = []
        for c in range(HALF):
            part = sum(
                shares[i][:, c : c + 1] * pieces[i][:, c * HD : (c + 1) * HD]
                for i in range(hit_count)
            )
            columns.append(part / total[:, c : c + 1])
        joined = jnp.concatenate(columns, axis=1)
    joined = joined.astype(jnp.bfloat16)
    result[:, :WIDE] = joined[:ROWS]
    result[:, WIDE:] = joined[ROWS:]


def vmem(count):
    return [pl.BlockSpec(memory_space=pltpu.VMEM)] * count


def smem(count):
    return [pl.BlockSpec(memory_space=pltpu.SMEM)] * count


def hbm(count):
    return [pl.BlockSpec(memory_space=pltpu.HBM)] * count


def body(prefix_len, hits, span_block, queries, fresh_keys, fresh_values, cache_keys, cache_values):
    devices = lax.axis_size("cache")
    hit_count = hits.shape[1]
    rows = devices * MSG
    owners = hits.reshape(REQUESTS * hit_count)
    fresh = (owners, queries, fresh_keys, fresh_values)

    def exchange(x):
        return lax.all_to_all(x, "cache", split_axis=0, concat_axis=0, tiled=True)

    def call(kernel, out_shape, name, grant=40, **kw):
        return pl.pallas_call(
            functools.partial(kernel, devices, hit_count),
            out_shape=[jax.ShapeDtypeStruct(*leaf) for leaf in out_shape],
            compiler_params=pltpu.CompilerParams(vmem_limit_bytes=grant * 2**20),
            name=name,
            **kw,
        )

    if hit_count == 1 and devices == 16:
        pairs = rows * (HALF + HALF // 2) * (REGION + rows)
        scalars = [pltpu.SMEM((devices,), jnp.int32)] * 2
        slot = ((REGION, HD), jnp.bfloat16)
        send, places, lent_keys = call(
            guest_pack_kernel,
            [((rows, GUEST_MSG), jnp.bfloat16), ((2, 4 * ROWS), jnp.int32), slot],
            "pack",
            in_specs=hbm(5),
            out_specs=vmem(2) + hbm(1),
            scratch_shapes=[
                pltpu.VMEM((2 * ROWS, WIDE + HD), jnp.bfloat16),
                pltpu.VMEM((4 * ROWS, WIDE // 2 + HD), jnp.bfloat16),
                pltpu.SMEM((REQUESTS,), jnp.int32),
                *scalars,
                pltpu.SemaphoreType.DMA((14,)),
            ],
        )(*(pltpu.with_memory_space_constraint(x, pltpu.HBM) for x in (*fresh, cache_keys)))
        got = exchange(send)
        shapes = [((HD, REGION), jnp.bfloat16), ((REGION, 2 * HD), jnp.bfloat16)]
        lent_values, plan, prompt_mask, cached_mask, turned, wide, picks, picks_guest = call(
            guest_prep_kernel,
            [slot, ((8,), jnp.int32), ((2 * rows, rows), jnp.float32), ((2, REGION), jnp.float32)]
            + shapes
            + [((2 * ROWS, rows), jnp.bfloat16), ((4 * ROWS, rows), jnp.bfloat16)],
            "prep",
            in_specs=smem(2) + vmem(4),
            out_specs=vmem(1) + smem(1) + vmem(6),
            scratch_shapes=scalars,
            cost_estimate=pl.CostEstimate(flops=10**6, bytes_accessed=2**22, transcendentals=0),
        )(owners, prefix_len, span_block, places, cache_keys, cache_values)

        def to_chip(way, x):
            pairs = [(d, d ^ (2 * way)) for d in range(1, devices, 2)]
            return lax.ppermute(x, "cache", pairs)

        def nothing(*operands):
            return jnp.zeros((2 * REGION, HD), jnp.bfloat16)

        def from_far(flags, keys, values):
            both = jnp.concatenate([keys, values], axis=0)
            ways = [
                lax.cond(flags[2 + way] == 1, functools.partial(to_chip, way), nothing, both)
                for way in (2, 3)
            ]
            return jnp.where(flags[2] == 3, ways[1], ways[0])

        near = [to_chip(1, lent_keys), to_chip(1, lent_values)]
        far = lax.cond(plan[6] == 1, from_far, nothing, plan, lent_keys, lent_values)
        (mine,) = call(
            lend_kernel,
            [((2 * REGION, HD), jnp.bfloat16)],
            "lend",
            in_specs=smem(1) + hbm(5),
            out_specs=vmem(1),
            scratch_shapes=[pltpu.SemaphoreType.DMA((2,))],
        )(plan, cache_keys, cache_values, *near, far)
        other = lax.ppermute(mine, "cache", [(d, d ^ 1) for d in range(devices)])
        turned_guest, wide_guest = call(
            host_kernel, shapes, "host", in_specs=smem(1) + vmem(2), out_specs=vmem(2)
        )(plan, mine, other)
        (answer,) = call(
            guest_attend_kernel,
            [((rows, WIDE + WIDE // 2), jnp.bfloat16)],
            "attend",
            in_specs=smem(1) + vmem(7),
            out_specs=vmem(1),
            cost_estimate=pl.CostEstimate(
                flops=4 * pairs * HD, bytes_accessed=8 * rows * WIDE, transcendentals=pairs
            ),
        )(plan, prompt_mask, cached_mask, got, turned, wide, turned_guest, wide_guest)
        return call(
            guest_unpack_kernel,
            [((ROWS, HEADS * HD), jnp.bfloat16)],
            "unpack",
            in_specs=vmem(3),
            out_specs=vmem(1),
        )(picks, picks_guest, exchange(answer))[0]
    send, places = call(
        pack_kernel,
        [((rows, CAP * (WIDE + HD)), jnp.bfloat16), ((CAP * hit_count, 2 * ROWS), jnp.int32)],
        "pack",
        in_specs=hbm(4),
        out_specs=vmem(2),
        scratch_shapes=[
            pltpu.VMEM((2 * ROWS, WIDE + HD), jnp.bfloat16),
            pltpu.SMEM((REQUESTS * hit_count,), jnp.int32),
            pltpu.SMEM((devices,), jnp.int32),
            pltpu.SemaphoreType.DMA((5,)),
        ],
    )(*(pltpu.with_memory_space_constraint(x, pltpu.HBM) for x in fresh))
    got = exchange(send)
    busy, prompt_mask, cached_mask, turned, wide, picks = call(
        prep_kernel,
        [
            ((CAP,), jnp.int32),
            ((CAP * rows, rows), jnp.float32),
            ((CAP, REGION), jnp.float32),
            ((HD, CAP * REGION), jnp.bfloat16),
            ((CAP * REGION, 2 * HD), jnp.bfloat16),
            ((CAP * hit_count * 2 * ROWS, rows), jnp.bfloat16),
        ],
        "prep",
        in_specs=smem(2) + vmem(4),
        out_specs=smem(1) + vmem(5),
        cost_estimate=pl.CostEstimate(flops=10**6, bytes_accessed=2**22, transcendentals=0),
    )(owners, prefix_len, span_block, places, cache_keys, cache_values)
    pairs = CAP * rows * HALF * (REGION + rows)
    answers = call(
        attend_kernel,
        [((rows, CAP * WIDE), jnp.bfloat16)]
        + [((rows, CAP * HD), jnp.float32)] * (hit_count > 1),
        "attend",
        in_specs=smem(1) + vmem(5),
        out_specs=vmem(1 + (hit_count > 1)),
        cost_estimate=pl.CostEstimate(
            flops=4 * pairs * HD, bytes_accessed=8 * rows * WIDE, transcendentals=pairs
        ),
    )(busy, prompt_mask, cached_mask, got, turned, wide)
    returned = [exchange(answer) for answer in answers]
    return call(
        unpack_kernel,
        [((ROWS, HEADS * HD), jnp.bfloat16)],
        "unpack",
        in_specs=vmem(1 + len(returned)),
        out_specs=vmem(1),
    )(picks, *returned)[0]


def solution(mesh):
    in_specs = (
        P("groups"),
        P("groups", None),
        P("groups", None),
        P(("groups", "cache"), None),
        P(("groups", "cache"), None),
        P(("groups", "cache"), None),
        P(("groups", "cache"), None),
        P(("groups", "cache"), None),
    )
    out_specs = P(("groups", "cache"), None)
    return jax.shard_map(body, mesh=mesh, in_specs=in_specs, out_specs=out_specs, check_vma=False)
```

```python
import functools
import math

import jax
import jax.numpy as jnp
from jax import lax
from jax.experimental import pallas as pl
from jax.experimental.pallas import tpu as pltpu
from jax.sharding import PartitionSpec as P

HEADS = 16
HD = 128
PAGE = 128
CAP = 2
REQUESTS = 16
TOK_REQ = 4
PAGES_DEV = 16

REGION = PAGES_DEV // CAP * PAGE
HALF = HEADS // 2
MSG = 2 * TOK_REQ
WIDE = HALF * HD
ROWS = REQUESTS * TOK_REQ
STRIP = 256
GUEST_MSG = WIDE + HD + WIDE // 2 + HD
SCALE = HD**-0.5
FLOOR = -1e30
NN = (((1,), (0,)), ((), ()))


def iota(shape, axis):
    return lax.broadcasted_iota(jnp.int32, shape, axis)


def dot(a, b, dims, **kw):
    return lax.dot_general(a, b, dims, preferred_element_type=jnp.float32, **kw)


def pack_kernel(devices, hit_count, owners, q, k, v, send, places, held, hits, count, sems):
    copies = [
        pltpu.make_async_copy(source, held.at[pl.ds(row, ROWS), pl.ds(column, width)], sems.at[n])
        for n, (source, row, column, width) in enumerate(
            [
                (q.at[:, pl.ds(0, WIDE)], 0, 0, WIDE),
                (q.at[:, pl.ds(WIDE, WIDE)], ROWS, 0, WIDE),
                (k, 0, WIDE, HD),
                (v, ROWS, WIDE, HD),
            ]
        )
    ]
    first = pltpu.make_async_copy(owners, hits, sems.at[4])
    first.start()
    for copy in copies:
        copy.start()
    lane = iota((1, 2 * ROWS), 1)
    lane_request = (lane % ROWS) // TOK_REQ
    first.wait()
    for r in range(REQUESTS):
        for i in range(hit_count):
            count[hits[r * hit_count + i]] = 0
    rows = [[jnp.full((1, 2 * ROWS), -4 * MSG, jnp.int32)] * hit_count for _ in range(CAP)]
    for r in range(REQUESTS):
        for i in range(hit_count):
            owner = hits[r * hit_count + i]
            rank = count[owner]
            count[owner] = rank + 1
            for s in range(CAP):
                place = jnp.where(rank == s, owner * MSG, -4 * MSG)
                rows[s][i] = jnp.where(lane_request == r, place, rows[s][i])
    inner = lane // ROWS * TOK_REQ + lane % TOK_REQ
    target = iota((devices * MSG, 2 * ROWS), 0)
    picks = []
    for s in range(CAP):
        chosen = None
        for i in range(hit_count):
            row = rows[s][i] + inner
            places[s * hit_count + i : s * hit_count + i + 1, :] = row
            hit = target == row
            chosen = hit if chosen is None else chosen | hit
        picks.append(jnp.where(chosen, 1.0, 0.0).astype(jnp.bfloat16))
    for copy in copies:
        copy.wait()
    packed = dot(jnp.concatenate(picks, axis=0), held[...], NN).astype(jnp.bfloat16)
    for s in range(CAP):
        rows = slice(s * devices * MSG, (s + 1) * devices * MSG)
        send[:, s * (WIDE + HD) : (s + 1) * (WIDE + HD)] = packed[rows]


def prep_kernel(
    devices, hit_count, hits, prefix_len, span, places, keys, values, *outs
):
    busy, prompt, cached, turned, wide, picks = outs
    rows = iota((devices * MSG, 2 * ROWS), 0)
    for n in range(CAP * hit_count):
        chosen = jnp.where(rows == places[n : n + 1, :], 1.0, 0.0)
        picks[n * 2 * ROWS : (n + 1) * 2 * ROWS, :] = chosen.T.astype(jnp.bfloat16)
    for n in range(0, CAP * REGION, STRIP):
        turned[:, n : n + STRIP] = keys[n : n + STRIP, :].T
    me = lax.axis_index("cache")
    wide[:, :HD] = values[...]
    wide[:, HD:] = jnp.ones((CAP * REGION, HD), jnp.bfloat16)
    for slot in range(CAP):
        seen = jnp.int32(0)
        request = jnp.int32(0)
        which = jnp.int32(0)
        for r in range(REQUESTS):
            for i in range(hit_count):
                mine = hits[r * hit_count + i] == me
                here = mine & (seen == slot)
                request = jnp.where(here, r, request)
                which = jnp.where(here, i, which)
                seen = seen + mine.astype(jnp.int32)
        limit = prefix_len[request] - which * REGION
        blocks = jnp.clip((limit + STRIP - 1) // STRIP, 1, REGION // STRIP)
        busy[slot] = jnp.where(seen > slot, blocks, 0)
        cached[slot : slot + 1, :] = jnp.where(iota((1, REGION), 1) < limit, 0.0, FLOOR)
        prompt_rows(devices, prompt, span, request, slot, hit_count == 1 or which == 0)


def prompt_rows(devices, prompt, span, request, slot, counted):
    total_rows = devices * MSG
    span_row = span[pl.ds(request, 1), :].astype(jnp.float32)
    source = iota((devices, total_rows), 0)
    spread = (iota((devices, total_rows), 1) // MSG == source).astype(jnp.bfloat16)
    spans = jnp.broadcast_to(span_row, (16, devices)).astype(jnp.bfloat16)
    key_span = dot(spans, spread, NN)[:1]
    lane = iota((1, total_rows), 1)
    key_spot = key_span.astype(jnp.int32) * TOK_REQ + lane % TOK_REQ
    is_key = (lane % MSG < TOK_REQ) & counted
    key_spot = jnp.where(is_key, key_spot, devices * TOK_REQ)
    block = 16 * MSG

    def one_block(at):
        row_source = at * 16 + iota((block, devices), 0) // MSG
        mine = iota((block, devices), 1) == row_source
        row_span = jnp.sum(jnp.where(mine, span_row, 0.0), axis=1, keepdims=True)
        row_spot = row_span.astype(jnp.int32) * TOK_REQ + iota((block, 1), 0) % TOK_REQ
        here = pl.ds(slot * total_rows + at * block, block)
        prompt[here, :] = jnp.where(key_spot <= row_spot, 0.0, FLOOR)

    each_block(devices, one_block)


def each_block(devices, one_block):
    blocks = devices // 16
    if blocks == 1:
        one_block(0)
    else:
        pl.loop(0, blocks)(one_block)


def lanes_max(parts):
    pieces = [part[:, n : n + HD] for part in parts for n in range(0, part.shape[1], HD)]
    return jnp.max(functools.reduce(jnp.maximum, pieces), axis=1, keepdims=True)


def attend_kernel(
    devices, hit_count, busy, prompt_mask, cached_mask, got, turned, wide, out, *levels
):
    total_rows = devices * MSG
    block = 16 * MSG
    factor = SCALE * math.log2(math.e)

    def nothing(slot):
        out[:, pl.ds(slot * WIDE, WIDE)] = jnp.zeros((total_rows, WIDE), jnp.bfloat16)
        for lse in levels:
            lse[:, pl.ds(slot * HD, HD)] = jnp.zeros((total_rows, HD), jnp.float32)

    def attend(slot, strips):
        whole = (strips - 1) * STRIP
        base = pl.multiple_of(slot * (WIDE + HD), HD)
        region = pl.multiple_of(slot * REGION, REGION)
        head = pl.ds(region, whole) if whole else None
        tail = pl.ds(pl.multiple_of(region + whole, STRIP), STRIP)
        tail_mask = cached_mask[pl.ds(slot, 1), whole : whole + STRIP]
        prompt_keys = got[:, pl.ds(base + WIDE, HD)].astype(jnp.float32)
        moved = pltpu.roll(prompt_keys, total_rows - TOK_REQ, 0)
        prompt_keys = prompt_keys.T.astype(jnp.bfloat16)
        prompt_values = jnp.concatenate(
            [moved.astype(jnp.bfloat16), jnp.ones((total_rows, HD), jnp.bfloat16)], axis=1
        )

        def one_block(at):
            here = pl.ds(at * block, block)
            prompt_bias = prompt_mask[pl.ds(slot * total_rows + at * block, block), :]
            prompt_bias = jnp.concatenate([prompt_bias, prompt_bias], axis=0)
            lane = iota((block, HD), 1)

            def scores(c):
                pair = jnp.concatenate(
                    [got[here, pl.ds(base + (c + n) * HD, HD)] for n in range(2)], axis=0
                )
                parts = [dot(pair, turned[:, head], NN)] if whole else []
                parts.append(dot(pair, turned[:, tail], NN) + tail_mask)
                parts.append(dot(pair, prompt_keys, NN) + prompt_bias)
                return parts

            logs = jnp.zeros((block, HD), jnp.float32)
            parts = scores(0)
            for c in range(0, HALF, 2):
                later = scores(c + 2) if c + 2 < HALF else None
                top = lanes_max(parts)
                if hit_count > 1:
                    top = jnp.maximum(top, 0.1 * FLOOR)
                parts = [jnp.exp2((x - top) * factor).astype(jnp.bfloat16) for x in parts]
                summed = dot(parts[-1], prompt_values, NN) + dot(parts[-2], wide[tail, :], NN)
                if whole:
                    summed = summed + dot(parts[0], wide[head, :], NN)
                totals = summed[:, HD:]
                if hit_count > 1:
                    totals = jnp.maximum(totals, 1.0)
                    level = top * SCALE + jnp.log(totals)
                    logs = jnp.where(lane == c, level[:block], logs)
                    logs = jnp.where(lane == c + 1, level[block:], logs)
                result = (summed[:, :HD] / totals).astype(jnp.bfloat16)
                for n in range(2):
                    column = pl.multiple_of(slot * WIDE + (c + n) * HD, HD)
                    out[here, pl.ds(column, HD)] = result[n * block : (n + 1) * block]
                parts = later
            for lse in levels:
                lse[here, pl.ds(pl.multiple_of(slot * HD, HD), HD)] = logs

        each_block(devices, one_block)

    @pl.loop(0, CAP)
    def _(slot):
        strips = busy[slot]
        pl.when(strips == 0)(lambda: nothing(slot))
        for count in range(1, REGION // STRIP + 1):
            pl.when(strips == count)(functools.partial(attend, slot, count))


def guest_plan(devices, owners, count, host):
    chips = devices // 2
    for d in range(devices):
        count[d] = 0
    ranks = []
    for r in range(REQUESTS):
        owner = owners[r]
        ranks.append(count[owner])
        count[owner] = ranks[r] + 1
    seconds = [count[d] > 1 for d in range(devices)]
    none = [jnp.logical_not(seconds[2 * x] | seconds[2 * x + 1]) for x in range(chips)]
    lends = []
    for x in range(chips):
        other = jnp.where(none[x ^ 1], 1, jnp.where(none[x ^ 2], 2, 3))
        lends.append(jnp.where(seconds[2 * x] & seconds[2 * x + 1], other, 0))
        host[2 * x] = jnp.int32(x)
        host[2 * x + 1] = lends[x] ^ x
    return ranks, lends


def guest_route_kernel(
    devices, hit_count, owners, keys, places, lent, hits, count, host, sems
):
    first = pltpu.make_async_copy(owners, hits, sems.at[0])
    second = pltpu.make_async_copy(keys.at[pl.ds(REGION, REGION)], lent, sems.at[1])
    first.start()
    second.start()
    first.wait()
    ranks, _ = guest_plan(devices, hits, count, host)
    lane = iota((1, 4 * ROWS), 1)
    lane_request = lane % ROWS // TOK_REQ
    nowhere = -4 * MSG
    own = jnp.full((1, 4 * ROWS), nowhere, jnp.int32)
    guest = own
    for r in range(REQUESTS):
        owner = hits[r]
        mine = lane_request == r
        own = jnp.where(mine, jnp.where(ranks[r] == 0, owner * MSG, nowhere), own)
        guest = jnp.where(mine, jnp.where(ranks[r] == 1, host[owner] * 2 * MSG, nowhere), guest)
    inner = lane // ROWS * TOK_REQ + lane % TOK_REQ
    places[0:1, :] = own + inner
    places[1:2, :] = guest + inner
    second.wait()


def guest_pack_kernel(devices, hit_count, places, q, k, v, send, same, held, held_guest, sems):
    same[...] = places[...]
    half = WIDE // 2
    moves = [
        (q.at[:, pl.ds(0, WIDE)], held.at[pl.ds(0, ROWS), pl.ds(0, WIDE)]),
        (q.at[:, pl.ds(WIDE, WIDE)], held.at[pl.ds(ROWS, ROWS), pl.ds(0, WIDE)]),
        (k, held.at[pl.ds(0, ROWS), pl.ds(WIDE, HD)]),
        (v, held.at[pl.ds(ROWS, ROWS), pl.ds(WIDE, HD)]),
    ]
    for g in range(4):
        here = pl.ds(g * ROWS, ROWS)
        moves.append((q.at[:, pl.ds(g * half, half)], held_guest.at[here, pl.ds(0, half)]))
        moves.append((v if g % 2 else k, held_guest.at[here, pl.ds(half, HD)]))
    copies = [pltpu.make_async_copy(a, b, sems.at[n]) for n, (a, b) in enumerate(moves)]
    for copy in copies:
        copy.start()
    target = iota((devices * MSG, 4 * ROWS), 0)
    own = target[:, : 2 * ROWS] == places[0:1, : 2 * ROWS]
    pick = jnp.where(own, 1.0, 0.0).astype(jnp.bfloat16)
    pick_guest = jnp.where(target == places[1:2, :], 1.0, 0.0).astype(jnp.bfloat16)
    for copy in copies:
        copy.wait()
    send[:, : WIDE + HD] = dot(pick, held[...], NN).astype(jnp.bfloat16)
    send[:, WIDE + HD :] = dot(pick_guest, held_guest[...], NN).astype(jnp.bfloat16)


def guest_prep_kernel(
    devices, hit_count, hits, prefix_len, span, places, keys, values, near, lent, *refs
):
    plan, prompt, cached, turned, wide, picks, picks_guest, count, host = refs
    me = lax.axis_index("cache")
    lent[...] = values[REGION:, :]
    chip = me // 2
    ranks, lends = guest_plan(devices, hits, count, host)
    for way in (2, 3):
        used = [jnp.where(lend == way, 1, 0) for lend in lends]
        plan[2 + way] = functools.reduce(jnp.maximum, used)
    plan[6] = jnp.maximum(plan[4], plan[5])
    rows = iota((devices * MSG, 4 * ROWS), 0)
    chosen = jnp.where(rows[:, : 2 * ROWS] == places[0:1, : 2 * ROWS], 1.0, 0.0)
    picks[...] = chosen.T.astype(jnp.bfloat16)
    chosen = jnp.where(rows == places[1:2, :], 1.0, 0.0)
    picks_guest[...] = chosen.T.astype(jnp.bfloat16)
    widen(keys[:REGION, :], values[:REGION, :], turned, wide)
    first, guest, source = jnp.int32(-1), jnp.int32(-1), jnp.int32(0)
    for r in range(REQUESTS):
        owner = hits[r]
        here = (ranks[r] == 1) & (host[owner] == chip)
        first = jnp.where((ranks[r] == 0) & (owner == me), r, first)
        guest = jnp.where(here, r, guest)
        source = jnp.where(here, owner, source)
    core = me % 2
    from_first_core = jnp.where(source == 2 * chip, 1, 0)
    plan[2] = jnp.where(core == 1, (source // 2) ^ chip, 0)
    plan[3] = jnp.where(core == from_first_core, 1, 0)
    for job, found in enumerate((first, guest)):
        request = jnp.maximum(found, 0)
        limit = prefix_len[request]
        strips = jnp.clip((limit + STRIP - 1) // STRIP, 1, REGION // STRIP)
        plan[job] = jnp.where(found >= 0, strips, 0)
        cached[job : job + 1, :] = jnp.where(iota((1, REGION), 1) < limit, 0.0, FLOOR)
        prompt_rows(devices, prompt, span, request, job, True)


def widen(keys, values, turned, wide):
    for n in range(0, REGION, STRIP):
        turned[:, n : n + STRIP] = keys[n : n + STRIP].T
    wide[:, :HD] = values
    wide[:, HD:] = jnp.ones((REGION, HD), jnp.bfloat16)


def lend_kernel(devices, hit_count, plan, keys, values, near_keys, near_values, far, out, sems):
    sources = [
        [x.at[pl.ds(REGION, REGION)] for x in (keys, values)],
        [near_keys, near_values],
        [far.at[pl.ds(n * REGION, REGION)] for n in range(2)],
    ]
    for choice, pair in enumerate(sources):

        @pl.when(jnp.minimum(plan[2], 2) == choice)
        def _():
            copies = [
                pltpu.make_async_copy(pair[n], out.at[pl.ds(n * REGION, REGION)], sems.at[n])
                for n in range(2)
            ]
            for copy in copies:
                copy.start()
            for copy in copies:
                copy.wait()


def host_kernel(devices, hit_count, plan, mine, other, turned, wide):
    for choice, rows in enumerate((mine, other)):

        @pl.when(plan[3] == choice)
        def _():
            widen(rows[:REGION, :], rows[REGION:, :], turned, wide)


def guest_attend_kernel(
    devices, hit_count, plan, prompt_mask, cached_mask, got, turned, wide, *refs
):
    turned_guest, wide_guest, out = refs
    jobs = [
        (0, 0, HALF, turned, wide),
        (WIDE + HD, WIDE, HALF // 2, turned_guest, wide_guest),
    ]
    for job, (base, first, blocks, keys, values) in enumerate(jobs):
        strips = plan[job]

        @pl.when(strips == 0)
        def _():
            empty = jnp.zeros((devices * MSG, blocks * HD), jnp.bfloat16)
            out[:, first : first + blocks * HD] = empty

        for count in range(1, REGION // STRIP + 1):

            @pl.when(strips == count)
            def _():
                whole = (count - 1) * STRIP
                mask = prompt_mask[job * devices * MSG : (job + 1) * devices * MSG, :]
                attend_rows(
                    got,
                    base,
                    blocks,
                    slice(0, devices * MSG),
                    prompt_parts(got[:, base + blocks * HD : base + (blocks + 1) * HD]),
                    mask,
                    cached_mask[job : job + 1, whole : whole + STRIP],
                    keys[:, :whole] if whole else None,
                    keys[:, whole : whole + STRIP],
                    values[:whole, :] if whole else None,
                    values[whole : whole + STRIP, :],
                    out,
                    first,
                )


def prompt_parts(rows):
    height = rows.shape[0]
    wide = rows.astype(jnp.float32)
    moved = pltpu.roll(wide, height - TOK_REQ, 0).astype(jnp.bfloat16)
    values = jnp.concatenate([moved, jnp.ones((height, HD), jnp.bfloat16)], axis=1)
    return wide.T.astype(jnp.bfloat16), values


def attend_rows(
    got, base, blocks, here, prompt, mask, tail_mask, head, tail, head_values, tail_values, out, first
):
    prompt_keys, prompt_values = prompt
    factor = SCALE * math.log2(math.e)
    mask = jnp.concatenate([mask, mask], axis=0)
    height = mask.shape[0] // 2

    def scores(c):
        pair = jnp.concatenate(
            [got[here, base + (c + n) * HD : base + (c + n + 1) * HD] for n in range(2)], axis=0
        )
        parts = [] if head is None else [dot(pair, head, NN)]
        parts.append(dot(pair, tail, NN) + tail_mask)
        parts.append(dot(pair, prompt_keys, NN) + mask)
        return parts

    parts = scores(0)
    for c in range(0, blocks, 2):
        later = scores(c + 2) if c + 2 < blocks else None
        top = lanes_max(parts)
        parts = [jnp.exp2((x - top) * factor).astype(jnp.bfloat16) for x in parts]
        summed = dot(parts[-1], prompt_values, NN) + dot(parts[-2], tail_values, NN)
        if head is not None:
            summed = summed + dot(parts[0], head_values, NN)
        result = (summed[:, :HD] / summed[:, HD:]).astype(jnp.bfloat16)
        for n in range(2):
            column = first + (c + n) * HD
            out[here, column : column + HD] = result[n * height : (n + 1) * height]
        parts = later


def guest_unpack_kernel(devices, hit_count, picks, picks_guest, outs, result):
    half = WIDE // 2
    own = dot(picks[...], outs[:, :WIDE], NN)
    guest = dot(picks_guest[...], outs[:, WIDE:], NN)
    for g in range(4):
        rows = own[g // 2 * ROWS : (g // 2 + 1) * ROWS, g % 2 * half : (g % 2 + 1) * half]
        rows = rows + guest[g * ROWS : (g + 1) * ROWS]
        result[:, g * half : (g + 1) * half] = rows.astype(jnp.bfloat16)


def unpack_kernel(devices, hit_count, picks, *refs):
    outs, logs, result = refs[0], refs[1:-1], refs[-1]

    def chosen(s, i):
        place = s * hit_count + i
        return picks[place * 2 * ROWS : (place + 1) * 2 * ROWS, :]

    def rows_of(i):
        parts = [
            dot(chosen(s, i), outs[:, s * WIDE : (s + 1) * WIDE], NN)
            for s in range(CAP)
        ]
        return sum(parts[1:], parts[0])

    def logs_of(i):
        parts = [
            dot(
                chosen(s, i).astype(jnp.float32),
                logs[0][:, s * HD : (s + 1) * HD],
                NN,
                precision=lax.Precision.HIGHEST,
            )
            for s in range(CAP)
        ]
        return sum(parts[1:], parts[0])

    if hit_count == 1:
        joined = rows_of(0)
    else:
        levels = [logs_of(i) for i in range(hit_count)]
        top = functools.reduce(jnp.maximum, levels)
        shares = [jnp.exp(level - top) for level in levels]
        total = sum(shares[1:], shares[0])
        pieces = [rows_of(i) for i in range(hit_count)]
        columns = []
        for c in range(HALF):
            part = sum(
                shares[i][:, c : c + 1] * pieces[i][:, c * HD : (c + 1) * HD]
                for i in range(hit_count)
            )
            columns.append(part / total[:, c : c + 1])
        joined = jnp.concatenate(columns, axis=1)
    joined = joined.astype(jnp.bfloat16)
    result[:, :WIDE] = joined[:ROWS]
    result[:, WIDE:] = joined[ROWS:]


def vmem(count):
    return [pl.BlockSpec(memory_space=pltpu.VMEM)] * count


def smem(count):
    return [pl.BlockSpec(memory_space=pltpu.SMEM)] * count


def hbm(count):
    return [pl.BlockSpec(memory_space=pltpu.HBM)] * count


def body(prefix_len, hits, span_block, queries, fresh_keys, fresh_values, cache_keys, cache_values):
    devices = lax.axis_size("cache")
    hit_count = hits.shape[1]
    rows = devices * MSG
    owners = hits.reshape(REQUESTS * hit_count)
    fresh = (owners, queries, fresh_keys, fresh_values)

    def exchange(x):
        return lax.all_to_all(x, "cache", split_axis=0, concat_axis=0, tiled=True)

    def call(kernel, out_shape, name, grant=40, **kw):
        return pl.pallas_call(
            functools.partial(kernel, devices, hit_count),
            out_shape=[jax.ShapeDtypeStruct(*leaf) for leaf in out_shape],
            compiler_params=pltpu.CompilerParams(vmem_limit_bytes=grant * 2**20),
            name=name,
            **kw,
        )

    if hit_count == 1 and devices == 16:
        pairs = rows * (HALF + HALF // 2) * (REGION + rows)
        scalars = [pltpu.SMEM((devices,), jnp.int32)] * 2
        slot = ((REGION, HD), jnp.bfloat16)
        in_place = [pltpu.with_memory_space_constraint(x, pltpu.HBM) for x in fresh]
        places, lent_keys = call(
            guest_route_kernel,
            [((2, 4 * ROWS), jnp.int32), slot],
            "route",
            in_specs=hbm(2),
            out_specs=vmem(2),
            scratch_shapes=[
                pltpu.SMEM((REQUESTS,), jnp.int32),
                *scalars,
                pltpu.SemaphoreType.DMA((2,)),
            ],
        )(in_place[0], pltpu.with_memory_space_constraint(cache_keys, pltpu.HBM))
        send, places = call(
            guest_pack_kernel,
            [((rows, GUEST_MSG), jnp.bfloat16), ((2, 4 * ROWS), jnp.int32)],
            "pack",
            in_specs=vmem(1) + hbm(3),
            out_specs=vmem(2),
            scratch_shapes=[
                pltpu.VMEM((2 * ROWS, WIDE + HD), jnp.bfloat16),
                pltpu.VMEM((4 * ROWS, WIDE // 2 + HD), jnp.bfloat16),
                pltpu.SemaphoreType.DMA((12,)),
            ],
        )(places, *in_place[1:])
        def to_chip(way, x):
            pairs = [(d, d ^ (2 * way)) for d in range(1, devices, 2)]
            return lax.ppermute(x, "cache", pairs)

        near_keys = to_chip(1, lent_keys)
        got = exchange(send)
        shapes = [((HD, REGION), jnp.bfloat16), ((REGION, 2 * HD), jnp.bfloat16)]
        lent_values, plan, prompt_mask, cached_mask, turned, wide, picks, picks_guest = call(
            guest_prep_kernel,
            [slot, ((8,), jnp.int32), ((2 * rows, rows), jnp.float32), ((2, REGION), jnp.float32)]
            + shapes
            + [((2 * ROWS, rows), jnp.bfloat16), ((4 * ROWS, rows), jnp.bfloat16)],
            "prep",
            in_specs=smem(2) + vmem(4) + [pl.BlockSpec(memory_space=pl.ANY)],
            out_specs=vmem(1) + smem(1) + vmem(6),
            scratch_shapes=scalars,
            cost_estimate=pl.CostEstimate(flops=10**6, bytes_accessed=2**22, transcendentals=0),
        )(owners, prefix_len, span_block, places, cache_keys, cache_values, near_keys)

        def nothing(*operands):
            return jnp.zeros((2 * REGION, HD), jnp.bfloat16)

        def from_far(flags, keys, values):
            both = jnp.concatenate([keys[REGION:], values[REGION:]], axis=0)
            ways = [
                lax.cond(flags[2 + way] == 1, functools.partial(to_chip, way), nothing, both)
                for way in (2, 3)
            ]
            return jnp.where(flags[2] == 3, ways[1], ways[0])

        near = [near_keys, to_chip(1, lent_values)]
        far = lax.cond(plan[6] == 1, from_far, nothing, plan, cache_keys, cache_values)
        (mine,) = call(
            lend_kernel,
            [((2 * REGION, HD), jnp.bfloat16)],
            "lend",
            in_specs=smem(1) + hbm(5),
            out_specs=vmem(1),
            scratch_shapes=[pltpu.SemaphoreType.DMA((2,))],
        )(plan, cache_keys, cache_values, *near, far)
        other = lax.ppermute(mine, "cache", [(d, d ^ 1) for d in range(devices)])
        turned_guest, wide_guest = call(
            host_kernel, shapes, "host", in_specs=smem(1) + vmem(2), out_specs=vmem(2)
        )(plan, mine, other)
        (answer,) = call(
            guest_attend_kernel,
            [((rows, WIDE + WIDE // 2), jnp.bfloat16)],
            "attend",
            in_specs=smem(1) + vmem(7),
            out_specs=vmem(1),
            cost_estimate=pl.CostEstimate(
                flops=4 * pairs * HD, bytes_accessed=8 * rows * WIDE, transcendentals=pairs
            ),
        )(plan, prompt_mask, cached_mask, got, turned, wide, turned_guest, wide_guest)
        return call(
            guest_unpack_kernel,
            [((ROWS, HEADS * HD), jnp.bfloat16)],
            "unpack",
            in_specs=vmem(3),
            out_specs=vmem(1),
        )(picks, picks_guest, exchange(answer))[0]
    send, places = call(
        pack_kernel,
        [((rows, CAP * (WIDE + HD)), jnp.bfloat16), ((CAP * hit_count, 2 * ROWS), jnp.int32)],
        "pack",
        in_specs=hbm(4),
        out_specs=vmem(2),
        scratch_shapes=[
            pltpu.VMEM((2 * ROWS, WIDE + HD), jnp.bfloat16),
            pltpu.SMEM((REQUESTS * hit_count,), jnp.int32),
            pltpu.SMEM((devices,), jnp.int32),
            pltpu.SemaphoreType.DMA((5,)),
        ],
    )(*(pltpu.with_memory_space_constraint(x, pltpu.HBM) for x in fresh))
    got = exchange(send)
    busy, prompt_mask, cached_mask, turned, wide, picks = call(
        prep_kernel,
        [
            ((CAP,), jnp.int32),
            ((CAP * rows, rows), jnp.float32),
            ((CAP, REGION), jnp.float32),
            ((HD, CAP * REGION), jnp.bfloat16),
            ((CAP * REGION, 2 * HD), jnp.bfloat16),
            ((CAP * hit_count * 2 * ROWS, rows), jnp.bfloat16),
        ],
        "prep",
        in_specs=smem(2) + vmem(4),
        out_specs=smem(1) + vmem(5),
        cost_estimate=pl.CostEstimate(flops=10**6, bytes_accessed=2**22, transcendentals=0),
    )(owners, prefix_len, span_block, places, cache_keys, cache_values)
    pairs = CAP * rows * HALF * (REGION + rows)
    answers = call(
        attend_kernel,
        [((rows, CAP * WIDE), jnp.bfloat16)]
        + [((rows, CAP * HD), jnp.float32)] * (hit_count > 1),
        "attend",
        in_specs=smem(1) + vmem(5),
        out_specs=vmem(1 + (hit_count > 1)),
        cost_estimate=pl.CostEstimate(
            flops=4 * pairs * HD, bytes_accessed=8 * rows * WIDE, transcendentals=pairs
        ),
    )(busy, prompt_mask, cached_mask, got, turned, wide)
    returned = [exchange(answer) for answer in answers]
    return call(
        unpack_kernel,
        [((ROWS, HEADS * HD), jnp.bfloat16)],
        "unpack",
        in_specs=vmem(1 + len(returned)),
        out_specs=vmem(1),
    )(picks, *returned)[0]


def solution(mesh):
    in_specs = (
        P("groups"),
        P("groups", None),
        P("groups", None),
        P(("groups", "cache"), None),
        P(("groups", "cache"), None),
        P(("groups", "cache"), None),
        P(("groups", "cache"), None),
        P(("groups", "cache"), None),
    )
    out_specs = P(("groups", "cache"), None)
    return jax.shard_map(body, mesh=mesh, in_specs=in_specs, out_specs=out_specs, check_vma=False)
```

```python
import functools
import math

import jax
import jax.numpy as jnp
from jax import lax
from jax.experimental import pallas as pl
from jax.experimental.pallas import tpu as pltpu
from jax.sharding import PartitionSpec as P

HEADS = 16
HD = 128
PAGE = 128
CAP = 2
REQUESTS = 16
TOK_REQ = 4
PAGES_DEV = 16

REGION = PAGES_DEV // CAP * PAGE
HALF = HEADS // 2
MSG = 2 * TOK_REQ
WIDE = HALF * HD
ROWS = REQUESTS * TOK_REQ
STRIP = 256
GUEST_MSG = WIDE + HD + WIDE // 2 + HD
SCALE = HD**-0.5
FLOOR = -1e30
NN = (((1,), (0,)), ((), ()))


def iota(shape, axis):
    return lax.broadcasted_iota(jnp.int32, shape, axis)


def dot(a, b, dims, **kw):
    return lax.dot_general(a, b, dims, preferred_element_type=jnp.float32, **kw)


def pack_kernel(devices, hit_count, owners, q, k, v, send, places, held, hits, count, sems):
    copies = [
        pltpu.make_async_copy(source, held.at[pl.ds(row, ROWS), pl.ds(column, width)], sems.at[n])
        for n, (source, row, column, width) in enumerate(
            [
                (q.at[:, pl.ds(0, WIDE)], 0, 0, WIDE),
                (q.at[:, pl.ds(WIDE, WIDE)], ROWS, 0, WIDE),
                (k, 0, WIDE, HD),
                (v, ROWS, WIDE, HD),
            ]
        )
    ]
    first = pltpu.make_async_copy(owners, hits, sems.at[4])
    first.start()
    for copy in copies:
        copy.start()
    lane = iota((1, 2 * ROWS), 1)
    lane_request = (lane % ROWS) // TOK_REQ
    first.wait()
    for r in range(REQUESTS):
        for i in range(hit_count):
            count[hits[r * hit_count + i]] = 0
    rows = [[jnp.full((1, 2 * ROWS), -4 * MSG, jnp.int32)] * hit_count for _ in range(CAP)]
    for r in range(REQUESTS):
        for i in range(hit_count):
            owner = hits[r * hit_count + i]
            rank = count[owner]
            count[owner] = rank + 1
            for s in range(CAP):
                place = jnp.where(rank == s, owner * MSG, -4 * MSG)
                rows[s][i] = jnp.where(lane_request == r, place, rows[s][i])
    inner = lane // ROWS * TOK_REQ + lane % TOK_REQ
    target = iota((devices * MSG, 2 * ROWS), 0)
    picks = []
    for s in range(CAP):
        chosen = None
        for i in range(hit_count):
            row = rows[s][i] + inner
            places[s * hit_count + i : s * hit_count + i + 1, :] = row
            hit = target == row
            chosen = hit if chosen is None else chosen | hit
        picks.append(jnp.where(chosen, 1.0, 0.0).astype(jnp.bfloat16))
    for copy in copies:
        copy.wait()
    packed = dot(jnp.concatenate(picks, axis=0), held[...], NN).astype(jnp.bfloat16)
    for s in range(CAP):
        rows = slice(s * devices * MSG, (s + 1) * devices * MSG)
        send[:, s * (WIDE + HD) : (s + 1) * (WIDE + HD)] = packed[rows]


def prep_kernel(
    devices, hit_count, hits, prefix_len, span, places, keys, values, *outs
):
    busy, prompt, cached, turned, wide, picks = outs
    rows = iota((devices * MSG, 2 * ROWS), 0)
    for n in range(CAP * hit_count):
        chosen = jnp.where(rows == places[n : n + 1, :], 1.0, 0.0)
        picks[n * 2 * ROWS : (n + 1) * 2 * ROWS, :] = chosen.T.astype(jnp.bfloat16)
    for n in range(0, CAP * REGION, STRIP):
        turned[:, n : n + STRIP] = keys[n : n + STRIP, :].T
    me = lax.axis_index("cache")
    wide[:, :HD] = values[...]
    wide[:, HD:] = jnp.ones((CAP * REGION, HD), jnp.bfloat16)
    for slot in range(CAP):
        seen = jnp.int32(0)
        request = jnp.int32(0)
        which = jnp.int32(0)
        for r in range(REQUESTS):
            for i in range(hit_count):
                mine = hits[r * hit_count + i] == me
                here = mine & (seen == slot)
                request = jnp.where(here, r, request)
                which = jnp.where(here, i, which)
                seen = seen + mine.astype(jnp.int32)
        limit = prefix_len[request] - which * REGION
        blocks = jnp.clip((limit + STRIP - 1) // STRIP, 1, REGION // STRIP)
        busy[slot] = jnp.where(seen > slot, blocks, 0)
        cached[slot : slot + 1, :] = jnp.where(iota((1, REGION), 1) < limit, 0.0, FLOOR)
        prompt_rows(devices, prompt, span, request, slot, hit_count == 1 or which == 0)


def prompt_rows(devices, prompt, span, request, slot, counted):
    total_rows = devices * MSG
    span_row = span[pl.ds(request, 1), :].astype(jnp.float32)
    source = iota((devices, total_rows), 0)
    spread = (iota((devices, total_rows), 1) // MSG == source).astype(jnp.bfloat16)
    spans = jnp.broadcast_to(span_row, (16, devices)).astype(jnp.bfloat16)
    key_span = dot(spans, spread, NN)[:1]
    lane = iota((1, total_rows), 1)
    key_spot = key_span.astype(jnp.int32) * TOK_REQ + lane % TOK_REQ
    is_key = (lane % MSG < TOK_REQ) & counted
    key_spot = jnp.where(is_key, key_spot, devices * TOK_REQ)
    block = 16 * MSG

    def one_block(at):
        row_source = at * 16 + iota((block, devices), 0) // MSG
        mine = iota((block, devices), 1) == row_source
        row_span = jnp.sum(jnp.where(mine, span_row, 0.0), axis=1, keepdims=True)
        row_spot = row_span.astype(jnp.int32) * TOK_REQ + iota((block, 1), 0) % TOK_REQ
        here = pl.ds(slot * total_rows + at * block, block)
        prompt[here, :] = jnp.where(key_spot <= row_spot, 0.0, FLOOR)

    each_block(devices, one_block)


def each_block(devices, one_block):
    blocks = devices // 16
    if blocks == 1:
        one_block(0)
    else:
        pl.loop(0, blocks)(one_block)


def lanes_max(parts):
    pieces = [part[:, n : n + HD] for part in parts for n in range(0, part.shape[1], HD)]
    return jnp.max(functools.reduce(jnp.maximum, pieces), axis=1, keepdims=True)


def attend_kernel(
    devices, hit_count, busy, prompt_mask, cached_mask, got, turned, wide, out, *levels
):
    total_rows = devices * MSG
    block = 16 * MSG
    factor = SCALE * math.log2(math.e)

    def nothing(slot):
        out[:, pl.ds(slot * WIDE, WIDE)] = jnp.zeros((total_rows, WIDE), jnp.bfloat16)
        for lse in levels:
            lse[:, pl.ds(slot * HD, HD)] = jnp.zeros((total_rows, HD), jnp.float32)

    def attend(slot, strips):
        whole = (strips - 1) * STRIP
        base = pl.multiple_of(slot * (WIDE + HD), HD)
        region = pl.multiple_of(slot * REGION, REGION)
        head = pl.ds(region, whole) if whole else None
        tail = pl.ds(pl.multiple_of(region + whole, STRIP), STRIP)
        tail_mask = cached_mask[pl.ds(slot, 1), whole : whole + STRIP]
        prompt_keys = got[:, pl.ds(base + WIDE, HD)].astype(jnp.float32)
        moved = pltpu.roll(prompt_keys, total_rows - TOK_REQ, 0)
        prompt_keys = prompt_keys.T.astype(jnp.bfloat16)
        prompt_values = jnp.concatenate(
            [moved.astype(jnp.bfloat16), jnp.ones((total_rows, HD), jnp.bfloat16)], axis=1
        )

        def one_block(at):
            here = pl.ds(at * block, block)
            prompt_bias = prompt_mask[pl.ds(slot * total_rows + at * block, block), :]
            prompt_bias = jnp.concatenate([prompt_bias, prompt_bias], axis=0)
            lane = iota((block, HD), 1)

            def scores(c):
                pair = jnp.concatenate(
                    [got[here, pl.ds(base + (c + n) * HD, HD)] for n in range(2)], axis=0
                )
                parts = [dot(pair, turned[:, head], NN)] if whole else []
                parts.append(dot(pair, turned[:, tail], NN) + tail_mask)
                parts.append(dot(pair, prompt_keys, NN) + prompt_bias)
                return parts

            logs = jnp.zeros((block, HD), jnp.float32)
            parts = scores(0)
            for c in range(0, HALF, 2):
                later = scores(c + 2) if c + 2 < HALF else None
                top = lanes_max(parts)
                if hit_count > 1:
                    top = jnp.maximum(top, 0.1 * FLOOR)
                parts = [jnp.exp2((x - top) * factor).astype(jnp.bfloat16) for x in parts]
                summed = dot(parts[-1], prompt_values, NN) + dot(parts[-2], wide[tail, :], NN)
                if whole:
                    summed = summed + dot(parts[0], wide[head, :], NN)
                totals = summed[:, HD:]
                if hit_count > 1:
                    totals = jnp.maximum(totals, 1.0)
                    level = top * SCALE + jnp.log(totals)
                    logs = jnp.where(lane == c, level[:block], logs)
                    logs = jnp.where(lane == c + 1, level[block:], logs)
                result = (summed[:, :HD] / totals).astype(jnp.bfloat16)
                for n in range(2):
                    column = pl.multiple_of(slot * WIDE + (c + n) * HD, HD)
                    out[here, pl.ds(column, HD)] = result[n * block : (n + 1) * block]
                parts = later
            for lse in levels:
                lse[here, pl.ds(pl.multiple_of(slot * HD, HD), HD)] = logs

        each_block(devices, one_block)

    @pl.loop(0, CAP)
    def _(slot):
        strips = busy[slot]
        pl.when(strips == 0)(lambda: nothing(slot))
        for count in range(1, REGION // STRIP + 1):
            pl.when(strips == count)(functools.partial(attend, slot, count))


def guest_plan(devices, owners, count, host):
    chips = devices // 2
    for d in range(devices):
        count[d] = 0
    ranks = []
    for r in range(REQUESTS):
        owner = owners[r]
        ranks.append(count[owner])
        count[owner] = ranks[r] + 1
    seconds = [count[d] > 1 for d in range(devices)]
    none = [jnp.logical_not(seconds[2 * x] | seconds[2 * x + 1]) for x in range(chips)]
    lends = []
    for x in range(chips):
        other = jnp.where(none[x ^ 1], 1, jnp.where(none[x ^ 2], 2, 3))
        lends.append(jnp.where(seconds[2 * x] & seconds[2 * x + 1], other, 0))
        host[2 * x] = jnp.int32(x)
        host[2 * x + 1] = lends[x] ^ x
    return ranks, lends


def guest_pack_kernel(
    devices, hit_count, owners, q, k, v, send, places, way, held, held_guest, hits, *scalars
):
    count, host, sems = scalars
    half = WIDE // 2
    moves = [
        (q.at[:, pl.ds(0, WIDE)], held.at[pl.ds(0, ROWS), pl.ds(0, WIDE)]),
        (q.at[:, pl.ds(WIDE, WIDE)], held.at[pl.ds(ROWS, ROWS), pl.ds(0, WIDE)]),
        (k, held.at[pl.ds(0, ROWS), pl.ds(WIDE, HD)]),
        (v, held.at[pl.ds(ROWS, ROWS), pl.ds(WIDE, HD)]),
    ]
    for g in range(4):
        here = pl.ds(g * ROWS, ROWS)
        moves.append((q.at[:, pl.ds(g * half, half)], held_guest.at[here, pl.ds(0, half)]))
        moves.append((v if g % 2 else k, held_guest.at[here, pl.ds(half, HD)]))
    first = pltpu.make_async_copy(owners, hits, sems.at[len(moves)])
    first.start()
    copies = [pltpu.make_async_copy(a, b, sems.at[n]) for n, (a, b) in enumerate(moves)]
    for copy in copies:
        copy.start()
    first.wait()
    ranks, lends = guest_plan(devices, hits, count, host)
    used = [
        functools.reduce(jnp.logical_or, [lend == n for lend in lends]) for n in range(1, 4)
    ]
    mixed = used[2] | (used[0] & used[1])
    way[0] = jnp.where(mixed, 3, jnp.where(used[0], 1, jnp.where(used[1], 2, 0)))
    lane = iota((1, 4 * ROWS), 1)
    lane_request = lane % ROWS // TOK_REQ
    part = lane // ROWS
    nowhere = -4 * MSG
    own = jnp.full((1, 4 * ROWS), nowhere, jnp.int32)
    guest = own
    for r in range(REQUESTS):
        owner = hits[r]
        mine = lane_request == r
        own = jnp.where(mine, jnp.where(ranks[r] == 0, owner * MSG, nowhere), own)
        guest = jnp.where(mine, jnp.where(ranks[r] == 1, host[owner] * 2 * MSG, nowhere), guest)
    own = own + part * TOK_REQ + lane % TOK_REQ
    guest = guest + part * TOK_REQ + lane % TOK_REQ
    places[0:1, :] = own
    places[1:2, :] = guest
    target = iota((devices * MSG, 4 * ROWS), 0)
    pick = jnp.where(target[:, : 2 * ROWS] == own[:, : 2 * ROWS], 1.0, 0.0).astype(jnp.bfloat16)
    pick_guest = jnp.where(target == guest, 1.0, 0.0).astype(jnp.bfloat16)
    for copy in copies:
        copy.wait()
    send[:, : WIDE + HD] = dot(pick, held[...], NN).astype(jnp.bfloat16)
    send[:, WIDE + HD :] = dot(pick_guest, held_guest[...], NN).astype(jnp.bfloat16)


def guest_prep_kernel(
    devices, hit_count, hits, prefix_len, span, places, keys, values, *refs
):
    plan, prompt, cached, turned, wide, picks, picks_guest, count, host = refs
    me = lax.axis_index("cache")
    chip = me // 2
    ranks, _ = guest_plan(devices, hits, count, host)
    rows = iota((devices * MSG, 4 * ROWS), 0)
    chosen = jnp.where(rows[:, : 2 * ROWS] == places[0:1, : 2 * ROWS], 1.0, 0.0)
    picks[...] = chosen.T.astype(jnp.bfloat16)
    chosen = jnp.where(rows == places[1:2, :], 1.0, 0.0)
    picks_guest[...] = chosen.T.astype(jnp.bfloat16)
    widen(keys[:REGION, :], values[:REGION, :], turned, wide)
    first, guest, source = jnp.int32(-1), jnp.int32(-1), jnp.int32(0)
    for r in range(REQUESTS):
        owner = hits[r]
        here = (ranks[r] == 1) & (host[owner] == chip)
        first = jnp.where((ranks[r] == 0) & (owner == me), r, first)
        guest = jnp.where(here, r, guest)
        source = jnp.where(here, owner, source)
    core = me % 2
    from_first_core = jnp.where(source == 2 * chip, 1, 0)
    plan[2] = jnp.where(core == 1, (source // 2) ^ chip, 0)
    plan[3] = jnp.where(core == from_first_core, 1, 0)
    for job, found in enumerate((first, guest)):
        request = jnp.maximum(found, 0)
        limit = prefix_len[request]
        strips = jnp.clip((limit + STRIP - 1) // STRIP, 1, REGION // STRIP)
        plan[job] = jnp.where(found >= 0, strips, 0)
        cached[job : job + 1, :] = jnp.where(iota((1, REGION), 1) < limit, 0.0, FLOOR)
        prompt_rows(devices, prompt, span, request, job, True)


def widen(keys, values, turned, wide):
    for n in range(0, REGION, STRIP):
        turned[:, n : n + STRIP] = keys[n : n + STRIP].T
    wide[:, :HD] = values
    wide[:, HD:] = jnp.ones((REGION, HD), jnp.bfloat16)


def host_kernel(devices, hit_count, plan, *refs):
    mine, other, turned, wide = refs[:2], refs[2:4], refs[4], refs[5]
    for choice, (keys, values) in enumerate((mine, other)):

        @pl.when(plan[3] == choice)
        def _():
            widen(keys[...], values[...], turned, wide)


def guest_attend_kernel(
    devices, hit_count, plan, prompt_mask, cached_mask, got, turned, wide, *refs
):
    turned_guest, wide_guest, out = refs
    jobs = [
        (0, 0, HALF, turned, wide),
        (WIDE + HD, WIDE, HALF // 2, turned_guest, wide_guest),
    ]
    for job, (base, first, blocks, keys, values) in enumerate(jobs):
        strips = plan[job]

        @pl.when(strips == 0)
        def _():
            empty = jnp.zeros((devices * MSG, blocks * HD), jnp.bfloat16)
            out[:, first : first + blocks * HD] = empty

        for count in range(1, REGION // STRIP + 1):

            @pl.when(strips == count)
            def _():
                whole = (count - 1) * STRIP
                mask = prompt_mask[job * devices * MSG : (job + 1) * devices * MSG, :]
                attend_rows(
                    got,
                    base,
                    blocks,
                    slice(0, devices * MSG),
                    prompt_parts(got[:, base + blocks * HD : base + (blocks + 1) * HD]),
                    mask,
                    cached_mask[job : job + 1, whole : whole + STRIP],
                    keys[:, :whole] if whole else None,
                    keys[:, whole : whole + STRIP],
                    values[:whole, :] if whole else None,
                    values[whole : whole + STRIP, :],
                    out,
                    first,
                )


def prompt_parts(rows):
    height = rows.shape[0]
    wide = rows.astype(jnp.float32)
    moved = pltpu.roll(wide, height - TOK_REQ, 0).astype(jnp.bfloat16)
    values = jnp.concatenate([moved, jnp.ones((height, HD), jnp.bfloat16)], axis=1)
    return wide.T.astype(jnp.bfloat16), values


def attend_rows(
    got, base, blocks, here, prompt, mask, tail_mask, head, tail, head_values, tail_values, out, first
):
    prompt_keys, prompt_values = prompt
    factor = SCALE * math.log2(math.e)
    mask = jnp.concatenate([mask, mask], axis=0)
    height = mask.shape[0] // 2

    def scores(c):
        pair = jnp.concatenate(
            [got[here, base + (c + n) * HD : base + (c + n + 1) * HD] for n in range(2)], axis=0
        )
        parts = [] if head is None else [dot(pair, head, NN)]
        parts.append(dot(pair, tail, NN) + tail_mask)
        parts.append(dot(pair, prompt_keys, NN) + mask)
        return parts

    parts = scores(0)
    for c in range(0, blocks, 2):
        later = scores(c + 2) if c + 2 < blocks else None
        top = lanes_max(parts)
        parts = [jnp.exp2((x - top) * factor).astype(jnp.bfloat16) for x in parts]
        summed = dot(parts[-1], prompt_values, NN) + dot(parts[-2], tail_values, NN)
        if head is not None:
            summed = summed + dot(parts[0], head_values, NN)
        result = (summed[:, :HD] / summed[:, HD:]).astype(jnp.bfloat16)
        for n in range(2):
            column = first + (c + n) * HD
            out[here, column : column + HD] = result[n * height : (n + 1) * height]
        parts = later


def guest_unpack_kernel(devices, hit_count, picks, picks_guest, outs, result):
    half = WIDE // 2
    own = dot(picks[...], outs[:, :WIDE], NN)
    guest = dot(picks_guest[...], outs[:, WIDE:], NN)
    for g in range(4):
        rows = own[g // 2 * ROWS : (g // 2 + 1) * ROWS, g % 2 * half : (g % 2 + 1) * half]
        rows = rows + guest[g * ROWS : (g + 1) * ROWS]
        result[:, g * half : (g + 1) * half] = rows.astype(jnp.bfloat16)


def unpack_kernel(devices, hit_count, picks, *refs):
    outs, logs, result = refs[0], refs[1:-1], refs[-1]

    def chosen(s, i):
        place = s * hit_count + i
        return picks[place * 2 * ROWS : (place + 1) * 2 * ROWS, :]

    def rows_of(i):
        parts = [
            dot(chosen(s, i), outs[:, s * WIDE : (s + 1) * WIDE], NN)
            for s in range(CAP)
        ]
        return sum(parts[1:], parts[0])

    def logs_of(i):
        parts = [
            dot(
                chosen(s, i).astype(jnp.float32),
                logs[0][:, s * HD : (s + 1) * HD],
                NN,
                precision=lax.Precision.HIGHEST,
            )
            for s in range(CAP)
        ]
        return sum(parts[1:], parts[0])

    if hit_count == 1:
        joined = rows_of(0)
    else:
        levels = [logs_of(i) for i in range(hit_count)]
        top = functools.reduce(jnp.maximum, levels)
        shares = [jnp.exp(level - top) for level in levels]
        total = sum(shares[1:], shares[0])
        pieces = [rows_of(i) for i in range(hit_count)]
        columns = []
        for c in range(HALF):
            part = sum(
                shares[i][:, c : c + 1] * pieces[i][:, c * HD : (c + 1) * HD]
                for i in range(hit_count)
            )
            columns.append(part / total[:, c : c + 1])
        joined = jnp.concatenate(columns, axis=1)
    joined = joined.astype(jnp.bfloat16)
    result[:, :WIDE] = joined[:ROWS]
    result[:, WIDE:] = joined[ROWS:]


def vmem(count):
    return [pl.BlockSpec(memory_space=pltpu.VMEM)] * count


def smem(count):
    return [pl.BlockSpec(memory_space=pltpu.SMEM)] * count


def hbm(count):
    return [pl.BlockSpec(memory_space=pltpu.HBM)] * count


def body(prefix_len, hits, span_block, queries, fresh_keys, fresh_values, cache_keys, cache_values):
    devices = lax.axis_size("cache")
    hit_count = hits.shape[1]
    rows = devices * MSG
    owners = hits.reshape(REQUESTS * hit_count)
    fresh = (owners, queries, fresh_keys, fresh_values)

    def exchange(x):
        return lax.all_to_all(x, "cache", split_axis=0, concat_axis=0, tiled=True)

    def call(kernel, out_shape, name, grant=40, **kw):
        return pl.pallas_call(
            functools.partial(kernel, devices, hit_count),
            out_shape=[jax.ShapeDtypeStruct(*leaf) for leaf in out_shape],
            compiler_params=pltpu.CompilerParams(vmem_limit_bytes=grant * 2**20),
            name=name,
            **kw,
        )

    if hit_count == 1 and devices == 16:
        pairs = rows * (HALF + HALF // 2) * (REGION + rows)
        scalars = [pltpu.SMEM((devices,), jnp.int32)] * 2
        send, places, way = call(
            guest_pack_kernel,
            [
                ((rows, GUEST_MSG), jnp.bfloat16),
                ((2, 4 * ROWS), jnp.int32),
                ((1,), jnp.int32),
            ],
            "pack",
            in_specs=hbm(4),
            out_specs=vmem(2) + smem(1),
            scratch_shapes=[
                pltpu.VMEM((2 * ROWS, WIDE + HD), jnp.bfloat16),
                pltpu.VMEM((4 * ROWS, WIDE // 2 + HD), jnp.bfloat16),
                pltpu.SMEM((REQUESTS,), jnp.int32),
                *scalars,
                pltpu.SemaphoreType.DMA((13,)),
            ],
        )(*(pltpu.with_memory_space_constraint(x, pltpu.HBM) for x in fresh))
        got = exchange(send)
        shapes = [((HD, REGION), jnp.bfloat16), ((REGION, 2 * HD), jnp.bfloat16)]
        def chain(ways, owners, prefix_len, span_block, places, cache_keys, cache_values):
            slots = [cache_keys[REGION:], cache_values[REGION:]]
            lent = [
                [
                    lax.ppermute(x, "cache", [(d, d ^ (2 * n)) for d in range(1, devices, 2)])
                    for x in slots
                ]
                for n in ways
            ]
            prepared = call(
                guest_prep_kernel,
                [((4,), jnp.int32), ((2 * rows, rows), jnp.float32), ((2, REGION), jnp.float32)]
                + shapes
                + [((2 * ROWS, rows), jnp.bfloat16), ((4 * ROWS, rows), jnp.bfloat16)],
                "prep",
                in_specs=smem(2) + vmem(4),
                out_specs=smem(1) + vmem(6),
                scratch_shapes=scalars,
                cost_estimate=pl.CostEstimate(
                    flops=10**6, bytes_accessed=2**22, transcendentals=0
                ),
            )(owners, prefix_len, span_block, places, cache_keys, cache_values)
            plan = prepared[0]
            for n, borrowed in zip(ways, lent):
                slots = [jnp.where(plan[2] == n, x, y) for x, y in zip(borrowed, slots)]
            swapped = [lax.ppermute(x, "cache", [(d, d ^ 1) for d in range(devices)]) for x in slots]
            guest = call(
                host_kernel, shapes, "host", in_specs=smem(1) + vmem(4), out_specs=vmem(2)
            )(plan, *slots, *swapped)
            return (*prepared, *guest)

        prepared = lax.switch(
            way.reshape(()),
            [functools.partial(chain, ways) for ways in ((), (1,), (2,), (1, 2, 3))],
            owners,
            prefix_len,
            span_block,
            places,
            cache_keys,
            cache_values,
        )
        plan, prompt_mask, cached_mask, turned, wide, picks, picks_guest = prepared[:7]
        turned_guest, wide_guest = prepared[7:]
        (answer,) = call(
            guest_attend_kernel,
            [((rows, WIDE + WIDE // 2), jnp.bfloat16)],
            "attend",
            in_specs=smem(1) + vmem(7),
            out_specs=vmem(1),
            cost_estimate=pl.CostEstimate(
                flops=4 * pairs * HD, bytes_accessed=8 * rows * WIDE, transcendentals=pairs
            ),
        )(plan, prompt_mask, cached_mask, got, turned, wide, turned_guest, wide_guest)
        return call(
            guest_unpack_kernel,
            [((ROWS, HEADS * HD), jnp.bfloat16)],
            "unpack",
            in_specs=vmem(3),
            out_specs=vmem(1),
        )(picks, picks_guest, exchange(answer))[0]
    send, places = call(
        pack_kernel,
        [((rows, CAP * (WIDE + HD)), jnp.bfloat16), ((CAP * hit_count, 2 * ROWS), jnp.int32)],
        "pack",
        in_specs=hbm(4),
        out_specs=vmem(2),
        scratch_shapes=[
            pltpu.VMEM((2 * ROWS, WIDE + HD), jnp.bfloat16),
            pltpu.SMEM((REQUESTS * hit_count,), jnp.int32),
            pltpu.SMEM((devices,), jnp.int32),
            pltpu.SemaphoreType.DMA((5,)),
        ],
    )(*(pltpu.with_memory_space_constraint(x, pltpu.HBM) for x in fresh))
    got = exchange(send)
    busy, prompt_mask, cached_mask, turned, wide, picks = call(
        prep_kernel,
        [
            ((CAP,), jnp.int32),
            ((CAP * rows, rows), jnp.float32),
            ((CAP, REGION), jnp.float32),
            ((HD, CAP * REGION), jnp.bfloat16),
            ((CAP * REGION, 2 * HD), jnp.bfloat16),
            ((CAP * hit_count * 2 * ROWS, rows), jnp.bfloat16),
        ],
        "prep",
        in_specs=smem(2) + vmem(4),
        out_specs=smem(1) + vmem(5),
        cost_estimate=pl.CostEstimate(flops=10**6, bytes_accessed=2**22, transcendentals=0),
    )(owners, prefix_len, span_block, places, cache_keys, cache_values)
    pairs = CAP * rows * HALF * (REGION + rows)
    answers = call(
        attend_kernel,
        [((rows, CAP * WIDE), jnp.bfloat16)]
        + [((rows, CAP * HD), jnp.float32)] * (hit_count > 1),
        "attend",
        in_specs=smem(1) + vmem(5),
        out_specs=vmem(1 + (hit_count > 1)),
        cost_estimate=pl.CostEstimate(
            flops=4 * pairs * HD, bytes_accessed=8 * rows * WIDE, transcendentals=pairs
        ),
    )(busy, prompt_mask, cached_mask, got, turned, wide)
    returned = [exchange(answer) for answer in answers]
    return call(
        unpack_kernel,
        [((ROWS, HEADS * HD), jnp.bfloat16)],
        "unpack",
        in_specs=vmem(1 + len(returned)),
        out_specs=vmem(1),
    )(picks, *returned)[0]


def solution(mesh):
    in_specs = (
        P("groups"),
        P("groups", None),
        P("groups", None),
        P(("groups", "cache"), None),
        P(("groups", "cache"), None),
        P(("groups", "cache"), None),
        P(("groups", "cache"), None),
        P(("groups", "cache"), None),
    )
    out_specs = P(("groups", "cache"), None)
    return jax.shard_map(body, mesh=mesh, in_specs=in_specs, out_specs=out_specs, check_vma=False)
```

```python
import functools
import math

import jax
import jax.numpy as jnp
from jax import lax
from jax.experimental import pallas as pl
from jax.experimental.pallas import tpu as pltpu
from jax.sharding import PartitionSpec as P

HEADS = 16
HD = 128
PAGE = 128
CAP = 2
REQUESTS = 16
TOK_REQ = 4
PAGES_DEV = 16

REGION = PAGES_DEV // CAP * PAGE
HALF = HEADS // 2
MSG = 2 * TOK_REQ
WIDE = HALF * HD
ROWS = REQUESTS * TOK_REQ
STRIP = 256
GUEST_MSG = WIDE + HD + WIDE // 2 + HD
SCALE = HD**-0.5
FLOOR = -1e30
NN = (((1,), (0,)), ((), ()))


def iota(shape, axis):
    return lax.broadcasted_iota(jnp.int32, shape, axis)


def dot(a, b, dims, **kw):
    return lax.dot_general(a, b, dims, preferred_element_type=jnp.float32, **kw)


def pack_kernel(devices, hit_count, owners, q, k, v, send, places, held, hits, count, sems):
    copies = [
        pltpu.make_async_copy(source, held.at[pl.ds(row, ROWS), pl.ds(column, width)], sems.at[n])
        for n, (source, row, column, width) in enumerate(
            [
                (q.at[:, pl.ds(0, WIDE)], 0, 0, WIDE),
                (q.at[:, pl.ds(WIDE, WIDE)], ROWS, 0, WIDE),
                (k, 0, WIDE, HD),
                (v, ROWS, WIDE, HD),
            ]
        )
    ]
    first = pltpu.make_async_copy(owners, hits, sems.at[4])
    first.start()
    for copy in copies:
        copy.start()
    lane = iota((1, 2 * ROWS), 1)
    lane_request = (lane % ROWS) // TOK_REQ
    first.wait()
    for r in range(REQUESTS):
        for i in range(hit_count):
            count[hits[r * hit_count + i]] = 0
    rows = [[jnp.full((1, 2 * ROWS), -4 * MSG, jnp.int32)] * hit_count for _ in range(CAP)]
    for r in range(REQUESTS):
        for i in range(hit_count):
            owner = hits[r * hit_count + i]
            rank = count[owner]
            count[owner] = rank + 1
            for s in range(CAP):
                place = jnp.where(rank == s, owner * MSG, -4 * MSG)
                rows[s][i] = jnp.where(lane_request == r, place, rows[s][i])
    inner = lane // ROWS * TOK_REQ + lane % TOK_REQ
    target = iota((devices * MSG, 2 * ROWS), 0)
    picks = []
    for s in range(CAP):
        chosen = None
        for i in range(hit_count):
            row = rows[s][i] + inner
            places[s * hit_count + i : s * hit_count + i + 1, :] = row
            hit = target == row
            chosen = hit if chosen is None else chosen | hit
        picks.append(jnp.where(chosen, 1.0, 0.0).astype(jnp.bfloat16))
    for copy in copies:
        copy.wait()
    packed = dot(jnp.concatenate(picks, axis=0), held[...], NN).astype(jnp.bfloat16)
    for s in range(CAP):
        rows = slice(s * devices * MSG, (s + 1) * devices * MSG)
        send[:, s * (WIDE + HD) : (s + 1) * (WIDE + HD)] = packed[rows]


def prep_kernel(
    devices, hit_count, hits, prefix_len, span, places, keys, values, *outs
):
    busy, prompt, cached, turned, wide, picks = outs
    rows = iota((devices * MSG, 2 * ROWS), 0)
    for n in range(CAP * hit_count):
        chosen = jnp.where(rows == places[n : n + 1, :], 1.0, 0.0)
        picks[n * 2 * ROWS : (n + 1) * 2 * ROWS, :] = chosen.T.astype(jnp.bfloat16)
    for n in range(0, CAP * REGION, STRIP):
        turned[:, n : n + STRIP] = keys[n : n + STRIP, :].T
    me = lax.axis_index("cache")
    wide[:, :HD] = values[...]
    wide[:, HD:] = jnp.ones((CAP * REGION, HD), jnp.bfloat16)
    for slot in range(CAP):
        seen = jnp.int32(0)
        request = jnp.int32(0)
        which = jnp.int32(0)
        for r in range(REQUESTS):
            for i in range(hit_count):
                mine = hits[r * hit_count + i] == me
                here = mine & (seen == slot)
                request = jnp.where(here, r, request)
                which = jnp.where(here, i, which)
                seen = seen + mine.astype(jnp.int32)
        limit = prefix_len[request] - which * REGION
        blocks = jnp.clip((limit + STRIP - 1) // STRIP, 1, REGION // STRIP)
        busy[slot] = jnp.where(seen > slot, blocks, 0)
        cached[slot : slot + 1, :] = jnp.where(iota((1, REGION), 1) < limit, 0.0, FLOOR)
        prompt_rows(devices, prompt, span, request, slot, hit_count == 1 or which == 0)


def prompt_rows(devices, prompt, span, request, slot, counted):
    total_rows = devices * MSG
    span_row = span[pl.ds(request, 1), :].astype(jnp.float32)
    source = iota((devices, total_rows), 0)
    spread = (iota((devices, total_rows), 1) // MSG == source).astype(jnp.bfloat16)
    spans = jnp.broadcast_to(span_row, (16, devices)).astype(jnp.bfloat16)
    key_span = dot(spans, spread, NN)[:1]
    lane = iota((1, total_rows), 1)
    key_spot = key_span.astype(jnp.int32) * TOK_REQ + lane % TOK_REQ
    is_key = (lane % MSG < TOK_REQ) & counted
    key_spot = jnp.where(is_key, key_spot, devices * TOK_REQ)
    block = 16 * MSG

    def one_block(at):
        row_source = at * 16 + iota((block, devices), 0) // MSG
        mine = iota((block, devices), 1) == row_source
        row_span = jnp.sum(jnp.where(mine, span_row, 0.0), axis=1, keepdims=True)
        row_spot = row_span.astype(jnp.int32) * TOK_REQ + iota((block, 1), 0) % TOK_REQ
        here = pl.ds(slot * total_rows + at * block, block)
        prompt[here, :] = jnp.where(key_spot <= row_spot, 0.0, FLOOR)

    each_block(devices, one_block)


def each_block(devices, one_block):
    blocks = devices // 16
    if blocks == 1:
        one_block(0)
    else:
        pl.loop(0, blocks)(one_block)


def lanes_max(parts):
    pieces = [part[:, n : n + HD] for part in parts for n in range(0, part.shape[1], HD)]
    return jnp.max(functools.reduce(jnp.maximum, pieces), axis=1, keepdims=True)


def attend_kernel(
    devices, hit_count, busy, prompt_mask, cached_mask, got, turned, wide, out, *levels
):
    total_rows = devices * MSG
    block = 16 * MSG
    factor = SCALE * math.log2(math.e)

    def nothing(slot):
        out[:, pl.ds(slot * WIDE, WIDE)] = jnp.zeros((total_rows, WIDE), jnp.bfloat16)
        for lse in levels:
            lse[:, pl.ds(slot * HD, HD)] = jnp.zeros((total_rows, HD), jnp.float32)

    def attend(slot, strips):
        whole = (strips - 1) * STRIP
        base = pl.multiple_of(slot * (WIDE + HD), HD)
        region = pl.multiple_of(slot * REGION, REGION)
        head = pl.ds(region, whole) if whole else None
        tail = pl.ds(pl.multiple_of(region + whole, STRIP), STRIP)
        tail_mask = cached_mask[pl.ds(slot, 1), whole : whole + STRIP]
        prompt_keys = got[:, pl.ds(base + WIDE, HD)].astype(jnp.float32)
        moved = pltpu.roll(prompt_keys, total_rows - TOK_REQ, 0)
        prompt_keys = prompt_keys.T.astype(jnp.bfloat16)
        prompt_values = jnp.concatenate(
            [moved.astype(jnp.bfloat16), jnp.ones((total_rows, HD), jnp.bfloat16)], axis=1
        )

        def one_block(at):
            here = pl.ds(at * block, block)
            prompt_bias = prompt_mask[pl.ds(slot * total_rows + at * block, block), :]
            prompt_bias = jnp.concatenate([prompt_bias, prompt_bias], axis=0)
            lane = iota((block, HD), 1)

            def scores(c):
                pair = jnp.concatenate(
                    [got[here, pl.ds(base + (c + n) * HD, HD)] for n in range(2)], axis=0
                )
                parts = [dot(pair, turned[:, head], NN)] if whole else []
                parts.append(dot(pair, turned[:, tail], NN) + tail_mask)
                parts.append(dot(pair, prompt_keys, NN) + prompt_bias)
                return parts

            logs = jnp.zeros((block, HD), jnp.float32)
            parts = scores(0)
            for c in range(0, HALF, 2):
                later = scores(c + 2) if c + 2 < HALF else None
                top = lanes_max(parts)
                if hit_count > 1:
                    top = jnp.maximum(top, 0.1 * FLOOR)
                parts = [jnp.exp2((x - top) * factor).astype(jnp.bfloat16) for x in parts]
                summed = dot(parts[-1], prompt_values, NN) + dot(parts[-2], wide[tail, :], NN)
                if whole:
                    summed = summed + dot(parts[0], wide[head, :], NN)
                totals = summed[:, HD:]
                if hit_count > 1:
                    totals = jnp.maximum(totals, 1.0)
                    level = top * SCALE + jnp.log(totals)
                    logs = jnp.where(lane == c, level[:block], logs)
                    logs = jnp.where(lane == c + 1, level[block:], logs)
                result = (summed[:, :HD] / totals).astype(jnp.bfloat16)
                for n in range(2):
                    column = pl.multiple_of(slot * WIDE + (c + n) * HD, HD)
                    out[here, pl.ds(column, HD)] = result[n * block : (n + 1) * block]
                parts = later
            for lse in levels:
                lse[here, pl.ds(pl.multiple_of(slot * HD, HD), HD)] = logs

        each_block(devices, one_block)

    @pl.loop(0, CAP)
    def _(slot):
        strips = busy[slot]
        pl.when(strips == 0)(lambda: nothing(slot))
        for count in range(1, REGION // STRIP + 1):
            pl.when(strips == count)(functools.partial(attend, slot, count))


def guest_plan(devices, owners, count, host):
    chips = devices // 2
    for d in range(devices):
        count[d] = 0
    ranks = []
    for r in range(REQUESTS):
        owner = owners[r]
        ranks.append(count[owner])
        count[owner] = ranks[r] + 1
    seconds = [count[d] > 1 for d in range(devices)]
    none = [jnp.logical_not(seconds[2 * x] | seconds[2 * x + 1]) for x in range(chips)]
    lends = []
    for x in range(chips):
        other = jnp.where(none[x ^ 1], 1, jnp.where(none[x ^ 2], 2, 3))
        lends.append(jnp.where(seconds[2 * x] & seconds[2 * x + 1], other, 0))
        host[2 * x] = jnp.int32(x)
        host[2 * x + 1] = lends[x] ^ x
    return ranks, lends


def guest_pack_kernel(
    devices, hit_count, owners, q, k, v, send, places, way, held, held_guest, hits, *scalars
):
    count, host, sems = scalars
    half = WIDE // 2
    moves = [
        (q.at[:, pl.ds(0, WIDE)], held.at[pl.ds(0, ROWS), pl.ds(0, WIDE)]),
        (q.at[:, pl.ds(WIDE, WIDE)], held.at[pl.ds(ROWS, ROWS), pl.ds(0, WIDE)]),
        (k, held.at[pl.ds(0, ROWS), pl.ds(WIDE, HD)]),
        (v, held.at[pl.ds(ROWS, ROWS), pl.ds(WIDE, HD)]),
    ]
    for g in range(4):
        here = pl.ds(g * ROWS, ROWS)
        moves.append((q.at[:, pl.ds(g * half, half)], held_guest.at[here, pl.ds(0, half)]))
        moves.append((v if g % 2 else k, held_guest.at[here, pl.ds(half, HD)]))
    first = pltpu.make_async_copy(owners, hits, sems.at[len(moves)])
    first.start()
    copies = [pltpu.make_async_copy(a, b, sems.at[n]) for n, (a, b) in enumerate(moves)]
    for copy in copies:
        copy.start()
    first.wait()
    ranks, lends = guest_plan(devices, hits, count, host)
    used = [
        functools.reduce(jnp.logical_or, [lend == n for lend in lends]) for n in range(1, 4)
    ]
    mixed = used[2] | (used[0] & used[1])
    way[0] = jnp.where(mixed, 3, jnp.where(used[0], 1, jnp.where(used[1], 2, 0)))
    lane = iota((1, 4 * ROWS), 1)
    lane_request = lane % ROWS // TOK_REQ
    part = lane // ROWS
    nowhere = -4 * MSG
    own = jnp.full((1, 4 * ROWS), nowhere, jnp.int32)
    guest = own
    for r in range(REQUESTS):
        owner = hits[r]
        mine = lane_request == r
        own = jnp.where(mine, jnp.where(ranks[r] == 0, owner * MSG, nowhere), own)
        guest = jnp.where(mine, jnp.where(ranks[r] == 1, host[owner] * 2 * MSG, nowhere), guest)
    own = own + part * TOK_REQ + lane % TOK_REQ
    guest = guest + part * TOK_REQ + lane % TOK_REQ
    places[0:1, :] = own
    places[1:2, :] = guest
    target = iota((devices * MSG, 4 * ROWS), 0)
    pick = jnp.where(target[:, : 2 * ROWS] == own[:, : 2 * ROWS], 1.0, 0.0).astype(jnp.bfloat16)
    pick_guest = jnp.where(target == guest, 1.0, 0.0).astype(jnp.bfloat16)
    for copy in copies:
        copy.wait()
    send[:, : WIDE + HD] = dot(pick, held[...], NN).astype(jnp.bfloat16)
    send[:, WIDE + HD :] = dot(pick_guest, held_guest[...], NN).astype(jnp.bfloat16)


def guest_prep_kernel(
    devices, hit_count, hits, prefix_len, span, places, keys, values, *refs
):
    plan, prompt, cached, turned, wide, picks, picks_guest, strips_of, count, host = refs
    me = lax.axis_index("cache")
    chip = me // 2
    ranks, _ = guest_plan(devices, hits, count, host)
    rows = iota((devices * MSG, 4 * ROWS), 0)
    chosen = jnp.where(rows[:, : 2 * ROWS] == places[0:1, : 2 * ROWS], 1.0, 0.0)
    picks[...] = chosen.T.astype(jnp.bfloat16)
    chosen = jnp.where(rows == places[1:2, :], 1.0, 0.0)
    picks_guest[...] = chosen.T.astype(jnp.bfloat16)
    widen(keys[:REGION, :], values[:REGION, :], turned, wide)
    first, guest, source = jnp.int32(-1), jnp.int32(-1), jnp.int32(0)
    for r in range(REQUESTS):
        owner = hits[r]
        here = (ranks[r] == 1) & (host[owner] == chip)
        first = jnp.where((ranks[r] == 0) & (owner == me), r, first)
        guest = jnp.where(here, r, guest)
        source = jnp.where(here, owner, source)
    core = me % 2
    from_first_core = jnp.where(source == 2 * chip, 1, 0)
    plan[0] = jnp.where(core == 1, (source // 2) ^ chip, 0)
    plan[1] = jnp.where(core == from_first_core, 1, 0)
    for job, found in enumerate((first, guest)):
        request = jnp.maximum(found, 0)
        limit = prefix_len[request]
        strips = jnp.clip((limit + STRIP - 1) // STRIP, 1, REGION // STRIP)
        strips_of[job : job + 1, :] = jnp.full((1, HD), jnp.where(found >= 0, strips, 0))
        cached[job : job + 1, :] = jnp.where(iota((1, REGION), 1) < limit, 0.0, FLOOR)
        prompt_rows(devices, prompt, span, request, job, True)


def widen(keys, values, turned, wide):
    for n in range(0, REGION, STRIP):
        turned[:, n : n + STRIP] = keys[n : n + STRIP].T
    wide[:, :HD] = values
    wide[:, HD:] = jnp.ones((REGION, HD), jnp.bfloat16)


def host_kernel(devices, hit_count, plan, *refs):
    mine, other, turned, wide = refs[:2], refs[2:4], refs[4], refs[5]
    for choice, (keys, values) in enumerate((mine, other)):

        @pl.when(plan[1] == choice)
        def _():
            widen(keys[...], values[...], turned, wide)


def guest_attend_kernel(
    devices, hit_count, strips_of, prompt_mask, cached_mask, got, turned, wide, *refs
):
    turned_guest, wide_guest, out = refs
    jobs = [
        (0, 0, HALF, turned, wide),
        (WIDE + HD, WIDE, HALF // 2, turned_guest, wide_guest),
    ]
    for job, (base, first, blocks, keys, values) in enumerate(jobs):
        strips = strips_of[job, 0]

        @pl.when(strips == 0)
        def _():
            empty = jnp.zeros((devices * MSG, blocks * HD), jnp.bfloat16)
            out[:, first : first + blocks * HD] = empty

        for count in range(1, REGION // STRIP + 1):

            @pl.when(strips == count)
            def _():
                whole = (count - 1) * STRIP
                mask = prompt_mask[job * devices * MSG : (job + 1) * devices * MSG, :]
                attend_rows(
                    got,
                    base,
                    blocks,
                    slice(0, devices * MSG),
                    prompt_parts(got[:, base + blocks * HD : base + (blocks + 1) * HD]),
                    mask,
                    cached_mask[job : job + 1, whole : whole + STRIP],
                    keys[:, :whole] if whole else None,
                    keys[:, whole : whole + STRIP],
                    values[:whole, :] if whole else None,
                    values[whole : whole + STRIP, :],
                    out,
                    first,
                )


def prompt_parts(rows):
    height = rows.shape[0]
    wide = rows.astype(jnp.float32)
    moved = pltpu.roll(wide, height - TOK_REQ, 0).astype(jnp.bfloat16)
    values = jnp.concatenate([moved, jnp.ones((height, HD), jnp.bfloat16)], axis=1)
    return wide.T.astype(jnp.bfloat16), values


def attend_rows(
    got, base, blocks, here, prompt, mask, tail_mask, head, tail, head_values, tail_values, out, first
):
    prompt_keys, prompt_values = prompt
    factor = SCALE * math.log2(math.e)
    mask = jnp.concatenate([mask, mask], axis=0)
    height = mask.shape[0] // 2

    def scores(c):
        pair = jnp.concatenate(
            [got[here, base + (c + n) * HD : base + (c + n + 1) * HD] for n in range(2)], axis=0
        )
        parts = [] if head is None else [dot(pair, head, NN)]
        parts.append(dot(pair, tail, NN) + tail_mask)
        parts.append(dot(pair, prompt_keys, NN) + mask)
        return parts

    parts = scores(0)
    for c in range(0, blocks, 2):
        later = scores(c + 2) if c + 2 < blocks else None
        top = lanes_max(parts)
        parts = [jnp.exp2((x - top) * factor).astype(jnp.bfloat16) for x in parts]
        summed = dot(parts[-1], prompt_values, NN) + dot(parts[-2], tail_values, NN)
        if head is not None:
            summed = summed + dot(parts[0], head_values, NN)
        result = (summed[:, :HD] / summed[:, HD:]).astype(jnp.bfloat16)
        for n in range(2):
            column = first + (c + n) * HD
            out[here, column : column + HD] = result[n * height : (n + 1) * height]
        parts = later


def guest_unpack_kernel(devices, hit_count, picks, picks_guest, outs, result):
    half = WIDE // 2
    own = dot(picks[...], outs[:, :WIDE], NN)
    guest = dot(picks_guest[...], outs[:, WIDE:], NN)
    for g in range(4):
        rows = own[g // 2 * ROWS : (g // 2 + 1) * ROWS, g % 2 * half : (g % 2 + 1) * half]
        rows = rows + guest[g * ROWS : (g + 1) * ROWS]
        result[:, g * half : (g + 1) * half] = rows.astype(jnp.bfloat16)


def unpack_kernel(devices, hit_count, picks, *refs):
    outs, logs, result = refs[0], refs[1:-1], refs[-1]

    def chosen(s, i):
        place = s * hit_count + i
        return picks[place * 2 * ROWS : (place + 1) * 2 * ROWS, :]

    def rows_of(i):
        parts = [
            dot(chosen(s, i), outs[:, s * WIDE : (s + 1) * WIDE], NN)
            for s in range(CAP)
        ]
        return sum(parts[1:], parts[0])

    def logs_of(i):
        parts = [
            dot(
                chosen(s, i).astype(jnp.float32),
                logs[0][:, s * HD : (s + 1) * HD],
                NN,
                precision=lax.Precision.HIGHEST,
            )
            for s in range(CAP)
        ]
        return sum(parts[1:], parts[0])

    if hit_count == 1:
        joined = rows_of(0)
    else:
        levels = [logs_of(i) for i in range(hit_count)]
        top = functools.reduce(jnp.maximum, levels)
        shares = [jnp.exp(level - top) for level in levels]
        total = sum(shares[1:], shares[0])
        pieces = [rows_of(i) for i in range(hit_count)]
        columns = []
        for c in range(HALF):
            part = sum(
                shares[i][:, c : c + 1] * pieces[i][:, c * HD : (c + 1) * HD]
                for i in range(hit_count)
            )
            columns.append(part / total[:, c : c + 1])
        joined = jnp.concatenate(columns, axis=1)
    joined = joined.astype(jnp.bfloat16)
    result[:, :WIDE] = joined[:ROWS]
    result[:, WIDE:] = joined[ROWS:]


def vmem(count):
    return [pl.BlockSpec(memory_space=pltpu.VMEM)] * count


def smem(count):
    return [pl.BlockSpec(memory_space=pltpu.SMEM)] * count


def hbm(count):
    return [pl.BlockSpec(memory_space=pltpu.HBM)] * count


def body(prefix_len, hits, span_block, queries, fresh_keys, fresh_values, cache_keys, cache_values):
    devices = lax.axis_size("cache")
    hit_count = hits.shape[1]
    rows = devices * MSG
    owners = hits.reshape(REQUESTS * hit_count)
    fresh = (owners, queries, fresh_keys, fresh_values)

    def exchange(x):
        return lax.all_to_all(x, "cache", split_axis=0, concat_axis=0, tiled=True)

    def call(kernel, out_shape, name, grant=40, **kw):
        return pl.pallas_call(
            functools.partial(kernel, devices, hit_count),
            out_shape=[jax.ShapeDtypeStruct(*leaf) for leaf in out_shape],
            compiler_params=pltpu.CompilerParams(vmem_limit_bytes=grant * 2**20),
            name=name,
            **kw,
        )

    if hit_count == 1 and devices == 16:
        pairs = rows * (HALF + HALF // 2) * (REGION + rows)
        scalars = [pltpu.SMEM((devices,), jnp.int32)] * 2
        send, places, way = call(
            guest_pack_kernel,
            [
                ((rows, GUEST_MSG), jnp.bfloat16),
                ((2, 4 * ROWS), jnp.int32),
                ((1,), jnp.int32),
            ],
            "pack",
            in_specs=hbm(4),
            out_specs=vmem(2) + smem(1),
            scratch_shapes=[
                pltpu.VMEM((2 * ROWS, WIDE + HD), jnp.bfloat16),
                pltpu.VMEM((4 * ROWS, WIDE // 2 + HD), jnp.bfloat16),
                pltpu.SMEM((REQUESTS,), jnp.int32),
                *scalars,
                pltpu.SemaphoreType.DMA((13,)),
            ],
        )(*(pltpu.with_memory_space_constraint(x, pltpu.HBM) for x in fresh))
        got = exchange(send)
        shapes = [((HD, REGION), jnp.bfloat16), ((REGION, 2 * HD), jnp.bfloat16)]
        def chain(ways, owners, prefix_len, span_block, places, cache_keys, cache_values):
            pinned = [
                pltpu.with_memory_space_constraint(x, pltpu.HBM)
                for x in (owners, prefix_len, span_block)
            ]
            slots = [cache_keys[REGION:], cache_values[REGION:]]
            lent = [
                [
                    lax.ppermute(x, "cache", [(d, d ^ (2 * n)) for d in range(1, devices, 2)])
                    for x in slots
                ]
                for n in ways
            ]
            prepared = call(
                guest_prep_kernel,
                [((2,), jnp.int32), ((2 * rows, rows), jnp.float32), ((2, REGION), jnp.float32)]
                + shapes
                + [((2 * ROWS, rows), jnp.bfloat16), ((4 * ROWS, rows), jnp.bfloat16)]
                + [((8, HD), jnp.int32)],
                "prep",
                in_specs=smem(2) + vmem(4),
                out_specs=smem(1) + vmem(7),
                scratch_shapes=scalars,
                cost_estimate=pl.CostEstimate(
                    flops=10**6, bytes_accessed=2**22, transcendentals=0
                ),
            )(*pinned, places, cache_keys, cache_values)
            plan = prepared[0]
            for n, borrowed in zip(ways, lent):
                slots = [jnp.where(plan[0] == n, x, y) for x, y in zip(borrowed, slots)]
            swapped = [lax.ppermute(x, "cache", [(d, d ^ 1) for d in range(devices)]) for x in slots]
            guest = call(
                host_kernel, shapes, "host", in_specs=smem(1) + vmem(4), out_specs=vmem(2)
            )(plan, *slots, *swapped)
            return (*prepared[1:], *guest)

        prepared = lax.switch(
            way.reshape(()),
            [functools.partial(chain, ways) for ways in ((), (1,), (2,), (1, 2, 3))],
            owners,
            prefix_len,
            span_block,
            places,
            cache_keys,
            cache_values,
        )
        prompt_mask, cached_mask, turned, wide, picks, picks_guest, strips_of = prepared[:7]
        turned_guest, wide_guest = prepared[7:]
        (answer,) = call(
            guest_attend_kernel,
            [((rows, WIDE + WIDE // 2), jnp.bfloat16)],
            "attend",
            in_specs=vmem(8),
            out_specs=vmem(1),
            cost_estimate=pl.CostEstimate(
                flops=4 * pairs * HD, bytes_accessed=8 * rows * WIDE, transcendentals=pairs
            ),
        )(strips_of, prompt_mask, cached_mask, got, turned, wide, turned_guest, wide_guest)
        return call(
            guest_unpack_kernel,
            [((ROWS, HEADS * HD), jnp.bfloat16)],
            "unpack",
            in_specs=vmem(3),
            out_specs=vmem(1),
        )(picks, picks_guest, exchange(answer))[0]
    send, places = call(
        pack_kernel,
        [((rows, CAP * (WIDE + HD)), jnp.bfloat16), ((CAP * hit_count, 2 * ROWS), jnp.int32)],
        "pack",
        in_specs=hbm(4),
        out_specs=vmem(2),
        scratch_shapes=[
            pltpu.VMEM((2 * ROWS, WIDE + HD), jnp.bfloat16),
            pltpu.SMEM((REQUESTS * hit_count,), jnp.int32),
            pltpu.SMEM((devices,), jnp.int32),
            pltpu.SemaphoreType.DMA((5,)),
        ],
    )(*(pltpu.with_memory_space_constraint(x, pltpu.HBM) for x in fresh))
    got = exchange(send)
    busy, prompt_mask, cached_mask, turned, wide, picks = call(
        prep_kernel,
        [
            ((CAP,), jnp.int32),
            ((CAP * rows, rows), jnp.float32),
            ((CAP, REGION), jnp.float32),
            ((HD, CAP * REGION), jnp.bfloat16),
            ((CAP * REGION, 2 * HD), jnp.bfloat16),
            ((CAP * hit_count * 2 * ROWS, rows), jnp.bfloat16),
        ],
        "prep",
        in_specs=smem(2) + vmem(4),
        out_specs=smem(1) + vmem(5),
        cost_estimate=pl.CostEstimate(flops=10**6, bytes_accessed=2**22, transcendentals=0),
    )(owners, prefix_len, span_block, places, cache_keys, cache_values)
    pairs = CAP * rows * HALF * (REGION + rows)
    answers = call(
        attend_kernel,
        [((rows, CAP * WIDE), jnp.bfloat16)]
        + [((rows, CAP * HD), jnp.float32)] * (hit_count > 1),
        "attend",
        in_specs=smem(1) + vmem(5),
        out_specs=vmem(1 + (hit_count > 1)),
        cost_estimate=pl.CostEstimate(
            flops=4 * pairs * HD, bytes_accessed=8 * rows * WIDE, transcendentals=pairs
        ),
    )(busy, prompt_mask, cached_mask, got, turned, wide)
    returned = [exchange(answer) for answer in answers]
    return call(
        unpack_kernel,
        [((ROWS, HEADS * HD), jnp.bfloat16)],
        "unpack",
        in_specs=vmem(1 + len(returned)),
        out_specs=vmem(1),
    )(picks, *returned)[0]


def solution(mesh):
    in_specs = (
        P("groups"),
        P("groups", None),
        P("groups", None),
        P(("groups", "cache"), None),
        P(("groups", "cache"), None),
        P(("groups", "cache"), None),
        P(("groups", "cache"), None),
        P(("groups", "cache"), None),
    )
    out_specs = P(("groups", "cache"), None)
    return jax.shard_map(body, mesh=mesh, in_specs=in_specs, out_specs=out_specs, check_vma=False)
```

```python
import functools
import math

import jax
import jax.numpy as jnp
from jax import lax
from jax.experimental import pallas as pl
from jax.experimental.pallas import tpu as pltpu
from jax.sharding import PartitionSpec as P

HEADS = 16
HD = 128
PAGE = 128
CAP = 2
REQUESTS = 16
TOK_REQ = 4
PAGES_DEV = 16

REGION = PAGES_DEV // CAP * PAGE
HALF = HEADS // 2
MSG = 2 * TOK_REQ
WIDE = HALF * HD
ROWS = REQUESTS * TOK_REQ
STRIP = 256
GUEST_MSG = WIDE + HD + WIDE // 2 + HD
SCALE = HD**-0.5
FLOOR = -1e30
NN = (((1,), (0,)), ((), ()))


def iota(shape, axis):
    return lax.broadcasted_iota(jnp.int32, shape, axis)


def dot(a, b, dims, **kw):
    return lax.dot_general(a, b, dims, preferred_element_type=jnp.float32, **kw)


def pack_kernel(devices, hit_count, owners, q, k, v, send, places, held, hits, count, sems):
    copies = [
        pltpu.make_async_copy(source, held.at[pl.ds(row, ROWS), pl.ds(column, width)], sems.at[n])
        for n, (source, row, column, width) in enumerate(
            [
                (q.at[:, pl.ds(0, WIDE)], 0, 0, WIDE),
                (q.at[:, pl.ds(WIDE, WIDE)], ROWS, 0, WIDE),
                (k, 0, WIDE, HD),
                (v, ROWS, WIDE, HD),
            ]
        )
    ]
    first = pltpu.make_async_copy(owners, hits, sems.at[4])
    first.start()
    for copy in copies:
        copy.start()
    lane = iota((1, 2 * ROWS), 1)
    lane_request = (lane % ROWS) // TOK_REQ
    first.wait()
    for r in range(REQUESTS):
        for i in range(hit_count):
            count[hits[r * hit_count + i]] = 0
    rows = [[jnp.full((1, 2 * ROWS), -4 * MSG, jnp.int32)] * hit_count for _ in range(CAP)]
    for r in range(REQUESTS):
        for i in range(hit_count):
            owner = hits[r * hit_count + i]
            rank = count[owner]
            count[owner] = rank + 1
            for s in range(CAP):
                place = jnp.where(rank == s, owner * MSG, -4 * MSG)
                rows[s][i] = jnp.where(lane_request == r, place, rows[s][i])
    inner = lane // ROWS * TOK_REQ + lane % TOK_REQ
    target = iota((devices * MSG, 2 * ROWS), 0)
    picks = []
    for s in range(CAP):
        chosen = None
        for i in range(hit_count):
            row = rows[s][i] + inner
            places[s * hit_count + i : s * hit_count + i + 1, :] = row
            hit = target == row
            chosen = hit if chosen is None else chosen | hit
        picks.append(jnp.where(chosen, 1.0, 0.0).astype(jnp.bfloat16))
    for copy in copies:
        copy.wait()
    packed = dot(jnp.concatenate(picks, axis=0), held[...], NN).astype(jnp.bfloat16)
    for s in range(CAP):
        rows = slice(s * devices * MSG, (s + 1) * devices * MSG)
        send[:, s * (WIDE + HD) : (s + 1) * (WIDE + HD)] = packed[rows]


def prep_kernel(
    devices, hit_count, hits, prefix_len, span, places, keys, values, *outs
):
    busy, prompt, cached, turned, wide, picks = outs
    rows = iota((devices * MSG, 2 * ROWS), 0)
    for n in range(CAP * hit_count):
        chosen = jnp.where(rows == places[n : n + 1, :], 1.0, 0.0)
        picks[n * 2 * ROWS : (n + 1) * 2 * ROWS, :] = chosen.T.astype(jnp.bfloat16)
    for n in range(0, CAP * REGION, STRIP):
        turned[:, n : n + STRIP] = keys[n : n + STRIP, :].T
    me = lax.axis_index("cache")
    wide[:, :HD] = values[...]
    wide[:, HD:] = jnp.ones((CAP * REGION, HD), jnp.bfloat16)
    for slot in range(CAP):
        seen = jnp.int32(0)
        request = jnp.int32(0)
        which = jnp.int32(0)
        for r in range(REQUESTS):
            for i in range(hit_count):
                mine = hits[r * hit_count + i] == me
                here = mine & (seen == slot)
                request = jnp.where(here, r, request)
                which = jnp.where(here, i, which)
                seen = seen + mine.astype(jnp.int32)
        limit = prefix_len[request] - which * REGION
        blocks = jnp.clip((limit + STRIP - 1) // STRIP, 1, REGION // STRIP)
        busy[slot] = jnp.where(seen > slot, blocks, 0)
        cached[slot : slot + 1, :] = jnp.where(iota((1, REGION), 1) < limit, 0.0, FLOOR)
        prompt_rows(devices, prompt, span, request, slot, hit_count == 1 or which == 0)


def prompt_rows(devices, prompt, span, request, slot, counted):
    total_rows = devices * MSG
    span_row = span[pl.ds(request, 1), :].astype(jnp.float32)
    source = iota((devices, total_rows), 0)
    spread = (iota((devices, total_rows), 1) // MSG == source).astype(jnp.bfloat16)
    spans = jnp.broadcast_to(span_row, (16, devices)).astype(jnp.bfloat16)
    key_span = dot(spans, spread, NN)[:1]
    lane = iota((1, total_rows), 1)
    key_spot = key_span.astype(jnp.int32) * TOK_REQ + lane % TOK_REQ
    is_key = (lane % MSG < TOK_REQ) & counted
    key_spot = jnp.where(is_key, key_spot, devices * TOK_REQ)
    block = 16 * MSG

    def one_block(at):
        row_source = at * 16 + iota((block, devices), 0) // MSG
        mine = iota((block, devices), 1) == row_source
        row_span = jnp.sum(jnp.where(mine, span_row, 0.0), axis=1, keepdims=True)
        row_spot = row_span.astype(jnp.int32) * TOK_REQ + iota((block, 1), 0) % TOK_REQ
        here = pl.ds(slot * total_rows + at * block, block)
        prompt[here, :] = jnp.where(key_spot <= row_spot, 0.0, FLOOR)

    each_block(devices, one_block)


def each_block(devices, one_block):
    blocks = devices // 16
    if blocks == 1:
        one_block(0)
    else:
        pl.loop(0, blocks)(one_block)


def lanes_max(parts):
    pieces = [part[:, n : n + HD] for part in parts for n in range(0, part.shape[1], HD)]
    return jnp.max(functools.reduce(jnp.maximum, pieces), axis=1, keepdims=True)


def attend_kernel(
    devices, hit_count, busy, prompt_mask, cached_mask, got, turned, wide, out, *levels
):
    total_rows = devices * MSG
    block = 16 * MSG
    factor = SCALE * math.log2(math.e)

    def nothing(slot):
        out[:, pl.ds(slot * WIDE, WIDE)] = jnp.zeros((total_rows, WIDE), jnp.bfloat16)
        for lse in levels:
            lse[:, pl.ds(slot * HD, HD)] = jnp.zeros((total_rows, HD), jnp.float32)

    def attend(slot, strips):
        whole = (strips - 1) * STRIP
        base = pl.multiple_of(slot * (WIDE + HD), HD)
        region = pl.multiple_of(slot * REGION, REGION)
        head = pl.ds(region, whole) if whole else None
        tail = pl.ds(pl.multiple_of(region + whole, STRIP), STRIP)
        tail_mask = cached_mask[pl.ds(slot, 1), whole : whole + STRIP]
        prompt_keys = got[:, pl.ds(base + WIDE, HD)].astype(jnp.float32)
        moved = pltpu.roll(prompt_keys, total_rows - TOK_REQ, 0)
        prompt_keys = prompt_keys.T.astype(jnp.bfloat16)
        prompt_values = jnp.concatenate(
            [moved.astype(jnp.bfloat16), jnp.ones((total_rows, HD), jnp.bfloat16)], axis=1
        )

        def one_block(at):
            here = pl.ds(at * block, block)
            prompt_bias = prompt_mask[pl.ds(slot * total_rows + at * block, block), :]
            prompt_bias = jnp.concatenate([prompt_bias, prompt_bias], axis=0)
            lane = iota((block, HD), 1)

            def scores(c):
                pair = jnp.concatenate(
                    [got[here, pl.ds(base + (c + n) * HD, HD)] for n in range(2)], axis=0
                )
                parts = [dot(pair, turned[:, head], NN)] if whole else []
                parts.append(dot(pair, turned[:, tail], NN) + tail_mask)
                parts.append(dot(pair, prompt_keys, NN) + prompt_bias)
                return parts

            logs = jnp.zeros((block, HD), jnp.float32)
            parts = scores(0)
            for c in range(0, HALF, 2):
                later = scores(c + 2) if c + 2 < HALF else None
                top = lanes_max(parts)
                if hit_count > 1:
                    top = jnp.maximum(top, 0.1 * FLOOR)
                parts = [jnp.exp2((x - top) * factor).astype(jnp.bfloat16) for x in parts]
                summed = dot(parts[-1], prompt_values, NN) + dot(parts[-2], wide[tail, :], NN)
                if whole:
                    summed = summed + dot(parts[0], wide[head, :], NN)
                totals = summed[:, HD:]
                if hit_count > 1:
                    totals = jnp.maximum(totals, 1.0)
                    level = top * SCALE + jnp.log(totals)
                    logs = jnp.where(lane == c, level[:block], logs)
                    logs = jnp.where(lane == c + 1, level[block:], logs)
                result = (summed[:, :HD] / totals).astype(jnp.bfloat16)
                for n in range(2):
                    column = pl.multiple_of(slot * WIDE + (c + n) * HD, HD)
                    out[here, pl.ds(column, HD)] = result[n * block : (n + 1) * block]
                parts = later
            for lse in levels:
                lse[here, pl.ds(pl.multiple_of(slot * HD, HD), HD)] = logs

        each_block(devices, one_block)

    @pl.loop(0, CAP)
    def _(slot):
        strips = busy[slot]
        pl.when(strips == 0)(lambda: nothing(slot))
        for count in range(1, REGION // STRIP + 1):
            pl.when(strips == count)(functools.partial(attend, slot, count))


def guest_plan(devices, owners, count, host):
    chips = devices // 2
    for d in range(devices):
        count[d] = 0
    ranks = []
    for r in range(REQUESTS):
        owner = owners[r]
        ranks.append(count[owner])
        count[owner] = ranks[r] + 1
    seconds = [count[d] > 1 for d in range(devices)]
    none = [jnp.logical_not(seconds[2 * x] | seconds[2 * x + 1]) for x in range(chips)]
    lends = []
    for x in range(chips):
        other = jnp.where(none[x ^ 1], 1, jnp.where(none[x ^ 2], 2, 3))
        lends.append(jnp.where(seconds[2 * x] & seconds[2 * x + 1], other, 0))
        host[2 * x] = jnp.int32(x)
        host[2 * x + 1] = lends[x] ^ x
    return ranks, lends


def guest_pack_kernel(
    devices, hit_count, hits, prefix_len, q, k, v, send, places, way, held, count, host, sems
):
    half = WIDE // 2
    moves = [
        (q.at[:, pl.ds(0, WIDE)], held.at[pl.ds(0, ROWS), pl.ds(0, WIDE)]),
        (q.at[:, pl.ds(WIDE, WIDE)], held.at[pl.ds(ROWS, ROWS), pl.ds(0, WIDE)]),
        (k, held.at[pl.ds(0, ROWS), pl.ds(WIDE, HD)]),
        (v, held.at[pl.ds(ROWS, ROWS), pl.ds(WIDE, HD)]),
    ]
    copies = [pltpu.make_async_copy(a, b, sems.at[n]) for n, (a, b) in enumerate(moves)]
    for copy in copies:
        copy.start()
    ranks, lends = guest_plan(devices, hits, count, host)
    lane = iota((1, 4 * ROWS), 1)
    lane_request = lane % ROWS // TOK_REQ
    part = lane // ROWS * TOK_REQ
    nowhere = -4 * MSG
    own = jnp.full((1, 4 * ROWS), nowhere, jnp.int32)
    guest = own
    longest = jnp.int32(0)
    for r in range(REQUESTS):
        owner = hits[r]
        mine = lane_request == r
        chip = host[owner]
        own = jnp.where(mine, jnp.where(ranks[r] == 0, owner * MSG, nowhere), own)
        guest = jnp.where(mine, jnp.where(ranks[r] == 1, chip * 2 * MSG, nowhere), guest)
        moves_on = (ranks[r] == 1) & (chip != owner // 2)
        longest = jnp.maximum(longest, jnp.where(moves_on, prefix_len[r], 0))
    used = [
        functools.reduce(jnp.logical_or, [lend == n for lend in lends]) for n in range(1, 4)
    ]
    mixed = used[2] | (used[0] & used[1])
    kind = jnp.where(mixed, 5, jnp.where(used[0], 1, jnp.where(used[1], 3, 0)))
    short = (longest <= REGION // 2) & (kind < 5)
    way[0] = kind + jnp.where(short, 0, jnp.where((kind == 1) | (kind == 3), 1, 0))
    own = own + lane % TOK_REQ
    guest = guest + lane % TOK_REQ
    places[0:1, :] = own + part
    places[1:2, :] = guest + part
    own, guest, part = own[:, : 2 * ROWS], guest[:, : 2 * ROWS], part[:, : 2 * ROWS]
    target = iota((devices * MSG, 2 * ROWS), 0)

    def rows_of(chosen, first, width):
        pick = jnp.where(chosen, 1.0, 0.0).astype(jnp.bfloat16)
        return dot(pick, held[:, first : first + width], NN)

    for copy in copies:
        copy.wait()
    send[:, : WIDE + HD] = rows_of(target == own + part, 0, WIDE + HD).astype(jnp.bfloat16)
    rows = rows_of(target == guest + 2 * part, 0, half)
    rows = rows + rows_of(target == guest + 2 * part + TOK_REQ, half, half)
    send[:, WIDE + HD : WIDE + HD + half] = rows.astype(jnp.bfloat16)
    both = (target == guest + part) | (target == guest + MSG + part)
    send[:, WIDE + HD + half :] = rows_of(both, WIDE, HD).astype(jnp.bfloat16)


def guest_prep_kernel(
    devices, hit_count, hits, prefix_len, span, places, keys, values, *refs
):
    plan, prompt, cached, turned, wide, picks, picks_guest, strips_of, count, host = refs
    me = lax.axis_index("cache")
    chip = me // 2
    ranks, _ = guest_plan(devices, hits, count, host)
    rows = iota((devices * MSG, 4 * ROWS), 0)
    chosen = jnp.where(rows[:, : 2 * ROWS] == places[0:1, : 2 * ROWS], 1.0, 0.0)
    picks[...] = chosen.T.astype(jnp.bfloat16)
    chosen = jnp.where(rows == places[1:2, :], 1.0, 0.0)
    picks_guest[...] = chosen.T.astype(jnp.bfloat16)
    widen(keys[:REGION, :], values[:REGION, :], turned, wide)
    first, guest, source = jnp.int32(-1), jnp.int32(-1), jnp.int32(0)
    for r in range(REQUESTS):
        owner = hits[r]
        here = (ranks[r] == 1) & (host[owner] == chip)
        first = jnp.where((ranks[r] == 0) & (owner == me), r, first)
        guest = jnp.where(here, r, guest)
        source = jnp.where(here, owner, source)
    core = me % 2
    from_first_core = jnp.where(source == 2 * chip, 1, 0)
    plan[0] = jnp.where(core == 1, (source // 2) ^ chip, 0)
    plan[1] = jnp.where(core == from_first_core, 1, 0)
    for job, found in enumerate((first, guest)):
        request = jnp.maximum(found, 0)
        limit = prefix_len[request]
        strips = jnp.clip((limit + STRIP - 1) // STRIP, 1, REGION // STRIP)
        strips_of[job : job + 1, :] = jnp.full((1, HD), jnp.where(found >= 0, strips, 0))
        cached[job : job + 1, :] = jnp.where(iota((1, REGION), 1) < limit, 0.0, FLOOR)
        prompt_rows(devices, prompt, span, request, job, True)


def widen(keys, values, turned, wide):
    for n in range(0, REGION, STRIP):
        turned[:, n : n + STRIP] = keys[n : n + STRIP].T
    wide[:, :HD] = values
    wide[:, HD:] = jnp.ones((REGION, HD), jnp.bfloat16)


def host_kernel(devices, hit_count, plan, *refs):
    mine, other, turned, wide = refs[:2], refs[2:4], refs[4], refs[5]
    for choice, (keys, values) in enumerate((mine, other)):

        @pl.when(plan[1] == choice)
        def _():
            widen(keys[...], values[...], turned, wide)


def guest_attend_kernel(
    devices, hit_count, strips_of, prompt_mask, cached_mask, got, turned, wide, *refs
):
    turned_guest, wide_guest, out = refs
    jobs = [
        (0, 0, HALF, turned, wide),
        (WIDE + HD, WIDE, HALF // 2, turned_guest, wide_guest),
    ]
    for job, (base, first, blocks, keys, values) in enumerate(jobs):
        strips = strips_of[job, 0]

        @pl.when(strips == 0)
        def _():
            empty = jnp.zeros((devices * MSG, blocks * HD), jnp.bfloat16)
            out[:, first : first + blocks * HD] = empty

        for count in range(1, REGION // STRIP + 1):

            @pl.when(strips == count)
            def _():
                whole = (count - 1) * STRIP
                mask = prompt_mask[job * devices * MSG : (job + 1) * devices * MSG, :]
                attend_rows(
                    got,
                    base,
                    blocks,
                    slice(0, devices * MSG),
                    prompt_parts(got[:, base + blocks * HD : base + (blocks + 1) * HD]),
                    mask,
                    cached_mask[job : job + 1, whole : whole + STRIP],
                    keys[:, :whole] if whole else None,
                    keys[:, whole : whole + STRIP],
                    values[:whole, :] if whole else None,
                    values[whole : whole + STRIP, :],
                    out,
                    first,
                )


def prompt_parts(rows):
    height = rows.shape[0]
    wide = rows.astype(jnp.float32)
    moved = pltpu.roll(wide, height - TOK_REQ, 0).astype(jnp.bfloat16)
    values = jnp.concatenate([moved, jnp.ones((height, HD), jnp.bfloat16)], axis=1)
    return wide.T.astype(jnp.bfloat16), values


def attend_rows(
    got, base, blocks, here, prompt, mask, tail_mask, head, tail, head_values, tail_values, out, first
):
    prompt_keys, prompt_values = prompt
    factor = SCALE * math.log2(math.e)
    mask = jnp.concatenate([mask, mask], axis=0)
    height = mask.shape[0] // 2

    def scores(c):
        pair = jnp.concatenate(
            [got[here, base + (c + n) * HD : base + (c + n + 1) * HD] for n in range(2)], axis=0
        )
        parts = [] if head is None else [dot(pair, head, NN)]
        parts.append(dot(pair, tail, NN) + tail_mask)
        parts.append(dot(pair, prompt_keys, NN) + mask)
        return parts

    parts = scores(0)
    for c in range(0, blocks, 2):
        later = scores(c + 2) if c + 2 < blocks else None
        top = lanes_max(parts)
        parts = [jnp.exp2((x - top) * factor).astype(jnp.bfloat16) for x in parts]
        summed = dot(parts[-1], prompt_values, NN) + dot(parts[-2], tail_values, NN)
        if head is not None:
            summed = summed + dot(parts[0], head_values, NN)
        result = (summed[:, :HD] / summed[:, HD:]).astype(jnp.bfloat16)
        for n in range(2):
            column = first + (c + n) * HD
            out[here, column : column + HD] = result[n * height : (n + 1) * height]
        parts = later


def guest_unpack_kernel(devices, hit_count, picks, picks_guest, outs, result):
    half = WIDE // 2
    own = dot(picks[...], outs[:, :WIDE], NN)
    guest = dot(picks_guest[...], outs[:, WIDE:], NN)
    for g in range(4):
        rows = own[g // 2 * ROWS : (g // 2 + 1) * ROWS, g % 2 * half : (g % 2 + 1) * half]
        rows = rows + guest[g * ROWS : (g + 1) * ROWS]
        result[:, g * half : (g + 1) * half] = rows.astype(jnp.bfloat16)


def unpack_kernel(devices, hit_count, picks, *refs):
    outs, logs, result = refs[0], refs[1:-1], refs[-1]

    def chosen(s, i):
        place = s * hit_count + i
        return picks[place * 2 * ROWS : (place + 1) * 2 * ROWS, :]

    def rows_of(i):
        parts = [
            dot(chosen(s, i), outs[:, s * WIDE : (s + 1) * WIDE], NN)
            for s in range(CAP)
        ]
        return sum(parts[1:], parts[0])

    def logs_of(i):
        parts = [
            dot(
                chosen(s, i).astype(jnp.float32),
                logs[0][:, s * HD : (s + 1) * HD],
                NN,
                precision=lax.Precision.HIGHEST,
            )
            for s in range(CAP)
        ]
        return sum(parts[1:], parts[0])

    if hit_count == 1:
        joined = rows_of(0)
    else:
        levels = [logs_of(i) for i in range(hit_count)]
        top = functools.reduce(jnp.maximum, levels)
        shares = [jnp.exp(level - top) for level in levels]
        total = sum(shares[1:], shares[0])
        pieces = [rows_of(i) for i in range(hit_count)]
        columns = []
        for c in range(HALF):
            part = sum(
                shares[i][:, c : c + 1] * pieces[i][:, c * HD : (c + 1) * HD]
                for i in range(hit_count)
            )
            columns.append(part / total[:, c : c + 1])
        joined = jnp.concatenate(columns, axis=1)
    joined = joined.astype(jnp.bfloat16)
    result[:, :WIDE] = joined[:ROWS]
    result[:, WIDE:] = joined[ROWS:]


def vmem(count):
    return [pl.BlockSpec(memory_space=pltpu.VMEM)] * count


def smem(count):
    return [pl.BlockSpec(memory_space=pltpu.SMEM)] * count


def hbm(count):
    return [pl.BlockSpec(memory_space=pltpu.HBM)] * count


def body(prefix_len, hits, span_block, queries, fresh_keys, fresh_values, cache_keys, cache_values):
    devices = lax.axis_size("cache")
    hit_count = hits.shape[1]
    rows = devices * MSG
    owners = hits.reshape(REQUESTS * hit_count)
    fresh = (owners, queries, fresh_keys, fresh_values)

    def exchange(x):
        return lax.all_to_all(x, "cache", split_axis=0, concat_axis=0, tiled=True)

    def call(kernel, out_shape, name, grant=40, **kw):
        return pl.pallas_call(
            functools.partial(kernel, devices, hit_count),
            out_shape=[jax.ShapeDtypeStruct(*leaf) for leaf in out_shape],
            compiler_params=pltpu.CompilerParams(vmem_limit_bytes=grant * 2**20),
            name=name,
            **kw,
        )

    if hit_count == 1 and devices == 16:
        pairs = rows * (HALF + HALF // 2) * (REGION + rows)
        scalars = [pltpu.SMEM((devices,), jnp.int32)] * 2
        send, places, way = call(
            guest_pack_kernel,
            [
                ((rows, GUEST_MSG), jnp.bfloat16),
                ((2, 4 * ROWS), jnp.int32),
                ((1,), jnp.int32),
            ],
            "pack",
            in_specs=smem(2) + hbm(3),
            out_specs=vmem(2) + smem(1),
            scratch_shapes=[
                pltpu.VMEM((2 * ROWS, WIDE + HD), jnp.bfloat16),
                *scalars,
                pltpu.SemaphoreType.DMA((4,)),
            ],
        )(
            *(
                pltpu.with_memory_space_constraint(x, pltpu.HBM)
                for x in (owners, prefix_len, queries, fresh_keys, fresh_values)
            )
        )
        got = exchange(send)
        shapes = [((HD, REGION), jnp.bfloat16), ((REGION, 2 * HD), jnp.bfloat16)]
        def chain(form, owners, prefix_len, span_block, places, cache_keys, cache_values):
            ways, height = form
            pinned = [
                pltpu.with_memory_space_constraint(x, pltpu.HBM)
                for x in (owners, prefix_len, span_block)
            ]
            slots = [cache_keys[REGION:], cache_values[REGION:]]
            lent = [
                [
                    lax.ppermute(
                        x[:height], "cache", [(d, d ^ (2 * n)) for d in range(1, devices, 2)]
                    )
                    for x in slots
                ]
                for n in ways
            ]
            prepared = call(
                guest_prep_kernel,
                [((2,), jnp.int32), ((2 * rows, rows), jnp.float32), ((2, REGION), jnp.float32)]
                + shapes
                + [((2 * ROWS, rows), jnp.bfloat16), ((4 * ROWS, rows), jnp.bfloat16)]
                + [((8, HD), jnp.int32)],
                "prep",
                in_specs=smem(2) + vmem(4),
                out_specs=smem(1) + vmem(7),
                scratch_shapes=scalars,
                cost_estimate=pl.CostEstimate(
                    flops=10**6, bytes_accessed=2**22, transcendentals=0
                ),
            )(*pinned, places, cache_keys, cache_values)
            plan = prepared[0]
            for n, borrowed in zip(ways, lent):
                slots = [
                    jnp.where(plan[0] == n, jnp.pad(x, ((0, REGION - height), (0, 0))), y)
                    for x, y in zip(borrowed, slots)
                ]
            swapped = [lax.ppermute(x, "cache", [(d, d ^ 1) for d in range(devices)]) for x in slots]
            guest = call(
                host_kernel, shapes, "host", in_specs=smem(1) + vmem(4), out_specs=vmem(2)
            )(plan, *slots, *swapped)
            return (*prepared[1:], *guest)

        forms = [
            ((), REGION),
            ((1,), REGION // 2),
            ((1,), REGION),
            ((2,), REGION // 2),
            ((2,), REGION),
            ((1, 2, 3), REGION),
        ]
        prepared = lax.switch(
            way.reshape(()),
            [functools.partial(chain, form) for form in forms],
            owners,
            prefix_len,
            span_block,
            places,
            cache_keys,
            cache_values,
        )
        prompt_mask, cached_mask, turned, wide, picks, picks_guest, strips_of = prepared[:7]
        turned_guest, wide_guest = prepared[7:]
        (answer,) = call(
            guest_attend_kernel,
            [((rows, WIDE + WIDE // 2), jnp.bfloat16)],
            "attend",
            in_specs=vmem(8),
            out_specs=vmem(1),
            cost_estimate=pl.CostEstimate(
                flops=4 * pairs * HD, bytes_accessed=8 * rows * WIDE, transcendentals=pairs
            ),
        )(strips_of, prompt_mask, cached_mask, got, turned, wide, turned_guest, wide_guest)
        return call(
            guest_unpack_kernel,
            [((ROWS, HEADS * HD), jnp.bfloat16)],
            "unpack",
            in_specs=vmem(3),
            out_specs=vmem(1),
        )(picks, picks_guest, exchange(answer))[0]
    send, places = call(
        pack_kernel,
        [((rows, CAP * (WIDE + HD)), jnp.bfloat16), ((CAP * hit_count, 2 * ROWS), jnp.int32)],
        "pack",
        in_specs=hbm(4),
        out_specs=vmem(2),
        scratch_shapes=[
            pltpu.VMEM((2 * ROWS, WIDE + HD), jnp.bfloat16),
            pltpu.SMEM((REQUESTS * hit_count,), jnp.int32),
            pltpu.SMEM((devices,), jnp.int32),
            pltpu.SemaphoreType.DMA((5,)),
        ],
    )(*(pltpu.with_memory_space_constraint(x, pltpu.HBM) for x in fresh))
    got = exchange(send)
    busy, prompt_mask, cached_mask, turned, wide, picks = call(
        prep_kernel,
        [
            ((CAP,), jnp.int32),
            ((CAP * rows, rows), jnp.float32),
            ((CAP, REGION), jnp.float32),
            ((HD, CAP * REGION), jnp.bfloat16),
            ((CAP * REGION, 2 * HD), jnp.bfloat16),
            ((CAP * hit_count * 2 * ROWS, rows), jnp.bfloat16),
        ],
        "prep",
        in_specs=smem(2) + vmem(4),
        out_specs=smem(1) + vmem(5),
        cost_estimate=pl.CostEstimate(flops=10**6, bytes_accessed=2**22, transcendentals=0),
    )(owners, prefix_len, span_block, places, cache_keys, cache_values)
    pairs = CAP * rows * HALF * (REGION + rows)
    answers = call(
        attend_kernel,
        [((rows, CAP * WIDE), jnp.bfloat16)]
        + [((rows, CAP * HD), jnp.float32)] * (hit_count > 1),
        "attend",
        in_specs=smem(1) + vmem(5),
        out_specs=vmem(1 + (hit_count > 1)),
        cost_estimate=pl.CostEstimate(
            flops=4 * pairs * HD, bytes_accessed=8 * rows * WIDE, transcendentals=pairs
        ),
    )(busy, prompt_mask, cached_mask, got, turned, wide)
    returned = [exchange(answer) for answer in answers]
    return call(
        unpack_kernel,
        [((ROWS, HEADS * HD), jnp.bfloat16)],
        "unpack",
        in_specs=vmem(1 + len(returned)),
        out_specs=vmem(1),
    )(picks, *returned)[0]


def solution(mesh):
    in_specs = (
        P("groups"),
        P("groups", None),
        P("groups", None),
        P(("groups", "cache"), None),
        P(("groups", "cache"), None),
        P(("groups", "cache"), None),
        P(("groups", "cache"), None),
        P(("groups", "cache"), None),
    )
    out_specs = P(("groups", "cache"), None)
    return jax.shard_map(body, mesh=mesh, in_specs=in_specs, out_specs=out_specs, check_vma=False)
```

```python
import functools
import math

import jax
import jax.numpy as jnp
from jax import lax
from jax.experimental import pallas as pl
from jax.experimental.pallas import tpu as pltpu
from jax.sharding import PartitionSpec as P

HEADS = 16
HD = 128
PAGE = 128
CAP = 2
REQUESTS = 16
TOK_REQ = 4
PAGES_DEV = 16

REGION = PAGES_DEV // CAP * PAGE
HALF = HEADS // 2
MSG = 2 * TOK_REQ
WIDE = HALF * HD
ROWS = REQUESTS * TOK_REQ
STRIP = 256
GUEST_MSG = WIDE + HD + WIDE // 2 + HD
SCALE = HD**-0.5
FLOOR = -1e30
NN = (((1,), (0,)), ((), ()))


def iota(shape, axis):
    return lax.broadcasted_iota(jnp.int32, shape, axis)


def dot(a, b, dims, **kw):
    return lax.dot_general(a, b, dims, preferred_element_type=jnp.float32, **kw)


def pack_kernel(devices, hit_count, owners, q, k, v, send, places, held, hits, count, sems):
    copies = [
        pltpu.make_async_copy(source, held.at[pl.ds(row, ROWS), pl.ds(column, width)], sems.at[n])
        for n, (source, row, column, width) in enumerate(
            [
                (q.at[:, pl.ds(0, WIDE)], 0, 0, WIDE),
                (q.at[:, pl.ds(WIDE, WIDE)], ROWS, 0, WIDE),
                (k, 0, WIDE, HD),
                (v, ROWS, WIDE, HD),
            ]
        )
    ]
    first = pltpu.make_async_copy(owners, hits, sems.at[4])
    first.start()
    for copy in copies:
        copy.start()
    lane = iota((1, 2 * ROWS), 1)
    lane_request = (lane % ROWS) // TOK_REQ
    first.wait()
    for r in range(REQUESTS):
        for i in range(hit_count):
            count[hits[r * hit_count + i]] = 0
    rows = [[jnp.full((1, 2 * ROWS), -4 * MSG, jnp.int32)] * hit_count for _ in range(CAP)]
    for r in range(REQUESTS):
        for i in range(hit_count):
            owner = hits[r * hit_count + i]
            rank = count[owner]
            count[owner] = rank + 1
            for s in range(CAP):
                place = jnp.where(rank == s, owner * MSG, -4 * MSG)
                rows[s][i] = jnp.where(lane_request == r, place, rows[s][i])
    inner = lane // ROWS * TOK_REQ + lane % TOK_REQ
    target = iota((devices * MSG, 2 * ROWS), 0)
    picks = []
    for s in range(CAP):
        chosen = None
        for i in range(hit_count):
            row = rows[s][i] + inner
            places[s * hit_count + i : s * hit_count + i + 1, :] = row
            hit = target == row
            chosen = hit if chosen is None else chosen | hit
        picks.append(jnp.where(chosen, 1.0, 0.0).astype(jnp.bfloat16))
    for copy in copies:
        copy.wait()
    packed = dot(jnp.concatenate(picks, axis=0), held[...], NN).astype(jnp.bfloat16)
    for s in range(CAP):
        rows = slice(s * devices * MSG, (s + 1) * devices * MSG)
        send[:, s * (WIDE + HD) : (s + 1) * (WIDE + HD)] = packed[rows]


def prep_kernel(
    devices, hit_count, hits, prefix_len, span, places, keys, values, *outs
):
    busy, prompt, cached, turned, wide, picks = outs
    rows = iota((devices * MSG, 2 * ROWS), 0)
    for n in range(CAP * hit_count):
        chosen = jnp.where(rows == places[n : n + 1, :], 1.0, 0.0)
        picks[n * 2 * ROWS : (n + 1) * 2 * ROWS, :] = chosen.T.astype(jnp.bfloat16)
    for n in range(0, CAP * REGION, STRIP):
        turned[:, n : n + STRIP] = keys[n : n + STRIP, :].T
    me = lax.axis_index("cache")
    wide[:, :HD] = values[...]
    wide[:, HD:] = jnp.ones((CAP * REGION, HD), jnp.bfloat16)
    for slot in range(CAP):
        seen = jnp.int32(0)
        request = jnp.int32(0)
        which = jnp.int32(0)
        for r in range(REQUESTS):
            for i in range(hit_count):
                mine = hits[r * hit_count + i] == me
                here = mine & (seen == slot)
                request = jnp.where(here, r, request)
                which = jnp.where(here, i, which)
                seen = seen + mine.astype(jnp.int32)
        limit = prefix_len[request] - which * REGION
        blocks = jnp.clip((limit + STRIP - 1) // STRIP, 1, REGION // STRIP)
        busy[slot] = jnp.where(seen > slot, blocks, 0)
        cached[slot : slot + 1, :] = jnp.where(iota((1, REGION), 1) < limit, 0.0, FLOOR)
        prompt_rows(devices, prompt, span, request, slot, hit_count == 1 or which == 0)


def prompt_rows(devices, prompt, span, request, slot, counted):
    total_rows = devices * MSG
    span_row = span[pl.ds(request, 1), :].astype(jnp.float32)
    source = iota((devices, total_rows), 0)
    spread = (iota((devices, total_rows), 1) // MSG == source).astype(jnp.bfloat16)
    spans = jnp.broadcast_to(span_row, (16, devices)).astype(jnp.bfloat16)
    key_span = dot(spans, spread, NN)[:1]
    lane = iota((1, total_rows), 1)
    key_spot = key_span.astype(jnp.int32) * TOK_REQ + lane % TOK_REQ
    is_key = (lane % MSG < TOK_REQ) & counted
    key_spot = jnp.where(is_key, key_spot, devices * TOK_REQ)
    block = 16 * MSG

    def one_block(at):
        row_source = at * 16 + iota((block, devices), 0) // MSG
        mine = iota((block, devices), 1) == row_source
        row_span = jnp.sum(jnp.where(mine, span_row, 0.0), axis=1, keepdims=True)
        row_spot = row_span.astype(jnp.int32) * TOK_REQ + iota((block, 1), 0) % TOK_REQ
        here = pl.ds(slot * total_rows + at * block, block)
        prompt[here, :] = jnp.where(key_spot <= row_spot, 0.0, FLOOR)

    each_block(devices, one_block)


def each_block(devices, one_block):
    blocks = devices // 16
    if blocks == 1:
        one_block(0)
    else:
        pl.loop(0, blocks)(one_block)


def lanes_max(parts):
    pieces = [part[:, n : n + HD] for part in parts for n in range(0, part.shape[1], HD)]
    return jnp.max(functools.reduce(jnp.maximum, pieces), axis=1, keepdims=True)


def attend_kernel(
    devices, hit_count, busy, prompt_mask, cached_mask, got, turned, wide, out, *levels
):
    total_rows = devices * MSG
    block = 16 * MSG
    factor = SCALE * math.log2(math.e)

    def nothing(slot):
        out[:, pl.ds(slot * WIDE, WIDE)] = jnp.zeros((total_rows, WIDE), jnp.bfloat16)
        for lse in levels:
            lse[:, pl.ds(slot * HD, HD)] = jnp.zeros((total_rows, HD), jnp.float32)

    def attend(slot, strips):
        whole = (strips - 1) * STRIP
        base = pl.multiple_of(slot * (WIDE + HD), HD)
        region = pl.multiple_of(slot * REGION, REGION)
        head = pl.ds(region, whole) if whole else None
        tail = pl.ds(pl.multiple_of(region + whole, STRIP), STRIP)
        tail_mask = cached_mask[pl.ds(slot, 1), whole : whole + STRIP]
        prompt_keys = got[:, pl.ds(base + WIDE, HD)].astype(jnp.float32)
        moved = pltpu.roll(prompt_keys, total_rows - TOK_REQ, 0)
        prompt_keys = prompt_keys.T.astype(jnp.bfloat16)
        prompt_values = jnp.concatenate(
            [moved.astype(jnp.bfloat16), jnp.ones((total_rows, HD), jnp.bfloat16)], axis=1
        )

        def one_block(at):
            here = pl.ds(at * block, block)
            prompt_bias = prompt_mask[pl.ds(slot * total_rows + at * block, block), :]
            prompt_bias = jnp.concatenate([prompt_bias, prompt_bias], axis=0)
            lane = iota((block, HD), 1)

            def scores(c):
                pair = jnp.concatenate(
                    [got[here, pl.ds(base + (c + n) * HD, HD)] for n in range(2)], axis=0
                )
                parts = [dot(pair, turned[:, head], NN)] if whole else []
                parts.append(dot(pair, turned[:, tail], NN) + tail_mask)
                parts.append(dot(pair, prompt_keys, NN) + prompt_bias)
                return parts

            logs = jnp.zeros((block, HD), jnp.float32)
            parts = scores(0)
            for c in range(0, HALF, 2):
                later = scores(c + 2) if c + 2 < HALF else None
                top = lanes_max(parts)
                if hit_count > 1:
                    top = jnp.maximum(top, 0.1 * FLOOR)
                parts = [jnp.exp2((x - top) * factor).astype(jnp.bfloat16) for x in parts]
                summed = dot(parts[-1], prompt_values, NN) + dot(parts[-2], wide[tail, :], NN)
                if whole:
                    summed = summed + dot(parts[0], wide[head, :], NN)
                totals = summed[:, HD:]
                if hit_count > 1:
                    totals = jnp.maximum(totals, 1.0)
                    level = top * SCALE + jnp.log(totals)
                    logs = jnp.where(lane == c, level[:block], logs)
                    logs = jnp.where(lane == c + 1, level[block:], logs)
                result = (summed[:, :HD] / totals).astype(jnp.bfloat16)
                for n in range(2):
                    column = pl.multiple_of(slot * WIDE + (c + n) * HD, HD)
                    out[here, pl.ds(column, HD)] = result[n * block : (n + 1) * block]
                parts = later
            for lse in levels:
                lse[here, pl.ds(pl.multiple_of(slot * HD, HD), HD)] = logs

        each_block(devices, one_block)

    @pl.loop(0, CAP)
    def _(slot):
        strips = busy[slot]
        pl.when(strips == 0)(lambda: nothing(slot))
        for count in range(1, REGION // STRIP + 1):
            pl.when(strips == count)(functools.partial(attend, slot, count))


def owner_ranks(devices, owners, count):
    for d in range(devices):
        count[d] = 0
    ranks = []
    for r in range(REQUESTS):
        owner = owners[r]
        ranks.append(count[owner])
        count[owner] = ranks[r] + 1
    return ranks


def guest_plan(devices, count, host):
    chips = devices // 2
    seconds = [count[d] > 1 for d in range(devices)]
    none = [jnp.logical_not(seconds[2 * x] | seconds[2 * x + 1]) for x in range(chips)]
    lends = []
    for x in range(chips):
        other = jnp.where(none[x ^ 1], 1, jnp.where(none[x ^ 2], 2, 3))
        lends.append(jnp.where(seconds[2 * x] & seconds[2 * x + 1], other, 0))
        host[2 * x] = jnp.int32(x)
        host[2 * x + 1] = lends[x] ^ x
    return lends


def guest_pack_kernel(devices, hit_count, owners, lengths, q, k, v, *refs):
    send, places, way, held, hits, prefix_len, count, host, sems = refs
    half = WIDE // 2
    moves = [
        (owners, hits),
        (q.at[:, pl.ds(0, WIDE)], held.at[pl.ds(0, ROWS), pl.ds(0, WIDE)]),
        (q.at[:, pl.ds(WIDE, WIDE)], held.at[pl.ds(ROWS, ROWS), pl.ds(0, WIDE)]),
        (k, held.at[pl.ds(0, ROWS), pl.ds(WIDE, HD)]),
        (v, held.at[pl.ds(ROWS, ROWS), pl.ds(WIDE, HD)]),
        (lengths, prefix_len),
    ]
    copies = [pltpu.make_async_copy(a, b, sems.at[n]) for n, (a, b) in enumerate(moves)]
    for copy in copies:
        copy.start()
    lane = iota((1, 4 * ROWS), 1)
    lane_request = lane % ROWS // TOK_REQ
    part = lane // ROWS * TOK_REQ
    nowhere = jnp.full((1, 4 * ROWS), -4 * MSG, jnp.int32)
    target = iota((devices * MSG, 2 * ROWS), 0)
    copies[0].wait()
    ranks = owner_ranks(devices, hits, count)
    own = nowhere
    for r in range(REQUESTS):
        place = jnp.where(ranks[r] == 0, hits[r] * MSG, -4 * MSG)
        own = jnp.where(lane_request == r, place, own)
    own = own + lane % TOK_REQ + part

    def rows_of(chosen, first, width):
        pick = jnp.where(chosen, 1.0, 0.0).astype(jnp.bfloat16)
        return dot(pick, held[:, first : first + width], NN)

    for copy in copies[1:]:
        copy.wait()
    rows = rows_of(target == own[:, : 2 * ROWS], 0, WIDE + HD)
    send[:, : WIDE + HD] = rows.astype(jnp.bfloat16)
    lends = guest_plan(devices, count, host)
    guest = nowhere
    longest = jnp.int32(0)
    for r in range(REQUESTS):
        chip = host[hits[r]]
        place = jnp.where(ranks[r] == 1, chip * 2 * MSG, -4 * MSG)
        guest = jnp.where(lane_request == r, place, guest)
        lent = (ranks[r] == 1) & (chip != hits[r] // 2)
        longest = jnp.maximum(longest, jnp.where(lent, prefix_len[r], 0))
    guest = guest + lane % TOK_REQ
    places[0:1, :] = own
    places[1:2, :] = guest + part
    guest, part = guest[:, : 2 * ROWS], part[:, : 2 * ROWS]
    rows = rows_of(target == guest + 2 * part, 0, half)
    rows = rows + rows_of(target == guest + 2 * part + TOK_REQ, half, half)
    send[:, WIDE + HD : WIDE + HD + half] = rows.astype(jnp.bfloat16)
    both = (target == guest + part) | (target == guest + MSG + part)
    send[:, WIDE + HD + half :] = rows_of(both, WIDE, HD).astype(jnp.bfloat16)
    used = [
        functools.reduce(jnp.logical_or, [lend == n for lend in lends]) for n in range(1, 4)
    ]
    mixed = used[2] | (used[0] & used[1])
    kind = jnp.where(mixed, 5, jnp.where(used[0], 1, jnp.where(used[1], 3, 0)))
    whole = (longest > REGION // 2) & (kind > 0) & (kind < 5)
    way[0] = kind + jnp.where(whole, 1, 0)


def guest_prep_kernel(
    devices, hit_count, hits, prefix_len, span, places, keys, values, *refs
):
    plan, prompt, cached, turned, wide, picks, picks_guest, strips_of, count, host = refs
    me = lax.axis_index("cache")
    chip = me // 2
    ranks = owner_ranks(devices, hits, count)
    guest_plan(devices, count, host)
    rows = iota((devices * MSG, 4 * ROWS), 0)
    chosen = jnp.where(rows[:, : 2 * ROWS] == places[0:1, : 2 * ROWS], 1.0, 0.0)
    picks[...] = chosen.T.astype(jnp.bfloat16)
    chosen = jnp.where(rows == places[1:2, :], 1.0, 0.0)
    picks_guest[...] = chosen.T.astype(jnp.bfloat16)
    widen(keys[:REGION, :], values[:REGION, :], turned, wide)
    first, guest, source = jnp.int32(-1), jnp.int32(-1), jnp.int32(0)
    for r in range(REQUESTS):
        owner = hits[r]
        here = (ranks[r] == 1) & (host[owner] == chip)
        first = jnp.where((ranks[r] == 0) & (owner == me), r, first)
        guest = jnp.where(here, r, guest)
        source = jnp.where(here, owner, source)
    core = me % 2
    from_first_core = jnp.where(source == 2 * chip, 1, 0)
    plan[0] = jnp.where(core == 1, (source // 2) ^ chip, 0)
    plan[1] = jnp.where(core == from_first_core, 1, 0)
    for job, found in enumerate((first, guest)):
        request = jnp.maximum(found, 0)
        limit = prefix_len[request]
        strips = jnp.clip((limit + STRIP - 1) // STRIP, 1, REGION // STRIP)
        strips_of[job : job + 1, :] = jnp.full((1, HD), jnp.where(found >= 0, strips, 0))
        cached[job : job + 1, :] = jnp.where(iota((1, REGION), 1) < limit, 0.0, FLOOR)
        prompt_rows(devices, prompt, span, request, job, True)


def widen(keys, values, turned, wide):
    for n in range(0, REGION, STRIP):
        turned[:, n : n + STRIP] = keys[n : n + STRIP].T
    wide[:, :HD] = values
    wide[:, HD:] = jnp.ones((REGION, HD), jnp.bfloat16)


def host_kernel(devices, hit_count, plan, *refs):
    mine, other, turned, wide = refs[:2], refs[2:4], refs[4], refs[5]
    for choice, (keys, values) in enumerate((mine, other)):

        @pl.when(plan[1] == choice)
        def _():
            widen(keys[...], values[...], turned, wide)


def guest_attend_kernel(
    devices, hit_count, strips_of, prompt_mask, cached_mask, got, turned, wide, *refs
):
    turned_guest, wide_guest, out = refs
    jobs = [
        (0, 0, HALF, turned, wide),
        (WIDE + HD, WIDE, HALF // 2, turned_guest, wide_guest),
    ]
    for job, (base, first, blocks, keys, values) in enumerate(jobs):
        strips = strips_of[job, 0]

        @pl.when(strips == 0)
        def _():
            empty = jnp.zeros((devices * MSG, blocks * HD), jnp.bfloat16)
            out[:, first : first + blocks * HD] = empty

        for count in range(1, REGION // STRIP + 1):

            @pl.when(strips == count)
            def _():
                whole = (count - 1) * STRIP
                mask = prompt_mask[job * devices * MSG : (job + 1) * devices * MSG, :]
                attend_rows(
                    got,
                    base,
                    blocks,
                    slice(0, devices * MSG),
                    prompt_parts(got[:, base + blocks * HD : base + (blocks + 1) * HD]),
                    mask,
                    cached_mask[job : job + 1, whole : whole + STRIP],
                    keys[:, :whole] if whole else None,
                    keys[:, whole : whole + STRIP],
                    values[:whole, :] if whole else None,
                    values[whole : whole + STRIP, :],
                    out,
                    first,
                )


def prompt_parts(rows):
    height = rows.shape[0]
    wide = rows.astype(jnp.float32)
    moved = pltpu.roll(wide, height - TOK_REQ, 0).astype(jnp.bfloat16)
    values = jnp.concatenate([moved, jnp.ones((height, HD), jnp.bfloat16)], axis=1)
    return wide.T.astype(jnp.bfloat16), values


def attend_rows(
    got, base, blocks, here, prompt, mask, tail_mask, head, tail, head_values, tail_values, out, first
):
    prompt_keys, prompt_values = prompt
    factor = SCALE * math.log2(math.e)
    mask = jnp.concatenate([mask, mask], axis=0)
    height = mask.shape[0] // 2

    def scores(c):
        pair = jnp.concatenate(
            [got[here, base + (c + n) * HD : base + (c + n + 1) * HD] for n in range(2)], axis=0
        )
        parts = [] if head is None else [dot(pair, head, NN)]
        parts.append(dot(pair, tail, NN) + tail_mask)
        parts.append(dot(pair, prompt_keys, NN) + mask)
        return parts

    parts = scores(0)
    for c in range(0, blocks, 2):
        later = scores(c + 2) if c + 2 < blocks else None
        top = lanes_max(parts)
        parts = [jnp.exp2((x - top) * factor).astype(jnp.bfloat16) for x in parts]
        summed = dot(parts[-1], prompt_values, NN) + dot(parts[-2], tail_values, NN)
        if head is not None:
            summed = summed + dot(parts[0], head_values, NN)
        result = (summed[:, :HD] / summed[:, HD:]).astype(jnp.bfloat16)
        for n in range(2):
            column = first + (c + n) * HD
            out[here, column : column + HD] = result[n * height : (n + 1) * height]
        parts = later


def guest_unpack_kernel(devices, hit_count, picks, picks_guest, outs, result):
    half = WIDE // 2
    own = dot(picks[...], outs[:, :WIDE], NN)
    guest = dot(picks_guest[...], outs[:, WIDE:], NN)
    for g in range(4):
        rows = own[g // 2 * ROWS : (g // 2 + 1) * ROWS, g % 2 * half : (g % 2 + 1) * half]
        rows = rows + guest[g * ROWS : (g + 1) * ROWS]
        result[:, g * half : (g + 1) * half] = rows.astype(jnp.bfloat16)


def unpack_kernel(devices, hit_count, picks, *refs):
    outs, logs, result = refs[0], refs[1:-1], refs[-1]

    def chosen(s, i):
        place = s * hit_count + i
        return picks[place * 2 * ROWS : (place + 1) * 2 * ROWS, :]

    def rows_of(i):
        parts = [
            dot(chosen(s, i), outs[:, s * WIDE : (s + 1) * WIDE], NN)
            for s in range(CAP)
        ]
        return sum(parts[1:], parts[0])

    def logs_of(i):
        parts = [
            dot(
                chosen(s, i).astype(jnp.float32),
                logs[0][:, s * HD : (s + 1) * HD],
                NN,
                precision=lax.Precision.HIGHEST,
            )
            for s in range(CAP)
        ]
        return sum(parts[1:], parts[0])

    if hit_count == 1:
        joined = rows_of(0)
    else:
        levels = [logs_of(i) for i in range(hit_count)]
        top = functools.reduce(jnp.maximum, levels)
        shares = [jnp.exp(level - top) for level in levels]
        total = sum(shares[1:], shares[0])
        pieces = [rows_of(i) for i in range(hit_count)]
        columns = []
        for c in range(HALF):
            part = sum(
                shares[i][:, c : c + 1] * pieces[i][:, c * HD : (c + 1) * HD]
                for i in range(hit_count)
            )
            columns.append(part / total[:, c : c + 1])
        joined = jnp.concatenate(columns, axis=1)
    joined = joined.astype(jnp.bfloat16)
    result[:, :WIDE] = joined[:ROWS]
    result[:, WIDE:] = joined[ROWS:]


def vmem(count):
    return [pl.BlockSpec(memory_space=pltpu.VMEM)] * count


def smem(count):
    return [pl.BlockSpec(memory_space=pltpu.SMEM)] * count


def hbm(count):
    return [pl.BlockSpec(memory_space=pltpu.HBM)] * count


def body(prefix_len, hits, span_block, queries, fresh_keys, fresh_values, cache_keys, cache_values):
    devices = lax.axis_size("cache")
    hit_count = hits.shape[1]
    rows = devices * MSG
    owners = hits.reshape(REQUESTS * hit_count)
    fresh = (owners, queries, fresh_keys, fresh_values)

    def exchange(x):
        return lax.all_to_all(x, "cache", split_axis=0, concat_axis=0, tiled=True)

    def call(kernel, out_shape, name, grant=40, **kw):
        return pl.pallas_call(
            functools.partial(kernel, devices, hit_count),
            out_shape=[jax.ShapeDtypeStruct(*leaf) for leaf in out_shape],
            compiler_params=pltpu.CompilerParams(vmem_limit_bytes=grant * 2**20),
            name=name,
            **kw,
        )

    if hit_count == 1 and devices == 16:
        pairs = rows * (HALF + HALF // 2) * (REGION + rows)
        scalars = [pltpu.SMEM((devices,), jnp.int32)] * 2
        send, places, way = call(
            guest_pack_kernel,
            [
                ((rows, GUEST_MSG), jnp.bfloat16),
                ((2, 4 * ROWS), jnp.int32),
                ((1,), jnp.int32),
            ],
            "pack",
            in_specs=hbm(5),
            out_specs=vmem(2) + smem(1),
            scratch_shapes=[
                pltpu.VMEM((2 * ROWS, WIDE + HD), jnp.bfloat16),
                *[pltpu.SMEM((REQUESTS,), jnp.int32)] * 2,
                *scalars,
                pltpu.SemaphoreType.DMA((6,)),
            ],
        )(
            *(
                pltpu.with_memory_space_constraint(x, pltpu.HBM)
                for x in (owners, prefix_len, queries, fresh_keys, fresh_values)
            )
        )
        got = exchange(send)
        shapes = [((HD, REGION), jnp.bfloat16), ((REGION, 2 * HD), jnp.bfloat16)]
        def chain(form, owners, prefix_len, span_block, places, cache_keys, cache_values):
            ways, height = form
            pinned = [
                pltpu.with_memory_space_constraint(x, pltpu.HBM)
                for x in (owners, prefix_len, span_block)
            ]
            slots = [cache_keys[REGION:], cache_values[REGION:]]
            lent = [
                [
                    lax.ppermute(
                        x[:height], "cache", [(d, d ^ (2 * n)) for d in range(1, devices, 2)]
                    )
                    for x in slots
                ]
                for n in ways
            ]
            prepared = call(
                guest_prep_kernel,
                [((2,), jnp.int32), ((2 * rows, rows), jnp.float32), ((2, REGION), jnp.float32)]
                + shapes
                + [((2 * ROWS, rows), jnp.bfloat16), ((4 * ROWS, rows), jnp.bfloat16)]
                + [((8, HD), jnp.int32)],
                "prep",
                in_specs=smem(2) + vmem(4),
                out_specs=smem(1) + vmem(7),
                scratch_shapes=scalars,
                cost_estimate=pl.CostEstimate(
                    flops=10**6, bytes_accessed=2**22, transcendentals=0
                ),
            )(*pinned, places, cache_keys, cache_values)
            plan = prepared[0]
            for n, borrowed in zip(ways, lent):
                slots = [
                    jnp.where(plan[0] == n, jnp.pad(x, ((0, REGION - height), (0, 0))), y)
                    for x, y in zip(borrowed, slots)
                ]
            swapped = [lax.ppermute(x, "cache", [(d, d ^ 1) for d in range(devices)]) for x in slots]
            guest = call(
                host_kernel, shapes, "host", in_specs=smem(1) + vmem(4), out_specs=vmem(2)
            )(plan, *slots, *swapped)
            return (*prepared[1:], *guest)

        forms = [
            ((), REGION),
            ((1,), REGION // 2),
            ((1,), REGION),
            ((2,), REGION // 2),
            ((2,), REGION),
            ((1, 2, 3), REGION),
        ]
        prepared = lax.switch(
            way.reshape(()),
            [functools.partial(chain, form) for form in forms],
            owners,
            prefix_len,
            span_block,
            places,
            cache_keys,
            cache_values,
        )
        prompt_mask, cached_mask, turned, wide, picks, picks_guest, strips_of = prepared[:7]
        turned_guest, wide_guest = prepared[7:]
        (answer,) = call(
            guest_attend_kernel,
            [((rows, WIDE + WIDE // 2), jnp.bfloat16)],
            "attend",
            in_specs=vmem(8),
            out_specs=vmem(1),
            cost_estimate=pl.CostEstimate(
                flops=4 * pairs * HD, bytes_accessed=8 * rows * WIDE, transcendentals=pairs
            ),
        )(strips_of, prompt_mask, cached_mask, got, turned, wide, turned_guest, wide_guest)
        return call(
            guest_unpack_kernel,
            [((ROWS, HEADS * HD), jnp.bfloat16)],
            "unpack",
            in_specs=vmem(3),
            out_specs=vmem(1),
        )(picks, picks_guest, exchange(answer))[0]
    send, places = call(
        pack_kernel,
        [((rows, CAP * (WIDE + HD)), jnp.bfloat16), ((CAP * hit_count, 2 * ROWS), jnp.int32)],
        "pack",
        in_specs=hbm(4),
        out_specs=vmem(2),
        scratch_shapes=[
            pltpu.VMEM((2 * ROWS, WIDE + HD), jnp.bfloat16),
            pltpu.SMEM((REQUESTS * hit_count,), jnp.int32),
            pltpu.SMEM((devices,), jnp.int32),
            pltpu.SemaphoreType.DMA((5,)),
        ],
    )(*(pltpu.with_memory_space_constraint(x, pltpu.HBM) for x in fresh))
    got = exchange(send)
    busy, prompt_mask, cached_mask, turned, wide, picks = call(
        prep_kernel,
        [
            ((CAP,), jnp.int32),
            ((CAP * rows, rows), jnp.float32),
            ((CAP, REGION), jnp.float32),
            ((HD, CAP * REGION), jnp.bfloat16),
            ((CAP * REGION, 2 * HD), jnp.bfloat16),
            ((CAP * hit_count * 2 * ROWS, rows), jnp.bfloat16),
        ],
        "prep",
        in_specs=smem(2) + vmem(4),
        out_specs=smem(1) + vmem(5),
        cost_estimate=pl.CostEstimate(flops=10**6, bytes_accessed=2**22, transcendentals=0),
    )(owners, prefix_len, span_block, places, cache_keys, cache_values)
    pairs = CAP * rows * HALF * (REGION + rows)
    answers = call(
        attend_kernel,
        [((rows, CAP * WIDE), jnp.bfloat16)]
        + [((rows, CAP * HD), jnp.float32)] * (hit_count > 1),
        "attend",
        in_specs=smem(1) + vmem(5),
        out_specs=vmem(1 + (hit_count > 1)),
        cost_estimate=pl.CostEstimate(
            flops=4 * pairs * HD, bytes_accessed=8 * rows * WIDE, transcendentals=pairs
        ),
    )(busy, prompt_mask, cached_mask, got, turned, wide)
    returned = [exchange(answer) for answer in answers]
    return call(
        unpack_kernel,
        [((ROWS, HEADS * HD), jnp.bfloat16)],
        "unpack",
        in_specs=vmem(1 + len(returned)),
        out_specs=vmem(1),
    )(picks, *returned)[0]


def solution(mesh):
    in_specs = (
        P("groups"),
        P("groups", None),
        P("groups", None),
        P(("groups", "cache"), None),
        P(("groups", "cache"), None),
        P(("groups", "cache"), None),
        P(("groups", "cache"), None),
        P(("groups", "cache"), None),
    )
    out_specs = P(("groups", "cache"), None)
    return jax.shard_map(body, mesh=mesh, in_specs=in_specs, out_specs=out_specs, check_vma=False)
```

```python
import functools
import math

import jax
import jax.numpy as jnp
from jax import lax
from jax.experimental import pallas as pl
from jax.experimental.pallas import tpu as pltpu
from jax.sharding import PartitionSpec as P

HEADS = 16
HD = 128
PAGE = 128
CAP = 2
REQUESTS = 16
TOK_REQ = 4
PAGES_DEV = 16

REGION = PAGES_DEV // CAP * PAGE
HALF = HEADS // 2
MSG = 2 * TOK_REQ
WIDE = HALF * HD
ROWS = REQUESTS * TOK_REQ
STRIP = 256
GUEST_MSG = WIDE + HD + WIDE // 2 + HD
SCALE = HD**-0.5
FLOOR = -1e30
NN = (((1,), (0,)), ((), ()))


def iota(shape, axis):
    return lax.broadcasted_iota(jnp.int32, shape, axis)


def dot(a, b, dims, **kw):
    return lax.dot_general(a, b, dims, preferred_element_type=jnp.float32, **kw)


def pack_kernel(devices, hit_count, owners, q, k, v, send, places, held, hits, count, sems):
    copies = [
        pltpu.make_async_copy(source, held.at[pl.ds(row, ROWS), pl.ds(column, width)], sems.at[n])
        for n, (source, row, column, width) in enumerate(
            [
                (q.at[:, pl.ds(0, WIDE)], 0, 0, WIDE),
                (q.at[:, pl.ds(WIDE, WIDE)], ROWS, 0, WIDE),
                (k, 0, WIDE, HD),
                (v, ROWS, WIDE, HD),
            ]
        )
    ]
    first = pltpu.make_async_copy(owners, hits, sems.at[4])
    first.start()
    for copy in copies:
        copy.start()
    lane = iota((1, 2 * ROWS), 1)
    lane_request = (lane % ROWS) // TOK_REQ
    first.wait()
    for r in range(REQUESTS):
        for i in range(hit_count):
            count[hits[r * hit_count + i]] = 0
    rows = [[jnp.full((1, 2 * ROWS), -4 * MSG, jnp.int32)] * hit_count for _ in range(CAP)]
    for r in range(REQUESTS):
        for i in range(hit_count):
            owner = hits[r * hit_count + i]
            rank = count[owner]
            count[owner] = rank + 1
            for s in range(CAP):
                place = jnp.where(rank == s, owner * MSG, -4 * MSG)
                rows[s][i] = jnp.where(lane_request == r, place, rows[s][i])
    inner = lane // ROWS * TOK_REQ + lane % TOK_REQ
    target = iota((devices * MSG, 2 * ROWS), 0)
    picks = []
    for s in range(CAP):
        chosen = None
        for i in range(hit_count):
            row = rows[s][i] + inner
            places[s * hit_count + i : s * hit_count + i + 1, :] = row
            hit = target == row
            chosen = hit if chosen is None else chosen | hit
        picks.append(jnp.where(chosen, 1.0, 0.0).astype(jnp.bfloat16))
    for copy in copies:
        copy.wait()
    packed = dot(jnp.concatenate(picks, axis=0), held[...], NN).astype(jnp.bfloat16)
    for s in range(CAP):
        rows = slice(s * devices * MSG, (s + 1) * devices * MSG)
        send[:, s * (WIDE + HD) : (s + 1) * (WIDE + HD)] = packed[rows]


def prep_kernel(
    devices, hit_count, hits, prefix_len, span, places, keys, values, *outs
):
    busy, prompt, cached, turned, wide, picks = outs
    rows = iota((devices * MSG, 2 * ROWS), 0)
    for n in range(CAP * hit_count):
        chosen = jnp.where(rows == places[n : n + 1, :], 1.0, 0.0)
        picks[n * 2 * ROWS : (n + 1) * 2 * ROWS, :] = chosen.T.astype(jnp.bfloat16)
    for n in range(0, CAP * REGION, STRIP):
        turned[:, n : n + STRIP] = keys[n : n + STRIP, :].T
    me = lax.axis_index("cache")
    wide[:, :HD] = values[...]
    wide[:, HD:] = jnp.ones((CAP * REGION, HD), jnp.bfloat16)
    for slot in range(CAP):
        seen = jnp.int32(0)
        request = jnp.int32(0)
        which = jnp.int32(0)
        for r in range(REQUESTS):
            for i in range(hit_count):
                mine = hits[r * hit_count + i] == me
                here = mine & (seen == slot)
                request = jnp.where(here, r, request)
                which = jnp.where(here, i, which)
                seen = seen + mine.astype(jnp.int32)
        limit = prefix_len[request] - which * REGION
        blocks = jnp.clip((limit + STRIP - 1) // STRIP, 1, REGION // STRIP)
        busy[slot] = jnp.where(seen > slot, blocks, 0)
        cached[slot : slot + 1, :] = jnp.where(iota((1, REGION), 1) < limit, 0.0, FLOOR)
        prompt_rows(devices, prompt, span, request, slot, hit_count == 1 or which == 0)


def prompt_rows(devices, prompt, span, request, slot, counted):
    total_rows = devices * MSG
    span_row = span[pl.ds(request, 1), :].astype(jnp.float32)
    source = iota((devices, total_rows), 0)
    spread = (iota((devices, total_rows), 1) // MSG == source).astype(jnp.bfloat16)
    spans = jnp.broadcast_to(span_row, (16, devices)).astype(jnp.bfloat16)
    key_span = dot(spans, spread, NN)[:1]
    lane = iota((1, total_rows), 1)
    key_spot = key_span.astype(jnp.int32) * TOK_REQ + lane % TOK_REQ
    is_key = (lane % MSG < TOK_REQ) & counted
    key_spot = jnp.where(is_key, key_spot, devices * TOK_REQ)
    block = 16 * MSG

    def one_block(at):
        row_source = at * 16 + iota((block, devices), 0) // MSG
        mine = iota((block, devices), 1) == row_source
        row_span = jnp.sum(jnp.where(mine, span_row, 0.0), axis=1, keepdims=True)
        row_spot = row_span.astype(jnp.int32) * TOK_REQ + iota((block, 1), 0) % TOK_REQ
        here = pl.ds(slot * total_rows + at * block, block)
        prompt[here, :] = jnp.where(key_spot <= row_spot, 0.0, FLOOR)

    each_block(devices, one_block)


def each_block(devices, one_block):
    blocks = devices // 16
    if blocks == 1:
        one_block(0)
    else:
        pl.loop(0, blocks)(one_block)


def lanes_max(parts):
    pieces = [part[:, n : n + HD] for part in parts for n in range(0, part.shape[1], HD)]
    return jnp.max(functools.reduce(jnp.maximum, pieces), axis=1, keepdims=True)


def attend_kernel(
    devices, hit_count, busy, prompt_mask, cached_mask, got, turned, wide, out, *levels
):
    total_rows = devices * MSG
    block = 16 * MSG
    factor = SCALE * math.log2(math.e)

    def nothing(slot):
        out[:, pl.ds(slot * WIDE, WIDE)] = jnp.zeros((total_rows, WIDE), jnp.bfloat16)
        for lse in levels:
            lse[:, pl.ds(slot * HD, HD)] = jnp.zeros((total_rows, HD), jnp.float32)

    def attend(slot, strips):
        whole = (strips - 1) * STRIP
        base = pl.multiple_of(slot * (WIDE + HD), HD)
        region = pl.multiple_of(slot * REGION, REGION)
        head = pl.ds(region, whole) if whole else None
        tail = pl.ds(pl.multiple_of(region + whole, STRIP), STRIP)
        tail_mask = cached_mask[pl.ds(slot, 1), whole : whole + STRIP]
        prompt_keys = got[:, pl.ds(base + WIDE, HD)].astype(jnp.float32)
        moved = pltpu.roll(prompt_keys, total_rows - TOK_REQ, 0)
        prompt_keys = prompt_keys.T.astype(jnp.bfloat16)
        prompt_values = jnp.concatenate(
            [moved.astype(jnp.bfloat16), jnp.ones((total_rows, HD), jnp.bfloat16)], axis=1
        )

        def one_block(at):
            here = pl.ds(at * block, block)
            prompt_bias = prompt_mask[pl.ds(slot * total_rows + at * block, block), :]
            prompt_bias = jnp.concatenate([prompt_bias, prompt_bias], axis=0)
            lane = iota((block, HD), 1)

            def scores(c):
                pair = jnp.concatenate(
                    [got[here, pl.ds(base + (c + n) * HD, HD)] for n in range(2)], axis=0
                )
                parts = [dot(pair, turned[:, head], NN)] if whole else []
                parts.append(dot(pair, turned[:, tail], NN) + tail_mask)
                parts.append(dot(pair, prompt_keys, NN) + prompt_bias)
                return parts

            logs = jnp.zeros((block, HD), jnp.float32)
            parts = scores(0)
            for c in range(0, HALF, 2):
                later = scores(c + 2) if c + 2 < HALF else None
                top = lanes_max(parts)
                if hit_count > 1:
                    top = jnp.maximum(top, 0.1 * FLOOR)
                parts = [jnp.exp2((x - top) * factor).astype(jnp.bfloat16) for x in parts]
                summed = dot(parts[-1], prompt_values, NN) + dot(parts[-2], wide[tail, :], NN)
                if whole:
                    summed = summed + dot(parts[0], wide[head, :], NN)
                totals = summed[:, HD:]
                if hit_count > 1:
                    totals = jnp.maximum(totals, 1.0)
                    level = top * SCALE + jnp.log(totals)
                    logs = jnp.where(lane == c, level[:block], logs)
                    logs = jnp.where(lane == c + 1, level[block:], logs)
                result = (summed[:, :HD] / totals).astype(jnp.bfloat16)
                for n in range(2):
                    column = pl.multiple_of(slot * WIDE + (c + n) * HD, HD)
                    out[here, pl.ds(column, HD)] = result[n * block : (n + 1) * block]
                parts = later
            for lse in levels:
                lse[here, pl.ds(pl.multiple_of(slot * HD, HD), HD)] = logs

        each_block(devices, one_block)

    @pl.loop(0, CAP)
    def _(slot):
        strips = busy[slot]
        pl.when(strips == 0)(lambda: nothing(slot))
        for count in range(1, REGION // STRIP + 1):
            pl.when(strips == count)(functools.partial(attend, slot, count))


def owner_ranks(devices, owners, count):
    for d in range(devices):
        count[d] = 0
    ranks = []
    for r in range(REQUESTS):
        owner = owners[r]
        ranks.append(count[owner])
        count[owner] = ranks[r] + 1
    return ranks


def guest_plan(devices, count, host):
    chips = devices // 2
    seconds = [count[d] > 1 for d in range(devices)]
    none = [jnp.logical_not(seconds[2 * x] | seconds[2 * x + 1]) for x in range(chips)]
    lends = []
    for x in range(chips):
        other = jnp.where(none[x ^ 1], 1, jnp.where(none[x ^ 2], 2, 3))
        lends.append(jnp.where(seconds[2 * x] & seconds[2 * x + 1], other, 0))
        host[2 * x] = jnp.int32(x)
        host[2 * x + 1] = lends[x] ^ x
    return lends


def guest_pack_kernel(devices, hit_count, owners, lengths, q, k, v, *refs):
    send, places, way, held, hits, prefix_len, count, host, sems = refs
    half = WIDE // 2
    moves = [
        (owners, hits),
        (q.at[:, pl.ds(0, WIDE)], held.at[pl.ds(0, ROWS), pl.ds(0, WIDE)]),
        (q.at[:, pl.ds(WIDE, WIDE)], held.at[pl.ds(ROWS, ROWS), pl.ds(0, WIDE)]),
        (k, held.at[pl.ds(0, ROWS), pl.ds(WIDE, HD)]),
        (v, held.at[pl.ds(ROWS, ROWS), pl.ds(WIDE, HD)]),
        (lengths, prefix_len),
    ]
    copies = [pltpu.make_async_copy(a, b, sems.at[n]) for n, (a, b) in enumerate(moves)]
    for copy in copies:
        copy.start()
    lane = iota((1, 4 * ROWS), 1)
    lane_request = lane % ROWS // TOK_REQ
    part = lane // ROWS * TOK_REQ
    nowhere = jnp.full((1, 4 * ROWS), -4 * MSG, jnp.int32)
    target = iota((devices * MSG, 2 * ROWS), 0)
    copies[0].wait()
    ranks = owner_ranks(devices, hits, count)
    own = nowhere
    for r in range(REQUESTS):
        place = jnp.where(ranks[r] == 0, hits[r] * MSG, -4 * MSG)
        own = jnp.where(lane_request == r, place, own)
    own = own + lane % TOK_REQ + part

    def rows_of(chosen, first, width):
        pick = jnp.where(chosen, 1.0, 0.0).astype(jnp.bfloat16)
        return dot(pick, held[:, first : first + width], NN)

    for copy in copies[1:]:
        copy.wait()
    rows = rows_of(target == own[:, : 2 * ROWS], 0, WIDE + HD)
    send[:, : WIDE + HD] = rows.astype(jnp.bfloat16)
    lends = guest_plan(devices, count, host)
    guest = nowhere
    longest = jnp.int32(0)
    for r in range(REQUESTS):
        chip = host[hits[r]]
        place = jnp.where(ranks[r] == 1, chip * 2 * MSG, -4 * MSG)
        guest = jnp.where(lane_request == r, place, guest)
        lent = (ranks[r] == 1) & (chip != hits[r] // 2)
        longest = jnp.maximum(longest, jnp.where(lent, prefix_len[r], 0))
    guest = guest + lane % TOK_REQ
    places[0:1, :] = own
    places[1:2, :] = guest + part
    guest, part = guest[:, : 2 * ROWS], part[:, : 2 * ROWS]
    rows = rows_of(target == guest + 2 * part, 0, half)
    rows = rows + rows_of(target == guest + 2 * part + TOK_REQ, half, half)
    send[:, WIDE + HD : WIDE + HD + half] = rows.astype(jnp.bfloat16)
    both = (target == guest + part) | (target == guest + MSG + part)
    send[:, WIDE + HD + half :] = rows_of(both, WIDE, HD).astype(jnp.bfloat16)
    used = [
        functools.reduce(jnp.logical_or, [lend == n for lend in lends]) for n in range(1, 4)
    ]
    mixed = used[2] | (used[0] & used[1])
    kind = jnp.where(mixed, 5, jnp.where(used[0], 1, jnp.where(used[1], 3, 0)))
    whole = (longest > REGION // 2) & (kind > 0) & (kind < 5)
    way[0] = kind + jnp.where(whole, 1, 0)


def guest_prep_kernel(
    devices, hit_count, hits, prefix_len, span, places, keys, values, *refs
):
    plan, prompt, cached, turned, wide, picks, picks_guest, strips_of, count, host = refs
    me = lax.axis_index("cache")
    chip = me // 2
    ranks = owner_ranks(devices, hits, count)
    guest_plan(devices, count, host)
    rows = iota((devices * MSG, 4 * ROWS), 0)
    chosen = jnp.where(rows[:, : 2 * ROWS] == places[0:1, : 2 * ROWS], 1.0, 0.0)
    picks[...] = chosen.T.astype(jnp.bfloat16)
    chosen = jnp.where(rows == places[1:2, :], 1.0, 0.0)
    picks_guest[...] = chosen.T.astype(jnp.bfloat16)
    widen(keys[:REGION, :], values[:REGION, :], turned, wide)
    first, guest, source = jnp.int32(-1), jnp.int32(-1), jnp.int32(0)
    for r in range(REQUESTS):
        owner = hits[r]
        here = (ranks[r] == 1) & (host[owner] == chip)
        first = jnp.where((ranks[r] == 0) & (owner == me), r, first)
        guest = jnp.where(here, r, guest)
        source = jnp.where(here, owner, source)
    core = me % 2
    from_first_core = jnp.where(source == 2 * chip, 1, 0)
    plan[0] = jnp.where(core == 1, (source // 2) ^ chip, 0)
    plan[1] = jnp.where(core == from_first_core, 1, 0)
    for job, found in enumerate((first, guest)):
        request = jnp.maximum(found, 0)
        limit = prefix_len[request]
        strips = jnp.clip((limit + STRIP - 1) // STRIP, 1, REGION // STRIP)
        strips_of[job : job + 1, :] = jnp.full((1, HD), jnp.where(found >= 0, strips, 0))
        cached[job : job + 1, :] = jnp.where(iota((1, REGION), 1) < limit, 0.0, FLOOR)
        prompt_rows(devices, prompt, span, request, job, True)


def widen(keys, values, turned, wide):
    for n in range(0, REGION, STRIP):
        turned[:, n : n + STRIP] = keys[n : n + STRIP].T
    wide[:, :HD] = values
    wide[:, HD:] = jnp.ones((REGION, HD), jnp.bfloat16)


def host_kernel(devices, hit_count, plan, *refs):
    mine, other, turned, wide = refs[:2], refs[2:4], refs[4], refs[5]
    for choice, (keys, values) in enumerate((mine, other)):

        @pl.when(plan[1] == choice)
        def _():
            widen(keys[...], values[...], turned, wide)


def guest_attend_kernel(
    devices, hit_count, strips_of, prompt_mask, cached_mask, got, turned, wide, *refs
):
    turned_guest, wide_guest, out = refs
    jobs = [
        (0, 0, HALF, turned, wide),
        (WIDE + HD, WIDE, HALF // 2, turned_guest, wide_guest),
    ]
    for job, (base, first, blocks, keys, values) in enumerate(jobs):
        strips = strips_of[job, 0]

        @pl.when(strips == 0)
        def _():
            empty = jnp.zeros((devices * MSG, blocks * HD), jnp.bfloat16)
            out[:, first : first + blocks * HD] = empty

        for count in range(1, REGION // STRIP + 1):

            @pl.when(strips == count)
            def _():
                whole = (count - 1) * STRIP
                mask = prompt_mask[job * devices * MSG : (job + 1) * devices * MSG, :]
                attend_rows(
                    got,
                    base,
                    blocks,
                    slice(0, devices * MSG),
                    prompt_parts(got[:, base + blocks * HD : base + (blocks + 1) * HD]),
                    mask,
                    cached_mask[job : job + 1, whole : whole + STRIP],
                    keys[:, :whole] if whole else None,
                    keys[:, whole : whole + STRIP],
                    values[:whole, :] if whole else None,
                    values[whole : whole + STRIP, :],
                    out,
                    first,
                )


def prompt_parts(rows):
    height = rows.shape[0]
    wide = rows.astype(jnp.float32)
    moved = pltpu.roll(wide, height - TOK_REQ, 0).astype(jnp.bfloat16)
    values = jnp.concatenate([moved, jnp.ones((height, HD), jnp.bfloat16)], axis=1)
    return wide.T.astype(jnp.bfloat16), values


def attend_rows(
    got, base, blocks, here, prompt, mask, tail_mask, head, tail, head_values, tail_values, out, first
):
    prompt_keys, prompt_values = prompt
    factor = SCALE * math.log2(math.e)
    mask = jnp.concatenate([mask, mask], axis=0)
    height = mask.shape[0] // 2

    def scores(c):
        pair = jnp.concatenate(
            [got[here, base + (c + n) * HD : base + (c + n + 1) * HD] for n in range(2)], axis=0
        )
        parts = [] if head is None else [dot(pair, head, NN)]
        parts.append(dot(pair, tail, NN) + tail_mask)
        parts.append(dot(pair, prompt_keys, NN) + mask)
        return parts

    parts = scores(0)
    for c in range(0, blocks, 2):
        later = scores(c + 2) if c + 2 < blocks else None
        top = lanes_max(parts)
        parts = [jnp.exp2((x - top) * factor).astype(jnp.bfloat16) for x in parts]
        summed = dot(parts[-1], prompt_values, NN) + dot(parts[-2], tail_values, NN)
        if head is not None:
            summed = summed + dot(parts[0], head_values, NN)
        result = (summed[:, :HD] / summed[:, HD:]).astype(jnp.bfloat16)
        for n in range(2):
            column = first + (c + n) * HD
            out[here, column : column + HD] = result[n * height : (n + 1) * height]
        parts = later


def guest_unpack_kernel(devices, hit_count, picks, picks_guest, outs, result, held, sems):
    half = WIDE // 2
    copies = []
    for n in range(2):
        own = dot(picks[n * ROWS : (n + 1) * ROWS, :], outs[:, :WIDE], NN)
        for g in (2 * n, 2 * n + 1):
            guest = dot(picks_guest[g * ROWS : (g + 1) * ROWS, :], outs[:, WIDE:], NN)
            rows = own[:, g % 2 * half : (g % 2 + 1) * half] + guest
            held[:, g * half : (g + 1) * half] = rows.astype(jnp.bfloat16)
        here = pl.ds(n * WIDE, WIDE)
        copies.append(pltpu.make_async_copy(held.at[:, here], result.at[:, here], sems.at[n]))
        copies[n].start()
    for copy in copies:
        copy.wait()


def unpack_kernel(devices, hit_count, picks, *refs):
    outs, logs, result = refs[0], refs[1:-1], refs[-1]

    def chosen(s, i):
        place = s * hit_count + i
        return picks[place * 2 * ROWS : (place + 1) * 2 * ROWS, :]

    def rows_of(i):
        parts = [
            dot(chosen(s, i), outs[:, s * WIDE : (s + 1) * WIDE], NN)
            for s in range(CAP)
        ]
        return sum(parts[1:], parts[0])

    def logs_of(i):
        parts = [
            dot(
                chosen(s, i).astype(jnp.float32),
                logs[0][:, s * HD : (s + 1) * HD],
                NN,
                precision=lax.Precision.HIGHEST,
            )
            for s in range(CAP)
        ]
        return sum(parts[1:], parts[0])

    if hit_count == 1:
        joined = rows_of(0)
    else:
        levels = [logs_of(i) for i in range(hit_count)]
        top = functools.reduce(jnp.maximum, levels)
        shares = [jnp.exp(level - top) for level in levels]
        total = sum(shares[1:], shares[0])
        pieces = [rows_of(i) for i in range(hit_count)]
        columns = []
        for c in range(HALF):
            part = sum(
                shares[i][:, c : c + 1] * pieces[i][:, c * HD : (c + 1) * HD]
                for i in range(hit_count)
            )
            columns.append(part / total[:, c : c + 1])
        joined = jnp.concatenate(columns, axis=1)
    joined = joined.astype(jnp.bfloat16)
    result[:, :WIDE] = joined[:ROWS]
    result[:, WIDE:] = joined[ROWS:]


def vmem(count):
    return [pl.BlockSpec(memory_space=pltpu.VMEM)] * count


def smem(count):
    return [pl.BlockSpec(memory_space=pltpu.SMEM)] * count


def hbm(count):
    return [pl.BlockSpec(memory_space=pltpu.HBM)] * count


def body(prefix_len, hits, span_block, queries, fresh_keys, fresh_values, cache_keys, cache_values):
    devices = lax.axis_size("cache")
    hit_count = hits.shape[1]
    rows = devices * MSG
    owners = hits.reshape(REQUESTS * hit_count)
    fresh = (owners, queries, fresh_keys, fresh_values)

    def exchange(x):
        return lax.all_to_all(x, "cache", split_axis=0, concat_axis=0, tiled=True)

    def call(kernel, out_shape, name, grant=40, **kw):
        return pl.pallas_call(
            functools.partial(kernel, devices, hit_count),
            out_shape=[
                jax.ShapeDtypeStruct(*leaf) if isinstance(leaf, tuple) else leaf
                for leaf in out_shape
            ],
            compiler_params=pltpu.CompilerParams(vmem_limit_bytes=grant * 2**20),
            name=name,
            **kw,
        )

    if hit_count == 1 and devices == 16:
        pairs = rows * (HALF + HALF // 2) * (REGION + rows)
        scalars = [pltpu.SMEM((devices,), jnp.int32)] * 2
        send, places, way = call(
            guest_pack_kernel,
            [
                pltpu.VMEM((rows, GUEST_MSG), jnp.bfloat16),
                ((2, 4 * ROWS), jnp.int32),
                ((1,), jnp.int32),
            ],
            "pack",
            in_specs=hbm(5),
            out_specs=vmem(2) + smem(1),
            scratch_shapes=[
                pltpu.VMEM((2 * ROWS, WIDE + HD), jnp.bfloat16),
                *[pltpu.SMEM((REQUESTS,), jnp.int32)] * 2,
                *scalars,
                pltpu.SemaphoreType.DMA((6,)),
            ],
        )(
            *(
                pltpu.with_memory_space_constraint(x, pltpu.HBM)
                for x in (owners, prefix_len, queries, fresh_keys, fresh_values)
            )
        )
        got = exchange(send)
        shapes = [((HD, REGION), jnp.bfloat16), ((REGION, 2 * HD), jnp.bfloat16)]
        def chain(form, owners, prefix_len, span_block, places, cache_keys, cache_values):
            ways, height = form
            pinned = [
                pltpu.with_memory_space_constraint(x, pltpu.HBM)
                for x in (owners, prefix_len, span_block)
            ]
            slots = [cache_keys[REGION:], cache_values[REGION:]]
            lent = [
                [
                    lax.ppermute(
                        x[:height], "cache", [(d, d ^ (2 * n)) for d in range(1, devices, 2)]
                    )
                    for x in slots
                ]
                for n in ways
            ]
            prepared = call(
                guest_prep_kernel,
                [((2,), jnp.int32), ((2 * rows, rows), jnp.float32), ((2, REGION), jnp.float32)]
                + shapes
                + [((2 * ROWS, rows), jnp.bfloat16), ((4 * ROWS, rows), jnp.bfloat16)]
                + [((8, HD), jnp.int32)],
                "prep",
                grant=12,
                in_specs=smem(2) + vmem(4),
                out_specs=smem(1) + vmem(7),
                scratch_shapes=scalars,
                cost_estimate=pl.CostEstimate(
                    flops=10**6, bytes_accessed=2**22, transcendentals=0
                ),
            )(*pinned, places, cache_keys, cache_values)
            plan = prepared[0]
            for n, borrowed in zip(ways, lent):
                slots = [
                    jnp.where(plan[0] == n, jnp.pad(x, ((0, REGION - height), (0, 0))), y)
                    for x, y in zip(borrowed, slots)
                ]
            swapped = [lax.ppermute(x, "cache", [(d, d ^ 1) for d in range(devices)]) for x in slots]
            guest = call(
                host_kernel,
                shapes,
                "host",
                grant=12,
                in_specs=smem(1) + vmem(4),
                out_specs=vmem(2),
            )(plan, *slots, *swapped)
            return (*prepared[1:], *guest)

        forms = [
            ((), REGION),
            ((1,), REGION // 2),
            ((1,), REGION),
            ((2,), REGION // 2),
            ((2,), REGION),
            ((1, 2, 3), REGION),
        ]
        prepared = lax.switch(
            way.reshape(()),
            [functools.partial(chain, form) for form in forms],
            owners,
            prefix_len,
            span_block,
            places,
            cache_keys,
            cache_values,
        )
        prompt_mask, cached_mask, turned, wide, picks, picks_guest, strips_of = prepared[:7]
        turned_guest, wide_guest = prepared[7:]
        (answer,) = call(
            guest_attend_kernel,
            [((rows, WIDE + WIDE // 2), jnp.bfloat16)],
            "attend",
            in_specs=vmem(8),
            out_specs=vmem(1),
            cost_estimate=pl.CostEstimate(
                flops=4 * pairs * HD, bytes_accessed=8 * rows * WIDE, transcendentals=pairs
            ),
        )(strips_of, prompt_mask, cached_mask, got, turned, wide, turned_guest, wide_guest)
        return call(
            guest_unpack_kernel,
            [((ROWS, HEADS * HD), jnp.bfloat16)],
            "unpack",
            in_specs=vmem(3),
            out_specs=hbm(1),
            scratch_shapes=[
                pltpu.VMEM((ROWS, HEADS * HD), jnp.bfloat16),
                pltpu.SemaphoreType.DMA((2,)),
            ],
        )(picks, picks_guest, exchange(answer))[0]
    send, places = call(
        pack_kernel,
        [((rows, CAP * (WIDE + HD)), jnp.bfloat16), ((CAP * hit_count, 2 * ROWS), jnp.int32)],
        "pack",
        in_specs=hbm(4),
        out_specs=vmem(2),
        scratch_shapes=[
            pltpu.VMEM((2 * ROWS, WIDE + HD), jnp.bfloat16),
            pltpu.SMEM((REQUESTS * hit_count,), jnp.int32),
            pltpu.SMEM((devices,), jnp.int32),
            pltpu.SemaphoreType.DMA((5,)),
        ],
    )(*(pltpu.with_memory_space_constraint(x, pltpu.HBM) for x in fresh))
    got = exchange(send)
    busy, prompt_mask, cached_mask, turned, wide, picks = call(
        prep_kernel,
        [
            ((CAP,), jnp.int32),
            ((CAP * rows, rows), jnp.float32),
            ((CAP, REGION), jnp.float32),
            ((HD, CAP * REGION), jnp.bfloat16),
            ((CAP * REGION, 2 * HD), jnp.bfloat16),
            ((CAP * hit_count * 2 * ROWS, rows), jnp.bfloat16),
        ],
        "prep",
        in_specs=smem(2) + vmem(4),
        out_specs=smem(1) + vmem(5),
        cost_estimate=pl.CostEstimate(flops=10**6, bytes_accessed=2**22, transcendentals=0),
    )(owners, prefix_len, span_block, places, cache_keys, cache_values)
    pairs = CAP * rows * HALF * (REGION + rows)
    answers = call(
        attend_kernel,
        [((rows, CAP * WIDE), jnp.bfloat16)]
        + [((rows, CAP * HD), jnp.float32)] * (hit_count > 1),
        "attend",
        in_specs=smem(1) + vmem(5),
        out_specs=vmem(1 + (hit_count > 1)),
        cost_estimate=pl.CostEstimate(
            flops=4 * pairs * HD, bytes_accessed=8 * rows * WIDE, transcendentals=pairs
        ),
    )(busy, prompt_mask, cached_mask, got, turned, wide)
    returned = [exchange(answer) for answer in answers]
    return call(
        unpack_kernel,
        [((ROWS, HEADS * HD), jnp.bfloat16)],
        "unpack",
        in_specs=vmem(1 + len(returned)),
        out_specs=vmem(1),
    )(picks, *returned)[0]


def solution(mesh):
    in_specs = (
        P("groups"),
        P("groups", None),
        P("groups", None),
        P(("groups", "cache"), None),
        P(("groups", "cache"), None),
        P(("groups", "cache"), None),
        P(("groups", "cache"), None),
        P(("groups", "cache"), None),
    )
    out_specs = P(("groups", "cache"), None)
    return jax.shard_map(body, mesh=mesh, in_specs=in_specs, out_specs=out_specs, check_vma=False)
```

```python
import functools
import math

import jax
import jax.numpy as jnp
from jax import lax
from jax.experimental import pallas as pl
from jax.experimental.pallas import tpu as pltpu
from jax.sharding import PartitionSpec as P

HEADS = 16
HD = 128
PAGE = 128
CAP = 2
REQUESTS = 16
TOK_REQ = 4
PAGES_DEV = 16

REGION = PAGES_DEV // CAP * PAGE
HALF = HEADS // 2
MSG = 2 * TOK_REQ
WIDE = HALF * HD
ROWS = REQUESTS * TOK_REQ
STRIP = 256
GUEST_MSG = WIDE + HD + WIDE // 2 + HD
SCALE = HD**-0.5
FLOOR = -1e30
NN = (((1,), (0,)), ((), ()))


def iota(shape, axis):
    return lax.broadcasted_iota(jnp.int32, shape, axis)


def dot(a, b, dims, **kw):
    return lax.dot_general(a, b, dims, preferred_element_type=jnp.float32, **kw)


def pack_kernel(devices, hit_count, owners, q, k, v, send, places, held, hits, count, sems):
    copies = [
        pltpu.make_async_copy(source, held.at[pl.ds(row, ROWS), pl.ds(column, width)], sems.at[n])
        for n, (source, row, column, width) in enumerate(
            [
                (q.at[:, pl.ds(0, WIDE)], 0, 0, WIDE),
                (q.at[:, pl.ds(WIDE, WIDE)], ROWS, 0, WIDE),
                (k, 0, WIDE, HD),
                (v, ROWS, WIDE, HD),
            ]
        )
    ]
    first = pltpu.make_async_copy(owners, hits, sems.at[4])
    first.start()
    for copy in copies:
        copy.start()
    lane = iota((1, 2 * ROWS), 1)
    lane_request = (lane % ROWS) // TOK_REQ
    first.wait()
    for r in range(REQUESTS):
        for i in range(hit_count):
            count[hits[r * hit_count + i]] = 0
    rows = [[jnp.full((1, 2 * ROWS), -4 * MSG, jnp.int32)] * hit_count for _ in range(CAP)]
    for r in range(REQUESTS):
        for i in range(hit_count):
            owner = hits[r * hit_count + i]
            rank = count[owner]
            count[owner] = rank + 1
            for s in range(CAP):
                place = jnp.where(rank == s, owner * MSG, -4 * MSG)
                rows[s][i] = jnp.where(lane_request == r, place, rows[s][i])
    inner = lane // ROWS * TOK_REQ + lane % TOK_REQ
    target = iota((devices * MSG, 2 * ROWS), 0)
    picks = []
    for s in range(CAP):
        chosen = None
        for i in range(hit_count):
            row = rows[s][i] + inner
            places[s * hit_count + i : s * hit_count + i + 1, :] = row
            hit = target == row
            chosen = hit if chosen is None else chosen | hit
        picks.append(jnp.where(chosen, 1.0, 0.0).astype(jnp.bfloat16))
    for copy in copies:
        copy.wait()
    packed = dot(jnp.concatenate(picks, axis=0), held[...], NN).astype(jnp.bfloat16)
    for s in range(CAP):
        rows = slice(s * devices * MSG, (s + 1) * devices * MSG)
        send[:, s * (WIDE + HD) : (s + 1) * (WIDE + HD)] = packed[rows]


def prep_kernel(
    devices, hit_count, hits, prefix_len, span, places, keys, values, *outs
):
    busy, prompt, cached, turned, wide, picks = outs
    rows = iota((devices * MSG, 2 * ROWS), 0)
    for n in range(CAP * hit_count):
        chosen = jnp.where(rows == places[n : n + 1, :], 1.0, 0.0)
        picks[n * 2 * ROWS : (n + 1) * 2 * ROWS, :] = chosen.T.astype(jnp.bfloat16)
    for n in range(0, CAP * REGION, STRIP):
        turned[:, n : n + STRIP] = keys[n : n + STRIP, :].T
    me = lax.axis_index("cache")
    wide[:, :HD] = values[...]
    wide[:, HD:] = jnp.ones((CAP * REGION, HD), jnp.bfloat16)
    for slot in range(CAP):
        seen = jnp.int32(0)
        request = jnp.int32(0)
        which = jnp.int32(0)
        for r in range(REQUESTS):
            for i in range(hit_count):
                mine = hits[r * hit_count + i] == me
                here = mine & (seen == slot)
                request = jnp.where(here, r, request)
                which = jnp.where(here, i, which)
                seen = seen + mine.astype(jnp.int32)
        limit = prefix_len[request] - which * REGION
        blocks = jnp.clip((limit + STRIP - 1) // STRIP, 1, REGION // STRIP)
        busy[slot] = jnp.where(seen > slot, blocks, 0)
        cached[slot : slot + 1, :] = jnp.where(iota((1, REGION), 1) < limit, 0.0, FLOOR)
        prompt_rows(devices, prompt, span, request, slot, hit_count == 1 or which == 0)


def prompt_rows(devices, prompt, span, request, slot, counted):
    total_rows = devices * MSG
    span_row = span[pl.ds(request, 1), :].astype(jnp.float32)
    source = iota((devices, total_rows), 0)
    spread = (iota((devices, total_rows), 1) // MSG == source).astype(jnp.bfloat16)
    spans = jnp.broadcast_to(span_row, (16, devices)).astype(jnp.bfloat16)
    key_span = dot(spans, spread, NN)[:1]
    lane = iota((1, total_rows), 1)
    key_spot = key_span.astype(jnp.int32) * TOK_REQ + lane % TOK_REQ
    is_key = (lane % MSG < TOK_REQ) & counted
    key_spot = jnp.where(is_key, key_spot, devices * TOK_REQ)
    block = 16 * MSG

    def one_block(at):
        row_source = at * 16 + iota((block, devices), 0) // MSG
        mine = iota((block, devices), 1) == row_source
        row_span = jnp.sum(jnp.where(mine, span_row, 0.0), axis=1, keepdims=True)
        row_spot = row_span.astype(jnp.int32) * TOK_REQ + iota((block, 1), 0) % TOK_REQ
        here = pl.ds(slot * total_rows + at * block, block)
        prompt[here, :] = jnp.where(key_spot <= row_spot, 0.0, FLOOR)

    each_block(devices, one_block)


def each_block(devices, one_block):
    blocks = devices // 16
    if blocks == 1:
        one_block(0)
    else:
        pl.loop(0, blocks)(one_block)


def lanes_max(parts):
    pieces = [part[:, n : n + HD] for part in parts for n in range(0, part.shape[1], HD)]
    return jnp.max(functools.reduce(jnp.maximum, pieces), axis=1, keepdims=True)


def attend_kernel(
    devices, hit_count, busy, prompt_mask, cached_mask, got, turned, wide, out, *levels
):
    total_rows = devices * MSG
    block = 16 * MSG
    factor = SCALE * math.log2(math.e)

    def nothing(slot):
        out[:, pl.ds(slot * WIDE, WIDE)] = jnp.zeros((total_rows, WIDE), jnp.bfloat16)
        for lse in levels:
            lse[:, pl.ds(slot * HD, HD)] = jnp.zeros((total_rows, HD), jnp.float32)

    def attend(slot, strips):
        whole = (strips - 1) * STRIP
        base = pl.multiple_of(slot * (WIDE + HD), HD)
        region = pl.multiple_of(slot * REGION, REGION)
        head = pl.ds(region, whole) if whole else None
        tail = pl.ds(pl.multiple_of(region + whole, STRIP), STRIP)
        tail_mask = cached_mask[pl.ds(slot, 1), whole : whole + STRIP]
        prompt_keys = got[:, pl.ds(base + WIDE, HD)].astype(jnp.float32)
        moved = pltpu.roll(prompt_keys, total_rows - TOK_REQ, 0)
        prompt_keys = prompt_keys.T.astype(jnp.bfloat16)
        prompt_values = jnp.concatenate(
            [moved.astype(jnp.bfloat16), jnp.ones((total_rows, HD), jnp.bfloat16)], axis=1
        )

        def one_block(at):
            here = pl.ds(at * block, block)
            prompt_bias = prompt_mask[pl.ds(slot * total_rows + at * block, block), :]
            prompt_bias = jnp.concatenate([prompt_bias, prompt_bias], axis=0)
            lane = iota((block, HD), 1)

            def scores(c):
                pair = jnp.concatenate(
                    [got[here, pl.ds(base + (c + n) * HD, HD)] for n in range(2)], axis=0
                )
                parts = [dot(pair, turned[:, head], NN)] if whole else []
                parts.append(dot(pair, turned[:, tail], NN) + tail_mask)
                parts.append(dot(pair, prompt_keys, NN) + prompt_bias)
                return parts

            logs = jnp.zeros((block, HD), jnp.float32)
            parts = scores(0)
            for c in range(0, HALF, 2):
                later = scores(c + 2) if c + 2 < HALF else None
                top = lanes_max(parts)
                if hit_count > 1:
                    top = jnp.maximum(top, 0.1 * FLOOR)
                parts = [jnp.exp2((x - top) * factor).astype(jnp.bfloat16) for x in parts]
                summed = dot(parts[-1], prompt_values, NN) + dot(parts[-2], wide[tail, :], NN)
                if whole:
                    summed = summed + dot(parts[0], wide[head, :], NN)
                totals = summed[:, HD:]
                if hit_count > 1:
                    totals = jnp.maximum(totals, 1.0)
                    level = top * SCALE + jnp.log(totals)
                    logs = jnp.where(lane == c, level[:block], logs)
                    logs = jnp.where(lane == c + 1, level[block:], logs)
                result = (summed[:, :HD] / totals).astype(jnp.bfloat16)
                for n in range(2):
                    column = pl.multiple_of(slot * WIDE + (c + n) * HD, HD)
                    out[here, pl.ds(column, HD)] = result[n * block : (n + 1) * block]
                parts = later
            for lse in levels:
                lse[here, pl.ds(pl.multiple_of(slot * HD, HD), HD)] = logs

        each_block(devices, one_block)

    @pl.loop(0, CAP)
    def _(slot):
        strips = busy[slot]
        pl.when(strips == 0)(lambda: nothing(slot))
        for count in range(1, REGION // STRIP + 1):
            pl.when(strips == count)(functools.partial(attend, slot, count))


def owner_ranks(devices, owners, count):
    for d in range(devices):
        count[d] = 0
    ranks = []
    for r in range(REQUESTS):
        owner = owners[r]
        ranks.append(count[owner])
        count[owner] = ranks[r] + 1
    return ranks


def guest_plan(devices, count, host):
    chips = devices // 2
    seconds = [count[d] > 1 for d in range(devices)]
    none = [jnp.logical_not(seconds[2 * x] | seconds[2 * x + 1]) for x in range(chips)]
    lends = []
    for x in range(chips):
        other = jnp.where(none[x ^ 1], 1, jnp.where(none[x ^ 2], 2, 3))
        lends.append(jnp.where(seconds[2 * x] & seconds[2 * x + 1], other, 0))
        host[2 * x] = jnp.int32(x)
        host[2 * x + 1] = lends[x] ^ x
    return lends


def guest_pack_kernel(devices, hit_count, owners, lengths, q, k, v, *refs):
    send, places, way, held, hits, prefix_len, count, host, sems = refs
    half = WIDE // 2
    moves = [
        (owners, hits),
        (q.at[:, pl.ds(0, WIDE)], held.at[pl.ds(0, ROWS), pl.ds(0, WIDE)]),
        (q.at[:, pl.ds(WIDE, WIDE)], held.at[pl.ds(ROWS, ROWS), pl.ds(0, WIDE)]),
        (k, held.at[pl.ds(0, ROWS), pl.ds(WIDE, HD)]),
        (v, held.at[pl.ds(ROWS, ROWS), pl.ds(WIDE, HD)]),
        (lengths, prefix_len),
    ]
    copies = [pltpu.make_async_copy(a, b, sems.at[n]) for n, (a, b) in enumerate(moves)]
    for copy in copies:
        copy.start()
    lane = iota((1, 4 * ROWS), 1)
    lane_request = lane % ROWS // TOK_REQ
    part = lane // ROWS * TOK_REQ
    nowhere = jnp.full((1, 4 * ROWS), -4 * MSG, jnp.int32)
    target = iota((devices * MSG, 2 * ROWS), 0)
    copies[0].wait()
    ranks = owner_ranks(devices, hits, count)
    own = nowhere
    for r in range(REQUESTS):
        place = jnp.where(ranks[r] == 0, hits[r] * MSG, -4 * MSG)
        own = jnp.where(lane_request == r, place, own)
    own = own + lane % TOK_REQ + part

    def rows_of(chosen, first, width):
        pick = jnp.where(chosen, 1.0, 0.0).astype(jnp.bfloat16)
        return dot(pick, held[:, first : first + width], NN)

    for copy in copies[1:]:
        copy.wait()
    rows = rows_of(target == own[:, : 2 * ROWS], 0, WIDE + HD)
    send[:, : WIDE + HD] = rows.astype(jnp.bfloat16)
    lends = guest_plan(devices, count, host)
    guest = nowhere
    longest = jnp.int32(0)
    for r in range(REQUESTS):
        chip = host[hits[r]]
        place = jnp.where(ranks[r] == 1, chip * 2 * MSG, -4 * MSG)
        guest = jnp.where(lane_request == r, place, guest)
        lent = (ranks[r] == 1) & (chip != hits[r] // 2)
        longest = jnp.maximum(longest, jnp.where(lent, prefix_len[r], 0))
    guest = guest + lane % TOK_REQ
    places[0:1, :] = own
    places[1:2, :] = guest + part
    guest, part = guest[:, : 2 * ROWS], part[:, : 2 * ROWS]
    rows = rows_of(target == guest + 2 * part, 0, half)
    rows = rows + rows_of(target == guest + 2 * part + TOK_REQ, half, half)
    send[:, WIDE + HD : WIDE + HD + half] = rows.astype(jnp.bfloat16)
    both = (target == guest + part) | (target == guest + MSG + part)
    send[:, WIDE + HD + half :] = rows_of(both, WIDE, HD).astype(jnp.bfloat16)
    used = [
        functools.reduce(jnp.logical_or, [lend == n for lend in lends]) for n in range(1, 4)
    ]
    mixed = used[2] | (used[0] & used[1])
    kind = jnp.where(mixed, 7, jnp.where(used[0], 1, jnp.where(used[1], 4, 0)))
    size = jnp.where(longest > 3 * STRIP, 2, jnp.where(longest > 2 * STRIP, 1, 0))
    way[0] = kind + jnp.where((kind > 0) & (kind < 7), size, 0)


def guest_prep_kernel(
    devices, hit_count, hits, prefix_len, span, places, keys, values, *refs
):
    plan, prompt, cached, turned, wide, picks, picks_guest, strips_of, *scratch = refs
    count, host, key_rows, value_rows, sems = scratch
    copies = [
        pltpu.make_async_copy(x.at[pl.ds(0, REGION)], rows, sems.at[n])
        for n, (x, rows) in enumerate([(keys, key_rows), (values, value_rows)])
    ]
    for copy in copies:
        copy.start()
    me = lax.axis_index("cache")
    chip = me // 2
    ranks = owner_ranks(devices, hits, count)
    guest_plan(devices, count, host)
    rows = iota((devices * MSG, 4 * ROWS), 0)
    chosen = jnp.where(rows[:, : 2 * ROWS] == places[0:1, : 2 * ROWS], 1.0, 0.0)
    picks[...] = chosen.T.astype(jnp.bfloat16)
    chosen = jnp.where(rows == places[1:2, :], 1.0, 0.0)
    picks_guest[...] = chosen.T.astype(jnp.bfloat16)
    for copy in copies:
        copy.wait()
    turn(key_rows, turned)
    widen(value_rows, wide)
    first, guest, source = jnp.int32(-1), jnp.int32(-1), jnp.int32(0)
    for r in range(REQUESTS):
        owner = hits[r]
        here = (ranks[r] == 1) & (host[owner] == chip)
        first = jnp.where((ranks[r] == 0) & (owner == me), r, first)
        guest = jnp.where(here, r, guest)
        source = jnp.where(here, owner, source)
    core = me % 2
    from_first_core = jnp.where(source == 2 * chip, 1, 0)
    plan[0] = jnp.where(core == 1, (source // 2) ^ chip, 0)
    plan[1] = jnp.where(core == from_first_core, 1, 0)
    for job, found in enumerate((first, guest)):
        request = jnp.maximum(found, 0)
        limit = prefix_len[request]
        strips = jnp.clip((limit + STRIP - 1) // STRIP, 1, REGION // STRIP)
        strips_of[job : job + 1, :] = jnp.full((1, HD), jnp.where(found >= 0, strips, 0))
        cached[job : job + 1, :] = jnp.where(iota((1, REGION), 1) < limit, 0.0, FLOOR)
        prompt_rows(devices, prompt, span, request, job, True)


def turn(keys, turned):
    for n in range(0, REGION, STRIP):
        turned[:, n : n + STRIP] = keys[n : n + STRIP, :].T


def widen(values, wide):
    wide[:, :HD] = values[...]
    wide[:, HD:] = jnp.ones((REGION, HD), jnp.bfloat16)


def host_kernel(prepare, devices, hit_count, plan, mine, other, out):
    for choice, rows in enumerate((mine, other)):
        pl.when(plan[1] == choice)(functools.partial(prepare, rows, out))


def guest_attend_kernel(
    devices, hit_count, strips_of, prompt_mask, cached_mask, got, turned, wide, *refs
):
    turned_guest, wide_guest, out = refs
    jobs = [
        (0, 0, HALF, turned, wide),
        (WIDE + HD, WIDE, HALF // 2, turned_guest, wide_guest),
    ]
    for job, (base, first, blocks, keys, values) in enumerate(jobs):
        strips = strips_of[job, 0]

        @pl.when(strips == 0)
        def _():
            empty = jnp.zeros((devices * MSG, blocks * HD), jnp.bfloat16)
            out[:, first : first + blocks * HD] = empty

        for count in range(1, REGION // STRIP + 1):

            @pl.when(strips == count)
            def _():
                whole = (count - 1) * STRIP
                mask = prompt_mask[job * devices * MSG : (job + 1) * devices * MSG, :]
                attend_rows(
                    got,
                    base,
                    blocks,
                    slice(0, devices * MSG),
                    prompt_parts(got[:, base + blocks * HD : base + (blocks + 1) * HD]),
                    mask,
                    cached_mask[job : job + 1, whole : whole + STRIP],
                    keys[:, :whole] if whole else None,
                    keys[:, whole : whole + STRIP],
                    values[:whole, :] if whole else None,
                    values[whole : whole + STRIP, :],
                    out,
                    first,
                )


def prompt_parts(rows):
    height = rows.shape[0]
    wide = rows.astype(jnp.float32)
    moved = pltpu.roll(wide, height - TOK_REQ, 0).astype(jnp.bfloat16)
    values = jnp.concatenate([moved, jnp.ones((height, HD), jnp.bfloat16)], axis=1)
    return wide.T.astype(jnp.bfloat16), values


def attend_rows(
    got, base, blocks, here, prompt, mask, tail_mask, head, tail, head_values, tail_values, out, first
):
    prompt_keys, prompt_values = prompt
    factor = SCALE * math.log2(math.e)
    mask = jnp.concatenate([mask, mask], axis=0)
    height = mask.shape[0] // 2

    def scores(c):
        pair = jnp.concatenate(
            [got[here, base + (c + n) * HD : base + (c + n + 1) * HD] for n in range(2)], axis=0
        )
        parts = [] if head is None else [dot(pair, head, NN)]
        parts.append(dot(pair, tail, NN) + tail_mask)
        parts.append(dot(pair, prompt_keys, NN) + mask)
        return parts

    parts = scores(0)
    for c in range(0, blocks, 2):
        later = scores(c + 2) if c + 2 < blocks else None
        top = lanes_max(parts)
        parts = [jnp.exp2((x - top) * factor).astype(jnp.bfloat16) for x in parts]
        summed = dot(parts[-1], prompt_values, NN) + dot(parts[-2], tail_values, NN)
        if head is not None:
            summed = summed + dot(parts[0], head_values, NN)
        result = (summed[:, :HD] / summed[:, HD:]).astype(jnp.bfloat16)
        for n in range(2):
            column = first + (c + n) * HD
            out[here, column : column + HD] = result[n * height : (n + 1) * height]
        parts = later


def guest_unpack_kernel(devices, hit_count, picks, picks_guest, outs, result, held, sems):
    half = WIDE // 2
    copies = []
    for n in range(2):
        own = dot(picks[n * ROWS : (n + 1) * ROWS, :], outs[:, :WIDE], NN)
        for g in (2 * n, 2 * n + 1):
            guest = dot(picks_guest[g * ROWS : (g + 1) * ROWS, :], outs[:, WIDE:], NN)
            rows = own[:, g % 2 * half : (g % 2 + 1) * half] + guest
            held[:, g * half : (g + 1) * half] = rows.astype(jnp.bfloat16)
        here = pl.ds(n * WIDE, WIDE)
        copies.append(pltpu.make_async_copy(held.at[:, here], result.at[:, here], sems.at[n]))
        copies[n].start()
    for copy in copies:
        copy.wait()


def unpack_kernel(devices, hit_count, picks, *refs):
    outs, logs, result = refs[0], refs[1:-1], refs[-1]

    def chosen(s, i):
        place = s * hit_count + i
        return picks[place * 2 * ROWS : (place + 1) * 2 * ROWS, :]

    def rows_of(i):
        parts = [
            dot(chosen(s, i), outs[:, s * WIDE : (s + 1) * WIDE], NN)
            for s in range(CAP)
        ]
        return sum(parts[1:], parts[0])

    def logs_of(i):
        parts = [
            dot(
                chosen(s, i).astype(jnp.float32),
                logs[0][:, s * HD : (s + 1) * HD],
                NN,
                precision=lax.Precision.HIGHEST,
            )
            for s in range(CAP)
        ]
        return sum(parts[1:], parts[0])

    if hit_count == 1:
        joined = rows_of(0)
    else:
        levels = [logs_of(i) for i in range(hit_count)]
        top = functools.reduce(jnp.maximum, levels)
        shares = [jnp.exp(level - top) for level in levels]
        total = sum(shares[1:], shares[0])
        pieces = [rows_of(i) for i in range(hit_count)]
        columns = []
        for c in range(HALF):
            part = sum(
                shares[i][:, c : c + 1] * pieces[i][:, c * HD : (c + 1) * HD]
                for i in range(hit_count)
            )
            columns.append(part / total[:, c : c + 1])
        joined = jnp.concatenate(columns, axis=1)
    joined = joined.astype(jnp.bfloat16)
    result[:, :WIDE] = joined[:ROWS]
    result[:, WIDE:] = joined[ROWS:]


def vmem(count):
    return [pl.BlockSpec(memory_space=pltpu.VMEM)] * count


def smem(count):
    return [pl.BlockSpec(memory_space=pltpu.SMEM)] * count


def hbm(count):
    return [pl.BlockSpec(memory_space=pltpu.HBM)] * count


def body(prefix_len, hits, span_block, queries, fresh_keys, fresh_values, cache_keys, cache_values):
    devices = lax.axis_size("cache")
    hit_count = hits.shape[1]
    rows = devices * MSG
    owners = hits.reshape(REQUESTS * hit_count)
    fresh = (owners, queries, fresh_keys, fresh_values)

    def exchange(x):
        return lax.all_to_all(x, "cache", split_axis=0, concat_axis=0, tiled=True)

    def call(kernel, out_shape, name, grant=40, **kw):
        return pl.pallas_call(
            functools.partial(kernel, devices, hit_count),
            out_shape=[
                jax.ShapeDtypeStruct(*leaf) if isinstance(leaf, tuple) else leaf
                for leaf in out_shape
            ],
            compiler_params=pltpu.CompilerParams(vmem_limit_bytes=grant * 2**20),
            name=name,
            **kw,
        )

    if hit_count == 1 and devices == 16:
        pairs = rows * (HALF + HALF // 2) * (REGION + rows)
        scalars = [pltpu.SMEM((devices,), jnp.int32)] * 2
        send, places, way = call(
            guest_pack_kernel,
            [
                pltpu.VMEM((rows, GUEST_MSG), jnp.bfloat16),
                ((2, 4 * ROWS), jnp.int32),
                ((1,), jnp.int32),
            ],
            "pack",
            in_specs=hbm(5),
            out_specs=vmem(2) + smem(1),
            scratch_shapes=[
                pltpu.VMEM((2 * ROWS, WIDE + HD), jnp.bfloat16),
                *[pltpu.SMEM((REQUESTS,), jnp.int32)] * 2,
                *scalars,
                pltpu.SemaphoreType.DMA((6,)),
            ],
        )(
            *(
                pltpu.with_memory_space_constraint(x, pltpu.HBM)
                for x in (owners, prefix_len, queries, fresh_keys, fresh_values)
            )
        )
        got = exchange(send)
        shapes = [((HD, REGION), jnp.bfloat16), ((REGION, 2 * HD), jnp.bfloat16)]
        def chain(form, owners, prefix_len, span_block, places, cache_keys, cache_values):
            ways, height = form
            pinned = [
                pltpu.with_memory_space_constraint(x, pltpu.HBM)
                for x in (owners, prefix_len, span_block, cache_keys, cache_values)
            ]
            slots = [cache_keys[REGION:], cache_values[REGION:]]
            lent = [
                [
                    lax.ppermute(
                        x[:height], "cache", [(d, d ^ (2 * n)) for d in range(1, devices, 2)]
                    )
                    for x in slots
                ]
                for n in ways
            ]
            prepared = call(
                guest_prep_kernel,
                [((2,), jnp.int32), ((2 * rows, rows), jnp.float32), ((2, REGION), jnp.float32)]
                + shapes
                + [((2 * ROWS, rows), jnp.bfloat16), ((4 * ROWS, rows), jnp.bfloat16)]
                + [((8, HD), jnp.int32)],
                "prep",
                grant=12,
                in_specs=smem(2) + vmem(2) + hbm(2),
                out_specs=smem(1) + vmem(7),
                scratch_shapes=[
                    *scalars,
                    *[pltpu.VMEM((REGION, HD), jnp.bfloat16)] * 2,
                    pltpu.SemaphoreType.DMA((2,)),
                ],
                cost_estimate=pl.CostEstimate(
                    flops=10**6, bytes_accessed=2**22, transcendentals=0
                ),
            )(*pinned[:3], places, *pinned[3:])
            plan = prepared[0]
            for n, borrowed in zip(ways, lent):
                slots = [
                    jnp.where(plan[0] == n, jnp.pad(x, ((0, REGION - height), (0, 0))), y)
                    for x, y in zip(borrowed, slots)
                ]
            swapped = [lax.ppermute(x, "cache", [(d, d ^ 1) for d in range(devices)]) for x in slots]
            guest = [
                call(
                    functools.partial(host_kernel, prepare),
                    [shape],
                    "host",
                    grant=12,
                    in_specs=smem(1) + vmem(2),
                    out_specs=vmem(1),
                )(plan, mine, other)[0]
                for prepare, shape, mine, other in zip((turn, widen), shapes, slots, swapped)
            ]
            return (*prepared[1:], *guest)

        forms = [
            ((), REGION),
            ((1,), 2 * STRIP),
            ((1,), 3 * STRIP),
            ((1,), REGION),
            ((2,), 2 * STRIP),
            ((2,), 3 * STRIP),
            ((2,), REGION),
            ((1, 2, 3), REGION),
        ]
        prepared = lax.switch(
            way.reshape(()),
            [functools.partial(chain, form) for form in forms],
            owners,
            prefix_len,
            span_block,
            places,
            cache_keys,
            cache_values,
        )
        prompt_mask, cached_mask, turned, wide, picks, picks_guest, strips_of = prepared[:7]
        turned_guest, wide_guest = prepared[7:]
        (answer,) = call(
            guest_attend_kernel,
            [((rows, WIDE + WIDE // 2), jnp.bfloat16)],
            "attend",
            in_specs=vmem(8),
            out_specs=vmem(1),
            cost_estimate=pl.CostEstimate(
                flops=4 * pairs * HD, bytes_accessed=8 * rows * WIDE, transcendentals=pairs
            ),
        )(strips_of, prompt_mask, cached_mask, got, turned, wide, turned_guest, wide_guest)
        return call(
            guest_unpack_kernel,
            [((ROWS, HEADS * HD), jnp.bfloat16)],
            "unpack",
            in_specs=vmem(3),
            out_specs=hbm(1),
            scratch_shapes=[
                pltpu.VMEM((ROWS, HEADS * HD), jnp.bfloat16),
                pltpu.SemaphoreType.DMA((2,)),
            ],
        )(picks, picks_guest, exchange(answer))[0]
    send, places = call(
        pack_kernel,
        [((rows, CAP * (WIDE + HD)), jnp.bfloat16), ((CAP * hit_count, 2 * ROWS), jnp.int32)],
        "pack",
        in_specs=hbm(4),
        out_specs=vmem(2),
        scratch_shapes=[
            pltpu.VMEM((2 * ROWS, WIDE + HD), jnp.bfloat16),
            pltpu.SMEM((REQUESTS * hit_count,), jnp.int32),
            pltpu.SMEM((devices,), jnp.int32),
            pltpu.SemaphoreType.DMA((5,)),
        ],
    )(*(pltpu.with_memory_space_constraint(x, pltpu.HBM) for x in fresh))
    got = exchange(send)
    busy, prompt_mask, cached_mask, turned, wide, picks = call(
        prep_kernel,
        [
            ((CAP,), jnp.int32),
            ((CAP * rows, rows), jnp.float32),
            ((CAP, REGION), jnp.float32),
            ((HD, CAP * REGION), jnp.bfloat16),
            ((CAP * REGION, 2 * HD), jnp.bfloat16),
            ((CAP * hit_count * 2 * ROWS, rows), jnp.bfloat16),
        ],
        "prep",
        in_specs=smem(2) + vmem(4),
        out_specs=smem(1) + vmem(5),
        cost_estimate=pl.CostEstimate(flops=10**6, bytes_accessed=2**22, transcendentals=0),
    )(owners, prefix_len, span_block, places, cache_keys, cache_values)
    pairs = CAP * rows * HALF * (REGION + rows)
    answers = call(
        attend_kernel,
        [((rows, CAP * WIDE), jnp.bfloat16)]
        + [((rows, CAP * HD), jnp.float32)] * (hit_count > 1),
        "attend",
        in_specs=smem(1) + vmem(5),
        out_specs=vmem(1 + (hit_count > 1)),
        cost_estimate=pl.CostEstimate(
            flops=4 * pairs * HD, bytes_accessed=8 * rows * WIDE, transcendentals=pairs
        ),
    )(busy, prompt_mask, cached_mask, got, turned, wide)
    returned = [exchange(answer) for answer in answers]
    return call(
        unpack_kernel,
        [((ROWS, HEADS * HD), jnp.bfloat16)],
        "unpack",
        in_specs=vmem(1 + len(returned)),
        out_specs=vmem(1),
    )(picks, *returned)[0]


def solution(mesh):
    in_specs = (
        P("groups"),
        P("groups", None),
        P("groups", None),
        P(("groups", "cache"), None),
        P(("groups", "cache"), None),
        P(("groups", "cache"), None),
        P(("groups", "cache"), None),
        P(("groups", "cache"), None),
    )
    out_specs = P(("groups", "cache"), None)
    return jax.shard_map(body, mesh=mesh, in_specs=in_specs, out_specs=out_specs, check_vma=False)
```

```python
import functools
import math

import jax
import jax.numpy as jnp
from jax import lax
from jax.experimental import pallas as pl
from jax.experimental.pallas import tpu as pltpu
from jax.sharding import PartitionSpec as P

HEADS = 16
HD = 128
PAGE = 128
CAP = 2
REQUESTS = 16
TOK_REQ = 4
PAGES_DEV = 16

REGION = PAGES_DEV // CAP * PAGE
HALF = HEADS // 2
MSG = 2 * TOK_REQ
WIDE = HALF * HD
ROWS = REQUESTS * TOK_REQ
STRIP = 256
GUEST_MSG = WIDE + HD + WIDE // 2 + HD
SCALE = HD**-0.5
FLOOR = -1e30
NN = (((1,), (0,)), ((), ()))


def iota(shape, axis):
    return lax.broadcasted_iota(jnp.int32, shape, axis)


def dot(a, b, dims, **kw):
    return lax.dot_general(a, b, dims, preferred_element_type=jnp.float32, **kw)


def pack_kernel(devices, hit_count, owners, q, k, v, send, places, held, hits, count, sems):
    copies = [
        pltpu.make_async_copy(source, held.at[pl.ds(row, ROWS), pl.ds(column, width)], sems.at[n])
        for n, (source, row, column, width) in enumerate(
            [
                (q.at[:, pl.ds(0, WIDE)], 0, 0, WIDE),
                (q.at[:, pl.ds(WIDE, WIDE)], ROWS, 0, WIDE),
                (k, 0, WIDE, HD),
                (v, ROWS, WIDE, HD),
            ]
        )
    ]
    first = pltpu.make_async_copy(owners, hits, sems.at[4])
    first.start()
    for copy in copies:
        copy.start()
    lane = iota((1, 2 * ROWS), 1)
    lane_request = (lane % ROWS) // TOK_REQ
    first.wait()
    for r in range(REQUESTS):
        for i in range(hit_count):
            count[hits[r * hit_count + i]] = 0
    rows = [[jnp.full((1, 2 * ROWS), -4 * MSG, jnp.int32)] * hit_count for _ in range(CAP)]
    for r in range(REQUESTS):
        for i in range(hit_count):
            owner = hits[r * hit_count + i]
            rank = count[owner]
            count[owner] = rank + 1
            for s in range(CAP):
                place = jnp.where(rank == s, owner * MSG, -4 * MSG)
                rows[s][i] = jnp.where(lane_request == r, place, rows[s][i])
    inner = lane // ROWS * TOK_REQ + lane % TOK_REQ
    target = iota((devices * MSG, 2 * ROWS), 0)
    picks = []
    for s in range(CAP):
        chosen = None
        for i in range(hit_count):
            row = rows[s][i] + inner
            places[s * hit_count + i : s * hit_count + i + 1, :] = row
            hit = target == row
            chosen = hit if chosen is None else chosen | hit
        picks.append(jnp.where(chosen, 1.0, 0.0).astype(jnp.bfloat16))
    for copy in copies:
        copy.wait()
    packed = dot(jnp.concatenate(picks, axis=0), held[...], NN).astype(jnp.bfloat16)
    for s in range(CAP):
        rows = slice(s * devices * MSG, (s + 1) * devices * MSG)
        send[:, s * (WIDE + HD) : (s + 1) * (WIDE + HD)] = packed[rows]


def prep_kernel(
    devices, hit_count, hits, prefix_len, span, places, keys, values, *outs
):
    busy, prompt, cached, turned, wide, picks = outs
    rows = iota((devices * MSG, 2 * ROWS), 0)
    for n in range(CAP * hit_count):
        chosen = jnp.where(rows == places[n : n + 1, :], 1.0, 0.0)
        picks[n * 2 * ROWS : (n + 1) * 2 * ROWS, :] = chosen.T.astype(jnp.bfloat16)
    for n in range(0, CAP * REGION, STRIP):
        turned[:, n : n + STRIP] = keys[n : n + STRIP, :].T
    me = lax.axis_index("cache")
    wide[:, :HD] = values[...]
    wide[:, HD:] = jnp.ones((CAP * REGION, HD), jnp.bfloat16)
    for slot in range(CAP):
        seen = jnp.int32(0)
        request = jnp.int32(0)
        which = jnp.int32(0)
        for r in range(REQUESTS):
            for i in range(hit_count):
                mine = hits[r * hit_count + i] == me
                here = mine & (seen == slot)
                request = jnp.where(here, r, request)
                which = jnp.where(here, i, which)
                seen = seen + mine.astype(jnp.int32)
        limit = prefix_len[request] - which * REGION
        blocks = jnp.clip((limit + STRIP - 1) // STRIP, 1, REGION // STRIP)
        busy[slot] = jnp.where(seen > slot, blocks, 0)
        cached[slot : slot + 1, :] = jnp.where(iota((1, REGION), 1) < limit, 0.0, FLOOR)
        prompt_rows(devices, prompt, span, request, slot, hit_count == 1 or which == 0)


def prompt_rows(devices, prompt, span, request, slot, counted):
    total_rows = devices * MSG
    span_row = span[pl.ds(request, 1), :].astype(jnp.float32)
    source = iota((devices, total_rows), 0)
    spread = (iota((devices, total_rows), 1) // MSG == source).astype(jnp.bfloat16)
    spans = jnp.broadcast_to(span_row, (16, devices)).astype(jnp.bfloat16)
    key_span = dot(spans, spread, NN)[:1]
    lane = iota((1, total_rows), 1)
    key_spot = key_span.astype(jnp.int32) * TOK_REQ + lane % TOK_REQ
    is_key = (lane % MSG < TOK_REQ) & counted
    key_spot = jnp.where(is_key, key_spot, devices * TOK_REQ)
    block = 16 * MSG

    def one_block(at):
        row_source = at * 16 + iota((block, devices), 0) // MSG
        mine = iota((block, devices), 1) == row_source
        row_span = jnp.sum(jnp.where(mine, span_row, 0.0), axis=1, keepdims=True)
        row_spot = row_span.astype(jnp.int32) * TOK_REQ + iota((block, 1), 0) % TOK_REQ
        here = pl.ds(slot * total_rows + at * block, block)
        prompt[here, :] = jnp.where(key_spot <= row_spot, 0.0, FLOOR)

    each_block(devices, one_block)


def each_block(devices, one_block):
    blocks = devices // 16
    if blocks == 1:
        one_block(0)
    else:
        pl.loop(0, blocks)(one_block)


def lanes_max(parts):
    pieces = [part[:, n : n + HD] for part in parts for n in range(0, part.shape[1], HD)]
    return jnp.max(functools.reduce(jnp.maximum, pieces), axis=1, keepdims=True)


def attend_kernel(
    devices, hit_count, busy, prompt_mask, cached_mask, got, turned, wide, out, *levels
):
    total_rows = devices * MSG
    block = 16 * MSG
    factor = SCALE * math.log2(math.e)

    def nothing(slot):
        out[:, pl.ds(slot * WIDE, WIDE)] = jnp.zeros((total_rows, WIDE), jnp.bfloat16)
        for lse in levels:
            lse[:, pl.ds(slot * HD, HD)] = jnp.zeros((total_rows, HD), jnp.float32)

    def attend(slot, strips):
        whole = (strips - 1) * STRIP
        base = pl.multiple_of(slot * (WIDE + HD), HD)
        region = pl.multiple_of(slot * REGION, REGION)
        head = pl.ds(region, whole) if whole else None
        tail = pl.ds(pl.multiple_of(region + whole, STRIP), STRIP)
        tail_mask = cached_mask[pl.ds(slot, 1), whole : whole + STRIP]
        prompt_keys = got[:, pl.ds(base + WIDE, HD)].astype(jnp.float32)
        moved = pltpu.roll(prompt_keys, total_rows - TOK_REQ, 0)
        prompt_keys = prompt_keys.T.astype(jnp.bfloat16)
        prompt_values = jnp.concatenate(
            [moved.astype(jnp.bfloat16), jnp.ones((total_rows, HD), jnp.bfloat16)], axis=1
        )

        def one_block(at):
            here = pl.ds(at * block, block)
            prompt_bias = prompt_mask[pl.ds(slot * total_rows + at * block, block), :]
            prompt_bias = jnp.concatenate([prompt_bias, prompt_bias], axis=0)
            lane = iota((block, HD), 1)

            def scores(c):
                pair = jnp.concatenate(
                    [got[here, pl.ds(base + (c + n) * HD, HD)] for n in range(2)], axis=0
                )
                parts = [dot(pair, turned[:, head], NN)] if whole else []
                parts.append(dot(pair, turned[:, tail], NN) + tail_mask)
                parts.append(dot(pair, prompt_keys, NN) + prompt_bias)
                return parts

            logs = jnp.zeros((block, HD), jnp.float32)
            parts = scores(0)
            for c in range(0, HALF, 2):
                later = scores(c + 2) if c + 2 < HALF else None
                top = lanes_max(parts)
                if hit_count > 1:
                    top = jnp.maximum(top, 0.1 * FLOOR)
                parts = [jnp.exp2((x - top) * factor).astype(jnp.bfloat16) for x in parts]
                summed = dot(parts[-1], prompt_values, NN) + dot(parts[-2], wide[tail, :], NN)
                if whole:
                    summed = summed + dot(parts[0], wide[head, :], NN)
                totals = summed[:, HD:]
                if hit_count > 1:
                    totals = jnp.maximum(totals, 1.0)
                    level = top * SCALE + jnp.log(totals)
                    logs = jnp.where(lane == c, level[:block], logs)
                    logs = jnp.where(lane == c + 1, level[block:], logs)
                result = (summed[:, :HD] / totals).astype(jnp.bfloat16)
                for n in range(2):
                    column = pl.multiple_of(slot * WIDE + (c + n) * HD, HD)
                    out[here, pl.ds(column, HD)] = result[n * block : (n + 1) * block]
                parts = later
            for lse in levels:
                lse[here, pl.ds(pl.multiple_of(slot * HD, HD), HD)] = logs

        each_block(devices, one_block)

    @pl.loop(0, CAP)
    def _(slot):
        strips = busy[slot]
        pl.when(strips == 0)(lambda: nothing(slot))
        for count in range(1, REGION // STRIP + 1):
            pl.when(strips == count)(functools.partial(attend, slot, count))


def owner_ranks(devices, owners, count):
    for d in range(devices):
        count[d] = 0
    ranks = []
    for r in range(REQUESTS):
        owner = owners[r]
        ranks.append(count[owner])
        count[owner] = ranks[r] + 1
    return ranks


def guest_plan(devices, count, host):
    chips = devices // 2
    seconds = [count[d] > 1 for d in range(devices)]
    none = [jnp.logical_not(seconds[2 * x] | seconds[2 * x + 1]) for x in range(chips)]
    lends = []
    for x in range(chips):
        other = jnp.where(none[x ^ 1], 1, jnp.where(none[x ^ 2], 2, 3))
        lends.append(jnp.where(seconds[2 * x] & seconds[2 * x + 1], other, 0))
        host[2 * x] = jnp.int32(x)
        host[2 * x + 1] = lends[x] ^ x
    return lends


def guest_pack_kernel(devices, hit_count, owners, lengths, q, k, v, *refs):
    send, places, way, held, hits, prefix_len, count, host, sems = refs
    half = WIDE // 2
    moves = [
        (owners, hits),
        (q.at[:, pl.ds(0, WIDE)], held.at[pl.ds(0, ROWS), pl.ds(0, WIDE)]),
        (q.at[:, pl.ds(WIDE, WIDE)], held.at[pl.ds(ROWS, ROWS), pl.ds(0, WIDE)]),
        (k, held.at[pl.ds(0, ROWS), pl.ds(WIDE, HD)]),
        (v, held.at[pl.ds(ROWS, ROWS), pl.ds(WIDE, HD)]),
        (lengths, prefix_len),
    ]
    copies = [pltpu.make_async_copy(a, b, sems.at[n]) for n, (a, b) in enumerate(moves)]
    for copy in copies:
        copy.start()
    lane = iota((1, 4 * ROWS), 1)
    lane_request = lane % ROWS // TOK_REQ
    part = lane // ROWS * TOK_REQ
    nowhere = jnp.full((1, 4 * ROWS), -4 * MSG, jnp.int32)
    target = iota((devices * MSG, 2 * ROWS), 0)
    copies[0].wait()
    ranks = owner_ranks(devices, hits, count)
    own = nowhere
    for r in range(REQUESTS):
        place = jnp.where(ranks[r] == 0, hits[r] * MSG, -4 * MSG)
        own = jnp.where(lane_request == r, place, own)
    own = own + lane % TOK_REQ + part

    def rows_of(chosen, first, width):
        pick = jnp.where(chosen, 1.0, 0.0).astype(jnp.bfloat16)
        return dot(pick, held[:, first : first + width], NN)

    for copy in copies[1:]:
        copy.wait()
    rows = rows_of(target == own[:, : 2 * ROWS], 0, WIDE + HD)
    send[:, : WIDE + HD] = rows.astype(jnp.bfloat16)
    lends = guest_plan(devices, count, host)
    guest = nowhere
    longest = jnp.int32(0)
    for r in range(REQUESTS):
        chip = host[hits[r]]
        place = jnp.where(ranks[r] == 1, chip * 2 * MSG, -4 * MSG)
        guest = jnp.where(lane_request == r, place, guest)
        lent = (ranks[r] == 1) & (chip != hits[r] // 2)
        longest = jnp.maximum(longest, jnp.where(lent, prefix_len[r], 0))
    guest = guest + lane % TOK_REQ
    places[0:1, :] = own
    places[1:2, :] = guest + part
    guest, part = guest[:, : 2 * ROWS], part[:, : 2 * ROWS]
    rows = rows_of(target == guest + 2 * part, 0, half)
    rows = rows + rows_of(target == guest + 2 * part + TOK_REQ, half, half)
    send[:, WIDE + HD : WIDE + HD + half] = rows.astype(jnp.bfloat16)
    both = (target == guest + part) | (target == guest + MSG + part)
    send[:, WIDE + HD + half :] = rows_of(both, WIDE, HD).astype(jnp.bfloat16)
    used = [
        functools.reduce(jnp.logical_or, [lend == n for lend in lends]) for n in range(1, 4)
    ]
    mixed = used[2] | (used[0] & used[1])
    kind = jnp.where(mixed, 7, jnp.where(used[0], 1, jnp.where(used[1], 4, 0)))
    size = jnp.where(longest > 3 * STRIP, 2, jnp.where(longest > 2 * STRIP, 1, 0))
    way[0] = kind + jnp.where((kind > 0) & (kind < 7), size, 0)


def guest_prep_kernel(
    devices, hit_count, hits, prefix_len, span, places, keys, values, *refs
):
    plan, prompt, cached, turned, wide, picks, picks_guest, strips_of, count, host = refs
    me = lax.axis_index("cache")
    chip = me // 2
    ranks = owner_ranks(devices, hits, count)
    guest_plan(devices, count, host)
    rows = iota((devices * MSG, 4 * ROWS), 0)
    chosen = jnp.where(rows[:, : 2 * ROWS] == places[0:1, : 2 * ROWS], 1.0, 0.0)
    picks[...] = chosen.T.astype(jnp.bfloat16)
    chosen = jnp.where(rows == places[1:2, :], 1.0, 0.0)
    picks_guest[...] = chosen.T.astype(jnp.bfloat16)
    turn(keys[:REGION, :], turned)
    widen(values[:REGION, :], wide)
    first, guest, source = jnp.int32(-1), jnp.int32(-1), jnp.int32(0)
    for r in range(REQUESTS):
        owner = hits[r]
        here = (ranks[r] == 1) & (host[owner] == chip)
        first = jnp.where((ranks[r] == 0) & (owner == me), r, first)
        guest = jnp.where(here, r, guest)
        source = jnp.where(here, owner, source)
    core = me % 2
    from_first_core = jnp.where(source == 2 * chip, 1, 0)
    plan[0] = jnp.where(core == 1, (source // 2) ^ chip, 0)
    plan[1] = jnp.where(core == from_first_core, 1, 0)
    for job, found in enumerate((first, guest)):
        request = jnp.maximum(found, 0)
        limit = prefix_len[request]
        strips = jnp.clip((limit + STRIP - 1) // STRIP, 1, REGION // STRIP)
        strips_of[job : job + 1, :] = jnp.full((1, HD), jnp.where(found >= 0, strips, 0))
        cached[job : job + 1, :] = jnp.where(iota((1, REGION), 1) < limit, 0.0, FLOOR)
        prompt_rows(devices, prompt, span, request, job, True)


def turn(keys, turned):
    for n in range(0, REGION, STRIP):
        turned[:, n : n + STRIP] = keys[n : n + STRIP].T


def widen(values, wide):
    wide[:, :HD] = values
    wide[:, HD:] = jnp.ones((REGION, HD), jnp.bfloat16)


def host_kernel(prepare, devices, hit_count, plan, mine, other, out):
    for choice, rows in enumerate((mine, other)):

        @pl.when(plan[1] == choice)
        def _():
            prepare(rows[...], out)


def guest_attend_kernel(
    devices, hit_count, strips_of, prompt_mask, cached_mask, got, turned, wide, *refs
):
    turned_guest, wide_guest, out = refs
    jobs = [
        (0, 0, HALF, turned, wide),
        (WIDE + HD, WIDE, HALF // 2, turned_guest, wide_guest),
    ]
    for job, (base, first, blocks, keys, values) in enumerate(jobs):
        strips = strips_of[job, 0]

        @pl.when(strips == 0)
        def _():
            empty = jnp.zeros((devices * MSG, blocks * HD), jnp.bfloat16)
            out[:, first : first + blocks * HD] = empty

        for count in range(1, REGION // STRIP + 1):

            @pl.when(strips == count)
            def _():
                whole = (count - 1) * STRIP
                mask = prompt_mask[job * devices * MSG : (job + 1) * devices * MSG, :]
                attend_rows(
                    got,
                    base,
                    blocks,
                    slice(0, devices * MSG),
                    prompt_parts(got[:, base + blocks * HD : base + (blocks + 1) * HD]),
                    mask,
                    cached_mask[job : job + 1, whole : whole + STRIP],
                    keys[:, :whole] if whole else None,
                    keys[:, whole : whole + STRIP],
                    values[:whole, :] if whole else None,
                    values[whole : whole + STRIP, :],
                    out,
                    first,
                )


def prompt_parts(rows):
    height = rows.shape[0]
    wide = rows.astype(jnp.float32)
    moved = pltpu.roll(wide, height - TOK_REQ, 0).astype(jnp.bfloat16)
    values = jnp.concatenate([moved, jnp.ones((height, HD), jnp.bfloat16)], axis=1)
    return wide.T.astype(jnp.bfloat16), values


def attend_rows(
    got, base, blocks, here, prompt, mask, tail_mask, head, tail, head_values, tail_values, out, first
):
    prompt_keys, prompt_values = prompt
    factor = SCALE * math.log2(math.e)
    mask = jnp.concatenate([mask, mask], axis=0)
    height = mask.shape[0] // 2

    def scores(c):
        pair = jnp.concatenate(
            [got[here, base + (c + n) * HD : base + (c + n + 1) * HD] for n in range(2)], axis=0
        )
        parts = [] if head is None else [dot(pair, head, NN)]
        parts.append(dot(pair, tail, NN) + tail_mask)
        parts.append(dot(pair, prompt_keys, NN) + mask)
        return parts

    parts = scores(0)
    for c in range(0, blocks, 2):
        later = scores(c + 2) if c + 2 < blocks else None
        top = lanes_max(parts)
        parts = [jnp.exp2((x - top) * factor).astype(jnp.bfloat16) for x in parts]
        summed = dot(parts[-1], prompt_values, NN) + dot(parts[-2], tail_values, NN)
        if head is not None:
            summed = summed + dot(parts[0], head_values, NN)
        result = (summed[:, :HD] / summed[:, HD:]).astype(jnp.bfloat16)
        for n in range(2):
            column = first + (c + n) * HD
            out[here, column : column + HD] = result[n * height : (n + 1) * height]
        parts = later


def guest_unpack_kernel(devices, hit_count, picks, picks_guest, outs, result, held, sems):
    half = WIDE // 2
    copies = []
    for n in range(2):
        own = dot(picks[n * ROWS : (n + 1) * ROWS, :], outs[:, :WIDE], NN)
        for g in (2 * n, 2 * n + 1):
            guest = dot(picks_guest[g * ROWS : (g + 1) * ROWS, :], outs[:, WIDE:], NN)
            rows = own[:, g % 2 * half : (g % 2 + 1) * half] + guest
            held[:, g * half : (g + 1) * half] = rows.astype(jnp.bfloat16)
        here = pl.ds(n * WIDE, WIDE)
        copies.append(pltpu.make_async_copy(held.at[:, here], result.at[:, here], sems.at[n]))
        copies[n].start()
    for copy in copies:
        copy.wait()


def unpack_kernel(devices, hit_count, picks, *refs):
    outs, logs, result = refs[0], refs[1:-1], refs[-1]

    def chosen(s, i):
        place = s * hit_count + i
        return picks[place * 2 * ROWS : (place + 1) * 2 * ROWS, :]

    def rows_of(i):
        parts = [
            dot(chosen(s, i), outs[:, s * WIDE : (s + 1) * WIDE], NN)
            for s in range(CAP)
        ]
        return sum(parts[1:], parts[0])

    def logs_of(i):
        parts = [
            dot(
                chosen(s, i).astype(jnp.float32),
                logs[0][:, s * HD : (s + 1) * HD],
                NN,
                precision=lax.Precision.HIGHEST,
            )
            for s in range(CAP)
        ]
        return sum(parts[1:], parts[0])

    if hit_count == 1:
        joined = rows_of(0)
    else:
        levels = [logs_of(i) for i in range(hit_count)]
        top = functools.reduce(jnp.maximum, levels)
        shares = [jnp.exp(level - top) for level in levels]
        total = sum(shares[1:], shares[0])
        pieces = [rows_of(i) for i in range(hit_count)]
        columns = []
        for c in range(HALF):
            part = sum(
                shares[i][:, c : c + 1] * pieces[i][:, c * HD : (c + 1) * HD]
                for i in range(hit_count)
            )
            columns.append(part / total[:, c : c + 1])
        joined = jnp.concatenate(columns, axis=1)
    joined = joined.astype(jnp.bfloat16)
    result[:, :WIDE] = joined[:ROWS]
    result[:, WIDE:] = joined[ROWS:]


def vmem(count):
    return [pl.BlockSpec(memory_space=pltpu.VMEM)] * count


def smem(count):
    return [pl.BlockSpec(memory_space=pltpu.SMEM)] * count


def hbm(count):
    return [pl.BlockSpec(memory_space=pltpu.HBM)] * count


def body(prefix_len, hits, span_block, queries, fresh_keys, fresh_values, cache_keys, cache_values):
    devices = lax.axis_size("cache")
    hit_count = hits.shape[1]
    rows = devices * MSG
    owners = hits.reshape(REQUESTS * hit_count)
    fresh = (owners, queries, fresh_keys, fresh_values)

    def exchange(x):
        return lax.all_to_all(x, "cache", split_axis=0, concat_axis=0, tiled=True)

    def call(kernel, out_shape, name, grant=40, **kw):
        return pl.pallas_call(
            functools.partial(kernel, devices, hit_count),
            out_shape=[
                jax.ShapeDtypeStruct(*leaf) if isinstance(leaf, tuple) else leaf
                for leaf in out_shape
            ],
            compiler_params=pltpu.CompilerParams(vmem_limit_bytes=grant * 2**20),
            name=name,
            **kw,
        )

    if hit_count == 1 and devices == 16:
        pairs = rows * (HALF + HALF // 2) * (REGION + rows)
        scalars = [pltpu.SMEM((devices,), jnp.int32)] * 2
        send, places, way = call(
            guest_pack_kernel,
            [
                pltpu.VMEM((rows, GUEST_MSG), jnp.bfloat16),
                ((2, 4 * ROWS), jnp.int32),
                ((1,), jnp.int32),
            ],
            "pack",
            in_specs=hbm(5),
            out_specs=vmem(2) + smem(1),
            scratch_shapes=[
                pltpu.VMEM((2 * ROWS, WIDE + HD), jnp.bfloat16),
                *[pltpu.SMEM((REQUESTS,), jnp.int32)] * 2,
                *scalars,
                pltpu.SemaphoreType.DMA((6,)),
            ],
        )(
            *(
                pltpu.with_memory_space_constraint(x, pltpu.HBM)
                for x in (owners, prefix_len, queries, fresh_keys, fresh_values)
            )
        )
        got = exchange(send)
        shapes = [((HD, REGION), jnp.bfloat16), ((REGION, 2 * HD), jnp.bfloat16)]
        def chain(form, owners, prefix_len, span_block, places, cache_keys, cache_values):
            ways, height = form
            pinned = [
                pltpu.with_memory_space_constraint(x, pltpu.HBM)
                for x in (owners, prefix_len, span_block)
            ]
            slots = [cache_keys[REGION:], cache_values[REGION:]]
            lent = [
                [
                    lax.ppermute(
                        x[:height], "cache", [(d, d ^ (2 * n)) for d in range(1, devices, 2)]
                    )
                    for x in slots
                ]
                for n in ways
            ]
            prepared = call(
                guest_prep_kernel,
                [((2,), jnp.int32), ((2 * rows, rows), jnp.float32), ((2, REGION), jnp.float32)]
                + shapes
                + [((2 * ROWS, rows), jnp.bfloat16), ((4 * ROWS, rows), jnp.bfloat16)]
                + [((8, HD), jnp.int32)],
                "prep",
                grant=12,
                in_specs=smem(2) + vmem(4),
                out_specs=smem(1) + vmem(7),
                scratch_shapes=scalars,
                cost_estimate=pl.CostEstimate(
                    flops=10**6, bytes_accessed=2**22, transcendentals=0
                ),
            )(*pinned, places, cache_keys, cache_values)
            plan = prepared[0]
            for n, borrowed in zip(ways, lent):
                slots = [
                    jnp.where(plan[0] == n, jnp.pad(x, ((0, REGION - height), (0, 0))), y)
                    for x, y in zip(borrowed, slots)
                ]
            swapped = [lax.ppermute(x, "cache", [(d, d ^ 1) for d in range(devices)]) for x in slots]
            guest = [
                call(
                    functools.partial(host_kernel, prepare),
                    [shape],
                    "host",
                    grant=12,
                    in_specs=smem(1) + vmem(2),
                    out_specs=vmem(1),
                )(plan, mine, other)[0]
                for prepare, shape, mine, other in zip((turn, widen), shapes, slots, swapped)
            ]
            return (*prepared[1:], *guest)

        forms = [
            ((), REGION),
            ((1,), 2 * STRIP),
            ((1,), 3 * STRIP),
            ((1,), REGION),
            ((2,), 2 * STRIP),
            ((2,), 3 * STRIP),
            ((2,), REGION),
            ((1, 2, 3), REGION),
        ]
        prepared = lax.switch(
            way.reshape(()),
            [functools.partial(chain, form) for form in forms],
            owners,
            prefix_len,
            span_block,
            places,
            cache_keys,
            cache_values,
        )
        prompt_mask, cached_mask, turned, wide, picks, picks_guest, strips_of = prepared[:7]
        turned_guest, wide_guest = prepared[7:]
        (answer,) = call(
            guest_attend_kernel,
            [((rows, WIDE + WIDE // 2), jnp.bfloat16)],
            "attend",
            in_specs=vmem(8),
            out_specs=vmem(1),
            cost_estimate=pl.CostEstimate(
                flops=4 * pairs * HD, bytes_accessed=8 * rows * WIDE, transcendentals=pairs
            ),
        )(strips_of, prompt_mask, cached_mask, got, turned, wide, turned_guest, wide_guest)
        return call(
            guest_unpack_kernel,
            [((ROWS, HEADS * HD), jnp.bfloat16)],
            "unpack",
            in_specs=vmem(3),
            out_specs=hbm(1),
            scratch_shapes=[
                pltpu.VMEM((ROWS, HEADS * HD), jnp.bfloat16),
                pltpu.SemaphoreType.DMA((2,)),
            ],
        )(picks, picks_guest, exchange(answer))[0]
    send, places = call(
        pack_kernel,
        [((rows, CAP * (WIDE + HD)), jnp.bfloat16), ((CAP * hit_count, 2 * ROWS), jnp.int32)],
        "pack",
        in_specs=hbm(4),
        out_specs=vmem(2),
        scratch_shapes=[
            pltpu.VMEM((2 * ROWS, WIDE + HD), jnp.bfloat16),
            pltpu.SMEM((REQUESTS * hit_count,), jnp.int32),
            pltpu.SMEM((devices,), jnp.int32),
            pltpu.SemaphoreType.DMA((5,)),
        ],
    )(*(pltpu.with_memory_space_constraint(x, pltpu.HBM) for x in fresh))
    got = exchange(send)
    busy, prompt_mask, cached_mask, turned, wide, picks = call(
        prep_kernel,
        [
            ((CAP,), jnp.int32),
            ((CAP * rows, rows), jnp.float32),
            ((CAP, REGION), jnp.float32),
            ((HD, CAP * REGION), jnp.bfloat16),
            ((CAP * REGION, 2 * HD), jnp.bfloat16),
            ((CAP * hit_count * 2 * ROWS, rows), jnp.bfloat16),
        ],
        "prep",
        in_specs=smem(2) + vmem(4),
        out_specs=smem(1) + vmem(5),
        cost_estimate=pl.CostEstimate(flops=10**6, bytes_accessed=2**22, transcendentals=0),
    )(owners, prefix_len, span_block, places, cache_keys, cache_values)
    pairs = CAP * rows * HALF * (REGION + rows)
    answers = call(
        attend_kernel,
        [((rows, CAP * WIDE), jnp.bfloat16)]
        + [((rows, CAP * HD), jnp.float32)] * (hit_count > 1),
        "attend",
        in_specs=smem(1) + vmem(5),
        out_specs=vmem(1 + (hit_count > 1)),
        cost_estimate=pl.CostEstimate(
            flops=4 * pairs * HD, bytes_accessed=8 * rows * WIDE, transcendentals=pairs
        ),
    )(busy, prompt_mask, cached_mask, got, turned, wide)
    returned = [exchange(answer) for answer in answers]
    return call(
        unpack_kernel,
        [((ROWS, HEADS * HD), jnp.bfloat16)],
        "unpack",
        in_specs=vmem(1 + len(returned)),
        out_specs=vmem(1),
    )(picks, *returned)[0]


def solution(mesh):
    in_specs = (
        P("groups"),
        P("groups", None),
        P("groups", None),
        P(("groups", "cache"), None),
        P(("groups", "cache"), None),
        P(("groups", "cache"), None),
        P(("groups", "cache"), None),
        P(("groups", "cache"), None),
    )
    out_specs = P(("groups", "cache"), None)
    return jax.shard_map(body, mesh=mesh, in_specs=in_specs, out_specs=out_specs, check_vma=False)
```

```python
import functools
import math

import jax
import jax.numpy as jnp
from jax import lax
from jax.experimental import pallas as pl
from jax.experimental.pallas import tpu as pltpu
from jax.sharding import PartitionSpec as P

HEADS = 16
HD = 128
PAGE = 128
CAP = 2
REQUESTS = 16
TOK_REQ = 4
PAGES_DEV = 16

REGION = PAGES_DEV // CAP * PAGE
HALF = HEADS // 2
MSG = 2 * TOK_REQ
WIDE = HALF * HD
ROWS = REQUESTS * TOK_REQ
STRIP = 256
GUEST_MSG = WIDE + HD + WIDE // 2 + HD
SCALE = HD**-0.5
FLOOR = -1e30
NN = (((1,), (0,)), ((), ()))


def iota(shape, axis):
    return lax.broadcasted_iota(jnp.int32, shape, axis)


def dot(a, b, dims, **kw):
    return lax.dot_general(a, b, dims, preferred_element_type=jnp.float32, **kw)


def pack_kernel(devices, hit_count, owners, q, k, v, send, places, held, hits, count, sems):
    copies = [
        pltpu.make_async_copy(source, held.at[pl.ds(row, ROWS), pl.ds(column, width)], sems.at[n])
        for n, (source, row, column, width) in enumerate(
            [
                (q.at[:, pl.ds(0, WIDE)], 0, 0, WIDE),
                (q.at[:, pl.ds(WIDE, WIDE)], ROWS, 0, WIDE),
                (k, 0, WIDE, HD),
                (v, ROWS, WIDE, HD),
            ]
        )
    ]
    first = pltpu.make_async_copy(owners, hits, sems.at[4])
    first.start()
    for copy in copies:
        copy.start()
    lane = iota((1, 2 * ROWS), 1)
    lane_request = (lane % ROWS) // TOK_REQ
    first.wait()
    for r in range(REQUESTS):
        for i in range(hit_count):
            count[hits[r * hit_count + i]] = 0
    rows = [[jnp.full((1, 2 * ROWS), -4 * MSG, jnp.int32)] * hit_count for _ in range(CAP)]
    for r in range(REQUESTS):
        for i in range(hit_count):
            owner = hits[r * hit_count + i]
            rank = count[owner]
            count[owner] = rank + 1
            for s in range(CAP):
                place = jnp.where(rank == s, owner * MSG, -4 * MSG)
                rows[s][i] = jnp.where(lane_request == r, place, rows[s][i])
    inner = lane // ROWS * TOK_REQ + lane % TOK_REQ
    target = iota((devices * MSG, 2 * ROWS), 0)
    picks = []
    for s in range(CAP):
        chosen = None
        for i in range(hit_count):
            row = rows[s][i] + inner
            places[s * hit_count + i : s * hit_count + i + 1, :] = row
            hit = target == row
            chosen = hit if chosen is None else chosen | hit
        picks.append(jnp.where(chosen, 1.0, 0.0).astype(jnp.bfloat16))
    for copy in copies:
        copy.wait()
    packed = dot(jnp.concatenate(picks, axis=0), held[...], NN).astype(jnp.bfloat16)
    for s in range(CAP):
        rows = slice(s * devices * MSG, (s + 1) * devices * MSG)
        send[:, s * (WIDE + HD) : (s + 1) * (WIDE + HD)] = packed[rows]


def prep_kernel(
    devices, hit_count, hits, prefix_len, span, places, keys, values, *outs
):
    busy, prompt, cached, turned, wide, picks = outs
    rows = iota((devices * MSG, 2 * ROWS), 0)
    for n in range(CAP * hit_count):
        chosen = jnp.where(rows == places[n : n + 1, :], 1.0, 0.0)
        picks[n * 2 * ROWS : (n + 1) * 2 * ROWS, :] = chosen.T.astype(jnp.bfloat16)
    for n in range(0, CAP * REGION, STRIP):
        turned[:, n : n + STRIP] = keys[n : n + STRIP, :].T
    me = lax.axis_index("cache")
    wide[:, :HD] = values[...]
    wide[:, HD:] = jnp.ones((CAP * REGION, HD), jnp.bfloat16)
    for slot in range(CAP):
        seen = jnp.int32(0)
        request = jnp.int32(0)
        which = jnp.int32(0)
        for r in range(REQUESTS):
            for i in range(hit_count):
                mine = hits[r * hit_count + i] == me
                here = mine & (seen == slot)
                request = jnp.where(here, r, request)
                which = jnp.where(here, i, which)
                seen = seen + mine.astype(jnp.int32)
        limit = prefix_len[request] - which * REGION
        blocks = jnp.clip((limit + STRIP - 1) // STRIP, 1, REGION // STRIP)
        busy[slot] = jnp.where(seen > slot, blocks, 0)
        cached[slot : slot + 1, :] = jnp.where(iota((1, REGION), 1) < limit, 0.0, FLOOR)
        prompt_rows(devices, prompt, span, request, slot, hit_count == 1 or which == 0)


def prompt_rows(devices, prompt, span, request, slot, counted):
    total_rows = devices * MSG
    span_row = span[pl.ds(request, 1), :].astype(jnp.float32)
    source = iota((devices, total_rows), 0)
    spread = (iota((devices, total_rows), 1) // MSG == source).astype(jnp.bfloat16)
    spans = jnp.broadcast_to(span_row, (16, devices)).astype(jnp.bfloat16)
    key_span = dot(spans, spread, NN)[:1]
    lane = iota((1, total_rows), 1)
    key_spot = key_span.astype(jnp.int32) * TOK_REQ + lane % TOK_REQ
    is_key = (lane % MSG < TOK_REQ) & counted
    key_spot = jnp.where(is_key, key_spot, devices * TOK_REQ)
    block = 16 * MSG

    def one_block(at):
        row_source = at * 16 + iota((block, devices), 0) // MSG
        mine = iota((block, devices), 1) == row_source
        row_span = jnp.sum(jnp.where(mine, span_row, 0.0), axis=1, keepdims=True)
        row_spot = row_span.astype(jnp.int32) * TOK_REQ + iota((block, 1), 0) % TOK_REQ
        here = pl.ds(slot * total_rows + at * block, block)
        prompt[here, :] = jnp.where(key_spot <= row_spot, 0.0, FLOOR)

    each_block(devices, one_block)


def each_block(devices, one_block):
    blocks = devices // 16
    if blocks == 1:
        one_block(0)
    else:
        pl.loop(0, blocks)(one_block)


def lanes_max(parts):
    pieces = [part[:, n : n + HD] for part in parts for n in range(0, part.shape[1], HD)]
    return jnp.max(functools.reduce(jnp.maximum, pieces), axis=1, keepdims=True)


def attend_kernel(
    devices, hit_count, busy, prompt_mask, cached_mask, got, turned, wide, out, *levels
):
    total_rows = devices * MSG
    block = 16 * MSG
    factor = SCALE * math.log2(math.e)

    def nothing(slot):
        out[:, pl.ds(slot * WIDE, WIDE)] = jnp.zeros((total_rows, WIDE), jnp.bfloat16)
        for lse in levels:
            lse[:, pl.ds(slot * HD, HD)] = jnp.zeros((total_rows, HD), jnp.float32)

    def attend(slot, strips):
        whole = (strips - 1) * STRIP
        base = pl.multiple_of(slot * (WIDE + HD), HD)
        region = pl.multiple_of(slot * REGION, REGION)
        head = pl.ds(region, whole) if whole else None
        tail = pl.ds(pl.multiple_of(region + whole, STRIP), STRIP)
        tail_mask = cached_mask[pl.ds(slot, 1), whole : whole + STRIP]
        prompt_keys = got[:, pl.ds(base + WIDE, HD)].astype(jnp.float32)
        moved = pltpu.roll(prompt_keys, total_rows - TOK_REQ, 0)
        prompt_keys = prompt_keys.T.astype(jnp.bfloat16)
        prompt_values = jnp.concatenate(
            [moved.astype(jnp.bfloat16), jnp.ones((total_rows, HD), jnp.bfloat16)], axis=1
        )

        def one_block(at):
            here = pl.ds(at * block, block)
            prompt_bias = prompt_mask[pl.ds(slot * total_rows + at * block, block), :]
            prompt_bias = jnp.concatenate([prompt_bias, prompt_bias], axis=0)
            lane = iota((block, HD), 1)

            def scores(c):
                pair = jnp.concatenate(
                    [got[here, pl.ds(base + (c + n) * HD, HD)] for n in range(2)], axis=0
                )
                parts = [dot(pair, turned[:, head], NN)] if whole else []
                parts.append(dot(pair, turned[:, tail], NN) + tail_mask)
                parts.append(dot(pair, prompt_keys, NN) + prompt_bias)
                return parts

            logs = jnp.zeros((block, HD), jnp.float32)
            parts = scores(0)
            for c in range(0, HALF, 2):
                later = scores(c + 2) if c + 2 < HALF else None
                top = lanes_max(parts)
                if hit_count > 1:
                    top = jnp.maximum(top, 0.1 * FLOOR)
                parts = [jnp.exp2((x - top) * factor).astype(jnp.bfloat16) for x in parts]
                summed = dot(parts[-1], prompt_values, NN) + dot(parts[-2], wide[tail, :], NN)
                if whole:
                    summed = summed + dot(parts[0], wide[head, :], NN)
                totals = summed[:, HD:]
                if hit_count > 1:
                    totals = jnp.maximum(totals, 1.0)
                    level = top * SCALE + jnp.log(totals)
                    logs = jnp.where(lane == c, level[:block], logs)
                    logs = jnp.where(lane == c + 1, level[block:], logs)
                result = (summed[:, :HD] / totals).astype(jnp.bfloat16)
                for n in range(2):
                    column = pl.multiple_of(slot * WIDE + (c + n) * HD, HD)
                    out[here, pl.ds(column, HD)] = result[n * block : (n + 1) * block]
                parts = later
            for lse in levels:
                lse[here, pl.ds(pl.multiple_of(slot * HD, HD), HD)] = logs

        each_block(devices, one_block)

    @pl.loop(0, CAP)
    def _(slot):
        strips = busy[slot]
        pl.when(strips == 0)(lambda: nothing(slot))
        for count in range(1, REGION // STRIP + 1):
            pl.when(strips == count)(functools.partial(attend, slot, count))


def owner_ranks(devices, owners, count):
    for d in range(devices):
        count[d] = 0
    ranks = []
    for r in range(REQUESTS):
        owner = owners[r]
        ranks.append(count[owner])
        count[owner] = ranks[r] + 1
    return ranks


def guest_plan(devices, count, host):
    chips = devices // 2
    seconds = [count[d] > 1 for d in range(devices)]
    none = [jnp.logical_not(seconds[2 * x] | seconds[2 * x + 1]) for x in range(chips)]
    lends = []
    for x in range(chips):
        other = jnp.where(none[x ^ 1], 1, jnp.where(none[x ^ 2], 2, 3))
        lends.append(jnp.where(seconds[2 * x] & seconds[2 * x + 1], other, 0))
        host[2 * x] = jnp.int32(x)
        host[2 * x + 1] = lends[x] ^ x
    return lends


def guest_pack_kernel(devices, hit_count, owners, lengths, q, k, v, *refs):
    send, places, way, held, hits, prefix_len, count, host, sems = refs
    half = WIDE // 2
    moves = [
        (owners, hits),
        (k, held.at[pl.ds(0, ROWS), pl.ds(WIDE, HD)]),
        (v, held.at[pl.ds(ROWS, ROWS), pl.ds(WIDE, HD)]),
        (lengths, prefix_len),
    ]
    for g in range(4):
        here = held.at[pl.ds(g // 2 * ROWS, ROWS), pl.ds(g % 2 * half, half)]
        moves.append((q.at[:, pl.ds(g * half, half)], here))
    copies = [pltpu.make_async_copy(a, b, sems.at[n]) for n, (a, b) in enumerate(moves)]
    for copy in copies:
        copy.start()
    lane = iota((1, 4 * ROWS), 1)
    lane_request = lane % ROWS // TOK_REQ
    part = lane // ROWS * TOK_REQ
    nowhere = jnp.full((1, 4 * ROWS), -4 * MSG, jnp.int32)
    target = iota((devices * MSG, 2 * ROWS), 0)
    copies[0].wait()
    ranks = owner_ranks(devices, hits, count)
    own = nowhere
    for r in range(REQUESTS):
        place = jnp.where(ranks[r] == 0, hits[r] * MSG, -4 * MSG)
        own = jnp.where(lane_request == r, place, own)
    own = own + lane % TOK_REQ + part

    def rows_of(chosen, first, width):
        pick = jnp.where(chosen, 1.0, 0.0).astype(jnp.bfloat16)
        return dot(pick, held[:, first : first + width], NN)

    for copy in copies[1:]:
        copy.wait()
    rows = rows_of(target == own[:, : 2 * ROWS], 0, WIDE + HD)
    send[:, : WIDE + HD] = rows.astype(jnp.bfloat16)
    lends = guest_plan(devices, count, host)
    guest = nowhere
    longest = jnp.int32(0)
    for r in range(REQUESTS):
        chip = host[hits[r]]
        place = jnp.where(ranks[r] == 1, chip * 2 * MSG, -4 * MSG)
        guest = jnp.where(lane_request == r, place, guest)
        lent = (ranks[r] == 1) & (chip != hits[r] // 2)
        longest = jnp.maximum(longest, jnp.where(lent, prefix_len[r], 0))
    guest = guest + lane % TOK_REQ
    places[0:1, :] = own
    places[1:2, :] = guest + part
    guest, part = guest[:, : 2 * ROWS], part[:, : 2 * ROWS]
    rows = rows_of(target == guest + 2 * part, 0, half)
    rows = rows + rows_of(target == guest + 2 * part + TOK_REQ, half, half)
    send[:, WIDE + HD : WIDE + HD + half] = rows.astype(jnp.bfloat16)
    both = (target == guest + part) | (target == guest + MSG + part)
    send[:, WIDE + HD + half :] = rows_of(both, WIDE, HD).astype(jnp.bfloat16)
    used = [
        functools.reduce(jnp.logical_or, [lend == n for lend in lends]) for n in range(1, 4)
    ]
    mixed = used[2] | (used[0] & used[1])
    kind = jnp.where(mixed, 7, jnp.where(used[0], 1, jnp.where(used[1], 4, 0)))
    size = jnp.where(longest > 3 * STRIP, 2, jnp.where(longest > 2 * STRIP, 1, 0))
    way[0] = kind + jnp.where((kind > 0) & (kind < 7), size, 0)


def guest_prep_kernel(
    devices, hit_count, hits, prefix_len, span, places, keys, values, *refs
):
    plan, prompt, cached, turned, wide, picks, picks_guest, strips_of, count, host = refs
    me = lax.axis_index("cache")
    chip = me // 2
    ranks = owner_ranks(devices, hits, count)
    guest_plan(devices, count, host)
    rows = iota((devices * MSG, 4 * ROWS), 0)
    chosen = jnp.where(rows[:, : 2 * ROWS] == places[0:1, : 2 * ROWS], 1.0, 0.0)
    picks[...] = chosen.T.astype(jnp.bfloat16)
    chosen = jnp.where(rows == places[1:2, :], 1.0, 0.0)
    picks_guest[...] = chosen.T.astype(jnp.bfloat16)
    turn(keys[:REGION, :], turned)
    widen(values[:REGION, :], wide)
    first, guest, source = jnp.int32(-1), jnp.int32(-1), jnp.int32(0)
    for r in range(REQUESTS):
        owner = hits[r]
        here = (ranks[r] == 1) & (host[owner] == chip)
        first = jnp.where((ranks[r] == 0) & (owner == me), r, first)
        guest = jnp.where(here, r, guest)
        source = jnp.where(here, owner, source)
    core = me % 2
    from_first_core = jnp.where(source == 2 * chip, 1, 0)
    plan[0] = jnp.where(core == 1, (source // 2) ^ chip, 0)
    plan[1] = jnp.where(core == from_first_core, 1, 0)
    for job, found in enumerate((first, guest)):
        request = jnp.maximum(found, 0)
        limit = prefix_len[request]
        strips = jnp.clip((limit + STRIP - 1) // STRIP, 1, REGION // STRIP)
        strips_of[job : job + 1, :] = jnp.full((1, HD), jnp.where(found >= 0, strips, 0))
        cached[job : job + 1, :] = jnp.where(iota((1, REGION), 1) < limit, 0.0, FLOOR)
        prompt_rows(devices, prompt, span, request, job, True)


def turn(keys, turned):
    for n in range(0, REGION, STRIP):
        turned[:, n : n + STRIP] = keys[n : n + STRIP].T


def widen(values, wide):
    wide[:, :HD] = values
    wide[:, HD:] = jnp.ones((REGION, HD), jnp.bfloat16)


def host_kernel(prepare, devices, hit_count, plan, mine, other, out):
    for choice, rows in enumerate((mine, other)):

        @pl.when(plan[1] == choice)
        def _():
            prepare(rows[...], out)


def guest_attend_kernel(
    devices, hit_count, strips_of, prompt_mask, cached_mask, got, turned, wide, *refs
):
    turned_guest, wide_guest, out = refs
    jobs = [
        (0, 0, HALF, turned, wide),
        (WIDE + HD, WIDE, HALF // 2, turned_guest, wide_guest),
    ]
    for job, (base, first, blocks, keys, values) in enumerate(jobs):
        strips = strips_of[job, 0]

        @pl.when(strips == 0)
        def _():
            empty = jnp.zeros((devices * MSG, blocks * HD), jnp.bfloat16)
            out[:, first : first + blocks * HD] = empty

        for count in range(1, REGION // STRIP + 1):

            @pl.when(strips == count)
            def _():
                whole = (count - 1) * STRIP
                mask = prompt_mask[job * devices * MSG : (job + 1) * devices * MSG, :]
                attend_rows(
                    got,
                    base,
                    blocks,
                    slice(0, devices * MSG),
                    prompt_parts(got[:, base + blocks * HD : base + (blocks + 1) * HD]),
                    mask,
                    cached_mask[job : job + 1, whole : whole + STRIP],
                    keys[:, : whole + STRIP],
                    values[: whole + STRIP, :],
                    out,
                    first,
                )


def prompt_parts(rows):
    height = rows.shape[0]
    wide = rows.astype(jnp.float32)
    moved = pltpu.roll(wide, height - TOK_REQ, 0).astype(jnp.bfloat16)
    values = jnp.concatenate([moved, jnp.ones((height, HD), jnp.bfloat16)], axis=1)
    return wide.T.astype(jnp.bfloat16), values


def attend_rows(
    got, base, blocks, here, prompt, mask, tail_mask, keys, values, out, first
):
    prompt_keys, prompt_values = prompt
    factor = SCALE * math.log2(math.e)
    mask = jnp.concatenate([mask, mask], axis=0)
    height = mask.shape[0] // 2

    def scores(c):
        pair = jnp.concatenate(
            [got[here, base + (c + n) * HD : base + (c + n + 1) * HD] for n in range(2)], axis=0
        )
        cached = dot(pair, keys, NN)
        whole = cached.shape[1] - STRIP
        tail = cached[:, whole:] + tail_mask
        cached = jnp.concatenate([cached[:, :whole], tail], axis=1) if whole else tail
        return [cached, dot(pair, prompt_keys, NN) + mask]

    parts = scores(0)
    for c in range(0, blocks, 2):
        later = scores(c + 2) if c + 2 < blocks else None
        top = lanes_max(parts)
        parts = [jnp.exp2((x - top) * factor).astype(jnp.bfloat16) for x in parts]
        summed = dot(parts[0], values, NN) + dot(parts[1], prompt_values, NN)
        result = (summed[:, :HD] / summed[:, HD:]).astype(jnp.bfloat16)
        for n in range(2):
            column = first + (c + n) * HD
            out[here, column : column + HD] = result[n * height : (n + 1) * height]
        parts = later


def guest_unpack_kernel(devices, hit_count, picks, picks_guest, outs, result, held, sems):
    half = WIDE // 2
    copies = []
    for n in range(2):
        own = dot(picks[n * ROWS : (n + 1) * ROWS, :], outs[:, :WIDE], NN)
        for g in (2 * n, 2 * n + 1):
            guest = dot(picks_guest[g * ROWS : (g + 1) * ROWS, :], outs[:, WIDE:], NN)
            rows = own[:, g % 2 * half : (g % 2 + 1) * half] + guest
            held[:, g * half : (g + 1) * half] = rows.astype(jnp.bfloat16)
        here = pl.ds(n * WIDE, WIDE)
        copies.append(pltpu.make_async_copy(held.at[:, here], result.at[:, here], sems.at[n]))
        copies[n].start()
    for copy in copies:
        copy.wait()


def unpack_kernel(devices, hit_count, picks, *refs):
    outs, logs, result = refs[0], refs[1:-1], refs[-1]

    def chosen(s, i):
        place = s * hit_count + i
        return picks[place * 2 * ROWS : (place + 1) * 2 * ROWS, :]

    def rows_of(i):
        parts = [
            dot(chosen(s, i), outs[:, s * WIDE : (s + 1) * WIDE], NN)
            for s in range(CAP)
        ]
        return sum(parts[1:], parts[0])

    def logs_of(i):
        parts = [
            dot(
                chosen(s, i).astype(jnp.float32),
                logs[0][:, s * HD : (s + 1) * HD],
                NN,
                precision=lax.Precision.HIGHEST,
            )
            for s in range(CAP)
        ]
        return sum(parts[1:], parts[0])

    if hit_count == 1:
        joined = rows_of(0)
    else:
        levels = [logs_of(i) for i in range(hit_count)]
        top = functools.reduce(jnp.maximum, levels)
        shares = [jnp.exp(level - top) for level in levels]
        total = sum(shares[1:], shares[0])
        pieces = [rows_of(i) for i in range(hit_count)]
        columns = []
        for c in range(HALF):
            part = sum(
                shares[i][:, c : c + 1] * pieces[i][:, c * HD : (c + 1) * HD]
                for i in range(hit_count)
            )
            columns.append(part / total[:, c : c + 1])
        joined = jnp.concatenate(columns, axis=1)
    joined = joined.astype(jnp.bfloat16)
    result[:, :WIDE] = joined[:ROWS]
    result[:, WIDE:] = joined[ROWS:]


def vmem(count):
    return [pl.BlockSpec(memory_space=pltpu.VMEM)] * count


def smem(count):
    return [pl.BlockSpec(memory_space=pltpu.SMEM)] * count


def hbm(count):
    return [pl.BlockSpec(memory_space=pltpu.HBM)] * count


def body(prefix_len, hits, span_block, queries, fresh_keys, fresh_values, cache_keys, cache_values):
    devices = lax.axis_size("cache")
    hit_count = hits.shape[1]
    rows = devices * MSG
    owners = hits.reshape(REQUESTS * hit_count)
    fresh = (owners, queries, fresh_keys, fresh_values)

    def exchange(x):
        return lax.all_to_all(x, "cache", split_axis=0, concat_axis=0, tiled=True)

    def call(kernel, out_shape, name, grant=40, **kw):
        return pl.pallas_call(
            functools.partial(kernel, devices, hit_count),
            out_shape=[
                jax.ShapeDtypeStruct(*leaf) if isinstance(leaf, tuple) else leaf
                for leaf in out_shape
            ],
            compiler_params=pltpu.CompilerParams(vmem_limit_bytes=grant * 2**20),
            name=name,
            **kw,
        )

    if hit_count == 1 and devices == 16:
        pairs = rows * (HALF + HALF // 2) * (REGION + rows)
        scalars = [pltpu.SMEM((devices,), jnp.int32)] * 2
        send, places, way = call(
            guest_pack_kernel,
            [
                pltpu.VMEM((rows, GUEST_MSG), jnp.bfloat16),
                ((2, 4 * ROWS), jnp.int32),
                ((1,), jnp.int32),
            ],
            "pack",
            in_specs=hbm(5),
            out_specs=vmem(2) + smem(1),
            scratch_shapes=[
                pltpu.VMEM((2 * ROWS, WIDE + HD), jnp.bfloat16),
                *[pltpu.SMEM((REQUESTS,), jnp.int32)] * 2,
                *scalars,
                pltpu.SemaphoreType.DMA((8,)),
            ],
        )(
            *(
                pltpu.with_memory_space_constraint(x, pltpu.HBM)
                for x in (owners, prefix_len, queries, fresh_keys, fresh_values)
            )
        )
        got = exchange(send)
        shapes = [((HD, REGION), jnp.bfloat16), ((REGION, 2 * HD), jnp.bfloat16)]
        def chain(form, owners, prefix_len, span_block, places, cache_keys, cache_values):
            ways, height = form
            pinned = [
                pltpu.with_memory_space_constraint(x, pltpu.HBM)
                for x in (owners, prefix_len, span_block)
            ]
            slots = [cache_keys[REGION:], cache_values[REGION:]]
            lent = [
                [
                    lax.ppermute(
                        x[:height], "cache", [(d, d ^ (2 * n)) for d in range(1, devices, 2)]
                    )
                    for x in slots
                ]
                for n in ways
            ]
            prepared = call(
                guest_prep_kernel,
                [((2,), jnp.int32), ((2 * rows, rows), jnp.float32), ((2, REGION), jnp.float32)]
                + shapes
                + [((2 * ROWS, rows), jnp.bfloat16), ((4 * ROWS, rows), jnp.bfloat16)]
                + [((8, HD), jnp.int32)],
                "prep",
                grant=12,
                in_specs=smem(2) + vmem(4),
                out_specs=smem(1) + vmem(7),
                scratch_shapes=scalars,
                cost_estimate=pl.CostEstimate(
                    flops=10**6, bytes_accessed=2**22, transcendentals=0
                ),
            )(*pinned, places, cache_keys, cache_values)
            plan = prepared[0]
            for n, borrowed in zip(ways, lent):
                slots = [
                    jnp.where(plan[0] == n, jnp.pad(x, ((0, REGION - height), (0, 0))), y)
                    for x, y in zip(borrowed, slots)
                ]
            swapped = [lax.ppermute(x, "cache", [(d, d ^ 1) for d in range(devices)]) for x in slots]
            guest = [
                call(
                    functools.partial(host_kernel, prepare),
                    [shape],
                    "host",
                    grant=12,
                    in_specs=smem(1) + vmem(2),
                    out_specs=vmem(1),
                )(plan, mine, other)[0]
                for prepare, shape, mine, other in zip((turn, widen), shapes, slots, swapped)
            ]
            return (*prepared[1:], *guest)

        forms = [
            ((), REGION),
            ((1,), 2 * STRIP),
            ((1,), 3 * STRIP),
            ((1,), REGION),
            ((2,), 2 * STRIP),
            ((2,), 3 * STRIP),
            ((2,), REGION),
            ((1, 2, 3), REGION),
        ]
        prepared = lax.switch(
            way.reshape(()),
            [functools.partial(chain, form) for form in forms],
            owners,
            prefix_len,
            span_block,
            places,
            cache_keys,
            cache_values,
        )
        prompt_mask, cached_mask, turned, wide, picks, picks_guest, strips_of = prepared[:7]
        turned_guest, wide_guest = prepared[7:]
        (answer,) = call(
            guest_attend_kernel,
            [((rows, WIDE + WIDE // 2), jnp.bfloat16)],
            "attend",
            in_specs=vmem(8),
            out_specs=vmem(1),
            cost_estimate=pl.CostEstimate(
                flops=4 * pairs * HD, bytes_accessed=8 * rows * WIDE, transcendentals=pairs
            ),
        )(strips_of, prompt_mask, cached_mask, got, turned, wide, turned_guest, wide_guest)
        return call(
            guest_unpack_kernel,
            [((ROWS, HEADS * HD), jnp.bfloat16)],
            "unpack",
            in_specs=vmem(3),
            out_specs=hbm(1),
            scratch_shapes=[
                pltpu.VMEM((ROWS, HEADS * HD), jnp.bfloat16),
                pltpu.SemaphoreType.DMA((2,)),
            ],
        )(picks, picks_guest, exchange(answer))[0]
    send, places = call(
        pack_kernel,
        [((rows, CAP * (WIDE + HD)), jnp.bfloat16), ((CAP * hit_count, 2 * ROWS), jnp.int32)],
        "pack",
        in_specs=hbm(4),
        out_specs=vmem(2),
        scratch_shapes=[
            pltpu.VMEM((2 * ROWS, WIDE + HD), jnp.bfloat16),
            pltpu.SMEM((REQUESTS * hit_count,), jnp.int32),
            pltpu.SMEM((devices,), jnp.int32),
            pltpu.SemaphoreType.DMA((5,)),
        ],
    )(*(pltpu.with_memory_space_constraint(x, pltpu.HBM) for x in fresh))
    got = exchange(send)
    busy, prompt_mask, cached_mask, turned, wide, picks = call(
        prep_kernel,
        [
            ((CAP,), jnp.int32),
            ((CAP * rows, rows), jnp.float32),
            ((CAP, REGION), jnp.float32),
            ((HD, CAP * REGION), jnp.bfloat16),
            ((CAP * REGION, 2 * HD), jnp.bfloat16),
            ((CAP * hit_count * 2 * ROWS, rows), jnp.bfloat16),
        ],
        "prep",
        in_specs=smem(2) + vmem(4),
        out_specs=smem(1) + vmem(5),
        cost_estimate=pl.CostEstimate(flops=10**6, bytes_accessed=2**22, transcendentals=0),
    )(owners, prefix_len, span_block, places, cache_keys, cache_values)
    pairs = CAP * rows * HALF * (REGION + rows)
    answers = call(
        attend_kernel,
        [((rows, CAP * WIDE), jnp.bfloat16)]
        + [((rows, CAP * HD), jnp.float32)] * (hit_count > 1),
        "attend",
        in_specs=smem(1) + vmem(5),
        out_specs=vmem(1 + (hit_count > 1)),
        cost_estimate=pl.CostEstimate(
            flops=4 * pairs * HD, bytes_accessed=8 * rows * WIDE, transcendentals=pairs
        ),
    )(busy, prompt_mask, cached_mask, got, turned, wide)
    returned = [exchange(answer) for answer in answers]
    return call(
        unpack_kernel,
        [((ROWS, HEADS * HD), jnp.bfloat16)],
        "unpack",
        in_specs=vmem(1 + len(returned)),
        out_specs=vmem(1),
    )(picks, *returned)[0]


def solution(mesh):
    in_specs = (
        P("groups"),
        P("groups", None),
        P("groups", None),
        P(("groups", "cache"), None),
        P(("groups", "cache"), None),
        P(("groups", "cache"), None),
        P(("groups", "cache"), None),
        P(("groups", "cache"), None),
    )
    out_specs = P(("groups", "cache"), None)
    return jax.shard_map(body, mesh=mesh, in_specs=in_specs, out_specs=out_specs, check_vma=False)
```

```python
import functools
import math

import jax
import jax.numpy as jnp
from jax import lax
from jax.experimental import pallas as pl
from jax.experimental.pallas import tpu as pltpu
from jax.sharding import PartitionSpec as P

HEADS = 16
HD = 128
PAGE = 128
CAP = 2
REQUESTS = 16
TOK_REQ = 4
PAGES_DEV = 16

REGION = PAGES_DEV // CAP * PAGE
HALF = HEADS // 2
MSG = 2 * TOK_REQ
WIDE = HALF * HD
ROWS = REQUESTS * TOK_REQ
STRIP = 256
GUEST_MSG = WIDE + HD + WIDE // 2 + HD
SCALE = HD**-0.5
FLOOR = -1e30
NN = (((1,), (0,)), ((), ()))


def iota(shape, axis):
    return lax.broadcasted_iota(jnp.int32, shape, axis)


def dot(a, b, dims, **kw):
    return lax.dot_general(a, b, dims, preferred_element_type=jnp.float32, **kw)


def pack_kernel(devices, hit_count, owners, q, k, v, send, places, held, hits, count, sems):
    copies = [
        pltpu.make_async_copy(source, held.at[pl.ds(row, ROWS), pl.ds(column, width)], sems.at[n])
        for n, (source, row, column, width) in enumerate(
            [
                (q.at[:, pl.ds(0, WIDE)], 0, 0, WIDE),
                (q.at[:, pl.ds(WIDE, WIDE)], ROWS, 0, WIDE),
                (k, 0, WIDE, HD),
                (v, ROWS, WIDE, HD),
            ]
        )
    ]
    first = pltpu.make_async_copy(owners, hits, sems.at[4])
    first.start()
    for copy in copies:
        copy.start()
    lane = iota((1, 2 * ROWS), 1)
    lane_request = (lane % ROWS) // TOK_REQ
    first.wait()
    for r in range(REQUESTS):
        for i in range(hit_count):
            count[hits[r * hit_count + i]] = 0
    rows = [[jnp.full((1, 2 * ROWS), -4 * MSG, jnp.int32)] * hit_count for _ in range(CAP)]
    for r in range(REQUESTS):
        for i in range(hit_count):
            owner = hits[r * hit_count + i]
            rank = count[owner]
            count[owner] = rank + 1
            for s in range(CAP):
                place = jnp.where(rank == s, owner * MSG, -4 * MSG)
                rows[s][i] = jnp.where(lane_request == r, place, rows[s][i])
    inner = lane // ROWS * TOK_REQ + lane % TOK_REQ
    target = iota((devices * MSG, 2 * ROWS), 0)
    picks = []
    for s in range(CAP):
        chosen = None
        for i in range(hit_count):
            row = rows[s][i] + inner
            places[s * hit_count + i : s * hit_count + i + 1, :] = row
            hit = target == row
            chosen = hit if chosen is None else chosen | hit
        picks.append(jnp.where(chosen, 1.0, 0.0).astype(jnp.bfloat16))
    for copy in copies:
        copy.wait()
    packed = dot(jnp.concatenate(picks, axis=0), held[...], NN).astype(jnp.bfloat16)
    for s in range(CAP):
        rows = slice(s * devices * MSG, (s + 1) * devices * MSG)
        send[:, s * (WIDE + HD) : (s + 1) * (WIDE + HD)] = packed[rows]


def prep_kernel(
    devices, hit_count, hits, prefix_len, span, places, keys, values, *outs
):
    busy, prompt, cached, turned, wide, picks = outs
    rows = iota((devices * MSG, 2 * ROWS), 0)
    for n in range(CAP * hit_count):
        chosen = jnp.where(rows == places[n : n + 1, :], 1.0, 0.0)
        picks[n * 2 * ROWS : (n + 1) * 2 * ROWS, :] = chosen.T.astype(jnp.bfloat16)
    for n in range(0, CAP * REGION, STRIP):
        turned[:, n : n + STRIP] = keys[n : n + STRIP, :].T
    me = lax.axis_index("cache")
    wide[:, :HD] = values[...]
    wide[:, HD:] = jnp.ones((CAP * REGION, HD), jnp.bfloat16)
    for slot in range(CAP):
        seen = jnp.int32(0)
        request = jnp.int32(0)
        which = jnp.int32(0)
        for r in range(REQUESTS):
            for i in range(hit_count):
                mine = hits[r * hit_count + i] == me
                here = mine & (seen == slot)
                request = jnp.where(here, r, request)
                which = jnp.where(here, i, which)
                seen = seen + mine.astype(jnp.int32)
        limit = prefix_len[request] - which * REGION
        blocks = jnp.clip((limit + STRIP - 1) // STRIP, 1, REGION // STRIP)
        busy[slot] = jnp.where(seen > slot, blocks, 0)
        cached[slot : slot + 1, :] = jnp.where(iota((1, REGION), 1) < limit, 0.0, FLOOR)
        prompt_rows(devices, prompt, span, request, slot, hit_count == 1 or which == 0)


def prompt_rows(devices, prompt, span, request, slot, counted):
    total_rows = devices * MSG
    span_row = span[pl.ds(request, 1), :].astype(jnp.float32)
    source = iota((devices, total_rows), 0)
    spread = (iota((devices, total_rows), 1) // MSG == source).astype(jnp.bfloat16)
    spans = jnp.broadcast_to(span_row, (16, devices)).astype(jnp.bfloat16)
    key_span = dot(spans, spread, NN)[:1]
    lane = iota((1, total_rows), 1)
    key_spot = key_span.astype(jnp.int32) * TOK_REQ + lane % TOK_REQ
    is_key = (lane % MSG < TOK_REQ) & counted
    key_spot = jnp.where(is_key, key_spot, devices * TOK_REQ)
    block = 16 * MSG

    def one_block(at):
        row_source = at * 16 + iota((block, devices), 0) // MSG
        mine = iota((block, devices), 1) == row_source
        row_span = jnp.sum(jnp.where(mine, span_row, 0.0), axis=1, keepdims=True)
        row_spot = row_span.astype(jnp.int32) * TOK_REQ + iota((block, 1), 0) % TOK_REQ
        here = pl.ds(slot * total_rows + at * block, block)
        prompt[here, :] = jnp.where(key_spot <= row_spot, 0.0, FLOOR)

    each_block(devices, one_block)


def each_block(devices, one_block):
    blocks = devices // 16
    if blocks == 1:
        one_block(0)
    else:
        pl.loop(0, blocks)(one_block)


def lanes_max(parts):
    pieces = [part[:, n : n + HD] for part in parts for n in range(0, part.shape[1], HD)]
    return jnp.max(functools.reduce(jnp.maximum, pieces), axis=1, keepdims=True)


def attend_kernel(
    devices, hit_count, busy, prompt_mask, cached_mask, got, turned, wide, out, *levels
):
    total_rows = devices * MSG
    block = 16 * MSG
    factor = SCALE * math.log2(math.e)

    def nothing(slot):
        out[:, pl.ds(slot * WIDE, WIDE)] = jnp.zeros((total_rows, WIDE), jnp.bfloat16)
        for lse in levels:
            lse[:, pl.ds(slot * HD, HD)] = jnp.zeros((total_rows, HD), jnp.float32)

    def attend(slot, strips):
        whole = (strips - 1) * STRIP
        base = pl.multiple_of(slot * (WIDE + HD), HD)
        region = pl.multiple_of(slot * REGION, REGION)
        head = pl.ds(region, whole) if whole else None
        tail = pl.ds(pl.multiple_of(region + whole, STRIP), STRIP)
        tail_mask = cached_mask[pl.ds(slot, 1), whole : whole + STRIP]
        prompt_keys = got[:, pl.ds(base + WIDE, HD)].astype(jnp.float32)
        moved = pltpu.roll(prompt_keys, total_rows - TOK_REQ, 0)
        prompt_keys = prompt_keys.T.astype(jnp.bfloat16)
        prompt_values = jnp.concatenate(
            [moved.astype(jnp.bfloat16), jnp.ones((total_rows, HD), jnp.bfloat16)], axis=1
        )

        def one_block(at):
            here = pl.ds(at * block, block)
            prompt_bias = prompt_mask[pl.ds(slot * total_rows + at * block, block), :]
            prompt_bias = jnp.concatenate([prompt_bias, prompt_bias], axis=0)
            lane = iota((block, HD), 1)

            def scores(c):
                pair = jnp.concatenate(
                    [got[here, pl.ds(base + (c + n) * HD, HD)] for n in range(2)], axis=0
                )
                parts = [dot(pair, turned[:, head], NN)] if whole else []
                parts.append(dot(pair, turned[:, tail], NN) + tail_mask)
                parts.append(dot(pair, prompt_keys, NN) + prompt_bias)
                return parts

            logs = jnp.zeros((block, HD), jnp.float32)
            parts = scores(0)
            for c in range(0, HALF, 2):
                later = scores(c + 2) if c + 2 < HALF else None
                top = lanes_max(parts)
                if hit_count > 1:
                    top = jnp.maximum(top, 0.1 * FLOOR)
                parts = [jnp.exp2((x - top) * factor).astype(jnp.bfloat16) for x in parts]
                summed = dot(parts[-1], prompt_values, NN) + dot(parts[-2], wide[tail, :], NN)
                if whole:
                    summed = summed + dot(parts[0], wide[head, :], NN)
                totals = summed[:, HD:]
                if hit_count > 1:
                    totals = jnp.maximum(totals, 1.0)
                    level = top * SCALE + jnp.log(totals)
                    logs = jnp.where(lane == c, level[:block], logs)
                    logs = jnp.where(lane == c + 1, level[block:], logs)
                result = (summed[:, :HD] / totals).astype(jnp.bfloat16)
                for n in range(2):
                    column = pl.multiple_of(slot * WIDE + (c + n) * HD, HD)
                    out[here, pl.ds(column, HD)] = result[n * block : (n + 1) * block]
                parts = later
            for lse in levels:
                lse[here, pl.ds(pl.multiple_of(slot * HD, HD), HD)] = logs

        each_block(devices, one_block)

    @pl.loop(0, CAP)
    def _(slot):
        strips = busy[slot]
        pl.when(strips == 0)(lambda: nothing(slot))
        for count in range(1, REGION // STRIP + 1):
            pl.when(strips == count)(functools.partial(attend, slot, count))


def owner_ranks(devices, owners, count):
    for d in range(devices):
        count[d] = 0
    ranks = []
    for r in range(REQUESTS):
        owner = owners[r]
        ranks.append(count[owner])
        count[owner] = ranks[r] + 1
    return ranks


def guest_plan(devices, count, host):
    chips = devices // 2
    seconds = [count[d] > 1 for d in range(devices)]
    none = [jnp.logical_not(seconds[2 * x] | seconds[2 * x + 1]) for x in range(chips)]
    lends = []
    for x in range(chips):
        other = jnp.where(none[x ^ 1], 1, jnp.where(none[x ^ 2], 2, 3))
        lends.append(jnp.where(seconds[2 * x] & seconds[2 * x + 1], other, 0))
        host[2 * x] = jnp.int32(x)
        host[2 * x + 1] = lends[x] ^ x
    return lends


def guest_pack_kernel(devices, hit_count, owners, lengths, q, k, v, *refs):
    send, places, way, held, hits, prefix_len, count, host, sems = refs
    half = WIDE // 2
    moves = [
        (owners, hits),
        (k, held.at[pl.ds(0, ROWS), pl.ds(WIDE, HD)]),
        (v, held.at[pl.ds(ROWS, ROWS), pl.ds(WIDE, HD)]),
        (lengths, prefix_len),
    ]
    for g in range(4):
        here = held.at[pl.ds(g // 2 * ROWS, ROWS), pl.ds(g % 2 * half, half)]
        moves.append((q.at[:, pl.ds(g * half, half)], here))
    copies = [pltpu.make_async_copy(a, b, sems.at[n]) for n, (a, b) in enumerate(moves)]
    for copy in copies:
        copy.start()
    lane = iota((1, 4 * ROWS), 1)
    lane_request = lane % ROWS // TOK_REQ
    part = lane // ROWS * TOK_REQ
    nowhere = jnp.full((1, 4 * ROWS), -4 * MSG, jnp.int32)
    target = iota((devices * MSG, 2 * ROWS), 0)
    copies[0].wait()
    ranks = owner_ranks(devices, hits, count)
    own = nowhere
    for r in range(REQUESTS):
        place = jnp.where(ranks[r] == 0, hits[r] * MSG, -4 * MSG)
        own = jnp.where(lane_request == r, place, own)
    own = own + lane % TOK_REQ + part

    def rows_of(chosen, first, width):
        pick = jnp.where(chosen, 1.0, 0.0).astype(jnp.bfloat16)
        return dot(pick, held[:, first : first + width], NN)

    for copy in copies[1:]:
        copy.wait()
    rows = rows_of(target == own[:, : 2 * ROWS], 0, WIDE + HD)
    send[:, : WIDE + HD] = rows.astype(jnp.bfloat16)
    lends = guest_plan(devices, count, host)
    guest = nowhere
    longest = jnp.int32(0)
    for r in range(REQUESTS):
        chip = host[hits[r]]
        place = jnp.where(ranks[r] == 1, chip * 2 * MSG, -4 * MSG)
        guest = jnp.where(lane_request == r, place, guest)
        lent = (ranks[r] == 1) & (chip != hits[r] // 2)
        longest = jnp.maximum(longest, jnp.where(lent, prefix_len[r], 0))
    guest = guest + lane % TOK_REQ
    places[0:1, :] = own
    places[1:2, :] = guest + part
    guest, part = guest[:, : 2 * ROWS], part[:, : 2 * ROWS]
    rows = rows_of(target == guest + 2 * part, 0, half)
    rows = rows + rows_of(target == guest + 2 * part + TOK_REQ, half, half)
    send[:, WIDE + HD : WIDE + HD + half] = rows.astype(jnp.bfloat16)
    both = (target == guest + part) | (target == guest + MSG + part)
    send[:, WIDE + HD + half :] = rows_of(both, WIDE, HD).astype(jnp.bfloat16)
    used = [
        functools.reduce(jnp.logical_or, [lend == n for lend in lends]) for n in range(1, 4)
    ]
    mixed = used[2] | (used[0] & used[1])
    kind = jnp.where(mixed, 7, jnp.where(used[0], 1, jnp.where(used[1], 4, 0)))
    size = jnp.where(longest > 3 * STRIP, 2, jnp.where(longest > 2 * STRIP, 1, 0))
    way[0] = kind + jnp.where((kind > 0) & (kind < 7), size, 0)


def guest_prep_kernel(
    split, devices, hit_count, hits, prefix_len, span, places, keys, values, *refs
):
    plan, prompt, cached, turned, wide, picks, picks_guest, strips_of, count, host = refs
    me = lax.axis_index("cache")
    chip = me // 2
    ranks = owner_ranks(devices, hits, count)
    guest_plan(devices, count, host)
    rows = iota((devices * MSG, 4 * ROWS), 0)
    chosen = jnp.where(rows[:, : 2 * ROWS] == places[0:1, : 2 * ROWS], 1.0, 0.0)
    picks[...] = chosen.T.astype(jnp.bfloat16)
    chosen = jnp.where(rows == places[1:2, :], 1.0, 0.0)
    picks_guest[...] = chosen.T.astype(jnp.bfloat16)
    turn(keys[:REGION, :], turned)
    widen(values[:REGION, :], wide)
    first, guest, source = jnp.int32(-1), jnp.int32(-1), jnp.int32(0)
    for r in range(REQUESTS):
        owner = hits[r]
        here = (ranks[r] == 1) & (host[owner] == chip)
        first = jnp.where((ranks[r] == 0) & (owner == me), r, first)
        guest = jnp.where(here, r, guest)
        source = jnp.where(here, owner, source)
    core = me % 2
    from_first_core = jnp.where(source == 2 * chip, 1, 0)
    way = (source // 2) ^ chip
    plan[0] = jnp.where(core == 1, way, 0)
    plan[1] = jnp.where(core == from_first_core, 1, 0)
    plan[2] = jnp.where(core == 0, way, 0) if split else plan[0]
    plan[3] = jnp.where(way > 0, core, plan[1]) if split else plan[1]
    for job, found in enumerate((first, guest)):
        request = jnp.maximum(found, 0)
        limit = prefix_len[request]
        strips = jnp.clip((limit + STRIP - 1) // STRIP, 1, REGION // STRIP)
        strips_of[job : job + 1, :] = jnp.full((1, HD), jnp.where(found >= 0, strips, 0))
        cached[job : job + 1, :] = jnp.where(iota((1, REGION), 1) < limit, 0.0, FLOOR)
        prompt_rows(devices, prompt, span, request, job, True)


def turn(keys, turned):
    for n in range(0, REGION, STRIP):
        turned[:, n : n + STRIP] = keys[n : n + STRIP].T


def widen(values, wide):
    wide[:, :HD] = values
    wide[:, HD:] = jnp.ones((REGION, HD), jnp.bfloat16)


def host_kernel(prepare, at, devices, hit_count, plan, mine, other, out):
    for choice, rows in enumerate((mine, other)):

        @pl.when(plan[at] == choice)
        def _():
            prepare(rows[...], out)


def guest_attend_kernel(
    devices, hit_count, strips_of, prompt_mask, cached_mask, got, turned, wide, *refs
):
    turned_guest, wide_guest, out = refs
    jobs = [
        (0, 0, HALF, turned, wide),
        (WIDE + HD, WIDE, HALF // 2, turned_guest, wide_guest),
    ]
    for job, (base, first, blocks, keys, values) in enumerate(jobs):
        strips = strips_of[job, 0]

        @pl.when(strips == 0)
        def _():
            empty = jnp.zeros((devices * MSG, blocks * HD), jnp.bfloat16)
            out[:, first : first + blocks * HD] = empty

        for count in range(1, REGION // STRIP + 1):

            @pl.when(strips == count)
            def _():
                whole = (count - 1) * STRIP
                mask = prompt_mask[job * devices * MSG : (job + 1) * devices * MSG, :]
                attend_rows(
                    got,
                    base,
                    blocks,
                    slice(0, devices * MSG),
                    prompt_parts(got[:, base + blocks * HD : base + (blocks + 1) * HD]),
                    mask,
                    cached_mask[job : job + 1, whole : whole + STRIP],
                    keys[:, : whole + STRIP],
                    values[: whole + STRIP, :],
                    out,
                    first,
                )


def prompt_parts(rows):
    height = rows.shape[0]
    wide = rows.astype(jnp.float32)
    moved = pltpu.roll(wide, height - TOK_REQ, 0).astype(jnp.bfloat16)
    values = jnp.concatenate([moved, jnp.ones((height, HD), jnp.bfloat16)], axis=1)
    return wide.T.astype(jnp.bfloat16), values


def attend_rows(
    got, base, blocks, here, prompt, mask, tail_mask, keys, values, out, first
):
    prompt_keys, prompt_values = prompt
    factor = SCALE * math.log2(math.e)
    mask = jnp.concatenate([mask, mask], axis=0)
    height = mask.shape[0] // 2

    def scores(c):
        pair = jnp.concatenate(
            [got[here, base + (c + n) * HD : base + (c + n + 1) * HD] for n in range(2)], axis=0
        )
        cached = dot(pair, keys, NN)
        whole = cached.shape[1] - STRIP
        tail = cached[:, whole:] + tail_mask
        cached = jnp.concatenate([cached[:, :whole], tail], axis=1) if whole else tail
        return [cached, dot(pair, prompt_keys, NN) + mask]

    parts = scores(0)
    for c in range(0, blocks, 2):
        later = scores(c + 2) if c + 2 < blocks else None
        top = lanes_max(parts)
        parts = [jnp.exp2((x - top) * factor).astype(jnp.bfloat16) for x in parts]
        summed = dot(parts[0], values, NN) + dot(parts[1], prompt_values, NN)
        result = (summed[:, :HD] / summed[:, HD:]).astype(jnp.bfloat16)
        for n in range(2):
            column = first + (c + n) * HD
            out[here, column : column + HD] = result[n * height : (n + 1) * height]
        parts = later


def guest_unpack_kernel(devices, hit_count, picks, picks_guest, outs, result, held, sems):
    half = WIDE // 2
    copies = []
    for n in range(2):
        own = dot(picks[n * ROWS : (n + 1) * ROWS, :], outs[:, :WIDE], NN)
        for g in (2 * n, 2 * n + 1):
            guest = dot(picks_guest[g * ROWS : (g + 1) * ROWS, :], outs[:, WIDE:], NN)
            rows = own[:, g % 2 * half : (g % 2 + 1) * half] + guest
            held[:, g * half : (g + 1) * half] = rows.astype(jnp.bfloat16)
        here = pl.ds(n * WIDE, WIDE)
        copies.append(pltpu.make_async_copy(held.at[:, here], result.at[:, here], sems.at[n]))
        copies[n].start()
    for copy in copies:
        copy.wait()


def unpack_kernel(devices, hit_count, picks, *refs):
    outs, logs, result = refs[0], refs[1:-1], refs[-1]

    def chosen(s, i):
        place = s * hit_count + i
        return picks[place * 2 * ROWS : (place + 1) * 2 * ROWS, :]

    def rows_of(i):
        parts = [
            dot(chosen(s, i), outs[:, s * WIDE : (s + 1) * WIDE], NN)
            for s in range(CAP)
        ]
        return sum(parts[1:], parts[0])

    def logs_of(i):
        parts = [
            dot(
                chosen(s, i).astype(jnp.float32),
                logs[0][:, s * HD : (s + 1) * HD],
                NN,
                precision=lax.Precision.HIGHEST,
            )
            for s in range(CAP)
        ]
        return sum(parts[1:], parts[0])

    if hit_count == 1:
        joined = rows_of(0)
    else:
        levels = [logs_of(i) for i in range(hit_count)]
        top = functools.reduce(jnp.maximum, levels)
        shares = [jnp.exp(level - top) for level in levels]
        total = sum(shares[1:], shares[0])
        pieces = [rows_of(i) for i in range(hit_count)]
        columns = []
        for c in range(HALF):
            part = sum(
                shares[i][:, c : c + 1] * pieces[i][:, c * HD : (c + 1) * HD]
                for i in range(hit_count)
            )
            columns.append(part / total[:, c : c + 1])
        joined = jnp.concatenate(columns, axis=1)
    joined = joined.astype(jnp.bfloat16)
    result[:, :WIDE] = joined[:ROWS]
    result[:, WIDE:] = joined[ROWS:]


def vmem(count):
    return [pl.BlockSpec(memory_space=pltpu.VMEM)] * count


def smem(count):
    return [pl.BlockSpec(memory_space=pltpu.SMEM)] * count


def hbm(count):
    return [pl.BlockSpec(memory_space=pltpu.HBM)] * count


def body(prefix_len, hits, span_block, queries, fresh_keys, fresh_values, cache_keys, cache_values):
    devices = lax.axis_size("cache")
    hit_count = hits.shape[1]
    rows = devices * MSG
    owners = hits.reshape(REQUESTS * hit_count)
    fresh = (owners, queries, fresh_keys, fresh_values)

    def exchange(x):
        return lax.all_to_all(x, "cache", split_axis=0, concat_axis=0, tiled=True)

    def call(kernel, out_shape, name, grant=40, **kw):
        return pl.pallas_call(
            functools.partial(kernel, devices, hit_count),
            out_shape=[
                jax.ShapeDtypeStruct(*leaf) if isinstance(leaf, tuple) else leaf
                for leaf in out_shape
            ],
            compiler_params=pltpu.CompilerParams(vmem_limit_bytes=grant * 2**20),
            name=name,
            **kw,
        )

    if hit_count == 1 and devices == 16:
        pairs = rows * (HALF + HALF // 2) * (REGION + rows)
        scalars = [pltpu.SMEM((devices,), jnp.int32)] * 2
        send, places, way = call(
            guest_pack_kernel,
            [
                pltpu.VMEM((rows, GUEST_MSG), jnp.bfloat16),
                ((2, 4 * ROWS), jnp.int32),
                ((1,), jnp.int32),
            ],
            "pack",
            in_specs=hbm(5),
            out_specs=vmem(2) + smem(1),
            scratch_shapes=[
                pltpu.VMEM((2 * ROWS, WIDE + HD), jnp.bfloat16),
                *[pltpu.SMEM((REQUESTS,), jnp.int32)] * 2,
                *scalars,
                pltpu.SemaphoreType.DMA((8,)),
            ],
        )(
            *(
                pltpu.with_memory_space_constraint(x, pltpu.HBM)
                for x in (owners, prefix_len, queries, fresh_keys, fresh_values)
            )
        )
        got = exchange(send)
        shapes = [((HD, REGION), jnp.bfloat16), ((REGION, 2 * HD), jnp.bfloat16)]
        def chain(form, owners, prefix_len, span_block, places, cache_keys, cache_values):
            ways, height, split = form

            pinned = [
                pltpu.with_memory_space_constraint(x, pltpu.HBM)
                for x in (owners, prefix_len, span_block)
            ]
            slots = [cache_keys[REGION:], cache_values[REGION:]]
            lent = []
            for n in ways:
                ends = [(d, d ^ (2 * n)) for d in range(devices)]
                sent = [x[:height] for x in slots]
                if split:
                    sent[1] = lax.ppermute(sent[1], "cache", [(d, d - 1) for d in range(1, devices, 2)])
                lent.append(
                    [
                        lax.ppermute(sent[0], "cache", ends[1::2]),
                        lax.ppermute(sent[1], "cache", ends[0::2] if split else ends[1::2]),
                    ]
                )
            prepared = call(
                functools.partial(guest_prep_kernel, split),
                [((4,), jnp.int32), ((2 * rows, rows), jnp.float32), ((2, REGION), jnp.float32)]
                + shapes
                + [((2 * ROWS, rows), jnp.bfloat16), ((4 * ROWS, rows), jnp.bfloat16)]
                + [((8, HD), jnp.int32)],
                "prep",
                grant=12,
                in_specs=smem(2) + vmem(4),
                out_specs=smem(1) + vmem(7),
                scratch_shapes=scalars,
                cost_estimate=pl.CostEstimate(
                    flops=10**6, bytes_accessed=2**22, transcendentals=0
                ),
            )(*pinned, places, cache_keys, cache_values)
            plan = prepared[0]
            for n, borrowed in zip(ways, lent):
                slots = [
                    jnp.where(plan[at] == n, jnp.pad(x, ((0, REGION - height), (0, 0))), y)
                    for at, x, y in zip((0, 2), borrowed, slots)
                ]
            swapped = [lax.ppermute(x, "cache", [(d, d ^ 1) for d in range(devices)]) for x in slots]
            guest = [
                call(
                    functools.partial(host_kernel, prepare, at),
                    [shape],
                    "host",
                    grant=12,
                    in_specs=smem(1) + vmem(2),
                    out_specs=vmem(1),
                )(plan, mine, other)[0]
                for prepare, at, shape, mine, other in zip(
                    (turn, widen), (1, 3), shapes, slots, swapped
                )
            ]
            return (*prepared[1:], *guest)

        forms = [
            ((), REGION, False),
            ((1,), 2 * STRIP, False),
            ((1,), 3 * STRIP, True),
            ((1,), REGION, True),
            ((2,), 2 * STRIP, False),
            ((2,), 3 * STRIP, True),
            ((2,), REGION, True),
            ((1, 2, 3), REGION, False),
        ]
        prepared = lax.switch(
            way.reshape(()),
            [functools.partial(chain, form) for form in forms],
            owners,
            prefix_len,
            span_block,
            places,
            cache_keys,
            cache_values,
        )
        prompt_mask, cached_mask, turned, wide, picks, picks_guest, strips_of = prepared[:7]
        turned_guest, wide_guest = prepared[7:]
        (answer,) = call(
            guest_attend_kernel,
            [((rows, WIDE + WIDE // 2), jnp.bfloat16)],
            "attend",
            in_specs=vmem(8),
            out_specs=vmem(1),
            cost_estimate=pl.CostEstimate(
                flops=4 * pairs * HD, bytes_accessed=8 * rows * WIDE, transcendentals=pairs
            ),
        )(strips_of, prompt_mask, cached_mask, got, turned, wide, turned_guest, wide_guest)
        return call(
            guest_unpack_kernel,
            [((ROWS, HEADS * HD), jnp.bfloat16)],
            "unpack",
            in_specs=vmem(3),
            out_specs=hbm(1),
            scratch_shapes=[
                pltpu.VMEM((ROWS, HEADS * HD), jnp.bfloat16),
                pltpu.SemaphoreType.DMA((2,)),
            ],
        )(picks, picks_guest, exchange(answer))[0]
    send, places = call(
        pack_kernel,
        [((rows, CAP * (WIDE + HD)), jnp.bfloat16), ((CAP * hit_count, 2 * ROWS), jnp.int32)],
        "pack",
        in_specs=hbm(4),
        out_specs=vmem(2),
        scratch_shapes=[
            pltpu.VMEM((2 * ROWS, WIDE + HD), jnp.bfloat16),
            pltpu.SMEM((REQUESTS * hit_count,), jnp.int32),
            pltpu.SMEM((devices,), jnp.int32),
            pltpu.SemaphoreType.DMA((5,)),
        ],
    )(*(pltpu.with_memory_space_constraint(x, pltpu.HBM) for x in fresh))
    got = exchange(send)
    busy, prompt_mask, cached_mask, turned, wide, picks = call(
        prep_kernel,
        [
            ((CAP,), jnp.int32),
            ((CAP * rows, rows), jnp.float32),
            ((CAP, REGION), jnp.float32),
            ((HD, CAP * REGION), jnp.bfloat16),
            ((CAP * REGION, 2 * HD), jnp.bfloat16),
            ((CAP * hit_count * 2 * ROWS, rows), jnp.bfloat16),
        ],
        "prep",
        in_specs=smem(2) + vmem(4),
        out_specs=smem(1) + vmem(5),
        cost_estimate=pl.CostEstimate(flops=10**6, bytes_accessed=2**22, transcendentals=0),
    )(owners, prefix_len, span_block, places, cache_keys, cache_values)
    pairs = CAP * rows * HALF * (REGION + rows)
    answers = call(
        attend_kernel,
        [((rows, CAP * WIDE), jnp.bfloat16)]
        + [((rows, CAP * HD), jnp.float32)] * (hit_count > 1),
        "attend",
        in_specs=smem(1) + vmem(5),
        out_specs=vmem(1 + (hit_count > 1)),
        cost_estimate=pl.CostEstimate(
            flops=4 * pairs * HD, bytes_accessed=8 * rows * WIDE, transcendentals=pairs
        ),
    )(busy, prompt_mask, cached_mask, got, turned, wide)
    returned = [exchange(answer) for answer in answers]
    return call(
        unpack_kernel,
        [((ROWS, HEADS * HD), jnp.bfloat16)],
        "unpack",
        in_specs=vmem(1 + len(returned)),
        out_specs=vmem(1),
    )(picks, *returned)[0]


def solution(mesh):
    in_specs = (
        P("groups"),
        P("groups", None),
        P("groups", None),
        P(("groups", "cache"), None),
        P(("groups", "cache"), None),
        P(("groups", "cache"), None),
        P(("groups", "cache"), None),
        P(("groups", "cache"), None),
    )
    out_specs = P(("groups", "cache"), None)
    return jax.shard_map(body, mesh=mesh, in_specs=in_specs, out_specs=out_specs, check_vma=False)
```

```python
import functools
import math

import jax
import jax.numpy as jnp
from jax import lax
from jax.experimental import pallas as pl
from jax.experimental.pallas import tpu as pltpu
from jax.sharding import PartitionSpec as P

HEADS = 16
HD = 128
PAGE = 128
CAP = 2
REQUESTS = 16
TOK_REQ = 4
PAGES_DEV = 16

REGION = PAGES_DEV // CAP * PAGE
HALF = HEADS // 2
MSG = 2 * TOK_REQ
WIDE = HALF * HD
ROWS = REQUESTS * TOK_REQ
STRIP = 256
GUEST_MSG = WIDE + HD + WIDE // 2 + HD
SCALE = HD**-0.5
FLOOR = -1e30
NN = (((1,), (0,)), ((), ()))


def iota(shape, axis):
    return lax.broadcasted_iota(jnp.int32, shape, axis)


def dot(a, b, dims, **kw):
    return lax.dot_general(a, b, dims, preferred_element_type=jnp.float32, **kw)


def pack_kernel(devices, hit_count, owners, q, k, v, send, places, held, hits, count, sems):
    copies = [
        pltpu.make_async_copy(source, held.at[pl.ds(row, ROWS), pl.ds(column, width)], sems.at[n])
        for n, (source, row, column, width) in enumerate(
            [
                (q.at[:, pl.ds(0, WIDE)], 0, 0, WIDE),
                (q.at[:, pl.ds(WIDE, WIDE)], ROWS, 0, WIDE),
                (k, 0, WIDE, HD),
                (v, ROWS, WIDE, HD),
            ]
        )
    ]
    first = pltpu.make_async_copy(owners, hits, sems.at[4])
    first.start()
    for copy in copies:
        copy.start()
    lane = iota((1, 2 * ROWS), 1)
    lane_request = (lane % ROWS) // TOK_REQ
    first.wait()
    for r in range(REQUESTS):
        for i in range(hit_count):
            count[hits[r * hit_count + i]] = 0
    rows = [[jnp.full((1, 2 * ROWS), -4 * MSG, jnp.int32)] * hit_count for _ in range(CAP)]
    for r in range(REQUESTS):
        for i in range(hit_count):
            owner = hits[r * hit_count + i]
            rank = count[owner]
            count[owner] = rank + 1
            for s in range(CAP):
                place = jnp.where(rank == s, owner * MSG, -4 * MSG)
                rows[s][i] = jnp.where(lane_request == r, place, rows[s][i])
    inner = lane // ROWS * TOK_REQ + lane % TOK_REQ
    target = iota((devices * MSG, 2 * ROWS), 0)
    picks = []
    for s in range(CAP):
        chosen = None
        for i in range(hit_count):
            row = rows[s][i] + inner
            places[s * hit_count + i : s * hit_count + i + 1, :] = row
            hit = target == row
            chosen = hit if chosen is None else chosen | hit
        picks.append(jnp.where(chosen, 1.0, 0.0).astype(jnp.bfloat16))
    for copy in copies:
        copy.wait()
    packed = dot(jnp.concatenate(picks, axis=0), held[...], NN).astype(jnp.bfloat16)
    for s in range(CAP):
        rows = slice(s * devices * MSG, (s + 1) * devices * MSG)
        send[:, s * (WIDE + HD) : (s + 1) * (WIDE + HD)] = packed[rows]


def prep_kernel(
    devices, hit_count, hits, prefix_len, span, places, keys, values, *outs
):
    busy, prompt, cached, turned, wide, picks = outs
    rows = iota((devices * MSG, 2 * ROWS), 0)
    for n in range(CAP * hit_count):
        chosen = jnp.where(rows == places[n : n + 1, :], 1.0, 0.0)
        picks[n * 2 * ROWS : (n + 1) * 2 * ROWS, :] = chosen.T.astype(jnp.bfloat16)
    for n in range(0, CAP * REGION, STRIP):
        turned[:, n : n + STRIP] = keys[n : n + STRIP, :].T
    me = lax.axis_index("cache")
    wide[:, :HD] = values[...]
    wide[:, HD:] = jnp.ones((CAP * REGION, HD), jnp.bfloat16)
    for slot in range(CAP):
        seen = jnp.int32(0)
        request = jnp.int32(0)
        which = jnp.int32(0)
        for r in range(REQUESTS):
            for i in range(hit_count):
                mine = hits[r * hit_count + i] == me
                here = mine & (seen == slot)
                request = jnp.where(here, r, request)
                which = jnp.where(here, i, which)
                seen = seen + mine.astype(jnp.int32)
        limit = prefix_len[request] - which * REGION
        blocks = jnp.clip((limit + STRIP - 1) // STRIP, 1, REGION // STRIP)
        busy[slot] = jnp.where(seen > slot, blocks, 0)
        cached[slot : slot + 1, :] = jnp.where(iota((1, REGION), 1) < limit, 0.0, FLOOR)
        prompt_rows(devices, prompt, span, request, slot, hit_count == 1 or which == 0)


def prompt_rows(devices, prompt, span, request, slot, counted):
    total_rows = devices * MSG
    span_row = span[pl.ds(request, 1), :].astype(jnp.float32)
    source = iota((devices, total_rows), 0)
    spread = (iota((devices, total_rows), 1) // MSG == source).astype(jnp.bfloat16)
    spans = jnp.broadcast_to(span_row, (16, devices)).astype(jnp.bfloat16)
    key_span = dot(spans, spread, NN)[:1]
    lane = iota((1, total_rows), 1)
    key_spot = key_span.astype(jnp.int32) * TOK_REQ + lane % TOK_REQ
    is_key = (lane % MSG < TOK_REQ) & counted
    key_spot = jnp.where(is_key, key_spot, devices * TOK_REQ)
    block = 16 * MSG

    def one_block(at):
        row_source = at * 16 + iota((block, devices), 0) // MSG
        mine = iota((block, devices), 1) == row_source
        row_span = jnp.sum(jnp.where(mine, span_row, 0.0), axis=1, keepdims=True)
        row_spot = row_span.astype(jnp.int32) * TOK_REQ + iota((block, 1), 0) % TOK_REQ
        here = pl.ds(slot * total_rows + at * block, block)
        prompt[here, :] = jnp.where(key_spot <= row_spot, 0.0, FLOOR)

    each_block(devices, one_block)


def each_block(devices, one_block):
    blocks = devices // 16
    if blocks == 1:
        one_block(0)
    else:
        pl.loop(0, blocks)(one_block)


def lanes_max(parts):
    pieces = [part[:, n : n + HD] for part in parts for n in range(0, part.shape[1], HD)]
    return jnp.max(functools.reduce(jnp.maximum, pieces), axis=1, keepdims=True)


def attend_kernel(
    devices, hit_count, busy, prompt_mask, cached_mask, got, turned, wide, out, *levels
):
    total_rows = devices * MSG
    block = 16 * MSG
    factor = SCALE * math.log2(math.e)

    def nothing(slot):
        out[:, pl.ds(slot * WIDE, WIDE)] = jnp.zeros((total_rows, WIDE), jnp.bfloat16)
        for lse in levels:
            lse[:, pl.ds(slot * HD, HD)] = jnp.zeros((total_rows, HD), jnp.float32)

    def attend(slot, strips):
        whole = (strips - 1) * STRIP
        base = pl.multiple_of(slot * (WIDE + HD), HD)
        region = pl.multiple_of(slot * REGION, REGION)
        head = pl.ds(region, whole) if whole else None
        tail = pl.ds(pl.multiple_of(region + whole, STRIP), STRIP)
        tail_mask = cached_mask[pl.ds(slot, 1), whole : whole + STRIP]
        prompt_keys = got[:, pl.ds(base + WIDE, HD)].astype(jnp.float32)
        moved = pltpu.roll(prompt_keys, total_rows - TOK_REQ, 0)
        prompt_keys = prompt_keys.T.astype(jnp.bfloat16)
        prompt_values = jnp.concatenate(
            [moved.astype(jnp.bfloat16), jnp.ones((total_rows, HD), jnp.bfloat16)], axis=1
        )

        def one_block(at):
            here = pl.ds(at * block, block)
            prompt_bias = prompt_mask[pl.ds(slot * total_rows + at * block, block), :]
            prompt_bias = jnp.concatenate([prompt_bias, prompt_bias], axis=0)
            lane = iota((block, HD), 1)

            def scores(c):
                pair = jnp.concatenate(
                    [got[here, pl.ds(base + (c + n) * HD, HD)] for n in range(2)], axis=0
                )
                parts = [dot(pair, turned[:, head], NN)] if whole else []
                parts.append(dot(pair, turned[:, tail], NN) + tail_mask)
                parts.append(dot(pair, prompt_keys, NN) + prompt_bias)
                return parts

            logs = jnp.zeros((block, HD), jnp.float32)
            parts = scores(0)
            for c in range(0, HALF, 2):
                later = scores(c + 2) if c + 2 < HALF else None
                top = lanes_max(parts)
                if hit_count > 1:
                    top = jnp.maximum(top, 0.1 * FLOOR)
                parts = [jnp.exp2((x - top) * factor).astype(jnp.bfloat16) for x in parts]
                summed = dot(parts[-1], prompt_values, NN) + dot(parts[-2], wide[tail, :], NN)
                if whole:
                    summed = summed + dot(parts[0], wide[head, :], NN)
                totals = summed[:, HD:]
                if hit_count > 1:
                    totals = jnp.maximum(totals, 1.0)
                    level = top * SCALE + jnp.log(totals)
                    logs = jnp.where(lane == c, level[:block], logs)
                    logs = jnp.where(lane == c + 1, level[block:], logs)
                result = (summed[:, :HD] / totals).astype(jnp.bfloat16)
                for n in range(2):
                    column = pl.multiple_of(slot * WIDE + (c + n) * HD, HD)
                    out[here, pl.ds(column, HD)] = result[n * block : (n + 1) * block]
                parts = later
            for lse in levels:
                lse[here, pl.ds(pl.multiple_of(slot * HD, HD), HD)] = logs

        each_block(devices, one_block)

    @pl.loop(0, CAP)
    def _(slot):
        strips = busy[slot]
        pl.when(strips == 0)(lambda: nothing(slot))
        for count in range(1, REGION // STRIP + 1):
            pl.when(strips == count)(functools.partial(attend, slot, count))


def owner_ranks(devices, owners, count):
    for d in range(devices):
        count[d] = 0
    ranks = []
    for r in range(REQUESTS):
        owner = owners[r]
        ranks.append(count[owner])
        count[owner] = ranks[r] + 1
    return ranks


def guest_plan(devices, count, host):
    chips = devices // 2
    seconds = [count[d] > 1 for d in range(devices)]
    none = [jnp.logical_not(seconds[2 * x] | seconds[2 * x + 1]) for x in range(chips)]
    lends = []
    for x in range(chips):
        other = jnp.where(none[x ^ 1], 1, jnp.where(none[x ^ 2], 2, 3))
        lends.append(jnp.where(seconds[2 * x] & seconds[2 * x + 1], other, 0))
        host[2 * x] = jnp.int32(x)
        host[2 * x + 1] = lends[x] ^ x
    return lends


def guest_pack_kernel(devices, hit_count, owners, lengths, q, k, v, *refs):
    send, places, way, held, hits, prefix_len, count, host, sems = refs
    half = WIDE // 2
    moves = [
        (owners, hits),
        (k, held.at[pl.ds(0, ROWS), pl.ds(WIDE, HD)]),
        (v, held.at[pl.ds(ROWS, ROWS), pl.ds(WIDE, HD)]),
        (lengths, prefix_len),
    ]
    for g in range(4):
        here = held.at[pl.ds(g // 2 * ROWS, ROWS), pl.ds(g % 2 * half, half)]
        moves.append((q.at[:, pl.ds(g * half, half)], here))
    copies = [pltpu.make_async_copy(a, b, sems.at[n]) for n, (a, b) in enumerate(moves)]
    for copy in copies:
        copy.start()
    lane = iota((1, 4 * ROWS), 1)
    lane_request = lane % ROWS // TOK_REQ
    part = lane // ROWS * TOK_REQ
    nowhere = jnp.full((1, 4 * ROWS), -4 * MSG, jnp.int32)
    target = iota((devices * MSG, 2 * ROWS), 0)
    copies[0].wait()
    ranks = owner_ranks(devices, hits, count)
    own = nowhere
    for r in range(REQUESTS):
        place = jnp.where(ranks[r] == 0, hits[r] * MSG, -4 * MSG)
        own = jnp.where(lane_request == r, place, own)
    own = own + lane % TOK_REQ + part

    def rows_of(chosen, first, width):
        pick = jnp.where(chosen, 1.0, 0.0).astype(jnp.bfloat16)
        return dot(pick, held[:, first : first + width], NN)

    for copy in copies[1:]:
        copy.wait()
    rows = rows_of(target == own[:, : 2 * ROWS], 0, WIDE + HD)
    send[:, : WIDE + HD] = rows.astype(jnp.bfloat16)
    lends = guest_plan(devices, count, host)
    guest = nowhere
    longest = jnp.int32(0)
    for r in range(REQUESTS):
        chip = host[hits[r]]
        place = jnp.where(ranks[r] == 1, chip * 2 * MSG, -4 * MSG)
        guest = jnp.where(lane_request == r, place, guest)
        lent = (ranks[r] == 1) & (chip != hits[r] // 2)
        longest = jnp.maximum(longest, jnp.where(lent, prefix_len[r], 0))
    guest = guest + lane % TOK_REQ
    places[0:1, :] = own
    places[1:2, :] = guest + part
    guest, part = guest[:, : 2 * ROWS], part[:, : 2 * ROWS]
    rows = rows_of(target == guest + 2 * part, 0, half)
    rows = rows + rows_of(target == guest + 2 * part + TOK_REQ, half, half)
    send[:, WIDE + HD : WIDE + HD + half] = rows.astype(jnp.bfloat16)
    both = (target == guest + part) | (target == guest + MSG + part)
    send[:, WIDE + HD + half :] = rows_of(both, WIDE, HD).astype(jnp.bfloat16)
    used = [
        functools.reduce(jnp.logical_or, [lend == n for lend in lends]) for n in range(1, 4)
    ]
    mixed = used[2] | (used[0] & used[1])
    kind = jnp.where(mixed, 7, jnp.where(used[0], 1, jnp.where(used[1], 4, 0)))
    size = jnp.where(longest > 3 * STRIP, 2, jnp.where(longest > 2 * STRIP, 1, 0))
    way[0] = kind + jnp.where((kind > 0) & (kind < 7), size, 0)


def guest_prep_kernel(
    split, devices, hit_count, hits, prefix_len, span, places, keys, values, *refs
):
    plan, prompt, cached, turned, wide, picks, picks_guest, strips_of, count, host = refs
    me = lax.axis_index("cache")
    chip = me // 2
    ranks = owner_ranks(devices, hits, count)
    guest_plan(devices, count, host)
    rows = iota((devices * MSG, 4 * ROWS), 0)
    chosen = jnp.where(rows[:, : 2 * ROWS] == places[0:1, : 2 * ROWS], 1.0, 0.0)
    picks[...] = chosen.T.astype(jnp.bfloat16)
    chosen = jnp.where(rows == places[1:2, :], 1.0, 0.0)
    picks_guest[...] = chosen.T.astype(jnp.bfloat16)
    turn(keys[:REGION, :], turned)
    widen(values[:REGION, :], wide)
    first, guest, source = jnp.int32(-1), jnp.int32(-1), jnp.int32(0)
    for r in range(REQUESTS):
        owner = hits[r]
        here = (ranks[r] == 1) & (host[owner] == chip)
        first = jnp.where((ranks[r] == 0) & (owner == me), r, first)
        guest = jnp.where(here, r, guest)
        source = jnp.where(here, owner, source)
    core = me % 2
    from_first_core = jnp.where(source == 2 * chip, 1, 0)
    way = (source // 2) ^ chip
    keys_way = jnp.where(core == 1, way, 0)
    values_way = jnp.where(core == 0, way, 0) if split else keys_way
    strips_of[2:3, :] = jnp.full((1, HD), keys_way)
    strips_of[3:4, :] = jnp.full((1, HD), values_way)
    from_other = jnp.where(core == from_first_core, 1, 0)
    plan[0] = from_other
    plan[1] = jnp.where(way > 0, core, from_other) if split else from_other
    for job, found in enumerate((first, guest)):
        request = jnp.maximum(found, 0)
        limit = prefix_len[request]
        strips = jnp.clip((limit + STRIP - 1) // STRIP, 1, REGION // STRIP)
        strips_of[job : job + 1, :] = jnp.full((1, HD), jnp.where(found >= 0, strips, 0))
        cached[job : job + 1, :] = jnp.where(iota((1, REGION), 1) < limit, 0.0, FLOOR)
        prompt_rows(devices, prompt, span, request, job, True)


def turn(keys, turned):
    for n in range(0, REGION, STRIP):
        turned[:, n : n + STRIP] = keys[n : n + STRIP].T


def widen(values, wide):
    wide[:, :HD] = values
    wide[:, HD:] = jnp.ones((REGION, HD), jnp.bfloat16)


def host_kernel(prepare, at, devices, hit_count, plan, mine, other, out):
    for choice, rows in enumerate((mine, other)):

        @pl.when(plan[at] == choice)
        def _():
            prepare(rows[...], out)


def guest_attend_kernel(
    devices, hit_count, strips_of, prompt_mask, cached_mask, got, turned, wide, *refs
):
    turned_guest, wide_guest, out = refs
    jobs = [
        (0, 0, HALF, turned, wide),
        (WIDE + HD, WIDE, HALF // 2, turned_guest, wide_guest),
    ]
    for job, (base, first, blocks, keys, values) in enumerate(jobs):
        strips = strips_of[job, 0]

        @pl.when(strips == 0)
        def _():
            empty = jnp.zeros((devices * MSG, blocks * HD), jnp.bfloat16)
            out[:, first : first + blocks * HD] = empty

        for count in range(1, REGION // STRIP + 1):

            @pl.when(strips == count)
            def _():
                whole = (count - 1) * STRIP
                mask = prompt_mask[job * devices * MSG : (job + 1) * devices * MSG, :]
                attend_rows(
                    got,
                    base,
                    blocks,
                    slice(0, devices * MSG),
                    prompt_parts(got[:, base + blocks * HD : base + (blocks + 1) * HD]),
                    mask,
                    cached_mask[job : job + 1, whole : whole + STRIP],
                    keys[:, : whole + STRIP],
                    values[: whole + STRIP, :],
                    out,
                    first,
                )


def prompt_parts(rows):
    height = rows.shape[0]
    wide = rows.astype(jnp.float32)
    moved = pltpu.roll(wide, height - TOK_REQ, 0).astype(jnp.bfloat16)
    values = jnp.concatenate([moved, jnp.ones((height, HD), jnp.bfloat16)], axis=1)
    return wide.T.astype(jnp.bfloat16), values


def attend_rows(
    got, base, blocks, here, prompt, mask, tail_mask, keys, values, out, first
):
    prompt_keys, prompt_values = prompt
    factor = SCALE * math.log2(math.e)
    mask = jnp.concatenate([mask, mask], axis=0)
    height = mask.shape[0] // 2

    def scores(c):
        pair = jnp.concatenate(
            [got[here, base + (c + n) * HD : base + (c + n + 1) * HD] for n in range(2)], axis=0
        )
        cached = dot(pair, keys, NN)
        whole = cached.shape[1] - STRIP
        tail = cached[:, whole:] + tail_mask
        cached = jnp.concatenate([cached[:, :whole], tail], axis=1) if whole else tail
        return [cached, dot(pair, prompt_keys, NN) + mask]

    parts = scores(0)
    for c in range(0, blocks, 2):
        later = scores(c + 2) if c + 2 < blocks else None
        top = lanes_max(parts)
        parts = [jnp.exp2((x - top) * factor).astype(jnp.bfloat16) for x in parts]
        summed = dot(parts[0], values, NN) + dot(parts[1], prompt_values, NN)
        result = (summed[:, :HD] / summed[:, HD:]).astype(jnp.bfloat16)
        for n in range(2):
            column = first + (c + n) * HD
            out[here, column : column + HD] = result[n * height : (n + 1) * height]
        parts = later


def guest_unpack_kernel(devices, hit_count, picks, picks_guest, outs, result, held, sems):
    half = WIDE // 2
    copies = []
    for n in range(2):
        own = dot(picks[n * ROWS : (n + 1) * ROWS, :], outs[:, :WIDE], NN)
        for g in (2 * n, 2 * n + 1):
            guest = dot(picks_guest[g * ROWS : (g + 1) * ROWS, :], outs[:, WIDE:], NN)
            rows = own[:, g % 2 * half : (g % 2 + 1) * half] + guest
            held[:, g * half : (g + 1) * half] = rows.astype(jnp.bfloat16)
        here = pl.ds(n * WIDE, WIDE)
        copies.append(pltpu.make_async_copy(held.at[:, here], result.at[:, here], sems.at[n]))
        copies[n].start()
    for copy in copies:
        copy.wait()


def unpack_kernel(devices, hit_count, picks, *refs):
    outs, logs, result = refs[0], refs[1:-1], refs[-1]

    def chosen(s, i):
        place = s * hit_count + i
        return picks[place * 2 * ROWS : (place + 1) * 2 * ROWS, :]

    def rows_of(i):
        parts = [
            dot(chosen(s, i), outs[:, s * WIDE : (s + 1) * WIDE], NN)
            for s in range(CAP)
        ]
        return sum(parts[1:], parts[0])

    def logs_of(i):
        parts = [
            dot(
                chosen(s, i).astype(jnp.float32),
                logs[0][:, s * HD : (s + 1) * HD],
                NN,
                precision=lax.Precision.HIGHEST,
            )
            for s in range(CAP)
        ]
        return sum(parts[1:], parts[0])

    if hit_count == 1:
        joined = rows_of(0)
    else:
        levels = [logs_of(i) for i in range(hit_count)]
        top = functools.reduce(jnp.maximum, levels)
        shares = [jnp.exp(level - top) for level in levels]
        total = sum(shares[1:], shares[0])
        pieces = [rows_of(i) for i in range(hit_count)]
        columns = []
        for c in range(HALF):
            part = sum(
                shares[i][:, c : c + 1] * pieces[i][:, c * HD : (c + 1) * HD]
                for i in range(hit_count)
            )
            columns.append(part / total[:, c : c + 1])
        joined = jnp.concatenate(columns, axis=1)
    joined = joined.astype(jnp.bfloat16)
    result[:, :WIDE] = joined[:ROWS]
    result[:, WIDE:] = joined[ROWS:]


def vmem(count):
    return [pl.BlockSpec(memory_space=pltpu.VMEM)] * count


def smem(count):
    return [pl.BlockSpec(memory_space=pltpu.SMEM)] * count


def hbm(count):
    return [pl.BlockSpec(memory_space=pltpu.HBM)] * count


def body(prefix_len, hits, span_block, queries, fresh_keys, fresh_values, cache_keys, cache_values):
    devices = lax.axis_size("cache")
    hit_count = hits.shape[1]
    rows = devices * MSG
    owners = hits.reshape(REQUESTS * hit_count)
    fresh = (owners, queries, fresh_keys, fresh_values)

    def exchange(x):
        return lax.all_to_all(x, "cache", split_axis=0, concat_axis=0, tiled=True)

    def call(kernel, out_shape, name, grant=40, **kw):
        return pl.pallas_call(
            functools.partial(kernel, devices, hit_count),
            out_shape=[
                jax.ShapeDtypeStruct(*leaf) if isinstance(leaf, tuple) else leaf
                for leaf in out_shape
            ],
            compiler_params=pltpu.CompilerParams(vmem_limit_bytes=grant * 2**20),
            name=name,
            **kw,
        )

    if hit_count == 1 and devices == 16:
        pairs = rows * (HALF + HALF // 2) * (REGION + rows)
        scalars = [pltpu.SMEM((devices,), jnp.int32)] * 2
        send, places, way = call(
            guest_pack_kernel,
            [
                pltpu.VMEM((rows, GUEST_MSG), jnp.bfloat16),
                ((2, 4 * ROWS), jnp.int32),
                ((1,), jnp.int32),
            ],
            "pack",
            in_specs=hbm(5),
            out_specs=vmem(2) + smem(1),
            scratch_shapes=[
                pltpu.VMEM((2 * ROWS, WIDE + HD), jnp.bfloat16),
                *[pltpu.SMEM((REQUESTS,), jnp.int32)] * 2,
                *scalars,
                pltpu.SemaphoreType.DMA((8,)),
            ],
        )(
            *(
                pltpu.with_memory_space_constraint(x, pltpu.HBM)
                for x in (owners, prefix_len, queries, fresh_keys, fresh_values)
            )
        )
        got = exchange(send)
        shapes = [((HD, REGION), jnp.bfloat16), ((REGION, 2 * HD), jnp.bfloat16)]
        def chain(form, owners, prefix_len, span_block, places, cache_keys, cache_values):
            ways, height, split = form

            pinned = [
                pltpu.with_memory_space_constraint(x, pltpu.HBM)
                for x in (owners, prefix_len, span_block)
            ]
            slots = [cache_keys[REGION:], cache_values[REGION:]]
            lent = []
            for n in ways:
                ends = [(d, d ^ (2 * n)) for d in range(devices)]
                sent = [x[:height] for x in slots]
                if split:
                    sent[1] = lax.ppermute(sent[1], "cache", [(d, d - 1) for d in range(1, devices, 2)])
                lent.append(
                    [
                        lax.ppermute(sent[0], "cache", ends[1::2]),
                        lax.ppermute(sent[1], "cache", ends[0::2] if split else ends[1::2]),
                    ]
                )
            prepared = call(
                functools.partial(guest_prep_kernel, split),
                [((2,), jnp.int32), ((2 * rows, rows), jnp.float32), ((2, REGION), jnp.float32)]
                + shapes
                + [((2 * ROWS, rows), jnp.bfloat16), ((4 * ROWS, rows), jnp.bfloat16)]
                + [((8, HD), jnp.int32)],
                "prep",
                grant=12,
                in_specs=smem(2) + vmem(4),
                out_specs=smem(1) + vmem(7),
                scratch_shapes=scalars,
                cost_estimate=pl.CostEstimate(
                    flops=10**6, bytes_accessed=2**22, transcendentals=0
                ),
            )(*pinned, places, cache_keys, cache_values)
            plan, chosen = prepared[0], prepared[-1]
            for n, borrowed in zip(ways, lent):
                slots = [
                    jnp.where(
                        chosen[at : at + 1] == n, jnp.pad(x, ((0, REGION - height), (0, 0))), y
                    )
                    for at, x, y in zip((2, 3), borrowed, slots)
                ]
            swapped = [lax.ppermute(x, "cache", [(d, d ^ 1) for d in range(devices)]) for x in slots]
            guest = [
                call(
                    functools.partial(host_kernel, prepare, at),
                    [shape],
                    "host",
                    grant=12,
                    in_specs=smem(1) + vmem(2),
                    out_specs=vmem(1),
                )(plan, mine, other)[0]
                for prepare, at, shape, mine, other in zip(
                    (turn, widen), (0, 1), shapes, slots, swapped
                )
            ]
            return (*prepared[1:], *guest)

        forms = [
            ((), REGION, False),
            ((1,), 2 * STRIP, False),
            ((1,), 3 * STRIP, True),
            ((1,), REGION, True),
            ((2,), 2 * STRIP, False),
            ((2,), 3 * STRIP, True),
            ((2,), REGION, True),
            ((1, 2, 3), REGION, False),
        ]
        prepared = lax.switch(
            way.reshape(()),
            [functools.partial(chain, form) for form in forms],
            owners,
            prefix_len,
            span_block,
            places,
            cache_keys,
            cache_values,
        )
        prompt_mask, cached_mask, turned, wide, picks, picks_guest, strips_of = prepared[:7]
        turned_guest, wide_guest = prepared[7:]
        (answer,) = call(
            guest_attend_kernel,
            [((rows, WIDE + WIDE // 2), jnp.bfloat16)],
            "attend",
            in_specs=vmem(8),
            out_specs=vmem(1),
            cost_estimate=pl.CostEstimate(
                flops=4 * pairs * HD, bytes_accessed=8 * rows * WIDE, transcendentals=pairs
            ),
        )(strips_of, prompt_mask, cached_mask, got, turned, wide, turned_guest, wide_guest)
        return call(
            guest_unpack_kernel,
            [((ROWS, HEADS * HD), jnp.bfloat16)],
            "unpack",
            in_specs=vmem(3),
            out_specs=hbm(1),
            scratch_shapes=[
                pltpu.VMEM((ROWS, HEADS * HD), jnp.bfloat16),
                pltpu.SemaphoreType.DMA((2,)),
            ],
        )(picks, picks_guest, exchange(answer))[0]
    send, places = call(
        pack_kernel,
        [((rows, CAP * (WIDE + HD)), jnp.bfloat16), ((CAP * hit_count, 2 * ROWS), jnp.int32)],
        "pack",
        in_specs=hbm(4),
        out_specs=vmem(2),
        scratch_shapes=[
            pltpu.VMEM((2 * ROWS, WIDE + HD), jnp.bfloat16),
            pltpu.SMEM((REQUESTS * hit_count,), jnp.int32),
            pltpu.SMEM((devices,), jnp.int32),
            pltpu.SemaphoreType.DMA((5,)),
        ],
    )(*(pltpu.with_memory_space_constraint(x, pltpu.HBM) for x in fresh))
    got = exchange(send)
    busy, prompt_mask, cached_mask, turned, wide, picks = call(
        prep_kernel,
        [
            ((CAP,), jnp.int32),
            ((CAP * rows, rows), jnp.float32),
            ((CAP, REGION), jnp.float32),
            ((HD, CAP * REGION), jnp.bfloat16),
            ((CAP * REGION, 2 * HD), jnp.bfloat16),
            ((CAP * hit_count * 2 * ROWS, rows), jnp.bfloat16),
        ],
        "prep",
        in_specs=smem(2) + vmem(4),
        out_specs=smem(1) + vmem(5),
        cost_estimate=pl.CostEstimate(flops=10**6, bytes_accessed=2**22, transcendentals=0),
    )(owners, prefix_len, span_block, places, cache_keys, cache_values)
    pairs = CAP * rows * HALF * (REGION + rows)
    answers = call(
        attend_kernel,
        [((rows, CAP * WIDE), jnp.bfloat16)]
        + [((rows, CAP * HD), jnp.float32)] * (hit_count > 1),
        "attend",
        in_specs=smem(1) + vmem(5),
        out_specs=vmem(1 + (hit_count > 1)),
        cost_estimate=pl.CostEstimate(
            flops=4 * pairs * HD, bytes_accessed=8 * rows * WIDE, transcendentals=pairs
        ),
    )(busy, prompt_mask, cached_mask, got, turned, wide)
    returned = [exchange(answer) for answer in answers]
    return call(
        unpack_kernel,
        [((ROWS, HEADS * HD), jnp.bfloat16)],
        "unpack",
        in_specs=vmem(1 + len(returned)),
        out_specs=vmem(1),
    )(picks, *returned)[0]


def solution(mesh):
    in_specs = (
        P("groups"),
        P("groups", None),
        P("groups", None),
        P(("groups", "cache"), None),
        P(("groups", "cache"), None),
        P(("groups", "cache"), None),
        P(("groups", "cache"), None),
        P(("groups", "cache"), None),
    )
    out_specs = P(("groups", "cache"), None)
    return jax.shard_map(body, mesh=mesh, in_specs=in_specs, out_specs=out_specs, check_vma=False)
```
